32 devices in a mesh: star: 4 (over y, x), tm: 8 (over z, core).
Axes of the slice: x: 2, y: 2, z: 4, core: 2. Of those that a mesh axis runs over, the one named last changes fastest.
Arguments:
- astro_coef: float32 [4, 5, 8192], P('star', None, 'tm'), may hold values from -1.5 to 1.5
- star_index: int32 [4, 8192], P('star', 'tm'), may hold values from 0 to 2047
- att_coef: float32 [4, 64, 64, 128], P('star', 'tm'), may hold values from -0.26516503 to 0.26516503
- att_start: int32 [4, 64], P('star', 'tm'), may hold values from 0 to 255, as said below
- inst_coef: float32 [4, 6, 8192], P('star', None, 'tm'), may hold values from -0.61237246 to 0.61237246
- inst_index: int32 [4, 6, 8192], P('star', None, 'tm'), may hold values from 0 to 1023
- observed: float32 [4, 8192], P('star', 'tm'), may hold values from -6 to 6
Outputs:
- solution_astro: float32 [5, 8192], P(None, ('star', 'tm'))
- solution_att: float32 [2048], P('tm')
- solution_inst: float32 [1024], replicated
The draws below stay inside these ranges and needn't reach their ends.
Inputs may be any that keep to these rules, and one draw needn't show every extreme that they name: `att_start`: within each time range, block b starts between 32 * b and 32 * b + 31, so starts increase with the block; the last block of every range starts at 255, so its unknowns run into the next time range.
All inputs are finite; a program needn't handle non-finite values.
Results may differ from the reference program's by a relative error of at most 0.00021.
Values sent between devices are 32-bit elements; how exact they have to be, the bound alone decides.
No kernel may reach another device: no remote copies, remote signals or barrier semaphores. Data moves between devices by JAX's collectives and lax.ppermute only.
A program may use at most 64 MiB of HBM per device.

```python
import jax
import jax.numpy as jnp
from jax import lax

BLK_DEV = 8
STARS_DEV = 2048
BROWS = 128
ATT_W = 64
STEP = 32
ASTRO = 5
NIC = 6
NINST = 1024
ITERS = 3
ROWS_DEV = 1024
ATT_DEV = 256
GROUPS = 4
BLOCKS_T = 64
ROWS_T = 8192
STARS = 8192
ATT = 2048
N_STAR = 4
DEVICES = 32


def draw_att_start(key, part):
    local_block = jnp.arange(BLOCKS_T, dtype=jnp.int32) % BLK_DEV
    jitter = jax.random.randint(jax.random.fold_in(key, 17), (GROUPS, BLOCKS_T), 0, STEP, dtype=jnp.int32)
    jitter = jnp.where(local_block[None, :] == BLK_DEV - 1, STEP - 1, jitter)
    return (local_block[None, :] * STEP + jitter).astype(jnp.int32)


def with_ends(result, key, least, top_value):
    longest = result.shape.index(max(result.shape))
    spots = []
    for shift in (0, 1):
        where = [jax.random.randint(jax.random.fold_in(key, axis), (), 0, length) for axis, length in enumerate(result.shape)]
        where[longest] = (where[longest] + shift) % result.shape[longest]
        spots.append(tuple(where))
    return result.at[spots[0]].set(least).at[spots[1]].set(top_value)


def block_scale(key, dims, cuts, least, largest):
    def one(dim, blocks):
        draws = jax.random.uniform(jax.random.fold_in(jax.random.fold_in(key, 6), dim), (blocks,), jnp.float32, least / len(cuts), largest / len(cuts))
        return jnp.repeat(jnp.exp(draws), dims[dim] // blocks).reshape((-1,) + (1,) * (len(dims) - dim - 1))

    loudness = one(*cuts[0])
    for cut in cuts[1:]:
        loudness = loudness * one(*cut)
    return loudness


def bell_draw(own_key, extent, spread, bound, pieces=(), held_as=jnp.bfloat16):
    result = jax.random.normal(own_key, extent, jnp.float32) * spread
    if len(pieces) > 0:
        result = block_scale(own_key, extent, pieces, -0.22, 0.18) * result
    return jnp.clip(result, min=-bound, max=bound).astype(held_as)


def setup_inputs(seed: int = 0) -> dict:
    keys = jax.random.split(jax.random.key(seed), 8)
    return {
        "astro_coef": bell_draw(keys[0], (GROUPS, ASTRO, ROWS_T), 0.25, 1.5, ((0, 4), (2, 8)), jnp.float32),
        "star_index": with_ends(jax.random.randint(keys[1], (GROUPS, ROWS_T), 0, STARS_DEV), jax.random.fold_in(keys[1], 1), 0, STARS_DEV - 1).astype(jnp.int32),
        "att_coef": bell_draw(keys[2], (GROUPS, BLOCKS_T, ATT_W, BROWS), ((2.0 / (256 * N_STAR)) ** 0.5), 0.26516503, ((0, 4), (1, 8)), jnp.float32),
        "att_start": draw_att_start(jax.random.fold_in(keys[7], 71), 0),
        "inst_coef": bell_draw(keys[4], (GROUPS, NIC, ROWS_T), ((2.0 * NINST / (NIC * DEVICES * ROWS_DEV)) ** 0.5), 0.61237246, ((0, 4), (2, 8)), jnp.float32),
        "inst_index": with_ends(jax.random.randint(keys[5], (GROUPS, NIC, ROWS_T), 0, NINST), jax.random.fold_in(keys[5], 1), 0, NINST - 1).astype(jnp.int32),
        "observed": bell_draw(keys[6], (GROUPS, ROWS_T), 1.0, 6.0, ((0, 4), (1, 8)), jnp.float32),
    }


epsilon = 1e-06

def reference(astro_coef, star_index, att_coef, att_start, inst_coef, inst_index, observed):
    highest = lax.Precision.HIGHEST
    offsets = jnp.arange(BLOCKS_T, dtype=jnp.int32) // BLK_DEV * ATT_DEV
    columns = att_start[:, :, None] + offsets[None, :, None] + jnp.arange(ATT_W, dtype=jnp.int32)[None, None, :]
    gstars = star_index + (jnp.arange(GROUPS, dtype=jnp.int32) * STARS_DEV)[:, None]

    def forward(basis):
        basis_astro, basis_att, basis_inst = basis
        extended = jnp.concatenate([basis_att, jnp.zeros((ATT_W,), jnp.float32)])

        def per_group(packed):
            coeffs, cols_here = packed
            windows = extended[cols_here]
            return jnp.einsum('bj,bjr->br', windows, coeffs, precision=highest).reshape(-1)
        y_att = lax.map(per_group, (att_coef, columns))
        picked = jnp.take(basis_astro, gstars, axis=1)
        y_astro = lax.optimization_barrier(jnp.sum(astro_coef * jnp.moveaxis(picked, 0, 1), axis=1))
        y_inst = lax.optimization_barrier(jnp.sum(inst_coef * basis_inst[inst_index], axis=1))
        return y_astro + y_att + y_inst

    def backward(left_vec):
        weighted = jnp.moveaxis(astro_coef * left_vec[:, None, :], 1, 0)
        flat_stars = gstars.reshape(-1)

        def astro_one(values):
            return jax.ops.segment_sum(values.reshape(-1), flat_stars, num_segments=STARS)
        part_astro = jax.vmap(astro_one)(weighted)

        def per_group(packed):
            coeffs, cols_here, rows_here = packed
            contrib = jnp.einsum('bjr,br->bj', coeffs, rows_here.reshape(BLOCKS_T, BROWS), precision=highest)
            return jax.ops.segment_sum(contrib.reshape(-1), cols_here.reshape(-1), num_segments=ATT + ATT_W)
        part_att = lax.optimization_barrier(jnp.sum(lax.map(per_group, (att_coef, columns, left_vec)), axis=0))[:ATT]
        part_inst = jax.ops.segment_sum((inst_coef * left_vec[:, None, :]).reshape(-1), inst_index.reshape(-1), num_segments=NINST)
        return (part_astro, part_att, part_inst)

    def squares(parts):
        return sum((jnp.sum(piece * piece) for piece in parts))
    beta_norm = jnp.sqrt(jnp.sum(observed * observed) + epsilon)
    left_vec = observed / beta_norm
    basis = backward(left_vec)
    alpha_norm = jnp.sqrt(squares(basis) + epsilon)
    basis = jax.tree.map(lambda piece: piece / alpha_norm, basis)
    search = basis
    solution = jax.tree.map(jnp.zeros_like, basis)
    phi_bar = beta_norm
    rho_bar = alpha_norm
    for iteration in range(ITERS):
        left_vec = forward(basis) - alpha_norm * left_vec
        beta_norm = jnp.sqrt(jnp.sum(left_vec * left_vec) + epsilon)
        left_vec = left_vec / beta_norm
        back = backward(left_vec)
        basis = jax.tree.map(lambda new, old: new - beta_norm * old, back, basis)
        alpha_norm = jnp.sqrt(squares(basis) + epsilon)
        basis = jax.tree.map(lambda piece: piece / alpha_norm, basis)
        rho_now = jnp.sqrt(rho_bar * rho_bar + beta_norm * beta_norm)
        cosine = rho_bar / rho_now
        sine_val = beta_norm / rho_now
        theta_val = sine_val * alpha_norm
        rho_bar = -cosine * alpha_norm
        phi_now = cosine * phi_bar
        phi_bar = sine_val * phi_bar
        solution = jax.tree.map(lambda sol, dirn: sol + phi_now / rho_now * dirn, solution, search)
        search = jax.tree.map(lambda new, dirn: new - theta_val / rho_now * dirn, basis, search)
    return (solution[0], solution[1], solution[2])
```

```python
import functools

import jax
import jax.numpy as jnp
from jax import lax
from jax.experimental import pallas as pl
from jax.experimental.pallas import tpu as pltpu
from jax.sharding import PartitionSpec as P

STARS_DEV = 2048
NINST = 1024
ITERS = 3
ATT_DEV = 256
LANES = 128

epsilon = 1e-06
f32 = jnp.float32
bf16 = jnp.bfloat16
VMEM_LIMIT = 40 * 1024 * 1024


def halves(value):
    top = value.astype(bf16).astype(f32)
    return top, (value - top).astype(bf16).astype(f32)


def dot_lanes(left, right):
    return lax.dot_general(left, right, (((1,), (1,)), ((), ())), preferred_element_type=f32)


def dot_plain(left, right):
    return lax.dot_general(left, right, (((1,), (0,)), ((), ())), preferred_element_type=f32)


def lane_pick(row, lane_index):
    table = jnp.broadcast_to(row, lane_index.shape)
    return jnp.take_along_axis(table, lane_index, axis=1, mode="promise_in_bounds")


def table_pick(rows, index):
    high, low = index >> 7, index & (LANES - 1)
    total = jnp.zeros(index.shape, f32)
    for place, row in enumerate(rows):
        total = jnp.where(high == place, lane_pick(row, low), total)
    return total


def one_hot_low(index_row):
    shape = (LANES, LANES)
    low = jnp.broadcast_to(index_row & (LANES - 1), shape)
    hit = lax.broadcasted_iota(jnp.int32, shape, 0) == low
    return jnp.where(hit, 1.0, 0.0).astype(bf16)


def spread_high(index_row, value_row, count):
    shape = (count, LANES)
    high = jnp.broadcast_to(index_row >> 7, shape)
    hit = lax.broadcasted_iota(jnp.int32, shape, 0) == high
    return jnp.where(hit, jnp.broadcast_to(value_row, shape), 0.0)


def block_masks(blocks, width):
    shape = (blocks, LANES)
    row = lax.broadcasted_iota(jnp.int32, shape, 0)
    lane = lax.broadcasted_iota(jnp.int32, shape, 1)
    per_tile = LANES // width
    tiles = blocks // per_tile
    return [row == tile * per_tile + lane // width for tile in range(tiles)], row, lane


def inst_back(rows, coef_ref, index_ref, table_ref, spread_ref):
    slots, blocks, _ = coef_ref.shape
    count = NINST // LANES
    for slot in range(slots):
        top, rest = halves(coef_ref[slot] * rows)
        index = index_ref[slot]
        for block in range(blocks):
            here = slice(block, block + 1)
            pieces = [spread_high(index[here], part[here], count) for part in (top, rest)]
            at = (slot * blocks + block) * LANES
            spread_ref[:, at : at + LANES] = jnp.concatenate(pieces, axis=0).astype(bf16)
    both = dot_lanes(spread_ref[...], table_ref[...])
    return both[:count] + both[count:]


def att_back(rows, att2, starts, width):
    blocks = rows.shape[0]
    size = att2.shape[0] // 2
    top, rest = halves(rows)
    both = dot_lanes(jnp.concatenate([top, rest], axis=0).astype(bf16), att2)
    both = both[:blocks] + both[blocks:]
    both = both[:, :size] + both[:, size:]
    masks, row, lane = block_masks(blocks, width)
    own = jnp.zeros((blocks, LANES), f32)
    for tile, mask in enumerate(masks):
        own = own + jnp.where(mask, both[:, tile * LANES : (tile + 1) * LANES], 0.0)
    shift = (row % (LANES // width)) * width
    out = []
    for tile in range((ATT_DEV + width + LANES - 1) // LANES):
        offset = lane + tile * LANES - starts
        inside = (offset >= 0) & (offset < width)
        picked = jnp.take_along_axis(
            own, jnp.where(inside, offset + shift, 0), axis=1, mode="promise_in_bounds"
        )
        out.append(jnp.sum(jnp.where(inside, picked, 0.0), axis=0, keepdims=True))
    return jnp.concatenate(out, axis=0)


def att_forward(att_rows, att2, starts, width):
    blocks = starts.shape[0]
    masks, row, lane = block_masks(blocks, width)
    tiles = [att_rows[tile : tile + 1] for tile in range(att_rows.shape[0])]
    window = table_pick(tiles, starts + lane % width)
    wide = jnp.concatenate([jnp.where(mask, window, 0.0) for mask in masks], axis=1)
    top, rest = halves(wide)
    left = jnp.concatenate([top, rest], axis=0).astype(bf16)
    both = dot_plain(jnp.concatenate([left, left], axis=1), att2)
    return both[:blocks] + both[blocks:]


def first_kernel(width, b_ref, astro_ref, star_ref, att_ref, starts_ref, coef_ref, index_ref,
                 send_ref, table_ref, att2_ref, spread_ref):
    rows = b_ref[...]
    blocks = rows.shape[0]
    slots = coef_ref.shape[0]
    comps = astro_ref.shape[0]
    for slot in range(slots):
        index = index_ref[slot]
        for block in range(blocks):
            at = (slot * blocks + block) * LANES
            table_ref[:, at : at + LANES] = one_hot_low(index[block : block + 1])
    att = att_ref[...]
    top = att.astype(bf16)
    att2_ref[...] = jnp.concatenate([top, (att - top.astype(f32)).astype(bf16)], axis=0)
    starts = jnp.broadcast_to(starts_ref[...], (blocks, LANES))
    send_ref[0:blocks] = rows
    send_ref[8:16] = inst_back(rows, coef_ref, index_ref, table_ref, spread_ref)
    send_ref[16:19] = att_back(rows, att2_ref[...], starts, width)
    send_ref[19:20] = jnp.sum(rows * rows, axis=0, keepdims=True)
    send_ref[20:24] = jnp.zeros((4, LANES), f32)
    for comp in range(comps):
        send_ref[24 + comp * 8 : 32 + comp * 8] = astro_ref[comp]
    send_ref[24 + comps * 8 : 32 + comps * 8] = star_ref[...].astype(f32)


def group_kernel(order, count, *refs):
    ins, out_ref = refs[:-1], refs[-1]
    me = lax.axis_index("tm")
    def part(device, start, size):
        if order == "all":
            return ins[0][device, start : start + size]
        return ins[device][start : start + size]
    total = part(0, 8, 8)
    scalars = part(0, 16, 8)
    lane = lax.broadcasted_iota(jnp.int32, (8, LANES), 1)
    row = lax.broadcasted_iota(jnp.int32, (8, LANES), 0)
    zero = jnp.zeros((8, LANES), f32)
    mine, prev, after = zero, zero, zero
    for device in range(count):
        low = part(device, 16, 8)
        who = device if order == "all" else me ^ device
        mine = jnp.where(who == me, low, mine)
        prev = jnp.where(who == me - 1, low, prev)
        after = jnp.where(who == me + 1, low, after)
    if order == "all":
        for device in range(1, count):
            total = total + part(device, 8, 8)
            scalars = scalars + part(device, 16, 8)
    else:
        totals = [part(device, 8, 8) for device in range(count)]
        lows = [part(device, 16, 8) for device in range(count)]
        while len(totals) > 1:
            totals = [totals[i] + totals[i + 1] for i in range(0, len(totals), 2)]
            lows = [lows[i] + lows[i + 1] for i in range(0, len(lows), 2)]
        total, scalars = totals[0], lows[0]
    half = lane[:1] < 64
    first = mine[0:1] + jnp.where(half, prev[2:3], 0.0)
    last = jnp.where(half & (me < count - 1), mine[2:3] + after[0:1], 0.0)
    out_ref[0:8] = total
    out_ref[8:16] = jnp.concatenate([first, mine[1:2], last, scalars[3:8]], axis=0)


def astro_kernel(first, order, count, *refs):
    high = STARS_DEV // LANES
    if first:
        all_ref, out_ref, table_ref, spread_ref = refs
        ins, rows_at = [all_ref], 0
    else:
        all_ref, table_ref, *ins, out_ref, spread_ref = refs
    comps = (all_ref.shape[1] - 24) // 8 - 1
    me = lax.axis_index("tm")

    def one(device, total):
        if order == "all":
            rows = ins[0][device, 0:8]
            where = device
        else:
            rows = ins[device][0:8]
            where = me ^ device
        packed = all_ref[where, 24:]
        index = packed[comps * 8 :].astype(jnp.int32)
        at0 = pl.multiple_of(where * 8 * LANES, 8 * LANES)
        split = [halves(packed[comp * 8 : comp * 8 + 8] * rows) for comp in range(comps)]
        for block in range(8):
            here = slice(block, block + 1)
            if first:
                table_ref[:, pl.ds(at0 + block * LANES, LANES)] = one_hot_low(index[here])
            pieces = []
            for part in range(2):
                for comp in range(comps):
                    pieces.append(spread_high(index[here], split[comp][part][here], high))
            spread_ref[:, block * LANES : (block + 1) * LANES] = jnp.concatenate(
                pieces, axis=0
            ).astype(bf16)
        return total + dot_lanes(spread_ref[...], table_ref[:, pl.ds(at0, 8 * LANES)])

    total = jnp.zeros((2 * comps * high, LANES), f32)
    if order == "all":
        total = lax.fori_loop(0, count, one, total)
    else:
        for device in range(count):
            total = one(device, total)
    out_ref[...] = total[: comps * high] + total[comps * high :]


def lane_sum(row):
    return jnp.broadcast_to(jnp.sum(row, axis=1, keepdims=True), row.shape)


def star_total(order, count, refs):
    if order == "all":
        total = refs[0][0]
        for device in range(1, count):
            total = total + refs[0][device]
        return total
    totals = [ref[...] for ref in refs]
    while len(totals) > 1:
        totals = [totals[i] + totals[i + 1] for i in range(0, len(totals), 2)]
    return totals[0]


def next_bidiagonal(total, state):
    squares, mixed, size = (lane_sum(total[row : row + 1]) for row in (11, 12, 13))
    alpha2 = size + epsilon
    alpha = jnp.sqrt(alpha2)
    rest = jnp.maximum(squares / alpha2 - 2.0 * mixed + alpha2 * state[0:1], 0.0)
    beta2 = rest + epsilon
    return alpha, jnp.sqrt(beta2), rest / beta2


def step_kernel(step, width, order, tm_count, star_count, *refs):
    (astro_ref, star_ref, att2_ref, starts_ref, coef_ref, index_ref, table_ref,
     sum_ref, rows_ref) = refs[:9]
    refs = refs[9:]
    if step > 0:
        state_ref, old_z_ref, old_g_ref, old_u_ref = refs[:4]
        refs = refs[4:]
    gathered = refs[: 1 if order == "all" else star_count]
    refs = refs[len(gathered) :]
    send_ref, state_out, z_ref, g_ref, u_ref, s_ref, spread_ref = refs
    comps, blocks, _ = astro_ref.shape
    high = STARS_DEV // LANES
    total = star_total(order, star_count, gathered)
    back = jnp.concatenate([sum_ref[...], total[0:8], total[8:16]], axis=0)
    if step == 0:
        squares = lane_sum(total[11:12])
        beta2 = squares + epsilon
        beta = jnp.sqrt(beta2)
        u = rows_ref[...] / beta
        g = back / beta
        z = g
        state_out[...] = jnp.concatenate(
            [squares / beta2, beta, jnp.zeros((14, LANES), f32)], axis=0
        )
        left2 = squares / beta2
    else:
        state = state_ref[...]
        alpha, beta, left2 = next_bidiagonal(total, state)
        u = (rows_ref[...] / alpha - alpha * old_u_ref[...]) / beta
        g = (back / alpha - alpha * old_g_ref[...]) / beta
        z = g - (beta / alpha) * old_z_ref[...]
        pieces = [left2, state[1 : 1 + step], beta]
        pieces += [jnp.zeros((7 - step, LANES), f32)] + ([state[9 : 8 + step]] if step > 1 else [])
        pieces += [alpha, jnp.zeros((15 - 8 - step + 1 - 1, LANES), f32)]
        state_out[...] = jnp.concatenate(pieces, axis=0)
    z_ref[...] = z
    g_ref[...] = g
    u_ref[...] = u
    base = comps * high
    inst_rows = z[base : base + 8]
    att_rows = z[base + 8 : base + 11]
    starts = jnp.broadcast_to(starts_ref[...], (blocks, LANES))
    rows = att_forward(att_rows, att2_ref[...], starts, width)
    star = star_ref[...]
    star_high, star_low = star >> 7, star & (LANES - 1)
    for comp in range(comps):
        picked = jnp.zeros((blocks, LANES), f32)
        for place in range(high):
            at = comp * high + place
            picked = jnp.where(star_high == place, lane_pick(z[at : at + 1], star_low), picked)
        rows = rows + astro_ref[comp] * picked
    pieces = [inst_rows[place : place + 1] for place in range(8)]
    for slot in range(coef_ref.shape[0]):
        rows = rows + coef_ref[slot] * table_pick(pieces, index_ref[slot])
    s_ref[...] = rows
    send_ref[0:8] = rows
    send_ref[19:20] = jnp.sum(rows * rows, axis=0, keepdims=True)
    send_ref[20:21] = jnp.sum(rows * u, axis=0, keepdims=True)
    astro_z = z[:base]
    size = jnp.sum(astro_z * astro_z, axis=0, keepdims=True) * (1.0 / tm_count)
    own = att_rows[: ATT_DEV // LANES]
    size = size + jnp.sum(own * own, axis=0, keepdims=True) * (1.0 / star_count)
    size = size + jnp.sum(inst_rows * inst_rows, axis=0, keepdims=True) * (
        1.0 / (star_count * tm_count)
    )
    send_ref[21:22] = size
    send_ref[22:24] = jnp.zeros((2, LANES), f32)
    if step < ITERS - 1:
        send_ref[8:16] = inst_back(rows, coef_ref, index_ref, table_ref, spread_ref)
        send_ref[16:19] = att_back(rows, att2_ref[...], starts, width)
    else:
        send_ref[8:19] = jnp.zeros((11, LANES), f32)


def last_kernel(comps, share, all_ref, state_ref, *refs):
    z_refs = refs[:ITERS]
    astro_ref, att_ref, inst_ref = refs[ITERS:]
    high = STARS_DEV // LANES
    me = lax.axis_index("tm")
    total = all_ref[0]
    for device in range(1, all_ref.shape[0]):
        total = total + all_ref[device]
    total = jnp.concatenate([jnp.zeros((11, LANES), f32), total[3:8]], axis=0)
    state = state_ref[...]
    alpha, beta, _ = next_bidiagonal(total, state)
    betas = [state[1 + k : 2 + k] for k in range(ITERS)] + [beta]
    alphas = [state[9 + k : 10 + k] for k in range(ITERS - 1)] + [alpha]
    rho_bar, phi_bar = alphas[0], betas[0]
    weights = [jnp.zeros((1, LANES), f32)] * ITERS
    search = [jnp.zeros((1, LANES), f32)] * ITERS
    search[0] = 1.0 / alphas[0]
    for k in range(ITERS):
        rho = jnp.sqrt(rho_bar * rho_bar + betas[k + 1] * betas[k + 1])
        cosine, sine = rho_bar / rho, betas[k + 1] / rho
        phi = cosine * phi_bar
        phi_bar = sine * phi_bar
        weights = [x + phi / rho * w for x, w in zip(weights, search)]
        if k + 1 < ITERS:
            theta = sine * alphas[k + 1]
            rho_bar = -cosine * alphas[k + 1]
            search = [-(theta / rho) * w for w in search]
            search[k + 1] = 1.0 / alphas[k + 1]
    base = comps * high
    tiles = share // LANES

    def mix(read):
        total = weights[0] * read(z_refs[0])
        for k in range(1, ITERS):
            total = total + weights[k] * read(z_refs[k])
        return total

    for comp in range(comps):
        for tile in range(tiles):
            at = comp * high + me * tiles + tile
            astro_ref[comp : comp + 1, tile * LANES : (tile + 1) * LANES] = mix(
                lambda ref: ref[pl.ds(at, 1)]
            )
    inst_ref[...] = mix(lambda ref: ref[base : base + 8])
    att_ref[...] = mix(lambda ref: ref[base + 8 : base + 8 + ATT_DEV // LANES])


def call(kernel, name, out, args, scratch=()):
    vmem = pl.BlockSpec(memory_space=pltpu.VMEM)
    return pl.pallas_call(
        kernel,
        name=name,
        out_shape=[jax.ShapeDtypeStruct(shape, dtype) for shape, dtype in out],
        in_specs=[vmem] * len(args),
        out_specs=[vmem] * len(out),
        scratch_shapes=[pltpu.VMEM(shape, dtype) for shape, dtype in scratch],
        compiler_params=pltpu.CompilerParams(vmem_limit_bytes=VMEM_LIMIT),
    )(*args)


def gather_all(value, axis):
    return [lax.all_gather(value, axis)]


def gather_exchange(value, axis):
    count = lax.axis_size(axis)
    spread = jnp.broadcast_to(value[None], (count,) + value.shape)
    return [lax.all_to_all(spread, axis, 0, 0)]


def gather_permute(value, axis):
    count = lax.axis_size(axis)
    return [value] + [
        lax.ppermute(value, axis, [(i, i ^ gap) for i in range(count)]) for gap in range(1, count)
    ]


FORMS = [("all", gather_all), ("xor", gather_permute), ("all", gather_exchange)]


def per_device(astro_coef, star_index, att_coef, att_start, inst_coef, inst_index, observed):
    tm_count, star_count = lax.axis_size("tm"), lax.axis_size("star")
    comps = astro_coef.shape[1]
    slots = inst_coef.shape[1]
    blocks, width, height = att_coef.shape[1:]
    share = STARS_DEV // tm_count
    high = STARS_DEV // LANES
    astro = astro_coef.reshape(comps, blocks, height)
    star = star_index.reshape(blocks, height)
    att = att_coef.reshape(blocks * width, height)
    starts = att_start.reshape(blocks, 1)
    coef = inst_coef.reshape(slots, blocks, height)
    index = inst_index.reshape(slots, blocks, height)
    rows = observed.reshape(blocks, height)
    long = slots * blocks * height
    send, table, att2 = call(
        functools.partial(first_kernel, width),
        "first",
        [((32 + 8 * comps, LANES), f32), ((LANES, long), bf16), ((2 * blocks * width, height), bf16)],
        [rows, astro, star, att, starts, coef, index],
        [((16, long), bf16)],
    )
    basics = [astro, star, att2, starts, coef, index, table]
    everything = star_table = None
    state = z = g = u = None
    kept = []
    for step in range(ITERS):
        order, gather = FORMS[step]
        got = gather(send, "tm")
        (group,) = call(
            functools.partial(group_kernel, order, tm_count), "group", [((16, LANES), f32)], got
        )
        across = gather(group, "star")
        wide = ((2 * comps * high, blocks * height), bf16)
        if step == 0:
            everything = got[0]
            sums, star_table = call(
                functools.partial(astro_kernel, True, order, tm_count),
                "astro",
                [((comps * high, LANES), f32), ((LANES, tm_count * blocks * height), bf16)],
                got,
                [wide],
            )
        else:
            (sums,) = call(
                functools.partial(astro_kernel, False, order, tm_count),
                "astro",
                [((comps * high, LANES), f32)],
                [everything, star_table] + got,
                [wide],
            )
        tall = comps * high + 16
        older = [] if step == 0 else [state, z, g, u]
        send, state, z, g, u, rows = call(
            functools.partial(step_kernel, step, width, order, tm_count, star_count),
            "step",
            [((24, LANES), f32), ((16, LANES), f32), ((tall, LANES), f32), ((tall, LANES), f32),
             ((blocks, height), f32), ((blocks, height), f32)],
            basics + [sums, rows] + older + across,
            [((16, long), bf16)],
        )
        kept.append(z)
    everyone = lax.all_gather(send[16:24], ("star", "tm"))
    out_astro, out_att, out_inst = call(
        functools.partial(last_kernel, comps, share),
        "last",
        [((comps, share), f32), ((ATT_DEV // LANES, LANES), f32), ((NINST // LANES, LANES), f32)],
        [everyone, state] + kept,
    )
    return out_astro, out_att.reshape(-1), out_inst.reshape(-1)


def solution(mesh):
    return jax.shard_map(
        per_device,
        mesh=mesh,
        in_specs=(
            P("star", None, "tm"),
            P("star", "tm"),
            P("star", "tm", None, None),
            P("star", "tm"),
            P("star", None, "tm"),
            P("star", None, "tm"),
            P("star", "tm"),
        ),
        out_specs=(P(None, ("star", "tm")), P("tm"), P()),
        check_vma=False,
    )
```

```python
import functools

import jax
import jax.numpy as jnp
from jax import lax
from jax.experimental import pallas as pl
from jax.experimental.pallas import tpu as pltpu
from jax.sharding import PartitionSpec as P

STARS_DEV = 2048
NINST = 1024
ITERS = 3
ATT_DEV = 256
LANES = 128

epsilon = 1e-06
f32 = jnp.float32
bf16 = jnp.bfloat16
VMEM_LIMIT = 16 * 1024 * 1024


def halves(value):
    top = value.astype(bf16).astype(f32)
    return top, (value - top).astype(bf16).astype(f32)


def dot_lanes(left, right):
    return lax.dot_general(left, right, (((1,), (1,)), ((), ())), preferred_element_type=f32)


def dot_plain(left, right):
    return lax.dot_general(left, right, (((1,), (0,)), ((), ())), preferred_element_type=f32)


def lane_pick(row, lane_index):
    table = jnp.broadcast_to(row, lane_index.shape)
    return jnp.take_along_axis(table, lane_index, axis=1, mode="promise_in_bounds")


def table_pick(rows, index):
    high, low = index >> 7, index & (LANES - 1)
    total = jnp.zeros(index.shape, f32)
    for place, row in enumerate(rows):
        total = jnp.where(high == place, lane_pick(row, low), total)
    return total


def one_hot_low(index_row):
    shape = (LANES, LANES)
    low = jnp.broadcast_to(index_row & (LANES - 1), shape)
    hit = lax.broadcasted_iota(jnp.int32, shape, 0) == low
    return jnp.where(hit, 1.0, 0.0).astype(bf16)


def spread_high(index_row, value_row, count):
    shape = (count, LANES)
    high = jnp.broadcast_to(index_row >> 7, shape)
    hit = lax.broadcasted_iota(jnp.int32, shape, 0) == high
    return jnp.where(hit, jnp.broadcast_to(value_row, shape), 0.0)


def block_masks(blocks, width):
    shape = (blocks, LANES)
    row = lax.broadcasted_iota(jnp.int32, shape, 0)
    lane = lax.broadcasted_iota(jnp.int32, shape, 1)
    per_tile = LANES // width
    tiles = blocks // per_tile
    return [row == tile * per_tile + lane // width for tile in range(tiles)], row, lane


def inst_back(rows, coef_ref, index_ref, table_ref, spread_ref):
    slots, blocks = len(coef_ref), rows.shape[0]
    count = NINST // LANES
    for slot in range(slots):
        top, rest = halves(coef_ref[slot][...] * rows)
        index = index_ref[slot][...]
        for block in range(blocks):
            here = slice(block, block + 1)
            pieces = [spread_high(index[here], part[here], count) for part in (top, rest)]
            at = (slot * blocks + block) * LANES
            spread_ref[:, at : at + LANES] = jnp.concatenate(pieces, axis=0).astype(bf16)
    both = dot_lanes(spread_ref[...], table_ref[...])
    return both[:count] + both[count:]


def att_back(rows, att2, starts, width):
    blocks = rows.shape[0]
    size = att2.shape[0] // 2
    top, rest = halves(rows)
    both = dot_lanes(jnp.concatenate([top, rest], axis=0).astype(bf16), att2)
    both = both[:blocks] + both[blocks:]
    both = both[:, :size] + both[:, size:]
    masks, row, lane = block_masks(blocks, width)
    own = jnp.zeros((blocks, LANES), f32)
    for tile, mask in enumerate(masks):
        own = own + jnp.where(mask, both[:, tile * LANES : (tile + 1) * LANES], 0.0)
    shift = (row % (LANES // width)) * width
    out = []
    for tile in range((ATT_DEV + width + LANES - 1) // LANES):
        offset = lane + tile * LANES - starts
        inside = (offset >= 0) & (offset < width)
        picked = jnp.take_along_axis(
            own, jnp.where(inside, offset + shift, 0), axis=1, mode="promise_in_bounds"
        )
        out.append(jnp.sum(jnp.where(inside, picked, 0.0), axis=0, keepdims=True))
    return jnp.concatenate(out, axis=0)


def att_forward(att_rows, att2, starts, width):
    blocks = starts.shape[0]
    masks, row, lane = block_masks(blocks, width)
    tiles = [att_rows[tile : tile + 1] for tile in range(att_rows.shape[0])]
    window = table_pick(tiles, starts + lane % width)
    wide = jnp.concatenate([jnp.where(mask, window, 0.0) for mask in masks], axis=1)
    top, rest = halves(wide)
    left = jnp.concatenate([top, rest], axis=0).astype(bf16)
    both = dot_plain(jnp.concatenate([left, left], axis=1), att2)
    return both[:blocks] + both[blocks:]


def first_kernel(width, b_hbm, astro_hbm, star_hbm, att_hbm, starts_hbm, coef_hbm, index_hbm,
                 send_ref, table_ref, att2_ref, floats_ref, ints_ref,
                 b_ref, astro_ref, star_ref, att_ref, starts_ref, coef_ref, index_ref,
                 spread_ref, sems):
    pairs = [(index_hbm, index_ref), (coef_hbm, coef_ref), (b_hbm, b_ref), (starts_hbm, starts_ref),
             (att_hbm, att_ref), (astro_hbm, astro_ref), (star_hbm, star_ref)]
    copies = [
        pltpu.make_async_copy(source, target, sems.at[place])
        for place, (source, target) in enumerate(pairs)
    ]
    for copy in copies:
        copy.start()
    copies[0].wait()
    slots, blocks, _ = index_ref.shape
    comps = astro_ref.shape[0]
    for slot in range(slots):
        index = index_ref[slot]
        ints_ref[16 + slot * 8 : 24 + slot * 8] = index
        for block in range(blocks):
            at = (slot * blocks + block) * LANES
            table_ref[:, at : at + LANES] = one_hot_low(index[block : block + 1])
    for copy in copies[1:]:
        copy.wait()
    rows = b_ref[...]
    att = att_ref[...]
    top = att.astype(bf16)
    att2_ref[...] = jnp.concatenate([top, (att - top.astype(f32)).astype(bf16)], axis=0)
    shape = (blocks, LANES)
    starts_row = jnp.broadcast_to(starts_ref[...].astype(f32), (blocks, blocks))
    diagonal = lax.broadcasted_iota(jnp.int32, (blocks, blocks), 0) == lax.broadcasted_iota(
        jnp.int32, (blocks, blocks), 1
    )
    starts = jnp.sum(jnp.where(diagonal, starts_row, 0.0), axis=1, keepdims=True)
    starts = jnp.broadcast_to(starts.astype(jnp.int32), shape)
    ints_ref[0:8] = star_ref[...]
    ints_ref[8:16] = starts
    send_ref[0:8] = rows
    coefs = [coef_ref.at[slot] for slot in range(slots)]
    indices = [index_ref.at[slot] for slot in range(slots)]
    send_ref[8:16] = inst_back(rows, coefs, indices, table_ref, spread_ref)
    send_ref[16:19] = att_back(rows, att2_ref[...], starts, width)
    send_ref[19:20] = jnp.sum(rows * rows, axis=0, keepdims=True)
    send_ref[20:24] = jnp.zeros((4, LANES), f32)
    for comp in range(comps):
        send_ref[24 + comp * 8 : 32 + comp * 8] = astro_ref[comp]
        floats_ref[comp * 8 : comp * 8 + 8] = astro_ref[comp]
    send_ref[24 + comps * 8 : 32 + comps * 8] = star_ref[...].astype(f32)
    for slot in range(slots):
        at = (comps + slot) * 8
        floats_ref[at : at + 8] = coef_ref[slot]


def tree_sum(values):
    while len(values) > 1:
        values = [values[i] + values[i + 1] for i in range(0, len(values), 2)]
    return values[0]


def chip_kernel(count, *refs):
    ins, out_ref = refs[:count], refs[count]
    chip = lax.axis_index("tm") // 2
    extra = ins[0].shape[0] - 24
    base = 8 * count + 16
    for gap in range(count):
        where = chip ^ gap
        out_ref[pl.ds(pl.multiple_of(where * 8, 8), 8)] = ins[gap][0:8]
        out_ref[pl.ds(pl.multiple_of(base + where * 8, 8), 8)] = ins[gap][16:24]
        if extra:
            at = pl.multiple_of(base + 8 * count + where * extra, 8)
            out_ref[pl.ds(at, extra)] = ins[gap][24:]
    out_ref[8 * count : 8 * count + 8] = tree_sum([ref[8:16] for ref in ins])
    out_ref[8 * count + 8 : base] = tree_sum([ref[16:24] for ref in ins])


def group_kernel(count, own_ref, other_ref, out_ref):
    me = lax.axis_index("tm")
    chip, core = me // 2, me % 2
    low = 8 * count
    base = low + 16

    def part(ref, where):
        where = jnp.clip(where, 0, count - 1)
        return ref[pl.ds(pl.multiple_of(base + where * 8, 8), 8)]

    mine = part(own_ref, chip)
    prev = part(other_ref, chip - 1 + core)
    after = part(other_ref, chip + core)
    half = lax.broadcasted_iota(jnp.int32, (1, LANES), 1) < 64
    first = mine[0:1] + jnp.where(half & (me > 0), prev[2:3], 0.0)
    last = jnp.where(half & (me < 2 * count - 1), mine[2:3] + after[0:1], 0.0)
    scalars = own_ref[low + 8 : low + 16] + other_ref[low + 8 : low + 16]
    out_ref[0:8] = own_ref[low : low + 8] + other_ref[low : low + 8]
    out_ref[8:16] = jnp.concatenate([first, mine[1:2], last, scalars[3:8]], axis=0)


def astro_kernel(first, count, *refs):
    high = STARS_DEV // LANES
    if first:
        keep, (out_ref, table_ref, spread_ref) = refs[:2], refs[2:]
        ins = keep
    else:
        keep, table_ref, ins, (out_ref, spread_ref) = refs[:2], refs[2], refs[3:5], refs[5:]
    base = 16 * count + 16
    extra = (keep[0].shape[0] - base) // count
    comps = extra // 8 - 1
    long = 8 * LANES

    def one(place, total):
        for half in range(2):
            rows = ins[half][pl.ds(pl.multiple_of(place * 8, 8), 8)]
            packed = keep[half][pl.ds(pl.multiple_of(base + place * extra, 8), extra)]
            index = packed[comps * 8 :].astype(jnp.int32)
            at0 = pl.multiple_of((half * count + place) * long, long)
            split = [halves(packed[comp * 8 : comp * 8 + 8] * rows) for comp in range(comps)]
            for block in range(8):
                here = slice(block, block + 1)
                if first:
                    table_ref[:, pl.ds(at0 + block * LANES, LANES)] = one_hot_low(index[here])
                pieces = []
                for part in range(2):
                    for comp in range(comps):
                        pieces.append(spread_high(index[here], split[comp][part][here], high))
                spread_ref[half, :, block * LANES : (block + 1) * LANES] = jnp.concatenate(
                    pieces, axis=0
                ).astype(bf16)
            total = total + dot_lanes(spread_ref[half], table_ref[:, pl.ds(at0, long)])
        return total

    total = lax.fori_loop(0, count, one, jnp.zeros((2 * comps * high, LANES), f32))
    out_ref[...] = total[: comps * high] + total[comps * high :]


def sum_kernel(*refs):
    refs[-1][...] = tree_sum([ref[...] for ref in refs[:-1]])


def lane_sum(row):
    return jnp.broadcast_to(jnp.sum(row, axis=1, keepdims=True), row.shape)


def next_bidiagonal(total, state):
    squares, mixed, size = (lane_sum(total[row : row + 1]) for row in (11, 12, 13))
    alpha2 = size + epsilon
    alpha = jnp.sqrt(alpha2)
    rest = jnp.maximum(squares / alpha2 - 2.0 * mixed + alpha2 * state[0:1], 0.0)
    beta2 = rest + epsilon
    return alpha, jnp.sqrt(beta2), rest / beta2


def step_kernel(step, width, tm_count, star_count, *refs):
    floats_ref, ints_ref, att2_ref, table_ref, sum_ref, rows_ref = refs[:6]
    refs = refs[6:]
    if step > 0:
        state_ref, old_z_ref, old_g_ref, old_u_ref = refs[:4]
        refs = refs[4:]
    gathered, refs = refs[:star_count], refs[star_count:]
    send_ref, state_out, z_ref, g_ref, u_ref, s_ref, spread_ref = refs
    high = STARS_DEV // LANES
    comps = sum_ref.shape[0] // high
    blocks = 8
    slots = floats_ref.shape[0] // 8 - comps
    coef_ref = [floats_ref.at[(comps + slot) * 8 : (comps + slot) * 8 + 8] for slot in range(slots)]
    index_ref = [ints_ref.at[16 + slot * 8 : 24 + slot * 8] for slot in range(slots)]
    total = tree_sum([ref[...] for ref in gathered])
    back = jnp.concatenate([sum_ref[...], total[0:8], total[8:16]], axis=0)
    if step == 0:
        squares = lane_sum(total[11:12])
        beta2 = squares + epsilon
        beta = jnp.sqrt(beta2)
        u = rows_ref[0:8] / beta
        g = back / beta
        z = g
        state_out[...] = jnp.concatenate(
            [squares / beta2, beta, jnp.zeros((14, LANES), f32)], axis=0
        )
        left2 = squares / beta2
    else:
        state = state_ref[...]
        alpha, beta, left2 = next_bidiagonal(total, state)
        u = (rows_ref[...] / alpha - alpha * old_u_ref[...]) / beta
        g = (back / alpha - alpha * old_g_ref[...]) / beta
        z = g - (beta / alpha) * old_z_ref[...]
        pieces = [left2, state[1 : 1 + step], beta]
        pieces += [jnp.zeros((7 - step, LANES), f32)] + ([state[9 : 8 + step]] if step > 1 else [])
        pieces += [alpha, jnp.zeros((15 - 8 - step + 1 - 1, LANES), f32)]
        state_out[...] = jnp.concatenate(pieces, axis=0)
    z_ref[...] = z
    g_ref[...] = g
    u_ref[...] = u
    base = comps * high
    inst_rows = z[base : base + 8]
    att_rows = z[base + 8 : base + 11]
    starts = ints_ref[8:16]
    rows = att_forward(att_rows, att2_ref[...], starts, width)
    star = ints_ref[0:8]
    star_high, star_low = star >> 7, star & (LANES - 1)
    for comp in range(comps):
        picked = jnp.zeros((blocks, LANES), f32)
        for place in range(high):
            at = comp * high + place
            picked = jnp.where(star_high == place, lane_pick(z[at : at + 1], star_low), picked)
        rows = rows + floats_ref[comp * 8 : comp * 8 + 8] * picked
    pieces = [inst_rows[place : place + 1] for place in range(8)]
    for slot in range(slots):
        rows = rows + coef_ref[slot][...] * table_pick(pieces, index_ref[slot][...])
    s_ref[...] = rows
    astro_z = z[:base]
    size = jnp.sum(astro_z * astro_z, axis=0, keepdims=True) * (1.0 / tm_count)
    own = att_rows[: ATT_DEV // LANES]
    size = size + jnp.sum(own * own, axis=0, keepdims=True) * (1.0 / star_count)
    size = size + jnp.sum(inst_rows * inst_rows, axis=0, keepdims=True) * (
        1.0 / (star_count * tm_count)
    )
    scalars = [
        jnp.sum(rows * rows, axis=0, keepdims=True),
        jnp.sum(rows * u, axis=0, keepdims=True),
        size,
        jnp.zeros((2, LANES), f32),
    ]
    if step == ITERS - 1:
        send_ref[...] = jnp.concatenate([jnp.zeros((3, LANES), f32)] + scalars, axis=0)
        return
    send_ref[0:8] = rows
    send_ref[8:16] = inst_back(rows, coef_ref, index_ref, table_ref, spread_ref)
    att = att_back(rows, att2_ref[...], starts, width)
    send_ref[16:24] = jnp.concatenate([att] + scalars, axis=0)


def last_kernel(comps, share, star_count, state_ref, *refs):
    gathered, refs = refs[:star_count], refs[star_count:]
    z_refs = refs[:ITERS]
    astro_ref, att_ref, inst_ref = refs[ITERS:]
    high = STARS_DEV // LANES
    me = lax.axis_index("tm")
    total = tree_sum([ref[...] for ref in gathered])
    total = jnp.concatenate([jnp.zeros((11, LANES), f32), total[3:8]], axis=0)
    state = state_ref[...]
    alpha, beta, _ = next_bidiagonal(total, state)
    betas = [state[1 + k : 2 + k] for k in range(ITERS)] + [beta]
    alphas = [state[9 + k : 10 + k] for k in range(ITERS - 1)] + [alpha]
    rho_bar, phi_bar = alphas[0], betas[0]
    weights = [jnp.zeros((1, LANES), f32)] * ITERS
    search = [jnp.zeros((1, LANES), f32)] * ITERS
    search[0] = 1.0 / alphas[0]
    for k in range(ITERS):
        rho = jnp.sqrt(rho_bar * rho_bar + betas[k + 1] * betas[k + 1])
        cosine, sine = rho_bar / rho, betas[k + 1] / rho
        phi = cosine * phi_bar
        phi_bar = sine * phi_bar
        weights = [x + phi / rho * w for x, w in zip(weights, search)]
        if k + 1 < ITERS:
            theta = sine * alphas[k + 1]
            rho_bar = -cosine * alphas[k + 1]
            search = [-(theta / rho) * w for w in search]
            search[k + 1] = 1.0 / alphas[k + 1]
    base = comps * high
    tiles = share // LANES

    def mix(read):
        total = weights[0] * read(z_refs[0])
        for k in range(1, ITERS):
            total = total + weights[k] * read(z_refs[k])
        return total

    for comp in range(comps):
        for tile in range(tiles):
            at = comp * high + me * tiles + tile
            astro_ref[comp : comp + 1, tile * LANES : (tile + 1) * LANES] = mix(
                lambda ref: ref[pl.ds(at, 1)]
            )
    inst_ref[...] = mix(lambda ref: ref[base : base + 8])
    att_ref[...] = mix(lambda ref: ref[base + 8 : base + 8 + ATT_DEV // LANES])


def call(kernel, name, out, args, scratch=(), space=pltpu.VMEM):
    vmem = pl.BlockSpec(memory_space=pltpu.VMEM)
    return pl.pallas_call(
        kernel,
        name=name,
        out_shape=[jax.ShapeDtypeStruct(shape, dtype) for shape, dtype in out],
        in_specs=[pl.BlockSpec(memory_space=space)] * len(args),
        out_specs=[vmem] * len(out),
        scratch_shapes=list(scratch),
        compiler_params=pltpu.CompilerParams(vmem_limit_bytes=VMEM_LIMIT),
    )(*args)


def exchange(value, axis, gaps):
    count = lax.axis_size(axis)
    return [value] + [
        lax.ppermute(value, axis, [(i, i ^ gap) for i in range(count)]) for gap in gaps
    ]


def per_device(astro_coef, star_index, att_coef, att_start, inst_coef, inst_index, observed):
    tm_count, star_count = lax.axis_size("tm"), lax.axis_size("star")
    comps = astro_coef.shape[1]
    slots = inst_coef.shape[1]
    blocks, width, height = att_coef.shape[1:]
    share = STARS_DEV // tm_count
    high = STARS_DEV // LANES
    chips = tm_count // 2
    far = [2 * gap for gap in range(1, chips)]
    args = [
        observed.reshape(blocks, height),
        astro_coef.reshape(comps, blocks, height),
        star_index.reshape(blocks, height),
        att_coef.reshape(blocks * width, height),
        att_start,
        inst_coef.reshape(slots, blocks, height),
        inst_index.reshape(slots, blocks, height),
    ]
    long = slots * blocks * height
    extra = 8 * comps + 8
    spread = pltpu.VMEM((16, long), bf16)
    send, table, att2, floats, ints = call(
        functools.partial(first_kernel, width),
        "first",
        [((24 + extra, LANES), f32), ((LANES, long), bf16), ((2 * blocks * width, height), bf16),
         ((8 * (comps + slots), LANES), f32), ((16 + 8 * slots, LANES), jnp.int32)],
        args,
        [pltpu.VMEM(arg.shape, arg.dtype) for arg in args]
        + [spread, pltpu.SemaphoreType.DMA((len(args),))],
        pltpu.HBM,
    )
    rows = send
    keep = star_table = state = z = g = u = None
    kept = []
    for step in range(ITERS):
        size = 16 * chips + 16 + (chips * extra if step == 0 else 0)
        (gathered,) = call(
            functools.partial(chip_kernel, chips),
            "chip",
            [((size, LANES), f32)],
            exchange(send, "tm", far),
        )
        pair = exchange(gathered, "tm", [1])
        (group,) = call(
            functools.partial(group_kernel, chips), "group", [((16, LANES), f32)], pair
        )
        across = exchange(group, "star", range(1, star_count))
        wide = [pltpu.VMEM((2, 2 * comps * high, blocks * height), bf16)]
        sums_type = ((comps * high, LANES), f32)
        if step == 0:
            keep = pair
            sums, star_table = call(
                functools.partial(astro_kernel, True, chips),
                "astro",
                [sums_type, ((LANES, tm_count * blocks * height), bf16)],
                pair,
                wide,
            )
        else:
            (sums,) = call(
                functools.partial(astro_kernel, False, chips),
                "astro",
                [sums_type],
                keep + [star_table] + pair,
                wide,
            )
        tall = comps * high + 16
        older = [] if step == 0 else [state, z, g, u]
        send, state, z, g, u, rows = call(
            functools.partial(step_kernel, step, width, tm_count, star_count),
            "step",
            [((24 if step < ITERS - 1 else 8, LANES), f32), ((16, LANES), f32),
             ((tall, LANES), f32), ((tall, LANES), f32),
             ((blocks, height), f32), ((blocks, height), f32)],
            [floats, ints, att2, table, sums, rows] + older + across,
            [spread],
        )
        kept.append(z)
    low = [((8, LANES), f32)]
    for gaps in (far, [1]):
        (send,) = call(sum_kernel, "sum", low, exchange(send, "tm", gaps))
    across = exchange(send, "star", range(1, star_count))
    out_astro, out_att, out_inst = call(
        functools.partial(last_kernel, comps, share, star_count),
        "last",
        [((comps, share), f32), ((ATT_DEV // LANES, LANES), f32), ((NINST // LANES, LANES), f32)],
        [state] + across + kept,
    )
    return out_astro, out_att.reshape(-1), out_inst.reshape(-1)


def solution(mesh):
    return jax.shard_map(
        per_device,
        mesh=mesh,
        in_specs=(
            P("star", None, "tm"),
            P("star", "tm"),
            P("star", "tm", None, None),
            P("star", "tm"),
            P("star", None, "tm"),
            P("star", None, "tm"),
            P("star", "tm"),
        ),
        out_specs=(P(None, ("star", "tm")), P("tm"), P()),
        check_vma=False,
    )
```

```python
import functools

import jax
import jax.numpy as jnp
from jax import lax
from jax.experimental import pallas as pl
from jax.experimental.pallas import tpu as pltpu
from jax.sharding import PartitionSpec as P

STARS_DEV = 2048
NINST = 1024
ITERS = 3
ATT_DEV = 256
LANES = 128

epsilon = 1e-06
f32 = jnp.float32
bf16 = jnp.bfloat16
VMEM_LIMIT = 16 * 1024 * 1024
FIRST_LIMIT = 60 * 1024 * 1024


def halves(value):
    top = value.astype(bf16).astype(f32)
    return top, (value - top).astype(bf16).astype(f32)


def dot_lanes(left, right):
    return lax.dot_general(left, right, (((1,), (1,)), ((), ())), preferred_element_type=f32)


def dot_plain(left, right):
    return lax.dot_general(left, right, (((1,), (0,)), ((), ())), preferred_element_type=f32)


def lane_pick(row, lane_index):
    table = jnp.broadcast_to(row, lane_index.shape)
    return jnp.take_along_axis(table, lane_index, axis=1, mode="promise_in_bounds")


def table_pick(rows, index):
    high, low = index >> 7, index & (LANES - 1)
    total = jnp.zeros(index.shape, f32)
    for place, row in enumerate(rows):
        total = jnp.where(high == place, lane_pick(row, low), total)
    return total


def one_hot_low(index_row):
    shape = (LANES, LANES)
    low = jnp.broadcast_to(index_row & (LANES - 1), shape)
    hit = lax.broadcasted_iota(jnp.int32, shape, 0) == low
    return jnp.where(hit, 1.0, 0.0).astype(bf16)


def spread_high(index_row, value_row, count):
    shape = (count, LANES)
    high = jnp.broadcast_to(index_row >> 7, shape)
    hit = lax.broadcasted_iota(jnp.int32, shape, 0) == high
    return jnp.where(hit, jnp.broadcast_to(value_row, shape), 0.0)


def block_masks(blocks, width):
    shape = (blocks, LANES)
    row = lax.broadcasted_iota(jnp.int32, shape, 0)
    lane = lax.broadcasted_iota(jnp.int32, shape, 1)
    per_tile = LANES // width
    tiles = blocks // per_tile
    return [row == tile * per_tile + lane // width for tile in range(tiles)], row, lane


def inst_back(rows, coef_ref, index_ref, table_ref, spread_ref):
    slots, blocks = len(coef_ref), rows.shape[0]
    count = NINST // LANES
    for slot in range(slots):
        top, rest = halves(coef_ref[slot][...] * rows)
        index = index_ref[slot][...]
        for block in range(blocks):
            here = slice(block, block + 1)
            pieces = [spread_high(index[here], part[here], count) for part in (top, rest)]
            at = (slot * blocks + block) * LANES
            spread_ref[:, at : at + LANES] = jnp.concatenate(pieces, axis=0).astype(bf16)
    both = dot_lanes(spread_ref[...], table_ref[...])
    return both[:count] + both[count:]


def att_back(rows, att2, starts, width):
    blocks = rows.shape[0]
    size = att2.shape[0] // 2
    top, rest = halves(rows)
    both = dot_lanes(jnp.concatenate([top, rest], axis=0).astype(bf16), att2)
    both = both[:blocks] + both[blocks:]
    both = both[:, :size] + both[:, size:]
    masks, row, lane = block_masks(blocks, width)
    own = jnp.zeros((blocks, LANES), f32)
    for tile, mask in enumerate(masks):
        own = own + jnp.where(mask, both[:, tile * LANES : (tile + 1) * LANES], 0.0)
    shift = (row % (LANES // width)) * width
    out = []
    for tile in range((ATT_DEV + width + LANES - 1) // LANES):
        offset = lane + tile * LANES - starts
        inside = (offset >= 0) & (offset < width)
        picked = jnp.take_along_axis(
            own, jnp.where(inside, offset + shift, 0), axis=1, mode="promise_in_bounds"
        )
        out.append(jnp.sum(jnp.where(inside, picked, 0.0), axis=0, keepdims=True))
    return jnp.concatenate(out, axis=0)


def att_forward(att_rows, att2, starts, width):
    blocks = starts.shape[0]
    masks, row, lane = block_masks(blocks, width)
    tiles = [att_rows[tile : tile + 1] for tile in range(att_rows.shape[0])]
    window = table_pick(tiles, starts + lane % width)
    wide = jnp.concatenate([jnp.where(mask, window, 0.0) for mask in masks], axis=1)
    top, rest = halves(wide)
    left = jnp.concatenate([top, rest], axis=0).astype(bf16)
    both = dot_plain(jnp.concatenate([left, left], axis=1), att2)
    return both[:blocks] + both[blocks:]


def first_kernel(width, b_hbm, astro_hbm, star_hbm, att_hbm, starts_hbm, coef_hbm, index_hbm,
                 send_ref, table_ref, att2_ref, floats_ref, ints_ref,
                 b_ref, astro_ref, star_ref, att_ref, starts_ref, coef_ref, index_ref,
                 spread_ref, sems):
    pairs = [(index_hbm, index_ref), (coef_hbm, coef_ref), (b_hbm, b_ref), (starts_hbm, starts_ref),
             (att_hbm, att_ref), (astro_hbm, astro_ref), (star_hbm, star_ref)]
    copies = [
        pltpu.make_async_copy(source, target, sems.at[place])
        for place, (source, target) in enumerate(pairs)
    ]
    for copy in copies:
        copy.start()
    copies[0].wait()
    slots, blocks, _ = index_ref.shape
    comps = astro_ref.shape[0]
    for slot in range(slots):
        index = index_ref[slot]
        ints_ref[16 + slot * 8 : 24 + slot * 8] = index
        for block in range(blocks):
            at = (slot * blocks + block) * LANES
            table_ref[:, at : at + LANES] = one_hot_low(index[block : block + 1])
    for copy in copies[1:]:
        copy.wait()
    rows = b_ref[...]
    att = att_ref[...]
    top = att.astype(bf16)
    att2_ref[...] = jnp.concatenate([top, (att - top.astype(f32)).astype(bf16)], axis=0)
    shape = (blocks, LANES)
    starts_row = jnp.broadcast_to(starts_ref[...].astype(f32), (blocks, blocks))
    diagonal = lax.broadcasted_iota(jnp.int32, (blocks, blocks), 0) == lax.broadcasted_iota(
        jnp.int32, (blocks, blocks), 1
    )
    starts = jnp.sum(jnp.where(diagonal, starts_row, 0.0), axis=1, keepdims=True)
    starts = jnp.broadcast_to(starts.astype(jnp.int32), shape)
    ints_ref[0:8] = star_ref[...]
    ints_ref[8:16] = starts
    send_ref[0:8] = rows
    coefs = [coef_ref.at[slot] for slot in range(slots)]
    indices = [index_ref.at[slot] for slot in range(slots)]
    send_ref[8:16] = inst_back(rows, coefs, indices, table_ref, spread_ref)
    send_ref[16:19] = att_back(rows, att2_ref[...], starts, width)
    send_ref[19:20] = jnp.sum(rows * rows, axis=0, keepdims=True)
    send_ref[20:24] = jnp.zeros((4, LANES), f32)
    for comp in range(comps):
        send_ref[24 + comp * 8 : 32 + comp * 8] = astro_ref[comp]
        floats_ref[comp * 8 : comp * 8 + 8] = astro_ref[comp]
    send_ref[24 + comps * 8 : 32 + comps * 8] = star_ref[...].astype(f32)
    for slot in range(slots):
        at = (comps + slot) * 8
        floats_ref[at : at + 8] = coef_ref[slot]


def tree_sum(values):
    while len(values) > 1:
        values = [values[i] + values[i + 1] for i in range(0, len(values), 2)]
    return values[0]


def chip_kernel(count, *refs):
    ins, out_ref = refs[:count], refs[count]
    chip = lax.axis_index("tm") // 2
    extra = ins[0].shape[0] - 24
    base = 8 * count + 16
    for gap in range(count):
        where = chip ^ gap
        out_ref[pl.ds(pl.multiple_of(where * 8, 8), 8)] = ins[gap][0:8]
        out_ref[pl.ds(pl.multiple_of(base + where * 8, 8), 8)] = ins[gap][16:24]
        if extra:
            at = pl.multiple_of(base + 8 * count + where * extra, 8)
            out_ref[pl.ds(at, extra)] = ins[gap][24:]
    out_ref[8 * count : 8 * count + 8] = tree_sum([ref[8:16] for ref in ins])
    out_ref[8 * count + 8 : base] = tree_sum([ref[16:24] for ref in ins])


def group_kernel(count, own_ref, other_ref, out_ref):
    me = lax.axis_index("tm")
    chip, core = me // 2, me % 2
    low = 8 * count
    base = low + 16

    def part(ref, where):
        where = jnp.clip(where, 0, count - 1)
        return ref[pl.ds(pl.multiple_of(base + where * 8, 8), 8)]

    mine = part(own_ref, chip)
    prev = part(other_ref, chip - 1 + core)
    after = part(other_ref, chip + core)
    half = lax.broadcasted_iota(jnp.int32, (1, LANES), 1) < 64
    first = mine[0:1] + jnp.where(half & (me > 0), prev[2:3], 0.0)
    last = jnp.where(half & (me < 2 * count - 1), mine[2:3] + after[0:1], 0.0)
    scalars = own_ref[low + 8 : low + 16] + other_ref[low + 8 : low + 16]
    out_ref[0:8] = own_ref[low : low + 8] + other_ref[low : low + 8]
    out_ref[8:16] = jnp.concatenate([first, mine[1:2], last, scalars[3:8]], axis=0)


def astro_kernel(first, count, *refs):
    high = STARS_DEV // LANES
    if first:
        keep, (out_ref, table_ref, spread_ref) = refs[:2], refs[2:]
        ins = keep
    else:
        keep, table_ref, ins, (out_ref, spread_ref) = refs[:2], refs[2], refs[3:5], refs[5:]
    base = 16 * count + 16
    extra = (keep[0].shape[0] - base) // count
    comps = extra // 8 - 1
    long = 8 * LANES

    def one(place, total):
        for half in range(2):
            rows = ins[half][pl.ds(pl.multiple_of(place * 8, 8), 8)]
            packed = keep[half][pl.ds(pl.multiple_of(base + place * extra, 8), extra)]
            index = packed[comps * 8 :].astype(jnp.int32)
            at0 = pl.multiple_of((half * count + place) * long, long)
            split = [halves(packed[comp * 8 : comp * 8 + 8] * rows) for comp in range(comps)]
            for block in range(8):
                here = slice(block, block + 1)
                if first:
                    table_ref[:, pl.ds(at0 + block * LANES, LANES)] = one_hot_low(index[here])
                pieces = []
                for part in range(2):
                    for comp in range(comps):
                        pieces.append(spread_high(index[here], split[comp][part][here], high))
                spread_ref[half, :, block * LANES : (block + 1) * LANES] = jnp.concatenate(
                    pieces, axis=0
                ).astype(bf16)
            total = total + dot_lanes(spread_ref[half], table_ref[:, pl.ds(at0, long)])
        return total

    total = lax.fori_loop(0, count, one, jnp.zeros((2 * comps * high, LANES), f32))
    out_ref[...] = total[: comps * high] + total[comps * high :]


def sum_kernel(*refs):
    refs[-1][...] = tree_sum([ref[...] for ref in refs[:-1]])


def lane_sum(row):
    return jnp.broadcast_to(jnp.sum(row, axis=1, keepdims=True), row.shape)


def next_bidiagonal(total, state):
    squares, mixed, size = (lane_sum(total[row : row + 1]) for row in (11, 12, 13))
    alpha2 = size + epsilon
    alpha = jnp.sqrt(alpha2)
    rest = jnp.maximum(squares / alpha2 - 2.0 * mixed + alpha2 * state[0:1], 0.0)
    beta2 = rest + epsilon
    return alpha, jnp.sqrt(beta2), rest / beta2


def step_kernel(step, width, tm_count, star_count, *refs):
    floats_ref, ints_ref, att2_ref, table_ref, sum_ref, rows_ref = refs[:6]
    refs = refs[6:]
    if step > 0:
        state_ref, old_z_ref, old_g_ref, old_u_ref = refs[:4]
        refs = refs[4:]
    gathered, refs = refs[:2], refs[2:]
    send_ref, state_out, z_ref, g_ref, u_ref, s_ref, spread_ref = refs
    high = STARS_DEV // LANES
    comps = sum_ref.shape[0] // high
    blocks = 8
    slots = floats_ref.shape[0] // 8 - comps
    coef_ref = [floats_ref.at[(comps + slot) * 8 : (comps + slot) * 8 + 8] for slot in range(slots)]
    index_ref = [ints_ref.at[16 + slot * 8 : 24 + slot * 8] for slot in range(slots)]
    total = tree_sum([ref[...] for ref in gathered])
    back = jnp.concatenate([sum_ref[...], total[0:8], total[8:16]], axis=0)
    if step == 0:
        squares = lane_sum(total[11:12])
        beta2 = squares + epsilon
        beta = jnp.sqrt(beta2)
        u = rows_ref[0:8] / beta
        g = back / beta
        z = g
        state_out[...] = jnp.concatenate(
            [squares / beta2, beta, jnp.zeros((14, LANES), f32)], axis=0
        )
        left2 = squares / beta2
    else:
        state = state_ref[...]
        alpha, beta, left2 = next_bidiagonal(total, state)
        u = (rows_ref[...] / alpha - alpha * old_u_ref[...]) / beta
        g = (back / alpha - alpha * old_g_ref[...]) / beta
        z = g - (beta / alpha) * old_z_ref[...]
        pieces = [left2, state[1 : 1 + step], beta]
        pieces += [jnp.zeros((7 - step, LANES), f32)] + ([state[9 : 8 + step]] if step > 1 else [])
        pieces += [alpha, jnp.zeros((15 - 8 - step + 1 - 1, LANES), f32)]
        state_out[...] = jnp.concatenate(pieces, axis=0)
    z_ref[...] = z
    g_ref[...] = g
    u_ref[...] = u
    base = comps * high
    inst_rows = z[base : base + 8]
    att_rows = z[base + 8 : base + 11]
    starts = ints_ref[8:16]
    rows = att_forward(att_rows, att2_ref[...], starts, width)
    star = ints_ref[0:8]
    star_high, star_low = star >> 7, star & (LANES - 1)
    for comp in range(comps):
        picked = jnp.zeros((blocks, LANES), f32)
        for place in range(high):
            at = comp * high + place
            picked = jnp.where(star_high == place, lane_pick(z[at : at + 1], star_low), picked)
        rows = rows + floats_ref[comp * 8 : comp * 8 + 8] * picked
    pieces = [inst_rows[place : place + 1] for place in range(8)]
    for slot in range(slots):
        rows = rows + coef_ref[slot][...] * table_pick(pieces, index_ref[slot][...])
    s_ref[...] = rows
    astro_z = z[:base]
    size = jnp.sum(astro_z * astro_z, axis=0, keepdims=True) * (1.0 / tm_count)
    own = att_rows[: ATT_DEV // LANES]
    size = size + jnp.sum(own * own, axis=0, keepdims=True) * (1.0 / star_count)
    size = size + jnp.sum(inst_rows * inst_rows, axis=0, keepdims=True) * (
        1.0 / (star_count * tm_count)
    )
    scalars = [
        jnp.sum(rows * rows, axis=0, keepdims=True),
        jnp.sum(rows * u, axis=0, keepdims=True),
        size,
        jnp.zeros((2, LANES), f32),
    ]
    if step == ITERS - 1:
        send_ref[...] = jnp.concatenate([jnp.zeros((3, LANES), f32)] + scalars, axis=0)
        return
    send_ref[0:8] = rows
    send_ref[8:16] = inst_back(rows, coef_ref, index_ref, table_ref, spread_ref)
    att = att_back(rows, att2_ref[...], starts, width)
    send_ref[16:24] = jnp.concatenate([att] + scalars, axis=0)


def last_kernel(comps, share, star_count, state_ref, *refs):
    gathered, refs = refs[:2], refs[2:]
    z_refs = refs[:ITERS]
    astro_ref, att_ref, inst_ref = refs[ITERS:]
    high = STARS_DEV // LANES
    me = lax.axis_index("tm")
    total = tree_sum([ref[...] for ref in gathered])
    total = jnp.concatenate([jnp.zeros((11, LANES), f32), total[3:8]], axis=0)
    state = state_ref[...]
    alpha, beta, _ = next_bidiagonal(total, state)
    betas = [state[1 + k : 2 + k] for k in range(ITERS)] + [beta]
    alphas = [state[9 + k : 10 + k] for k in range(ITERS - 1)] + [alpha]
    rho_bar, phi_bar = alphas[0], betas[0]
    weights = [jnp.zeros((1, LANES), f32)] * ITERS
    search = [jnp.zeros((1, LANES), f32)] * ITERS
    search[0] = 1.0 / alphas[0]
    for k in range(ITERS):
        rho = jnp.sqrt(rho_bar * rho_bar + betas[k + 1] * betas[k + 1])
        cosine, sine = rho_bar / rho, betas[k + 1] / rho
        phi = cosine * phi_bar
        phi_bar = sine * phi_bar
        weights = [x + phi / rho * w for x, w in zip(weights, search)]
        if k + 1 < ITERS:
            theta = sine * alphas[k + 1]
            rho_bar = -cosine * alphas[k + 1]
            search = [-(theta / rho) * w for w in search]
            search[k + 1] = 1.0 / alphas[k + 1]
    base = comps * high
    tiles = share // LANES

    def mix(read):
        total = weights[0] * read(z_refs[0])
        for k in range(1, ITERS):
            total = total + weights[k] * read(z_refs[k])
        return total

    for comp in range(comps):
        for tile in range(tiles):
            at = comp * high + me * tiles + tile
            astro_ref[comp : comp + 1, tile * LANES : (tile + 1) * LANES] = mix(
                lambda ref: ref[pl.ds(at, 1)]
            )
    inst_ref[...] = mix(lambda ref: ref[base : base + 8])
    att_ref[...] = mix(lambda ref: ref[base + 8 : base + 8 + ATT_DEV // LANES])


def call(kernel, name, out, args, scratch=(), space=pltpu.VMEM, limit=VMEM_LIMIT):
    vmem = pl.BlockSpec(memory_space=pltpu.VMEM)
    return pl.pallas_call(
        kernel,
        name=name,
        out_shape=[jax.ShapeDtypeStruct(shape, dtype) for shape, dtype in out],
        in_specs=[pl.BlockSpec(memory_space=space)] * len(args),
        out_specs=[vmem] * len(out),
        scratch_shapes=list(scratch),
        compiler_params=pltpu.CompilerParams(vmem_limit_bytes=limit),
    )(*args)


def exchange(value, axis, gaps):
    count = lax.axis_size(axis)
    return [value] + [
        lax.ppermute(value, axis, [(i, i ^ gap) for i in range(count)]) for gap in gaps
    ]


def star_pairs(value, count):
    gap = 1
    while True:
        pair = exchange(value, "star", [gap])
        gap *= 2
        if gap >= count:
            return pair
        (value,) = call(sum_kernel, "sum", [(value.shape, f32)], pair)


def per_device(astro_coef, star_index, att_coef, att_start, inst_coef, inst_index, observed):
    tm_count, star_count = lax.axis_size("tm"), lax.axis_size("star")
    comps = astro_coef.shape[1]
    slots = inst_coef.shape[1]
    blocks, width, height = att_coef.shape[1:]
    share = STARS_DEV // tm_count
    high = STARS_DEV // LANES
    chips = tm_count // 2
    far = [2 * gap for gap in range(1, chips)]
    args = [
        observed.reshape(blocks, height),
        astro_coef.reshape(comps, blocks, height),
        star_index.reshape(blocks, height),
        att_coef.reshape(blocks * width, height),
        att_start,
        inst_coef.reshape(slots, blocks, height),
        inst_index.reshape(slots, blocks, height),
    ]
    long = slots * blocks * height
    extra = 8 * comps + 8
    spread = pltpu.VMEM((16, long), bf16)
    send, table, att2, floats, ints = call(
        functools.partial(first_kernel, width),
        "first",
        [((24 + extra, LANES), f32), ((LANES, long), bf16), ((2 * blocks * width, height), bf16),
         ((8 * (comps + slots), LANES), f32), ((16 + 8 * slots, LANES), jnp.int32)],
        args,
        [pltpu.VMEM(arg.shape, arg.dtype) for arg in args]
        + [spread, pltpu.SemaphoreType.DMA((len(args),))],
        pl.ANY,
        FIRST_LIMIT,
    )
    rows = send
    keep = star_table = state = z = g = u = None
    kept = []
    for step in range(ITERS):
        size = 16 * chips + 16 + (chips * extra if step == 0 else 0)
        (gathered,) = call(
            functools.partial(chip_kernel, chips),
            "chip",
            [((size, LANES), f32)],
            exchange(send, "tm", far),
        )
        pair = exchange(gathered, "tm", [1])
        (group,) = call(
            functools.partial(group_kernel, chips), "group", [((16, LANES), f32)], pair
        )
        across = star_pairs(group, star_count)
        wide = [pltpu.VMEM((2, 2 * comps * high, blocks * height), bf16)]
        sums_type = ((comps * high, LANES), f32)
        if step == 0:
            keep = pair
            sums, star_table = call(
                functools.partial(astro_kernel, True, chips),
                "astro",
                [sums_type, ((LANES, tm_count * blocks * height), bf16)],
                pair,
                wide,
            )
        else:
            (sums,) = call(
                functools.partial(astro_kernel, False, chips),
                "astro",
                [sums_type],
                keep + [star_table] + pair,
                wide,
            )
        tall = comps * high + 16
        older = [] if step == 0 else [state, z, g, u]
        send, state, z, g, u, rows = call(
            functools.partial(step_kernel, step, width, tm_count, star_count),
            "step",
            [((24 if step < ITERS - 1 else 8, LANES), f32), ((16, LANES), f32),
             ((tall, LANES), f32), ((tall, LANES), f32),
             ((blocks, height), f32), ((blocks, height), f32)],
            [floats, ints, att2, table, sums, rows] + older + across,
            [spread],
        )
        kept.append(z)
    low = [((8, LANES), f32)]
    for gaps in (far, [1]):
        (send,) = call(sum_kernel, "sum", low, exchange(send, "tm", gaps))
    across = star_pairs(send, star_count)
    out_astro, out_att, out_inst = call(
        functools.partial(last_kernel, comps, share, star_count),
        "last",
        [((comps, share), f32), ((ATT_DEV // LANES, LANES), f32), ((NINST // LANES, LANES), f32)],
        [state] + across + kept,
    )
    return out_astro, out_att.reshape(-1), out_inst.reshape(-1)


def solution(mesh):
    return jax.shard_map(
        per_device,
        mesh=mesh,
        in_specs=(
            P("star", None, "tm"),
            P("star", "tm"),
            P("star", "tm", None, None),
            P("star", "tm"),
            P("star", None, "tm"),
            P("star", None, "tm"),
            P("star", "tm"),
        ),
        out_specs=(P(None, ("star", "tm")), P("tm"), P()),
        check_vma=False,
    )
```

```python
import functools

import jax
import jax.numpy as jnp
from jax import lax
from jax.experimental import pallas as pl
from jax.experimental.pallas import tpu as pltpu
from jax.sharding import PartitionSpec as P

STARS_DEV = 2048
NINST = 1024
ITERS = 3
ATT_DEV = 256
LANES = 128

epsilon = 1e-06
f32 = jnp.float32
bf16 = jnp.bfloat16
VMEM_LIMIT = 16 * 1024 * 1024


def halves(value):
    top = value.astype(bf16).astype(f32)
    return top, (value - top).astype(bf16).astype(f32)


def dot_lanes(left, right):
    return lax.dot_general(left, right, (((1,), (1,)), ((), ())), preferred_element_type=f32)


def dot_plain(left, right):
    return lax.dot_general(left, right, (((1,), (0,)), ((), ())), preferred_element_type=f32)


def lane_pick(row, lane_index):
    table = jnp.broadcast_to(row, lane_index.shape)
    return jnp.take_along_axis(table, lane_index, axis=1, mode="promise_in_bounds")


def table_pick(rows, index):
    high, low = index >> 7, index & (LANES - 1)
    total = jnp.zeros(index.shape, f32)
    for place, row in enumerate(rows):
        total = jnp.where(high == place, lane_pick(row, low), total)
    return total


def one_hot_low(index_row):
    shape = (LANES, LANES)
    low = jnp.broadcast_to(index_row & (LANES - 1), shape)
    hit = lax.broadcasted_iota(jnp.int32, shape, 0) == low
    return jnp.where(hit, 1.0, 0.0).astype(bf16)


def spread_high(index_row, value_row, count):
    shape = (count, LANES)
    high = jnp.broadcast_to(index_row >> 7, shape)
    hit = lax.broadcasted_iota(jnp.int32, shape, 0) == high
    return jnp.where(hit, jnp.broadcast_to(value_row, shape), 0.0)


def block_masks(blocks, width):
    shape = (blocks, LANES)
    row = lax.broadcasted_iota(jnp.int32, shape, 0)
    lane = lax.broadcasted_iota(jnp.int32, shape, 1)
    per_tile = LANES // width
    tiles = blocks // per_tile
    return [row == tile * per_tile + lane // width for tile in range(tiles)], row, lane


def inst_back(rows, coef_ref, index_ref, table_ref, spread_ref):
    slots, blocks = len(coef_ref), rows.shape[0]
    count = NINST // LANES
    for slot in range(slots):
        top, rest = halves(coef_ref[slot][...] * rows)
        index = index_ref[slot][...]
        for block in range(blocks):
            here = slice(block, block + 1)
            pieces = [spread_high(index[here], part[here], count) for part in (top, rest)]
            at = (slot * blocks + block) * LANES
            spread_ref[:, at : at + LANES] = jnp.concatenate(pieces, axis=0).astype(bf16)
    both = dot_lanes(spread_ref[...], table_ref[...])
    return both[:count] + both[count:]


def att_back(rows, att2, starts, width):
    blocks = rows.shape[0]
    size = att2.shape[0] // 2
    top, rest = halves(rows)
    both = dot_lanes(jnp.concatenate([top, rest], axis=0).astype(bf16), att2)
    both = both[:blocks] + both[blocks:]
    both = both[:, :size] + both[:, size:]
    masks, row, lane = block_masks(blocks, width)
    own = jnp.zeros((blocks, LANES), f32)
    for tile, mask in enumerate(masks):
        own = own + jnp.where(mask, both[:, tile * LANES : (tile + 1) * LANES], 0.0)
    shift = (row % (LANES // width)) * width
    out = []
    for tile in range((ATT_DEV + width + LANES - 1) // LANES):
        offset = lane + tile * LANES - starts
        inside = (offset >= 0) & (offset < width)
        picked = jnp.take_along_axis(
            own, jnp.where(inside, offset + shift, 0), axis=1, mode="promise_in_bounds"
        )
        out.append(jnp.sum(jnp.where(inside, picked, 0.0), axis=0, keepdims=True))
    return jnp.concatenate(out, axis=0)


def att_forward(att_rows, att2, starts, width):
    blocks = starts.shape[0]
    masks, row, lane = block_masks(blocks, width)
    tiles = [att_rows[tile : tile + 1] for tile in range(att_rows.shape[0])]
    window = table_pick(tiles, starts + lane % width)
    wide = jnp.concatenate([jnp.where(mask, window, 0.0) for mask in masks], axis=1)
    top, rest = halves(wide)
    left = jnp.concatenate([top, rest], axis=0).astype(bf16)
    both = dot_plain(jnp.concatenate([left, left], axis=1), att2)
    return both[:blocks] + both[blocks:]


def first_kernel(width, b_hbm, astro_hbm, star_hbm, att_hbm, starts_hbm, coef_hbm, index_hbm,
                 send_ref, table_ref, att2_ref, floats_ref, ints_ref,
                 b_ref, astro_ref, star_ref, att_ref, starts_ref, coef_ref, index_ref,
                 spread_ref, sems):
    pairs = [(index_hbm, index_ref), (coef_hbm, coef_ref), (b_hbm, b_ref), (starts_hbm, starts_ref),
             (att_hbm, att_ref), (astro_hbm, astro_ref), (star_hbm, star_ref)]
    copies = [
        pltpu.make_async_copy(source, target, sems.at[place])
        for place, (source, target) in enumerate(pairs)
    ]
    for copy in copies:
        copy.start()
    copies[0].wait()
    slots, blocks, _ = index_ref.shape
    comps = astro_ref.shape[0]
    for slot in range(slots):
        index = index_ref[slot]
        ints_ref[16 + slot * 8 : 24 + slot * 8] = index
        for block in range(blocks):
            at = (slot * blocks + block) * LANES
            table_ref[:, at : at + LANES] = one_hot_low(index[block : block + 1])
    for copy in copies[1:]:
        copy.wait()
    rows = b_ref[...]
    att = att_ref[...]
    top = att.astype(bf16)
    att2_ref[...] = jnp.concatenate([top, (att - top.astype(f32)).astype(bf16)], axis=0)
    shape = (blocks, LANES)
    starts_row = jnp.broadcast_to(starts_ref[...].astype(f32), (blocks, blocks))
    diagonal = lax.broadcasted_iota(jnp.int32, (blocks, blocks), 0) == lax.broadcasted_iota(
        jnp.int32, (blocks, blocks), 1
    )
    starts = jnp.sum(jnp.where(diagonal, starts_row, 0.0), axis=1, keepdims=True)
    starts = jnp.broadcast_to(starts.astype(jnp.int32), shape)
    ints_ref[0:8] = star_ref[...]
    ints_ref[8:16] = starts
    send_ref[0:8] = rows
    coefs = [coef_ref.at[slot] for slot in range(slots)]
    indices = [index_ref.at[slot] for slot in range(slots)]
    send_ref[8:16] = inst_back(rows, coefs, indices, table_ref, spread_ref)
    send_ref[16:19] = att_back(rows, att2_ref[...], starts, width)
    send_ref[19:20] = jnp.sum(rows * rows, axis=0, keepdims=True)
    send_ref[20:24] = jnp.zeros((4, LANES), f32)
    for comp in range(comps):
        send_ref[24 + comp * 8 : 32 + comp * 8] = astro_ref[comp]
        floats_ref[comp * 8 : comp * 8 + 8] = astro_ref[comp]
    send_ref[24 + comps * 8 : 32 + comps * 8] = star_ref[...].astype(f32)
    for slot in range(slots):
        at = (comps + slot) * 8
        floats_ref[at : at + 8] = coef_ref[slot]


def tree_sum(values):
    while len(values) > 1:
        values = [values[i] + values[i + 1] for i in range(0, len(values), 2)]
    return values[0]


def chip_kernel(count, *refs):
    ins, out_ref = refs[:count], refs[count]
    chip = lax.axis_index("tm") // 2
    extra = ins[0].shape[0] - 24
    base = 8 * count + 16
    for gap in range(count):
        where = chip ^ gap
        out_ref[pl.ds(pl.multiple_of(where * 8, 8), 8)] = ins[gap][0:8]
        out_ref[pl.ds(pl.multiple_of(base + where * 8, 8), 8)] = ins[gap][16:24]
        if extra:
            at = pl.multiple_of(base + 8 * count + where * extra, 8)
            out_ref[pl.ds(at, extra)] = ins[gap][24:]
    out_ref[8 * count : 8 * count + 8] = tree_sum([ref[8:16] for ref in ins])
    out_ref[8 * count + 8 : base] = tree_sum([ref[16:24] for ref in ins])


def group_kernel(count, own_ref, other_ref, out_ref):
    me = lax.axis_index("tm")
    chip, core = me // 2, me % 2
    low = 8 * count
    base = low + 16

    def part(ref, where):
        where = jnp.clip(where, 0, count - 1)
        return ref[pl.ds(pl.multiple_of(base + where * 8, 8), 8)]

    mine = part(own_ref, chip)
    prev = part(other_ref, chip - 1 + core)
    after = part(other_ref, chip + core)
    half = lax.broadcasted_iota(jnp.int32, (1, LANES), 1) < 64
    first = mine[0:1] + jnp.where(half & (me > 0), prev[2:3], 0.0)
    last = jnp.where(half & (me < 2 * count - 1), mine[2:3] + after[0:1], 0.0)
    scalars = own_ref[low + 8 : low + 16] + other_ref[low + 8 : low + 16]
    out_ref[0:8] = own_ref[low : low + 8] + other_ref[low : low + 8]
    out_ref[8:16] = jnp.concatenate([first, mine[1:2], last, scalars[3:8]], axis=0)


def astro_kernel(first, count, *refs):
    high = STARS_DEV // LANES
    if first:
        keep, (out_ref, table_ref, spread_ref) = refs[:2], refs[2:]
        ins = keep
    else:
        keep, table_ref, ins, (out_ref, spread_ref) = refs[:2], refs[2], refs[3:5], refs[5:]
    base = 16 * count + 16
    extra = (keep[0].shape[0] - base) // count
    comps = extra // 8 - 1
    long = 8 * LANES

    def one(place, total):
        for half in range(2):
            rows = ins[half][pl.ds(pl.multiple_of(place * 8, 8), 8)]
            packed = keep[half][pl.ds(pl.multiple_of(base + place * extra, 8), extra)]
            index = packed[comps * 8 :].astype(jnp.int32)
            at0 = pl.multiple_of((half * count + place) * long, long)
            split = [halves(packed[comp * 8 : comp * 8 + 8] * rows) for comp in range(comps)]
            for block in range(8):
                here = slice(block, block + 1)
                if first:
                    table_ref[:, pl.ds(at0 + block * LANES, LANES)] = one_hot_low(index[here])
                pieces = []
                for part in range(2):
                    for comp in range(comps):
                        pieces.append(spread_high(index[here], split[comp][part][here], high))
                spread_ref[half, :, block * LANES : (block + 1) * LANES] = jnp.concatenate(
                    pieces, axis=0
                ).astype(bf16)
            total = total + dot_lanes(spread_ref[half], table_ref[:, pl.ds(at0, long)])
        return total

    total = lax.fori_loop(0, count, one, jnp.zeros((2 * comps * high, LANES), f32))
    out_ref[...] = total[: comps * high] + total[comps * high :]


def sum_kernel(*refs):
    refs[-1][...] = tree_sum([ref[...] for ref in refs[:-1]])


def lane_sum(row):
    return jnp.broadcast_to(jnp.sum(row, axis=1, keepdims=True), row.shape)


def next_bidiagonal(total, state):
    squares, mixed, size = (lane_sum(total[row : row + 1]) for row in (11, 12, 13))
    alpha2 = size + epsilon
    alpha = jnp.sqrt(alpha2)
    rest = jnp.maximum(squares / alpha2 - 2.0 * mixed + alpha2 * state[0:1], 0.0)
    beta2 = rest + epsilon
    return alpha, jnp.sqrt(beta2), rest / beta2


def step_kernel(step, width, tm_count, star_count, *refs):
    floats_ref, ints_ref, att2_ref, table_ref, sum_ref, rows_ref = refs[:6]
    refs = refs[6:]
    if step > 0:
        state_ref, old_z_ref, old_g_ref, old_u_ref = refs[:4]
        refs = refs[4:]
    gathered, refs = refs[:star_count], refs[star_count:]
    send_ref, state_out, z_ref, g_ref, u_ref, s_ref, spread_ref = refs
    high = STARS_DEV // LANES
    comps = sum_ref.shape[0] // high
    blocks = 8
    slots = floats_ref.shape[0] // 8 - comps
    coef_ref = [floats_ref.at[(comps + slot) * 8 : (comps + slot) * 8 + 8] for slot in range(slots)]
    index_ref = [ints_ref.at[16 + slot * 8 : 24 + slot * 8] for slot in range(slots)]
    total = tree_sum([ref[...] for ref in gathered])
    back = jnp.concatenate([sum_ref[...], total[0:8], total[8:16]], axis=0)
    if step == 0:
        squares = lane_sum(total[11:12])
        beta2 = squares + epsilon
        beta = jnp.sqrt(beta2)
        u = rows_ref[0:8] / beta
        g = back / beta
        z = g
        state_out[...] = jnp.concatenate(
            [squares / beta2, beta, jnp.zeros((14, LANES), f32)], axis=0
        )
        left2 = squares / beta2
    else:
        state = state_ref[...]
        alpha, beta, left2 = next_bidiagonal(total, state)
        u = (rows_ref[...] / alpha - alpha * old_u_ref[...]) / beta
        g = (back / alpha - alpha * old_g_ref[...]) / beta
        z = g - (beta / alpha) * old_z_ref[...]
        pieces = [left2, state[1 : 1 + step], beta]
        pieces += [jnp.zeros((7 - step, LANES), f32)] + ([state[9 : 8 + step]] if step > 1 else [])
        pieces += [alpha, jnp.zeros((15 - 8 - step + 1 - 1, LANES), f32)]
        state_out[...] = jnp.concatenate(pieces, axis=0)
    z_ref[...] = z
    g_ref[...] = g
    u_ref[...] = u
    base = comps * high
    inst_rows = z[base : base + 8]
    att_rows = z[base + 8 : base + 11]
    starts = ints_ref[8:16]
    rows = att_forward(att_rows, att2_ref[...], starts, width)
    star = ints_ref[0:8]
    star_high, star_low = star >> 7, star & (LANES - 1)
    for comp in range(comps):
        picked = jnp.zeros((blocks, LANES), f32)
        for place in range(high):
            at = comp * high + place
            picked = jnp.where(star_high == place, lane_pick(z[at : at + 1], star_low), picked)
        rows = rows + floats_ref[comp * 8 : comp * 8 + 8] * picked
    pieces = [inst_rows[place : place + 1] for place in range(8)]
    for slot in range(slots):
        rows = rows + coef_ref[slot][...] * table_pick(pieces, index_ref[slot][...])
    s_ref[...] = rows
    astro_z = z[:base]
    size = jnp.sum(astro_z * astro_z, axis=0, keepdims=True) * (1.0 / tm_count)
    own = att_rows[: ATT_DEV // LANES]
    size = size + jnp.sum(own * own, axis=0, keepdims=True) * (1.0 / star_count)
    size = size + jnp.sum(inst_rows * inst_rows, axis=0, keepdims=True) * (
        1.0 / (star_count * tm_count)
    )
    scalars = [
        jnp.sum(rows * rows, axis=0, keepdims=True),
        jnp.sum(rows * u, axis=0, keepdims=True),
        size,
        jnp.zeros((2, LANES), f32),
    ]
    if step == ITERS - 1:
        send_ref[...] = jnp.concatenate([jnp.zeros((3, LANES), f32)] + scalars, axis=0)
        return
    send_ref[0:8] = rows
    send_ref[8:16] = inst_back(rows, coef_ref, index_ref, table_ref, spread_ref)
    att = att_back(rows, att2_ref[...], starts, width)
    send_ref[16:24] = jnp.concatenate([att] + scalars, axis=0)


def last_kernel(comps, share, star_count, state_ref, *refs):
    gathered, refs = refs[:star_count], refs[star_count:]
    z_refs = refs[:ITERS]
    astro_ref, att_ref, inst_ref = refs[ITERS:]
    high = STARS_DEV // LANES
    me = lax.axis_index("tm")
    total = tree_sum([ref[...] for ref in gathered])
    total = jnp.concatenate([jnp.zeros((11, LANES), f32), total[3:8]], axis=0)
    state = state_ref[...]
    alpha, beta, _ = next_bidiagonal(total, state)
    betas = [state[1 + k : 2 + k] for k in range(ITERS)] + [beta]
    alphas = [state[9 + k : 10 + k] for k in range(ITERS - 1)] + [alpha]
    rho_bar, phi_bar = alphas[0], betas[0]
    weights = [jnp.zeros((1, LANES), f32)] * ITERS
    search = [jnp.zeros((1, LANES), f32)] * ITERS
    search[0] = 1.0 / alphas[0]
    for k in range(ITERS):
        rho = jnp.sqrt(rho_bar * rho_bar + betas[k + 1] * betas[k + 1])
        cosine, sine = rho_bar / rho, betas[k + 1] / rho
        phi = cosine * phi_bar
        phi_bar = sine * phi_bar
        weights = [x + phi / rho * w for x, w in zip(weights, search)]
        if k + 1 < ITERS:
            theta = sine * alphas[k + 1]
            rho_bar = -cosine * alphas[k + 1]
            search = [-(theta / rho) * w for w in search]
            search[k + 1] = 1.0 / alphas[k + 1]
    base = comps * high
    tiles = share // LANES

    def mix(read):
        total = weights[0] * read(z_refs[0])
        for k in range(1, ITERS):
            total = total + weights[k] * read(z_refs[k])
        return total

    for comp in range(comps):
        for tile in range(tiles):
            at = comp * high + me * tiles + tile
            astro_ref[comp : comp + 1, tile * LANES : (tile + 1) * LANES] = mix(
                lambda ref: ref[pl.ds(at, 1)]
            )
    inst_ref[...] = mix(lambda ref: ref[base : base + 8])
    att_ref[...] = mix(lambda ref: ref[base + 8 : base + 8 + ATT_DEV // LANES])


def call(kernel, name, out, args, scratch=(), space=pltpu.VMEM):
    vmem = pl.BlockSpec(memory_space=pltpu.VMEM)
    return pl.pallas_call(
        kernel,
        name=name,
        out_shape=[jax.ShapeDtypeStruct(shape, dtype) for shape, dtype in out],
        in_specs=[pl.BlockSpec(memory_space=space)] * len(args),
        out_specs=[vmem] * len(out),
        scratch_shapes=list(scratch),
        compiler_params=pltpu.CompilerParams(vmem_limit_bytes=VMEM_LIMIT),
    )(*args)


def exchange(value, axis, gaps):
    count = lax.axis_size(axis)
    return [value] + [
        lax.ppermute(value, axis, [(i, i ^ gap) for i in range(count)]) for gap in gaps
    ]


def per_device(astro_coef, star_index, att_coef, att_start, inst_coef, inst_index, observed):
    tm_count, star_count = lax.axis_size("tm"), lax.axis_size("star")
    comps = astro_coef.shape[1]
    slots = inst_coef.shape[1]
    blocks, width, height = att_coef.shape[1:]
    share = STARS_DEV // tm_count
    high = STARS_DEV // LANES
    chips = tm_count // 2
    far = [2 * gap for gap in range(1, chips)]
    args = [
        observed.reshape(blocks, height),
        astro_coef.reshape(comps, blocks, height),
        star_index.reshape(blocks, height),
        att_coef.reshape(blocks * width, height),
        att_start,
        inst_coef.reshape(slots, blocks, height),
        inst_index.reshape(slots, blocks, height),
    ]
    long = slots * blocks * height
    extra = 8 * comps + 8
    spread = pltpu.VMEM((16, long), bf16)
    send, table, att2, floats, ints = call(
        functools.partial(first_kernel, width),
        "first",
        [((24 + extra, LANES), f32), ((LANES, long), bf16), ((2 * blocks * width, height), bf16),
         ((8 * (comps + slots), LANES), f32), ((16 + 8 * slots, LANES), jnp.int32)],
        [pltpu.with_memory_space_constraint(arg, pltpu.HBM) for arg in args],
        [pltpu.VMEM(arg.shape, arg.dtype) for arg in args]
        + [spread, pltpu.SemaphoreType.DMA((len(args),))],
        pltpu.HBM,
    )
    rows = send
    keep = star_table = state = z = g = u = None
    kept = []
    for step in range(ITERS):
        size = 16 * chips + 16 + (chips * extra if step == 0 else 0)
        (gathered,) = call(
            functools.partial(chip_kernel, chips),
            "chip",
            [((size, LANES), f32)],
            exchange(send, "tm", far),
        )
        pair = exchange(gathered, "tm", [1])
        (group,) = call(
            functools.partial(group_kernel, chips), "group", [((16, LANES), f32)], pair
        )
        across = exchange(group, "star", range(1, star_count))
        wide = [pltpu.VMEM((2, 2 * comps * high, blocks * height), bf16)]
        sums_type = ((comps * high, LANES), f32)
        if step == 0:
            keep = pair
            sums, star_table = call(
                functools.partial(astro_kernel, True, chips),
                "astro",
                [sums_type, ((LANES, tm_count * blocks * height), bf16)],
                pair,
                wide,
            )
        else:
            (sums,) = call(
                functools.partial(astro_kernel, False, chips),
                "astro",
                [sums_type],
                keep + [star_table] + pair,
                wide,
            )
        tall = comps * high + 16
        older = [] if step == 0 else [state, z, g, u]
        send, state, z, g, u, rows = call(
            functools.partial(step_kernel, step, width, tm_count, star_count),
            "step",
            [((24 if step < ITERS - 1 else 8, LANES), f32), ((16, LANES), f32),
             ((tall, LANES), f32), ((tall, LANES), f32),
             ((blocks, height), f32), ((blocks, height), f32)],
            [floats, ints, att2, table, sums, rows] + older + across,
            [spread],
        )
        kept.append(z)
    low = [((8, LANES), f32)]
    for gaps in (far, [1]):
        (send,) = call(sum_kernel, "sum", low, exchange(send, "tm", gaps))
    across = exchange(send, "star", range(1, star_count))
    out_astro, out_att, out_inst = call(
        functools.partial(last_kernel, comps, share, star_count),
        "last",
        [((comps, share), f32), ((ATT_DEV // LANES, LANES), f32), ((NINST // LANES, LANES), f32)],
        [state] + across + kept,
    )
    return out_astro, out_att.reshape(-1), out_inst.reshape(-1)


def solution(mesh):
    return jax.shard_map(
        per_device,
        mesh=mesh,
        in_specs=(
            P("star", None, "tm"),
            P("star", "tm"),
            P("star", "tm", None, None),
            P("star", "tm"),
            P("star", None, "tm"),
            P("star", None, "tm"),
            P("star", "tm"),
        ),
        out_specs=(P(None, ("star", "tm")), P("tm"), P()),
        check_vma=False,
    )
```

```python
import functools

import jax
import jax.numpy as jnp
from jax import lax
from jax.experimental import pallas as pl
from jax.experimental.pallas import tpu as pltpu
from jax.sharding import PartitionSpec as P

STARS_DEV = 2048
NINST = 1024
ITERS = 3
ATT_DEV = 256
LANES = 128

epsilon = 1e-06
f32 = jnp.float32
bf16 = jnp.bfloat16
VMEM_LIMIT = 16 * 1024 * 1024


def halves(value):
    top = value.astype(bf16).astype(f32)
    return top, (value - top).astype(bf16).astype(f32)


def dot_lanes(left, right):
    return lax.dot_general(left, right, (((1,), (1,)), ((), ())), preferred_element_type=f32)


def dot_plain(left, right):
    return lax.dot_general(left, right, (((1,), (0,)), ((), ())), preferred_element_type=f32)


def lane_pick(row, lane_index):
    table = jnp.broadcast_to(row, lane_index.shape)
    return jnp.take_along_axis(table, lane_index, axis=1, mode="promise_in_bounds")


def table_pick(rows, index):
    high, low = index >> 7, index & (LANES - 1)
    total = jnp.zeros(index.shape, f32)
    for place, row in enumerate(rows):
        total = jnp.where(high == place, lane_pick(row, low), total)
    return total


def one_hot_low(index_row):
    shape = (LANES, LANES)
    low = jnp.broadcast_to(index_row & (LANES - 1), shape)
    hit = lax.broadcasted_iota(jnp.int32, shape, 0) == low
    return jnp.where(hit, 1.0, 0.0).astype(bf16)


def spread_high(index_row, value_row, count):
    shape = (count, LANES)
    high = jnp.broadcast_to(index_row >> 7, shape)
    hit = lax.broadcasted_iota(jnp.int32, shape, 0) == high
    return jnp.where(hit, jnp.broadcast_to(value_row, shape), 0.0)


def block_masks(blocks, width):
    shape = (blocks, LANES)
    row = lax.broadcasted_iota(jnp.int32, shape, 0)
    lane = lax.broadcasted_iota(jnp.int32, shape, 1)
    per_tile = LANES // width
    tiles = blocks // per_tile
    return [row == tile * per_tile + lane // width for tile in range(tiles)], row, lane


def inst_back(rows, coef_ref, index_ref, table_ref, spread_ref):
    slots, blocks = len(coef_ref), rows.shape[0]
    count = NINST // LANES
    for slot in range(slots):
        top, rest = halves(coef_ref[slot][...] * rows)
        index = index_ref[slot][...]
        for block in range(blocks):
            here = slice(block, block + 1)
            pieces = [spread_high(index[here], part[here], count) for part in (top, rest)]
            at = (slot * blocks + block) * LANES
            spread_ref[:, at : at + LANES] = jnp.concatenate(pieces, axis=0).astype(bf16)
    both = dot_lanes(spread_ref[...], table_ref[...])
    return both[:count] + both[count:]


def att_back(rows, att2, starts, width):
    blocks = rows.shape[0]
    size = att2.shape[0] // 2
    top, rest = halves(rows)
    both = dot_lanes(jnp.concatenate([top, rest], axis=0).astype(bf16), att2)
    both = both[:blocks] + both[blocks:]
    both = both[:, :size] + both[:, size:]
    masks, row, lane = block_masks(blocks, width)
    own = jnp.zeros((blocks, LANES), f32)
    for tile, mask in enumerate(masks):
        own = own + jnp.where(mask, both[:, tile * LANES : (tile + 1) * LANES], 0.0)
    shift = (row % (LANES // width)) * width
    out = []
    for tile in range((ATT_DEV + width + LANES - 1) // LANES):
        offset = lane + tile * LANES - starts
        inside = (offset >= 0) & (offset < width)
        picked = jnp.take_along_axis(
            own, jnp.where(inside, offset + shift, 0), axis=1, mode="promise_in_bounds"
        )
        out.append(jnp.sum(jnp.where(inside, picked, 0.0), axis=0, keepdims=True))
    return jnp.concatenate(out, axis=0)


def att_forward(att_rows, att2, starts, width):
    blocks = starts.shape[0]
    masks, row, lane = block_masks(blocks, width)
    tiles = [att_rows[tile : tile + 1] for tile in range(att_rows.shape[0])]
    window = table_pick(tiles, starts + lane % width)
    wide = jnp.concatenate([jnp.where(mask, window, 0.0) for mask in masks], axis=1)
    top, rest = halves(wide)
    left = jnp.concatenate([top, rest], axis=0).astype(bf16)
    both = dot_plain(jnp.concatenate([left, left], axis=1), att2)
    return both[:blocks] + both[blocks:]


def pack_places(slots, blocks, width):
    at = slots * 8
    return slice(0, at), slice(at, 2 * at), slice(2 * at, 2 * at + 8), slice(
        2 * at + 8, 2 * at + 8 + blocks * width
    )


def prepare(pack_ref, index_rows, starts, places, table_ref, att2_ref, ints_ref):
    count = index_rows.shape[0] // 8
    ints_ref[0 : count * 8] = index_rows
    ints_ref[count * 8 :] = starts
    for place in range(count * 8):
        table_ref[:, place * LANES : (place + 1) * LANES] = one_hot_low(
            index_rows[place : place + 1]
        )
    att = pack_ref[places[3]]
    top = att.astype(bf16)
    att2_ref[...] = jnp.concatenate([top, (att - top.astype(f32)).astype(bf16)], axis=0)


def first_kernel(width, b_hbm, astro_hbm, star_hbm, att_hbm, starts_hbm, coef_hbm, index_hbm,
                 send_ref, pack_ref, table_ref, att2_ref, ints_ref,
                 b_ref, astro_ref, star_ref, starts_ref, coef_ref, index_ref,
                 spread_ref, sems):
    slots, blocks, _ = index_ref.shape
    comps = astro_ref.shape[0]
    places = pack_places(slots, blocks, width)
    pairs = [(index_hbm, index_ref), (starts_hbm, starts_ref), (att_hbm, pack_ref.at[places[3]]),
             (coef_hbm, coef_ref), (b_hbm, b_ref), (astro_hbm, astro_ref), (star_hbm, star_ref)]
    copies = [
        pltpu.make_async_copy(source, target, sems.at[place])
        for place, (source, target) in enumerate(pairs)
    ]
    for copy in copies:
        copy.start()
    for copy in copies[:3]:
        copy.wait()
    index = jnp.concatenate([index_ref[slot] for slot in range(slots)], axis=0)
    starts_row = jnp.broadcast_to(starts_ref[...].astype(f32), (blocks, blocks))
    diagonal = lax.broadcasted_iota(jnp.int32, (blocks, blocks), 0) == lax.broadcasted_iota(
        jnp.int32, (blocks, blocks), 1
    )
    starts = jnp.sum(jnp.where(diagonal, starts_row, 0.0), axis=1, keepdims=True)
    starts = jnp.broadcast_to(starts, (blocks, LANES))
    pack_ref[places[1]] = index.astype(f32)
    pack_ref[places[2]] = starts
    starts = starts.astype(jnp.int32)
    prepare(pack_ref, index, starts, places, table_ref, att2_ref, ints_ref)
    for copy in copies[3:]:
        copy.wait()
    rows = b_ref[...]
    coefs = [coef_ref.at[slot] for slot in range(slots)]
    indices = [index_ref.at[slot] for slot in range(slots)]
    for slot in range(slots):
        pack_ref[slot * 8 : slot * 8 + 8] = coef_ref[slot]
    send_ref[0:8] = rows
    send_ref[8:16] = inst_back(rows, coefs, indices, table_ref, spread_ref)
    send_ref[16:19] = att_back(rows, att2_ref[...], starts, width)
    send_ref[19:20] = jnp.sum(rows * rows, axis=0, keepdims=True)
    send_ref[20:24] = jnp.zeros((4, LANES), f32)
    for comp in range(comps):
        send_ref[24 + comp * 8 : 32 + comp * 8] = astro_ref[comp]
    send_ref[24 + comps * 8 : 32 + comps * 8] = star_ref[...].astype(f32)


def prepare_kernel(slots, blocks, width, pack_ref, table_ref, att2_ref, ints_ref):
    places = pack_places(slots, blocks, width)
    index = pack_ref[places[1]].astype(jnp.int32)
    starts = pack_ref[places[2]].astype(jnp.int32)
    prepare(pack_ref, index, starts, places, table_ref, att2_ref, ints_ref)


def tree_sum(values):
    while len(values) > 1:
        values = [values[i] + values[i + 1] for i in range(0, len(values), 2)]
    return values[0]


def first_chip_kernel(count, *refs):
    ins, out_ref = refs[:count], refs[count]
    chip = lax.axis_index("tm") // 2
    extra = ins[0].shape[0] - 24
    base = 8 * count + 16
    for gap in range(count):
        where = chip ^ gap
        out_ref[pl.ds(pl.multiple_of(where * 8, 8), 8)] = ins[gap][0:8]
        out_ref[pl.ds(pl.multiple_of(base + where * 8, 8), 8)] = ins[gap][16:24]
        at = pl.multiple_of(base + 8 * count + where * extra, 8)
        out_ref[pl.ds(at, extra)] = ins[gap][24:]
    out_ref[8 * count : 8 * count + 8] = tree_sum([ref[8:16] for ref in ins])
    out_ref[8 * count + 8 : base] = tree_sum([ref[16:24] for ref in ins])


def group_rows(chip, count, mine, prev_row, after_row):
    half = lax.broadcasted_iota(jnp.int32, (1, LANES), 1) < 64
    first = mine[0:1] + jnp.where(half & (chip > 0), prev_row, 0.0)
    last = jnp.where(half & (chip < count - 1), mine[4:5] + after_row, 0.0)
    return [first, mine[1:4], last]


def chip_parts(core, own, other):
    low = jnp.where(core == 0, own, other)
    top = jnp.where(core == 0, other, own)
    return jnp.concatenate([low[0:2], low[2:3] + top[0:1], top[1:3]], axis=0)


def first_group_kernel(count, own_ref, other_ref, out_ref):
    me = lax.axis_index("tm")
    chip, core = me // 2, me % 2
    low = 8 * count
    base = low + 16

    def part(ref, where):
        where = jnp.clip(where, 0, count - 1)
        return ref[pl.ds(pl.multiple_of(base + where * 8, 8), 8)]

    def of_core(which, where):
        return jnp.where(core == which, part(own_ref, where), part(other_ref, where))

    mine = chip_parts(core, part(own_ref, chip)[0:3], part(other_ref, chip)[0:3])
    prev, after = of_core(1, chip - 1), of_core(0, chip + 1)
    scalars = own_ref[low + 8 : low + 16] + other_ref[low + 8 : low + 16]
    out_ref[0:8] = own_ref[low : low + 8] + other_ref[low : low + 8]
    out_ref[8:16] = jnp.concatenate(
        group_rows(chip, count, mine, prev[2:3], after[0:1]) + [scalars[3:6]], axis=0
    )


def group_kernel(count, *refs):
    ins, (rows_ref, out_ref) = refs[:count], refs[count:]
    chip = lax.axis_index("tm") // 2
    zero = jnp.zeros((8, LANES), f32)
    prev, after = zero, zero
    for gap in range(count):
        where = chip ^ gap
        for half in range(2):
            at = pl.multiple_of((half * count + where) * 8, 8)
            rows_ref[pl.ds(at, 8)] = ins[gap][half * 8 : half * 8 + 8]
        low = ins[gap][24:32]
        prev = jnp.where(where == chip - 1, low, prev)
        after = jnp.where(where == chip + 1, low, after)
    mine = ins[0][24:32]
    scalars = tree_sum([ref[24:32] for ref in ins])
    out_ref[0:8] = tree_sum([ref[16:24] for ref in ins])
    out_ref[8:16] = jnp.concatenate(
        group_rows(chip, count, mine, prev[4:5], after[0:1]) + [scalars[5:8]], axis=0
    )


def astro_kernel(first, count, *refs):
    high = STARS_DEV // LANES
    if first:
        keep, (out_ref, table_ref, spread_ref) = refs[:2], refs[2:]
    else:
        keep, (table_ref, rows_ref, out_ref, spread_ref) = refs[:2], refs[2:]
    base = 16 * count + 16
    extra = (keep[0].shape[0] - base) // count
    comps = extra // 8 - 1
    long = 8 * LANES

    def one(place, totals):
        new = []
        for half in range(2):
            if first:
                rows = keep[half][pl.ds(pl.multiple_of(place * 8, 8), 8)]
            else:
                rows = rows_ref[pl.ds(pl.multiple_of((half * count + place) * 8, 8), 8)]
            packed = keep[half][pl.ds(pl.multiple_of(base + place * extra, 8), extra)]
            index = packed[comps * 8 :].astype(jnp.int32)
            at0 = pl.multiple_of((half * count + place) * long, long)
            split = [halves(packed[comp * 8 : comp * 8 + 8] * rows) for comp in range(comps)]
            for block in range(8):
                here = slice(block, block + 1)
                if first:
                    table_ref[:, pl.ds(at0 + block * LANES, LANES)] = one_hot_low(index[here])
                pieces = []
                for part in range(2):
                    for comp in range(comps):
                        pieces.append(spread_high(index[here], split[comp][part][here], high))
                spread_ref[half, :, block * LANES : (block + 1) * LANES] = jnp.concatenate(
                    pieces, axis=0
                ).astype(bf16)
            new.append(
                totals[half] + dot_lanes(spread_ref[half], table_ref[:, pl.ds(at0, long)])
            )
        return tuple(new)

    zero = jnp.zeros((2 * comps * high, LANES), f32)
    own, other = lax.fori_loop(0, count, one, (zero, zero))
    total = own + other
    out_ref[...] = total[: comps * high] + total[comps * high :]


def sum_kernel(*refs):
    refs[-1][...] = tree_sum([ref[...] for ref in refs[:-1]])


def lane_sum(row):
    return jnp.broadcast_to(jnp.sum(row, axis=1, keepdims=True), row.shape)


def next_bidiagonal(total, state):
    squares, mixed, size = (lane_sum(total[row : row + 1]) for row in (13, 14, 15))
    alpha2 = size + epsilon
    alpha = jnp.sqrt(alpha2)
    rest = jnp.maximum(squares / alpha2 - 2.0 * mixed + alpha2 * state[0:1], 0.0)
    beta2 = rest + epsilon
    return alpha, jnp.sqrt(beta2), rest / beta2


def step_kernel(step, width, slots, chips, star_count, *refs):
    keep, packs, tables, att2s, ints, sum_ref = refs[:2], refs[2:4], refs[4:6], refs[6:8], refs[8:10], refs[10]
    refs = refs[11:]
    if step > 0:
        state_ref, old_z_ref, old_g_ref, old_u_ref, old_s_ref = refs[:5]
        refs = refs[5:]
    gathered, refs = refs[:star_count], refs[star_count:]
    send_ref, state_out, z_ref, g_ref, u_ref, s_ref, spread_ref = refs
    me = lax.axis_index("tm")
    chip, core = me // 2, me % 2
    high = STARS_DEV // LANES
    comps = sum_ref.shape[0] // high
    blocks = 8
    total = tree_sum([ref[...] for ref in gathered])
    back = jnp.concatenate([sum_ref[...], total], axis=0)
    if step == 0:
        squares = lane_sum(total[13:14])
        beta2 = squares + epsilon
        beta = jnp.sqrt(beta2)
        at = pl.ds(pl.multiple_of(chip * 8, 8), 8)
        u = jnp.concatenate([ref[at] for ref in keep], axis=0) / beta
        g = back / beta
        z = g
        state_out[...] = jnp.concatenate(
            [squares / beta2, beta, jnp.zeros((14, LANES), f32)], axis=0
        )
    else:
        state = state_ref[...]
        alpha, beta, left2 = next_bidiagonal(total, state)
        u = (old_s_ref[...] / alpha - alpha * old_u_ref[...]) / beta
        g = (back / alpha - alpha * old_g_ref[...]) / beta
        z = g - (beta / alpha) * old_z_ref[...]
        pieces = [left2, state[1 : 1 + step], beta, jnp.zeros((7 - step, LANES), f32)]
        pieces += [state[9 : 8 + step]] if step > 1 else []
        pieces += [alpha, jnp.zeros((7 - step, LANES), f32)]
        state_out[...] = jnp.concatenate(pieces, axis=0)
    z_ref[...] = z
    g_ref[...] = g
    u_ref[...] = u
    base = comps * high
    inst_rows = z[base : base + 8]
    att_rows = z[base + 8 : base + 13]
    extra = 8 * comps + 8
    here = 16 * chips + 16 + chip * extra
    pieces = [inst_rows[place : place + 1] for place in range(8)]
    rows, insts, atts = [], [], []
    for half in range(2):
        starts = ints[half][slots * 8 :]
        own = jnp.where(core == half, att_rows[0:3], att_rows[2:5])
        part = att_forward(own, att2s[half][...], starts, width)
        packed = keep[half][pl.ds(pl.multiple_of(here, 8), extra)]
        star = packed[comps * 8 :].astype(jnp.int32)
        star_high, star_low = star >> 7, star & (LANES - 1)
        for comp in range(comps):
            picked = jnp.zeros((blocks, LANES), f32)
            for place in range(high):
                at = comp * high + place
                picked = jnp.where(star_high == place, lane_pick(z[at : at + 1], star_low), picked)
            part = part + packed[comp * 8 : comp * 8 + 8] * picked
        coefs = [packs[half].at[slot * 8 : slot * 8 + 8] for slot in range(slots)]
        indices = [ints[half].at[slot * 8 : slot * 8 + 8] for slot in range(slots)]
        for slot in range(slots):
            part = part + coefs[slot][...] * table_pick(pieces, indices[slot][...])
        rows.append(part)
        if step < ITERS - 1:
            insts.append(inst_back(part, coefs, indices, tables[half], spread_ref.at[half]))
            atts.append(att_back(part, att2s[half][...], starts, width))
    both = jnp.concatenate(rows, axis=0)
    s_ref[...] = both

    def squared(value):
        return jnp.sum(value * value, axis=0, keepdims=True)

    size = squared(z[:base]) * (1.0 / chips) + squared(att_rows[:4]) * (1.0 / star_count)
    size = size + squared(inst_rows) * (1.0 / (star_count * chips))
    mixed = [jnp.sum(rows[half] * u[half * 8 : half * 8 + 8], axis=0, keepdims=True) for half in range(2)]
    scalars = [squared(rows[0]) + squared(rows[1]), mixed[0] + mixed[1], size]
    if step == ITERS - 1:
        send_ref[...] = jnp.concatenate([jnp.zeros((5, LANES), f32)] + scalars, axis=0)
        return
    send_ref[0:16] = both
    send_ref[16:24] = insts[0] + insts[1]
    send_ref[24:32] = jnp.concatenate([chip_parts(core, *atts)] + scalars, axis=0)


def last_kernel(comps, share, star_count, state_ref, *refs):
    gathered, refs = refs[:star_count], refs[star_count:]
    z_refs = refs[:ITERS]
    astro_ref, att_ref, inst_ref = refs[ITERS:]
    high = STARS_DEV // LANES
    me = lax.axis_index("tm")
    total = tree_sum([ref[...] for ref in gathered])
    total = jnp.concatenate([jnp.zeros((8, LANES), f32), total], axis=0)
    state = state_ref[...]
    alpha, beta, _ = next_bidiagonal(total, state)
    betas = [state[1 + k : 2 + k] for k in range(ITERS)] + [beta]
    alphas = [state[9 + k : 10 + k] for k in range(ITERS - 1)] + [alpha]
    rho_bar, phi_bar = alphas[0], betas[0]
    weights = [jnp.zeros((1, LANES), f32)] * ITERS
    search = [jnp.zeros((1, LANES), f32)] * ITERS
    search[0] = 1.0 / alphas[0]
    for k in range(ITERS):
        rho = jnp.sqrt(rho_bar * rho_bar + betas[k + 1] * betas[k + 1])
        cosine, sine = rho_bar / rho, betas[k + 1] / rho
        phi = cosine * phi_bar
        phi_bar = sine * phi_bar
        weights = [x + phi / rho * w for x, w in zip(weights, search)]
        if k + 1 < ITERS:
            theta = sine * alphas[k + 1]
            rho_bar = -cosine * alphas[k + 1]
            search = [-(theta / rho) * w for w in search]
            search[k + 1] = 1.0 / alphas[k + 1]
    base = comps * high
    tiles = share // LANES

    def mix(read):
        total = weights[0] * read(z_refs[0])
        for k in range(1, ITERS):
            total = total + weights[k] * read(z_refs[k])
        return total

    for comp in range(comps):
        for tile in range(tiles):
            at = comp * high + me * tiles + tile
            astro_ref[comp : comp + 1, tile * LANES : (tile + 1) * LANES] = mix(
                lambda ref: ref[pl.ds(at, 1)]
            )
    inst_ref[...] = mix(lambda ref: ref[base : base + 8])
    rows = ATT_DEV // LANES
    att_ref[...] = mix(lambda ref: ref[pl.ds(base + 8 + (me % 2) * rows, rows)])


def call(kernel, name, out, args, scratch=(), space=pltpu.VMEM):
    vmem = pl.BlockSpec(memory_space=pltpu.VMEM)
    return pl.pallas_call(
        kernel,
        name=name,
        out_shape=[jax.ShapeDtypeStruct(shape, dtype) for shape, dtype in out],
        in_specs=[pl.BlockSpec(memory_space=space)] * len(args),
        out_specs=[vmem] * len(out),
        scratch_shapes=list(scratch),
        compiler_params=pltpu.CompilerParams(vmem_limit_bytes=VMEM_LIMIT),
    )(*args)


def exchange(value, axis, gaps):
    count = lax.axis_size(axis)
    return [value] + [
        lax.ppermute(value, axis, [(i, i ^ gap) for i in range(count)]) for gap in gaps
    ]


def per_device(astro_coef, star_index, att_coef, att_start, inst_coef, inst_index, observed):
    tm_count, star_count = lax.axis_size("tm"), lax.axis_size("star")
    comps = astro_coef.shape[1]
    slots = inst_coef.shape[1]
    blocks, width, height = att_coef.shape[1:]
    share = STARS_DEV // tm_count
    high = STARS_DEV // LANES
    chips = tm_count // 2
    far = [2 * gap for gap in range(1, chips)]
    args = [
        observed.reshape(blocks, height),
        astro_coef.reshape(comps, blocks, height),
        star_index.reshape(blocks, height),
        att_coef.reshape(blocks * width, height),
        att_start,
        inst_coef.reshape(slots, blocks, height),
        inst_index.reshape(slots, blocks, height),
    ]
    long = slots * blocks * height
    extra = 8 * comps + 8
    spread = pltpu.VMEM((16, long), bf16)
    prepared = [((LANES, long), bf16), ((2 * blocks * width, height), bf16),
                ((8 * slots + 8, LANES), jnp.int32)]
    here = [pltpu.with_memory_space_constraint(arg, pltpu.HBM) for arg in args]
    send, pack, *mine = call(
        functools.partial(first_kernel, width),
        "first",
        [((24 + extra, LANES), f32), ((16 * slots + 8 + blocks * width, LANES), f32)] + prepared,
        here,
        [pltpu.VMEM(arg.shape, arg.dtype) for arg in args if arg is not args[3]]
        + [spread, pltpu.SemaphoreType.DMA((len(args),))],
        pl.ANY,
    )
    _, other_pack = exchange(pack, "tm", [1])
    theirs = call(
        functools.partial(prepare_kernel, slots, blocks, width), "prepare", prepared, [other_pack]
    )
    basics = [pack, other_pack] + [value for pair in zip(mine, theirs) for value in pair]
    keep = star_table = state = z = g = u = rows = None
    kept = []
    group_type = ((16, LANES), f32)
    for step in range(ITERS):
        wide = [pltpu.VMEM((2, 2 * comps * high, blocks * height), bf16)]
        sums_type = ((comps * high, LANES), f32)
        got = exchange(send, "tm", far)
        if step == 0:
            (gathered,) = call(
                functools.partial(first_chip_kernel, chips),
                "chip",
                [((16 * chips + 16 + chips * extra, LANES), f32)],
                got,
            )
            keep = exchange(gathered, "tm", [1])
            (group,) = call(
                functools.partial(first_group_kernel, chips), "group", [group_type], keep
            )
        else:
            all_rows, group = call(
                functools.partial(group_kernel, chips),
                "group",
                [((16 * chips, LANES), f32), group_type],
                got,
            )
        across = exchange(group, "star", range(1, star_count))
        if step == 0:
            sums, star_table = call(
                functools.partial(astro_kernel, True, chips),
                "astro",
                [sums_type, ((LANES, tm_count * blocks * height), bf16)],
                keep,
                wide,
            )
        else:
            (sums,) = call(
                functools.partial(astro_kernel, False, chips),
                "astro",
                [sums_type],
                keep + [star_table, all_rows],
                wide,
            )
        tall = ((comps * high + 16, LANES), f32)
        pair = ((2 * blocks, height), f32)
        older = [] if step == 0 else [state, z, g, u, rows]
        send, state, z, g, u, rows = call(
            functools.partial(step_kernel, step, width, slots, chips, star_count),
            "step",
            [((32 if step < ITERS - 1 else 8, LANES), f32), group_type, tall, tall, pair, pair],
            keep + basics + [sums] + older + across,
            [pltpu.VMEM((2, 16, long), bf16)],
        )
        kept.append(z)
    (send,) = call(sum_kernel, "sum", [((8, LANES), f32)], exchange(send, "tm", far))
    across = exchange(send, "star", range(1, star_count))
    out_astro, out_att, out_inst = call(
        functools.partial(last_kernel, comps, share, star_count),
        "last",
        [((comps, share), f32), ((ATT_DEV // LANES, LANES), f32), ((NINST // LANES, LANES), f32)],
        [state] + across + kept,
    )
    return out_astro, out_att.reshape(-1), out_inst.reshape(-1)


def solution(mesh):
    return jax.shard_map(
        per_device,
        mesh=mesh,
        in_specs=(
            P("star", None, "tm"),
            P("star", "tm"),
            P("star", "tm", None, None),
            P("star", "tm"),
            P("star", None, "tm"),
            P("star", None, "tm"),
            P("star", "tm"),
        ),
        out_specs=(P(None, ("star", "tm")), P("tm"), P()),
        check_vma=False,
    )
```

```python
import functools

import jax
import jax.numpy as jnp
from jax import lax
from jax.experimental import pallas as pl
from jax.experimental.pallas import tpu as pltpu
from jax.sharding import PartitionSpec as P

STARS_DEV = 2048
NINST = 1024
ITERS = 3
ATT_DEV = 256
LANES = 128

epsilon = 1e-06
STAR_COPIES = True
TM_COPIES = [False, True, True]
f32 = jnp.float32
bf16 = jnp.bfloat16
VMEM_LIMIT = 16 * 1024 * 1024


def halves(value):
    top = value.astype(bf16).astype(f32)
    return top, (value - top).astype(bf16).astype(f32)


def dot_lanes(left, right):
    return lax.dot_general(left, right, (((1,), (1,)), ((), ())), preferred_element_type=f32)


def dot_plain(left, right):
    return lax.dot_general(left, right, (((1,), (0,)), ((), ())), preferred_element_type=f32)


def lane_pick(row, lane_index):
    table = jnp.broadcast_to(row, lane_index.shape)
    return jnp.take_along_axis(table, lane_index, axis=1, mode="promise_in_bounds")


def table_pick(rows, index):
    high, low = index >> 7, index & (LANES - 1)
    total = jnp.zeros(index.shape, f32)
    for place, row in enumerate(rows):
        total = jnp.where(high == place, lane_pick(row, low), total)
    return total


def one_hot_low(index_row):
    shape = (LANES, LANES)
    low = jnp.broadcast_to(index_row & (LANES - 1), shape)
    hit = lax.broadcasted_iota(jnp.int32, shape, 0) == low
    return jnp.where(hit, 1.0, 0.0).astype(bf16)


def spread_high(index_row, value_row, count):
    shape = (count, LANES)
    high = jnp.broadcast_to(index_row >> 7, shape)
    hit = lax.broadcasted_iota(jnp.int32, shape, 0) == high
    return jnp.where(hit, jnp.broadcast_to(value_row, shape), 0.0)


def block_masks(blocks, width):
    shape = (blocks, LANES)
    row = lax.broadcasted_iota(jnp.int32, shape, 0)
    lane = lax.broadcasted_iota(jnp.int32, shape, 1)
    per_tile = LANES // width
    tiles = blocks // per_tile
    return [row == tile * per_tile + lane // width for tile in range(tiles)], row, lane


def inst_back(rows, coef_ref, index_ref, table_ref, spread_ref):
    slots, blocks = len(coef_ref), rows.shape[0]
    count = NINST // LANES
    for slot in range(slots):
        top, rest = halves(coef_ref[slot][...] * rows)
        index = index_ref[slot][...]
        for block in range(blocks):
            here = slice(block, block + 1)
            pieces = [spread_high(index[here], part[here], count) for part in (top, rest)]
            at = (slot * blocks + block) * LANES
            spread_ref[:, at : at + LANES] = jnp.concatenate(pieces, axis=0).astype(bf16)
    both = dot_lanes(spread_ref[...], table_ref[...])
    return both[:count] + both[count:]


def att_back(rows, att2, starts, width):
    blocks = rows.shape[0]
    size = att2.shape[0] // 2
    top, rest = halves(rows)
    both = dot_lanes(jnp.concatenate([top, rest], axis=0).astype(bf16), att2)
    both = both[:blocks] + both[blocks:]
    both = both[:, :size] + both[:, size:]
    masks, row, lane = block_masks(blocks, width)
    own = jnp.zeros((blocks, LANES), f32)
    for tile, mask in enumerate(masks):
        own = own + jnp.where(mask, both[:, tile * LANES : (tile + 1) * LANES], 0.0)
    shift = (row % (LANES // width)) * width
    out = []
    for tile in range((ATT_DEV + width + LANES - 1) // LANES):
        offset = lane + tile * LANES - starts
        inside = (offset >= 0) & (offset < width)
        picked = jnp.take_along_axis(
            own, jnp.where(inside, offset + shift, 0), axis=1, mode="promise_in_bounds"
        )
        out.append(jnp.sum(jnp.where(inside, picked, 0.0), axis=0, keepdims=True))
    return jnp.concatenate(out, axis=0)


def att_forward(att_rows, att2, starts, width):
    blocks = starts.shape[0]
    masks, row, lane = block_masks(blocks, width)
    tiles = [att_rows[tile : tile + 1] for tile in range(att_rows.shape[0])]
    window = table_pick(tiles, starts + lane % width)
    wide = jnp.concatenate([jnp.where(mask, window, 0.0) for mask in masks], axis=1)
    top, rest = halves(wide)
    left = jnp.concatenate([top, rest], axis=0).astype(bf16)
    both = dot_plain(jnp.concatenate([left, left], axis=1), att2)
    return both[:blocks] + both[blocks:]


def pack_places(slots, blocks, width):
    at = slots * 8
    return slice(0, at), slice(at, 2 * at), slice(2 * at, 2 * at + 8), slice(
        2 * at + 8, 2 * at + 8 + blocks * width
    )


def prepare_index(index_rows, starts, table_ref, ints_ref):
    count = index_rows.shape[0] // 8
    ints_ref[0 : count * 8] = index_rows
    ints_ref[count * 8 :] = starts
    for place in range(count * 8):
        table_ref[:, place * LANES : (place + 1) * LANES] = one_hot_low(
            index_rows[place : place + 1]
        )


def prepare_att(att, att2_ref):
    top = att.astype(bf16)
    att2_ref[...] = jnp.concatenate([top, (att - top.astype(f32)).astype(bf16)], axis=0)


def first_kernel(width, b_hbm, astro_hbm, star_hbm, att_hbm, starts_hbm, coef_hbm, index_hbm,
                 send_ref, pack_ref, table_ref, att2_ref, ints_ref,
                 b_ref, astro_ref, star_ref, starts_ref, coef_ref, index_ref,
                 spread_ref, sems):
    slots, blocks, _ = index_ref.shape
    comps = astro_ref.shape[0]
    places = pack_places(slots, blocks, width)
    pairs = [(index_hbm, index_ref), (starts_hbm, starts_ref), (att_hbm, pack_ref.at[places[3]]),
             (coef_hbm, coef_ref), (b_hbm, b_ref), (astro_hbm, astro_ref), (star_hbm, star_ref)]
    copies = [
        pltpu.make_async_copy(source, target, sems.at[place])
        for place, (source, target) in enumerate(pairs)
    ]
    for copy in copies:
        copy.start()
    for copy in copies[:2]:
        copy.wait()
    index = jnp.concatenate([index_ref[slot] for slot in range(slots)], axis=0)
    starts_row = jnp.broadcast_to(starts_ref[...].astype(f32), (blocks, blocks))
    diagonal = lax.broadcasted_iota(jnp.int32, (blocks, blocks), 0) == lax.broadcasted_iota(
        jnp.int32, (blocks, blocks), 1
    )
    starts = jnp.sum(jnp.where(diagonal, starts_row, 0.0), axis=1, keepdims=True)
    starts = jnp.broadcast_to(starts, (blocks, LANES))
    pack_ref[places[1]] = index.astype(f32)
    pack_ref[places[2]] = starts
    starts = starts.astype(jnp.int32)
    prepare_index(index, starts, table_ref, ints_ref)
    for copy in copies[2:]:
        copy.wait()
    prepare_att(pack_ref[places[3]], att2_ref)
    rows = b_ref[...]
    coefs = [coef_ref.at[slot] for slot in range(slots)]
    indices = [index_ref.at[slot] for slot in range(slots)]
    for slot in range(slots):
        pack_ref[slot * 8 : slot * 8 + 8] = coef_ref[slot]
    send_ref[0:8] = rows
    send_ref[8:16] = inst_back(rows, coefs, indices, table_ref, spread_ref)
    send_ref[16:19] = att_back(rows, att2_ref[...], starts, width)
    send_ref[19:20] = jnp.sum(rows * rows, axis=0, keepdims=True)
    send_ref[20:24] = jnp.zeros((4, LANES), f32)
    for comp in range(comps):
        send_ref[24 + comp * 8 : 32 + comp * 8] = astro_ref[comp]
    send_ref[24 + comps * 8 : 32 + comps * 8] = star_ref[...].astype(f32)


def prepare_kernel(slots, blocks, width, pack_ref, table_ref, att2_ref, ints_ref):
    places = pack_places(slots, blocks, width)
    index = pack_ref[places[1]].astype(jnp.int32)
    starts = pack_ref[places[2]].astype(jnp.int32)
    prepare_index(index, starts, table_ref, ints_ref)
    prepare_att(pack_ref[places[3]], att2_ref)


def put(ref, start, value):
    rows = slice(start, start + value.shape[0])
    if len(ref.shape) == 2:
        ref[rows] = value
    else:
        for copy in range(ref.shape[0]):
            ref[copy, rows] = value


def arrived(refs, count, here):
    if len(refs) == 1:
        return [refs[0].at[place] for place in range(count)], list(range(count))
    return list(refs), [here ^ gap for gap in range(count)]


def tree_sum(values):
    while len(values) > 1:
        values = [values[i] + values[i + 1] for i in range(0, len(values), 2)]
    return values[0]


def first_chip_kernel(count, *refs):
    ins, out_ref = refs[:count], refs[count]
    chip = lax.axis_index("tm") // 2
    extra = ins[0].shape[0] - 24
    base = 8 * count + 16
    for gap in range(count):
        where = chip ^ gap
        out_ref[pl.ds(pl.multiple_of(where * 8, 8), 8)] = ins[gap][0:8]
        out_ref[pl.ds(pl.multiple_of(base + where * 8, 8), 8)] = ins[gap][16:24]
        at = pl.multiple_of(base + 8 * count + where * extra, 8)
        out_ref[pl.ds(at, extra)] = ins[gap][24:]
    out_ref[8 * count : 8 * count + 8] = tree_sum([ref[8:16] for ref in ins])
    out_ref[8 * count + 8 : base] = tree_sum([ref[16:24] for ref in ins])


def group_rows(chip, count, mine, prev_row, after_row):
    half = lax.broadcasted_iota(jnp.int32, (1, LANES), 1) < 64
    first = mine[0:1] + jnp.where(half & (chip > 0), prev_row, 0.0)
    last = jnp.where(half & (chip < count - 1), mine[4:5] + after_row, 0.0)
    return [first, mine[1:4], last]


def chip_parts(core, own, other):
    low = jnp.where(core == 0, own, other)
    top = jnp.where(core == 0, other, own)
    return jnp.concatenate([low[0:2], low[2:3] + top[0:1], top[1:3]], axis=0)


def first_group_kernel(count, own_ref, other_ref, out_ref):
    me = lax.axis_index("tm")
    chip, core = me // 2, me % 2
    low = 8 * count
    base = low + 16

    def part(ref, where):
        where = jnp.clip(where, 0, count - 1)
        return ref[pl.ds(pl.multiple_of(base + where * 8, 8), 8)]

    def of_core(which, where):
        return jnp.where(core == which, part(own_ref, where), part(other_ref, where))

    mine = chip_parts(core, part(own_ref, chip)[0:3], part(other_ref, chip)[0:3])
    prev, after = of_core(1, chip - 1), of_core(0, chip + 1)
    scalars = own_ref[low + 8 : low + 16] + other_ref[low + 8 : low + 16]
    put(out_ref, 0, own_ref[low : low + 8] + other_ref[low : low + 8])
    att = group_rows(chip, count, mine, prev[2:3], after[0:1])
    put(out_ref, 8, jnp.concatenate(att + [scalars[3:6]], axis=0))


def group_kernel(count, *refs):
    *refs, rows_ref, out_ref = refs
    chip = lax.axis_index("tm") // 2
    ins, places = arrived(refs, count, chip)
    zero = jnp.zeros((8, LANES), f32)
    mine, prev, after = zero, zero, zero
    for ref, where in zip(ins, places):
        for half in range(2):
            at = (half * count + where) * 8
            at = at if isinstance(at, int) else pl.multiple_of(at, 8)
            rows_ref[pl.ds(at, 8)] = ref[half * 8 : half * 8 + 8]
        low = ref[24:32]
        mine = jnp.where(where == chip, low, mine)
        prev = jnp.where(where == chip - 1, low, prev)
        after = jnp.where(where == chip + 1, low, after)
    scalars = tree_sum([ref[24:32] for ref in ins])
    put(out_ref, 0, tree_sum([ref[16:24] for ref in ins]))
    att = group_rows(chip, count, mine, prev[4:5], after[0:1])
    put(out_ref, 8, jnp.concatenate(att + [scalars[5:8]], axis=0))


def astro_kernel(first, count, *refs):
    high = STARS_DEV // LANES
    if first:
        keep, (out_ref, table_ref, spread_ref) = refs[:2], refs[2:]
    else:
        keep, (table_ref, rows_ref, out_ref, spread_ref) = refs[:2], refs[2:]
    base = 16 * count + 16
    extra = (keep[0].shape[0] - base) // count
    comps = extra // 8 - 1
    long = 8 * LANES

    def one(place, totals):
        new = []
        for half in range(2):
            if first:
                rows = keep[half][pl.ds(pl.multiple_of(place * 8, 8), 8)]
            else:
                rows = rows_ref[pl.ds(pl.multiple_of((half * count + place) * 8, 8), 8)]
            packed = keep[half][pl.ds(pl.multiple_of(base + place * extra, 8), extra)]
            index = packed[comps * 8 :].astype(jnp.int32)
            at0 = pl.multiple_of((half * count + place) * long, long)
            split = [halves(packed[comp * 8 : comp * 8 + 8] * rows) for comp in range(comps)]
            for block in range(8):
                here = slice(block, block + 1)
                if first:
                    table_ref[:, pl.ds(at0 + block * LANES, LANES)] = one_hot_low(index[here])
                pieces = []
                for part in range(2):
                    for comp in range(comps):
                        pieces.append(spread_high(index[here], split[comp][part][here], high))
                spread_ref[half, :, block * LANES : (block + 1) * LANES] = jnp.concatenate(
                    pieces, axis=0
                ).astype(bf16)
            new.append(
                totals[half] + dot_lanes(spread_ref[half], table_ref[:, pl.ds(at0, long)])
            )
        return tuple(new)

    zero = jnp.zeros((2 * comps * high, LANES), f32)
    own, other = lax.fori_loop(0, count, one, (zero, zero))
    total = own + other
    out_ref[...] = total[: comps * high] + total[comps * high :]


def sum_kernel(count, *refs):
    ins, _ = arrived(refs[:-1], count, 0)
    put(refs[-1], 0, tree_sum([ref[...] for ref in ins]))


def lane_sum(row):
    return jnp.broadcast_to(jnp.sum(row, axis=1, keepdims=True), row.shape)


def next_bidiagonal(total, state):
    squares, mixed, size = (lane_sum(total[row : row + 1]) for row in (13, 14, 15))
    alpha2 = size + epsilon
    alpha = jnp.sqrt(alpha2)
    rest = jnp.maximum(squares / alpha2 - 2.0 * mixed + alpha2 * state[0:1], 0.0)
    beta2 = rest + epsilon
    return alpha, jnp.sqrt(beta2), rest / beta2


def step_kernel(step, width, slots, chips, star_count, *refs):
    keep, packs, tables, att2s, ints, sum_ref = refs[:2], refs[2:4], refs[4:6], refs[6:8], refs[8:10], refs[10]
    refs = refs[11:]
    if step > 0:
        state_ref, old_z_ref, old_g_ref, old_u_ref, old_s_ref = refs[:5]
        refs = refs[5:]
    gathered, refs = refs[:-7], refs[-7:]
    gathered, _ = arrived(gathered, star_count, 0)
    send_ref, state_out, z_ref, g_ref, u_ref, s_ref, spread_ref = refs
    me = lax.axis_index("tm")
    chip, core = me // 2, me % 2
    high = STARS_DEV // LANES
    comps = sum_ref.shape[0] // high
    blocks = 8
    total = tree_sum([ref[...] for ref in gathered])
    back = jnp.concatenate([sum_ref[...], total], axis=0)
    if step == 0:
        squares = lane_sum(total[13:14])
        beta2 = squares + epsilon
        beta = jnp.sqrt(beta2)
        at = pl.ds(pl.multiple_of(chip * 8, 8), 8)
        u = jnp.concatenate([ref[at] for ref in keep], axis=0) / beta
        g = back / beta
        z = g
        state_out[...] = jnp.concatenate(
            [squares / beta2, beta, jnp.zeros((14, LANES), f32)], axis=0
        )
    else:
        state = state_ref[...]
        alpha, beta, left2 = next_bidiagonal(total, state)
        u = (old_s_ref[...] / alpha - alpha * old_u_ref[...]) / beta
        g = (back / alpha - alpha * old_g_ref[...]) / beta
        z = g - (beta / alpha) * old_z_ref[...]
        pieces = [left2, state[1 : 1 + step], beta, jnp.zeros((7 - step, LANES), f32)]
        pieces += [state[9 : 8 + step]] if step > 1 else []
        pieces += [alpha, jnp.zeros((7 - step, LANES), f32)]
        state_out[...] = jnp.concatenate(pieces, axis=0)
    z_ref[...] = z
    g_ref[...] = g
    u_ref[...] = u
    base = comps * high
    inst_rows = z[base : base + 8]
    att_rows = z[base + 8 : base + 13]
    extra = 8 * comps + 8
    here = 16 * chips + 16 + chip * extra
    pieces = [inst_rows[place : place + 1] for place in range(8)]
    rows, insts, atts = [], [], []
    for half in range(2):
        starts = ints[half][slots * 8 :]
        own = jnp.where(core == half, att_rows[0:3], att_rows[2:5])
        part = att_forward(own, att2s[half][...], starts, width)
        packed = keep[half][pl.ds(pl.multiple_of(here, 8), extra)]
        star = packed[comps * 8 :].astype(jnp.int32)
        star_high, star_low = star >> 7, star & (LANES - 1)
        for comp in range(comps):
            picked = jnp.zeros((blocks, LANES), f32)
            for place in range(high):
                at = comp * high + place
                picked = jnp.where(star_high == place, lane_pick(z[at : at + 1], star_low), picked)
            part = part + packed[comp * 8 : comp * 8 + 8] * picked
        coefs = [packs[half].at[slot * 8 : slot * 8 + 8] for slot in range(slots)]
        indices = [ints[half].at[slot * 8 : slot * 8 + 8] for slot in range(slots)]
        for slot in range(slots):
            part = part + coefs[slot][...] * table_pick(pieces, indices[slot][...])
        rows.append(part)
        if step < ITERS - 1:
            insts.append(inst_back(part, coefs, indices, tables[half], spread_ref.at[half]))
            atts.append(att_back(part, att2s[half][...], starts, width))
    both = jnp.concatenate(rows, axis=0)
    s_ref[...] = both

    def squared(value):
        return jnp.sum(value * value, axis=0, keepdims=True)

    size = squared(z[:base]) * (1.0 / chips) + squared(att_rows[:4]) * (1.0 / star_count)
    size = size + squared(inst_rows) * (1.0 / (star_count * chips))
    mixed = [jnp.sum(rows[half] * u[half * 8 : half * 8 + 8], axis=0, keepdims=True) for half in range(2)]
    scalars = [squared(rows[0]) + squared(rows[1]), mixed[0] + mixed[1], size]
    if step == ITERS - 1:
        put(send_ref, 0, jnp.concatenate([jnp.zeros((5, LANES), f32)] + scalars, axis=0))
        return
    put(send_ref, 0, both)
    put(send_ref, 16, insts[0] + insts[1])
    put(send_ref, 24, jnp.concatenate([chip_parts(core, *atts)] + scalars, axis=0))


def last_kernel(comps, share, star_count, state_ref, *refs):
    gathered, refs = refs[: -ITERS - 3], refs[-ITERS - 3 :]
    gathered, _ = arrived(gathered, star_count, 0)
    z_refs = refs[:ITERS]
    astro_ref, att_ref, inst_ref = refs[ITERS:]
    high = STARS_DEV // LANES
    me = lax.axis_index("tm")
    total = tree_sum([ref[...] for ref in gathered])
    total = jnp.concatenate([jnp.zeros((8, LANES), f32), total], axis=0)
    state = state_ref[...]
    alpha, beta, _ = next_bidiagonal(total, state)
    betas = [state[1 + k : 2 + k] for k in range(ITERS)] + [beta]
    alphas = [state[9 + k : 10 + k] for k in range(ITERS - 1)] + [alpha]
    rho_bar, phi_bar = alphas[0], betas[0]
    weights = [jnp.zeros((1, LANES), f32)] * ITERS
    search = [jnp.zeros((1, LANES), f32)] * ITERS
    search[0] = 1.0 / alphas[0]
    for k in range(ITERS):
        rho = jnp.sqrt(rho_bar * rho_bar + betas[k + 1] * betas[k + 1])
        cosine, sine = rho_bar / rho, betas[k + 1] / rho
        phi = cosine * phi_bar
        phi_bar = sine * phi_bar
        weights = [x + phi / rho * w for x, w in zip(weights, search)]
        if k + 1 < ITERS:
            theta = sine * alphas[k + 1]
            rho_bar = -cosine * alphas[k + 1]
            search = [-(theta / rho) * w for w in search]
            search[k + 1] = 1.0 / alphas[k + 1]
    base = comps * high
    tiles = share // LANES

    def mix(read):
        total = weights[0] * read(z_refs[0])
        for k in range(1, ITERS):
            total = total + weights[k] * read(z_refs[k])
        return total

    for comp in range(comps):
        for tile in range(tiles):
            at = comp * high + me * tiles + tile
            astro_ref[comp : comp + 1, tile * LANES : (tile + 1) * LANES] = mix(
                lambda ref: ref[pl.ds(at, 1)]
            )
    inst_ref[...] = mix(lambda ref: ref[base : base + 8])
    rows = ATT_DEV // LANES
    att_ref[...] = mix(lambda ref: ref[pl.ds(base + 8 + (me % 2) * rows, rows)])


def call(kernel, name, out, args, scratch=(), space=pltpu.VMEM):
    vmem = pl.BlockSpec(memory_space=pltpu.VMEM)
    return pl.pallas_call(
        kernel,
        name=name,
        out_shape=[jax.ShapeDtypeStruct(shape, dtype) for shape, dtype in out],
        in_specs=[pl.BlockSpec(memory_space=space)] * len(args),
        out_specs=[vmem] * len(out),
        scratch_shapes=list(scratch),
        compiler_params=pltpu.CompilerParams(vmem_limit_bytes=VMEM_LIMIT),
    )(*args)


def exchange(value, axis, gaps):
    count = lax.axis_size(axis)
    if value.ndim == 3:
        members = [0] + list(gaps)
        groups = [[i ^ gap for gap in members] for i in range(count) if i == min(i ^ gap for gap in members)]
        return [lax.all_to_all(value, axis, 0, 0, axis_index_groups=groups if len(groups) > 1 else None)]
    return [value] + [
        lax.ppermute(value, axis, [(i, i ^ gap) for i in range(count)]) for gap in gaps
    ]


def rows_type(rows, copies=0):
    return ((copies, rows, LANES) if copies else (rows, LANES), f32)


def per_device(astro_coef, star_index, att_coef, att_start, inst_coef, inst_index, observed):
    tm_count, star_count = lax.axis_size("tm"), lax.axis_size("star")
    comps = astro_coef.shape[1]
    slots = inst_coef.shape[1]
    blocks, width, height = att_coef.shape[1:]
    share = STARS_DEV // tm_count
    high = STARS_DEV // LANES
    chips = tm_count // 2
    far = [2 * gap for gap in range(1, chips)]
    args = [
        observed.reshape(blocks, height),
        astro_coef.reshape(comps, blocks, height),
        star_index.reshape(blocks, height),
        att_coef.reshape(blocks * width, height),
        att_start,
        inst_coef.reshape(slots, blocks, height),
        inst_index.reshape(slots, blocks, height),
    ]
    long = slots * blocks * height
    extra = 8 * comps + 8
    spread = pltpu.VMEM((16, long), bf16)
    prepared = [((LANES, long), bf16), ((2 * blocks * width, height), bf16),
                ((8 * slots + 8, LANES), jnp.int32)]
    here = [pltpu.with_memory_space_constraint(arg, pltpu.HBM) for arg in args]
    send, pack, *mine = call(
        functools.partial(first_kernel, width),
        "first",
        [((24 + extra, LANES), f32), ((16 * slots + 8 + blocks * width, LANES), f32)] + prepared,
        here,
        [pltpu.VMEM(arg.shape, arg.dtype) for arg in args if arg is not args[3]]
        + [spread, pltpu.SemaphoreType.DMA((len(args),))],
        pl.ANY,
    )
    keep = star_table = state = z = g = u = rows = None
    kept = []
    group_type = rows_type(16)
    star_type = rows_type(16, STAR_COPIES and star_count)
    tm_copies = [TM_COPIES[step] and chips for step in range(ITERS)]
    for step in range(ITERS):
        wide = [pltpu.VMEM((2, 2 * comps * high, blocks * height), bf16)]
        sums_type = ((comps * high, LANES), f32)
        got = exchange(send, "tm", far)
        if step == 0:
            (gathered,) = call(
                functools.partial(first_chip_kernel, chips),
                "chip",
                [((16 * chips + 16 + chips * extra, LANES), f32)],
                got,
            )
            keep = exchange(gathered, "tm", [1])
            (group,) = call(
                functools.partial(first_group_kernel, chips), "group", [star_type], keep
            )
            group, late_pack = lax.optimization_barrier((group, pack))
            _, other_pack = exchange(late_pack, "tm", [1])
            theirs = call(
                functools.partial(prepare_kernel, slots, blocks, width),
                "prepare",
                prepared,
                [other_pack],
            )
            basics = [pack, other_pack] + [value for both in zip(mine, theirs) for value in both]
        else:
            all_rows, group = call(
                functools.partial(group_kernel, chips),
                "group",
                [rows_type(16 * chips), star_type],
                got,
            )
        across = exchange(group, "star", range(1, star_count))
        if step == 0:
            sums, star_table = call(
                functools.partial(astro_kernel, True, chips),
                "astro",
                [sums_type, ((LANES, tm_count * blocks * height), bf16)],
                keep,
                wide,
            )
        else:
            (sums,) = call(
                functools.partial(astro_kernel, False, chips),
                "astro",
                [sums_type],
                keep + [star_table, all_rows],
                wide,
            )
        tall = ((comps * high + 16, LANES), f32)
        pair = ((2 * blocks, height), f32)
        older = [] if step == 0 else [state, z, g, u, rows]
        send, state, z, g, u, rows = call(
            functools.partial(step_kernel, step, width, slots, chips, star_count),
            "step",
            [rows_type(32 if step < ITERS - 1 else 8, tm_copies[step]), group_type, tall, tall,
             pair, pair],
            keep + basics + [sums] + older + across,
            [pltpu.VMEM((2, 16, long), bf16)],
        )
        kept.append(z)
    (send,) = call(
        functools.partial(sum_kernel, chips),
        "sum",
        [rows_type(8, STAR_COPIES and star_count)],
        exchange(send, "tm", far),
    )
    across = exchange(send, "star", range(1, star_count))
    out_astro, out_att, out_inst = call(
        functools.partial(last_kernel, comps, share, star_count),
        "last",
        [((comps, share), f32), ((ATT_DEV // LANES, LANES), f32), ((NINST // LANES, LANES), f32)],
        [state] + across + kept,
    )
    return out_astro, out_att.reshape(-1), out_inst.reshape(-1)


def solution(mesh):
    return jax.shard_map(
        per_device,
        mesh=mesh,
        in_specs=(
            P("star", None, "tm"),
            P("star", "tm"),
            P("star", "tm", None, None),
            P("star", "tm"),
            P("star", None, "tm"),
            P("star", None, "tm"),
            P("star", "tm"),
        ),
        out_specs=(P(None, ("star", "tm")), P("tm"), P()),
        check_vma=False,
    )
```

```python
import functools

import jax
import jax.numpy as jnp
from jax import lax
from jax.experimental import pallas as pl
from jax.experimental.pallas import tpu as pltpu
from jax.sharding import PartitionSpec as P

STARS_DEV = 2048
NINST = 1024
ITERS = 3
ATT_DEV = 256
LANES = 128

epsilon = 1e-06
STAR_COPIES = False
TM_COPIES = [False, False, False]
f32 = jnp.float32
bf16 = jnp.bfloat16
VMEM_LIMIT = 16 * 1024 * 1024


def halves(value):
    top = value.astype(bf16).astype(f32)
    return top, (value - top).astype(bf16).astype(f32)


def dot_lanes(left, right):
    return lax.dot_general(left, right, (((1,), (1,)), ((), ())), preferred_element_type=f32)


def dot_plain(left, right):
    return lax.dot_general(left, right, (((1,), (0,)), ((), ())), preferred_element_type=f32)


def lane_pick(row, lane_index):
    table = jnp.broadcast_to(row, lane_index.shape)
    return jnp.take_along_axis(table, lane_index, axis=1, mode="promise_in_bounds")


def table_pick(rows, index):
    high, low = index >> 7, index & (LANES - 1)
    total = jnp.zeros(index.shape, f32)
    for place, row in enumerate(rows):
        total = jnp.where(high == place, lane_pick(row, low), total)
    return total


def one_hot_low(index_row):
    shape = (LANES, LANES)
    low = jnp.broadcast_to(index_row & (LANES - 1), shape)
    hit = lax.broadcasted_iota(jnp.int32, shape, 0) == low
    return jnp.where(hit, 1.0, 0.0).astype(bf16)


def spread_high(index_row, value_row, count):
    shape = (count, LANES)
    high = jnp.broadcast_to(index_row >> 7, shape)
    hit = lax.broadcasted_iota(jnp.int32, shape, 0) == high
    return jnp.where(hit, jnp.broadcast_to(value_row, shape), 0.0)


def block_masks(blocks, width):
    shape = (blocks, LANES)
    row = lax.broadcasted_iota(jnp.int32, shape, 0)
    lane = lax.broadcasted_iota(jnp.int32, shape, 1)
    per_tile = LANES // width
    tiles = blocks // per_tile
    return [row == tile * per_tile + lane // width for tile in range(tiles)], row, lane


def inst_back(rows, coef_ref, index_ref, table_ref, spread_ref):
    slots, blocks = len(coef_ref), rows.shape[0]
    count = NINST // LANES
    for slot in range(slots):
        top, rest = halves(coef_ref[slot][...] * rows)
        index = index_ref[slot][...]
        for block in range(blocks):
            here = slice(block, block + 1)
            pieces = [spread_high(index[here], part[here], count) for part in (top, rest)]
            at = (slot * blocks + block) * LANES
            spread_ref[:, at : at + LANES] = jnp.concatenate(pieces, axis=0).astype(bf16)
    both = dot_lanes(spread_ref[...], table_ref[...])
    return both[:count] + both[count:]


def att_back(rows, att2, starts, width):
    blocks = rows.shape[0]
    size = att2.shape[0] // 2
    top, rest = halves(rows)
    both = dot_lanes(jnp.concatenate([top, rest], axis=0).astype(bf16), att2)
    both = both[:blocks] + both[blocks:]
    both = both[:, :size] + both[:, size:]
    masks, row, lane = block_masks(blocks, width)
    own = jnp.zeros((blocks, LANES), f32)
    for tile, mask in enumerate(masks):
        own = own + jnp.where(mask, both[:, tile * LANES : (tile + 1) * LANES], 0.0)
    shift = (row % (LANES // width)) * width
    out = []
    for tile in range((ATT_DEV + width + LANES - 1) // LANES):
        offset = lane + tile * LANES - starts
        inside = (offset >= 0) & (offset < width)
        picked = jnp.take_along_axis(
            own, jnp.where(inside, offset + shift, 0), axis=1, mode="promise_in_bounds"
        )
        out.append(jnp.sum(jnp.where(inside, picked, 0.0), axis=0, keepdims=True))
    return jnp.concatenate(out, axis=0)


def att_forward(att_rows, att2, starts, width):
    blocks = starts.shape[0]
    masks, row, lane = block_masks(blocks, width)
    tiles = [att_rows[tile : tile + 1] for tile in range(att_rows.shape[0])]
    window = table_pick(tiles, starts + lane % width)
    wide = jnp.concatenate([jnp.where(mask, window, 0.0) for mask in masks], axis=1)
    top, rest = halves(wide)
    left = jnp.concatenate([top, rest], axis=0).astype(bf16)
    both = dot_plain(jnp.concatenate([left, left], axis=1), att2)
    return both[:blocks] + both[blocks:]


def pack_places(slots, blocks, width):
    at = slots * 8
    return slice(0, at), slice(at, 2 * at), slice(2 * at, 2 * at + 8), slice(
        2 * at + 8, 2 * at + 8 + blocks * width
    )


def prepare_index(index_rows, starts, table_ref, ints_ref):
    count = index_rows.shape[0] // 8
    ints_ref[0 : count * 8] = index_rows
    ints_ref[count * 8 :] = starts
    for place in range(count * 8):
        table_ref[:, place * LANES : (place + 1) * LANES] = one_hot_low(
            index_rows[place : place + 1]
        )


def prepare_att(att, att2_ref):
    top = att.astype(bf16)
    att2_ref[...] = jnp.concatenate([top, (att - top.astype(f32)).astype(bf16)], axis=0)


def first_kernel(width, b_hbm, astro_hbm, star_hbm, att_hbm, starts_hbm, coef_hbm, index_hbm,
                 send_ref, pack_ref, table_ref, att2_ref, ints_ref,
                 b_ref, astro_ref, star_ref, starts_ref, coef_ref, index_ref,
                 spread_ref, sems):
    slots, blocks, _ = index_ref.shape
    comps = astro_ref.shape[0]
    places = pack_places(slots, blocks, width)
    pairs = [(index_hbm, index_ref), (starts_hbm, starts_ref), (att_hbm, pack_ref.at[places[3]]),
             (coef_hbm, coef_ref), (b_hbm, b_ref), (astro_hbm, astro_ref), (star_hbm, star_ref)]
    copies = [
        pltpu.make_async_copy(source, target, sems.at[place])
        for place, (source, target) in enumerate(pairs)
    ]
    for copy in copies:
        copy.start()
    for copy in copies[:2]:
        copy.wait()
    index = jnp.concatenate([index_ref[slot] for slot in range(slots)], axis=0)
    starts_row = jnp.broadcast_to(starts_ref[...].astype(f32), (blocks, blocks))
    diagonal = lax.broadcasted_iota(jnp.int32, (blocks, blocks), 0) == lax.broadcasted_iota(
        jnp.int32, (blocks, blocks), 1
    )
    starts = jnp.sum(jnp.where(diagonal, starts_row, 0.0), axis=1, keepdims=True)
    starts = jnp.broadcast_to(starts, (blocks, LANES))
    pack_ref[places[1]] = index.astype(f32)
    pack_ref[places[2]] = starts
    starts = starts.astype(jnp.int32)
    prepare_index(index, starts, table_ref, ints_ref)
    for copy in copies[2:]:
        copy.wait()
    prepare_att(pack_ref[places[3]], att2_ref)
    rows = b_ref[...]
    coefs = [coef_ref.at[slot] for slot in range(slots)]
    indices = [index_ref.at[slot] for slot in range(slots)]
    for slot in range(slots):
        pack_ref[slot * 8 : slot * 8 + 8] = coef_ref[slot]
    send_ref[0:8] = rows
    send_ref[8:16] = inst_back(rows, coefs, indices, table_ref, spread_ref)
    send_ref[16:19] = att_back(rows, att2_ref[...], starts, width)
    send_ref[19:20] = jnp.sum(rows * rows, axis=0, keepdims=True)
    send_ref[20:24] = jnp.zeros((4, LANES), f32)
    for comp in range(comps):
        send_ref[24 + comp * 8 : 32 + comp * 8] = astro_ref[comp]
    send_ref[24 + comps * 8 : 32 + comps * 8] = star_ref[...].astype(f32)


def prepare_kernel(slots, blocks, width, pack_ref, table_ref, att2_ref, ints_ref):
    places = pack_places(slots, blocks, width)
    index = pack_ref[places[1]].astype(jnp.int32)
    starts = pack_ref[places[2]].astype(jnp.int32)
    prepare_index(index, starts, table_ref, ints_ref)
    prepare_att(pack_ref[places[3]], att2_ref)


def put(ref, start, value):
    rows = slice(start, start + value.shape[0])
    if len(ref.shape) == 2:
        ref[rows] = value
    else:
        for copy in range(ref.shape[0]):
            ref[copy, rows] = value


def arrived(refs, count, here):
    if len(refs) == 1:
        return [refs[0].at[place] for place in range(count)], list(range(count))
    return list(refs), [here ^ gap for gap in range(count)]


def tree_sum(values):
    while len(values) > 1:
        values = [values[i] + values[i + 1] for i in range(0, len(values), 2)]
    return values[0]


def first_chip_kernel(count, *refs):
    ins, out_ref = refs[:count], refs[count]
    chip = lax.axis_index("tm") // 2
    extra = ins[0].shape[0] - 24
    base = 8 * count + 16
    for gap in range(count):
        where = chip ^ gap
        out_ref[pl.ds(pl.multiple_of(where * 8, 8), 8)] = ins[gap][0:8]
        out_ref[pl.ds(pl.multiple_of(base + where * 8, 8), 8)] = ins[gap][16:24]
        at = pl.multiple_of(base + 8 * count + where * extra, 8)
        out_ref[pl.ds(at, extra)] = ins[gap][24:]
    out_ref[8 * count : 8 * count + 8] = tree_sum([ref[8:16] for ref in ins])
    out_ref[8 * count + 8 : base] = tree_sum([ref[16:24] for ref in ins])


def group_rows(chip, count, mine, prev_row, after_row):
    half = lax.broadcasted_iota(jnp.int32, (1, LANES), 1) < 64
    first = mine[0:1] + jnp.where(half & (chip > 0), prev_row, 0.0)
    last = jnp.where(half & (chip < count - 1), mine[4:5] + after_row, 0.0)
    return [first, mine[1:4], last]


def chip_parts(core, own, other):
    low = jnp.where(core == 0, own, other)
    top = jnp.where(core == 0, other, own)
    return jnp.concatenate([low[0:2], low[2:3] + top[0:1], top[1:3]], axis=0)


def first_group_kernel(count, own_ref, other_ref, out_ref):
    me = lax.axis_index("tm")
    chip, core = me // 2, me % 2
    low = 8 * count
    base = low + 16

    def part(ref, where):
        where = jnp.clip(where, 0, count - 1)
        return ref[pl.ds(pl.multiple_of(base + where * 8, 8), 8)]

    def of_core(which, where):
        return jnp.where(core == which, part(own_ref, where), part(other_ref, where))

    mine = chip_parts(core, part(own_ref, chip)[0:3], part(other_ref, chip)[0:3])
    prev, after = of_core(1, chip - 1), of_core(0, chip + 1)
    scalars = own_ref[low + 8 : low + 16] + other_ref[low + 8 : low + 16]
    put(out_ref, 0, own_ref[low : low + 8] + other_ref[low : low + 8])
    att = group_rows(chip, count, mine, prev[2:3], after[0:1])
    put(out_ref, 8, jnp.concatenate(att + [scalars[3:6]], axis=0))


def group_kernel(count, *refs):
    *refs, rows_ref, out_ref = refs
    chip = lax.axis_index("tm") // 2
    ins, places = arrived(refs, count, chip)
    zero = jnp.zeros((8, LANES), f32)
    mine, prev, after = zero, zero, zero
    for ref, where in zip(ins, places):
        for half in range(2):
            at = (half * count + where) * 8
            at = at if isinstance(at, int) else pl.multiple_of(at, 8)
            rows_ref[pl.ds(at, 8)] = ref[half * 8 : half * 8 + 8]
        low = ref[24:32]
        mine = jnp.where(where == chip, low, mine)
        prev = jnp.where(where == chip - 1, low, prev)
        after = jnp.where(where == chip + 1, low, after)
    scalars = tree_sum([ref[24:32] for ref in ins])
    put(out_ref, 0, tree_sum([ref[16:24] for ref in ins]))
    att = group_rows(chip, count, mine, prev[4:5], after[0:1])
    put(out_ref, 8, jnp.concatenate(att + [scalars[5:8]], axis=0))


def astro_kernel(first, count, *refs):
    high = STARS_DEV // LANES
    if first:
        keep, (out_ref, table_ref, spread_ref) = refs[:2], refs[2:]
    else:
        keep, (table_ref, rows_ref, out_ref, spread_ref) = refs[:2], refs[2:]
    base = 16 * count + 16
    extra = (keep[0].shape[0] - base) // count
    comps = extra // 8 - 1
    long = 8 * LANES

    def one(place, totals):
        new = []
        for half in range(2):
            if first:
                rows = keep[half][pl.ds(pl.multiple_of(place * 8, 8), 8)]
            else:
                rows = rows_ref[pl.ds(pl.multiple_of((half * count + place) * 8, 8), 8)]
            packed = keep[half][pl.ds(pl.multiple_of(base + place * extra, 8), extra)]
            index = packed[comps * 8 :].astype(jnp.int32)
            at0 = pl.multiple_of((half * count + place) * long, long)
            split = [halves(packed[comp * 8 : comp * 8 + 8] * rows) for comp in range(comps)]
            for block in range(8):
                here = slice(block, block + 1)
                if first:
                    table_ref[:, pl.ds(at0 + block * LANES, LANES)] = one_hot_low(index[here])
                pieces = []
                for part in range(2):
                    for comp in range(comps):
                        pieces.append(spread_high(index[here], split[comp][part][here], high))
                spread_ref[half, :, block * LANES : (block + 1) * LANES] = jnp.concatenate(
                    pieces, axis=0
                ).astype(bf16)
            new.append(
                totals[half] + dot_lanes(spread_ref[half], table_ref[:, pl.ds(at0, long)])
            )
        return tuple(new)

    zero = jnp.zeros((2 * comps * high, LANES), f32)
    own, other = lax.fori_loop(0, count, one, (zero, zero))
    total = own + other
    out_ref[...] = total[: comps * high] + total[comps * high :]


def sum_kernel(count, *refs):
    ins, _ = arrived(refs[:-1], count, 0)
    put(refs[-1], 0, tree_sum([ref[...] for ref in ins]))


def lane_sum(row):
    return jnp.broadcast_to(jnp.sum(row, axis=1, keepdims=True), row.shape)


def next_bidiagonal(total, state):
    squares, mixed, size = (lane_sum(total[row : row + 1]) for row in (13, 14, 15))
    alpha2 = size + epsilon
    alpha = jnp.sqrt(alpha2)
    rest = jnp.maximum(squares / alpha2 - 2.0 * mixed + alpha2 * state[0:1], 0.0)
    beta2 = rest + epsilon
    return alpha, jnp.sqrt(beta2), rest / beta2


def step_kernel(step, width, slots, chips, star_count, *refs):
    keep, packs, tables, att2s, ints, sum_ref = refs[:2], refs[2:4], refs[4:6], refs[6:8], refs[8:10], refs[10]
    refs = refs[11:]
    if step > 0:
        state_ref, old_z_ref, old_g_ref, old_u_ref, old_s_ref = refs[:5]
        refs = refs[5:]
    gathered, refs = refs[:-7], refs[-7:]
    gathered, _ = arrived(gathered, star_count, 0)
    send_ref, state_out, z_ref, g_ref, u_ref, s_ref, spread_ref = refs
    me = lax.axis_index("tm")
    chip, core = me // 2, me % 2
    high = STARS_DEV // LANES
    comps = sum_ref.shape[0] // high
    blocks = 8
    total = tree_sum([ref[...] for ref in gathered])
    back = jnp.concatenate([sum_ref[...], total], axis=0)
    if step == 0:
        squares = lane_sum(total[13:14])
        beta2 = squares + epsilon
        beta = jnp.sqrt(beta2)
        at = pl.ds(pl.multiple_of(chip * 8, 8), 8)
        u = jnp.concatenate([ref[at] for ref in keep], axis=0) / beta
        g = back / beta
        z = g
        state_out[...] = jnp.concatenate(
            [squares / beta2, beta, jnp.zeros((14, LANES), f32)], axis=0
        )
    else:
        state = state_ref[...]
        alpha, beta, left2 = next_bidiagonal(total, state)
        u = (old_s_ref[...] / alpha - alpha * old_u_ref[...]) / beta
        g = (back / alpha - alpha * old_g_ref[...]) / beta
        z = g - (beta / alpha) * old_z_ref[...]
        pieces = [left2, state[1 : 1 + step], beta, jnp.zeros((7 - step, LANES), f32)]
        pieces += [state[9 : 8 + step]] if step > 1 else []
        pieces += [alpha, jnp.zeros((7 - step, LANES), f32)]
        state_out[...] = jnp.concatenate(pieces, axis=0)
    z_ref[...] = z
    g_ref[...] = g
    u_ref[...] = u
    base = comps * high
    inst_rows = z[base : base + 8]
    att_rows = z[base + 8 : base + 13]
    extra = 8 * comps + 8
    here = 16 * chips + 16 + chip * extra
    pieces = [inst_rows[place : place + 1] for place in range(8)]
    rows, insts, atts = [], [], []
    for half in range(2):
        starts = ints[half][slots * 8 :]
        own = jnp.where(core == half, att_rows[0:3], att_rows[2:5])
        part = att_forward(own, att2s[half][...], starts, width)
        packed = keep[half][pl.ds(pl.multiple_of(here, 8), extra)]
        star = packed[comps * 8 :].astype(jnp.int32)
        star_high, star_low = star >> 7, star & (LANES - 1)
        for comp in range(comps):
            picked = jnp.zeros((blocks, LANES), f32)
            for place in range(high):
                at = comp * high + place
                picked = jnp.where(star_high == place, lane_pick(z[at : at + 1], star_low), picked)
            part = part + packed[comp * 8 : comp * 8 + 8] * picked
        coefs = [packs[half].at[slot * 8 : slot * 8 + 8] for slot in range(slots)]
        indices = [ints[half].at[slot * 8 : slot * 8 + 8] for slot in range(slots)]
        for slot in range(slots):
            part = part + coefs[slot][...] * table_pick(pieces, indices[slot][...])
        rows.append(part)
        if step < ITERS - 1:
            insts.append(inst_back(part, coefs, indices, tables[half], spread_ref.at[half]))
            atts.append(att_back(part, att2s[half][...], starts, width))
    both = jnp.concatenate(rows, axis=0)
    s_ref[...] = both

    def squared(value):
        return jnp.sum(value * value, axis=0, keepdims=True)

    size = squared(z[:base]) * (1.0 / chips) + squared(att_rows[:4]) * (1.0 / star_count)
    size = size + squared(inst_rows) * (1.0 / (star_count * chips))
    mixed = [jnp.sum(rows[half] * u[half * 8 : half * 8 + 8], axis=0, keepdims=True) for half in range(2)]
    scalars = [squared(rows[0]) + squared(rows[1]), mixed[0] + mixed[1], size]
    if step == ITERS - 1:
        put(send_ref, 0, jnp.concatenate([jnp.zeros((5, LANES), f32)] + scalars, axis=0))
        return
    put(send_ref, 0, both)
    put(send_ref, 16, insts[0] + insts[1])
    put(send_ref, 24, jnp.concatenate([chip_parts(core, *atts)] + scalars, axis=0))


def last_kernel(comps, share, star_count, state_ref, *refs):
    gathered, refs = refs[: -ITERS - 3], refs[-ITERS - 3 :]
    gathered, _ = arrived(gathered, star_count, 0)
    z_refs = refs[:ITERS]
    astro_ref, att_ref, inst_ref = refs[ITERS:]
    high = STARS_DEV // LANES
    me = lax.axis_index("tm")
    total = tree_sum([ref[...] for ref in gathered])
    total = jnp.concatenate([jnp.zeros((8, LANES), f32), total], axis=0)
    state = state_ref[...]
    alpha, beta, _ = next_bidiagonal(total, state)
    betas = [state[1 + k : 2 + k] for k in range(ITERS)] + [beta]
    alphas = [state[9 + k : 10 + k] for k in range(ITERS - 1)] + [alpha]
    rho_bar, phi_bar = alphas[0], betas[0]
    weights = [jnp.zeros((1, LANES), f32)] * ITERS
    search = [jnp.zeros((1, LANES), f32)] * ITERS
    search[0] = 1.0 / alphas[0]
    for k in range(ITERS):
        rho = jnp.sqrt(rho_bar * rho_bar + betas[k + 1] * betas[k + 1])
        cosine, sine = rho_bar / rho, betas[k + 1] / rho
        phi = cosine * phi_bar
        phi_bar = sine * phi_bar
        weights = [x + phi / rho * w for x, w in zip(weights, search)]
        if k + 1 < ITERS:
            theta = sine * alphas[k + 1]
            rho_bar = -cosine * alphas[k + 1]
            search = [-(theta / rho) * w for w in search]
            search[k + 1] = 1.0 / alphas[k + 1]
    base = comps * high
    tiles = share // LANES

    def mix(read):
        total = weights[0] * read(z_refs[0])
        for k in range(1, ITERS):
            total = total + weights[k] * read(z_refs[k])
        return total

    for comp in range(comps):
        for tile in range(tiles):
            at = comp * high + me * tiles + tile
            astro_ref[comp : comp + 1, tile * LANES : (tile + 1) * LANES] = mix(
                lambda ref: ref[pl.ds(at, 1)]
            )
    inst_ref[...] = mix(lambda ref: ref[base : base + 8])
    rows = ATT_DEV // LANES
    att_ref[...] = mix(lambda ref: ref[pl.ds(base + 8 + (me % 2) * rows, rows)])


def call(kernel, name, out, args, scratch=(), space=pltpu.VMEM):
    vmem = pl.BlockSpec(memory_space=pltpu.VMEM)
    return pl.pallas_call(
        kernel,
        name=name,
        out_shape=[jax.ShapeDtypeStruct(shape, dtype) for shape, dtype in out],
        in_specs=[pl.BlockSpec(memory_space=space)] * len(args),
        out_specs=[vmem] * len(out),
        scratch_shapes=list(scratch),
        compiler_params=pltpu.CompilerParams(vmem_limit_bytes=VMEM_LIMIT),
    )(*args)


def exchange(value, axis, gaps):
    count = lax.axis_size(axis)
    if value.ndim == 3:
        members = [0] + list(gaps)
        groups = [[i ^ gap for gap in members] for i in range(count) if i == min(i ^ gap for gap in members)]
        return [lax.all_to_all(value, axis, 0, 0, axis_index_groups=groups if len(groups) > 1 else None)]
    return [value] + [
        lax.ppermute(value, axis, [(i, i ^ gap) for i in range(count)]) for gap in gaps
    ]


def rows_type(rows, copies=0):
    return ((copies, rows, LANES) if copies else (rows, LANES), f32)


def per_device(astro_coef, star_index, att_coef, att_start, inst_coef, inst_index, observed):
    tm_count, star_count = lax.axis_size("tm"), lax.axis_size("star")
    comps = astro_coef.shape[1]
    slots = inst_coef.shape[1]
    blocks, width, height = att_coef.shape[1:]
    share = STARS_DEV // tm_count
    high = STARS_DEV // LANES
    chips = tm_count // 2
    far = [2 * gap for gap in range(1, chips)]
    args = [
        observed.reshape(blocks, height),
        astro_coef.reshape(comps, blocks, height),
        star_index.reshape(blocks, height),
        att_coef.reshape(blocks * width, height),
        att_start,
        inst_coef.reshape(slots, blocks, height),
        inst_index.reshape(slots, blocks, height),
    ]
    long = slots * blocks * height
    extra = 8 * comps + 8
    spread = pltpu.VMEM((16, long), bf16)
    prepared = [((LANES, long), bf16), ((2 * blocks * width, height), bf16),
                ((8 * slots + 8, LANES), jnp.int32)]
    here = [pltpu.with_memory_space_constraint(arg, pltpu.HBM) for arg in args]
    send, pack, *mine = call(
        functools.partial(first_kernel, width),
        "first",
        [((24 + extra, LANES), f32), ((16 * slots + 8 + blocks * width, LANES), f32)] + prepared,
        here,
        [pltpu.VMEM(arg.shape, arg.dtype) for arg in args if arg is not args[3]]
        + [spread, pltpu.SemaphoreType.DMA((len(args),))],
        pl.ANY,
    )
    keep = star_table = state = z = g = u = rows = None
    kept = []
    group_type = rows_type(16)
    star_type = rows_type(16, STAR_COPIES and star_count)
    tm_copies = [TM_COPIES[step] and chips for step in range(ITERS)]
    for step in range(ITERS):
        wide = [pltpu.VMEM((2, 2 * comps * high, blocks * height), bf16)]
        sums_type = ((comps * high, LANES), f32)
        got = exchange(send, "tm", far)
        if step == 0:
            (gathered,) = call(
                functools.partial(first_chip_kernel, chips),
                "chip",
                [((16 * chips + 16 + chips * extra, LANES), f32)],
                got,
            )
            keep = exchange(gathered, "tm", [1])
            (group,) = call(
                functools.partial(first_group_kernel, chips), "group", [star_type], keep
            )
            group, late_pack = lax.optimization_barrier((group, pack))
            _, other_pack = exchange(late_pack, "tm", [1])
            theirs = call(
                functools.partial(prepare_kernel, slots, blocks, width),
                "prepare",
                prepared,
                [other_pack],
            )
            basics = [pack, other_pack] + [value for both in zip(mine, theirs) for value in both]
        else:
            all_rows, group = call(
                functools.partial(group_kernel, chips),
                "group",
                [rows_type(16 * chips), star_type],
                got,
            )
        across = exchange(group, "star", range(1, star_count))
        if step == 0:
            sums, star_table = call(
                functools.partial(astro_kernel, True, chips),
                "astro",
                [sums_type, ((LANES, tm_count * blocks * height), bf16)],
                keep,
                wide,
            )
        else:
            (sums,) = call(
                functools.partial(astro_kernel, False, chips),
                "astro",
                [sums_type],
                keep + [star_table, all_rows],
                wide,
            )
        tall = ((comps * high + 16, LANES), f32)
        pair = ((2 * blocks, height), f32)
        older = [] if step == 0 else [state, z, g, u, rows]
        send, state, z, g, u, rows = call(
            functools.partial(step_kernel, step, width, slots, chips, star_count),
            "step",
            [rows_type(32 if step < ITERS - 1 else 8, tm_copies[step]), group_type, tall, tall,
             pair, pair],
            keep + basics + [sums] + older + across,
            [pltpu.VMEM((2, 16, long), bf16)],
        )
        kept.append(z)
    (send,) = call(
        functools.partial(sum_kernel, chips),
        "sum",
        [rows_type(8, STAR_COPIES and star_count)],
        exchange(send, "tm", far),
    )
    across = exchange(send, "star", range(1, star_count))
    out_astro, out_att, out_inst = call(
        functools.partial(last_kernel, comps, share, star_count),
        "last",
        [((comps, share), f32), ((ATT_DEV // LANES, LANES), f32), ((NINST // LANES, LANES), f32)],
        [state] + across + kept,
    )
    return out_astro, out_att.reshape(-1), out_inst.reshape(-1)


def solution(mesh):
    return jax.shard_map(
        per_device,
        mesh=mesh,
        in_specs=(
            P("star", None, "tm"),
            P("star", "tm"),
            P("star", "tm", None, None),
            P("star", "tm"),
            P("star", None, "tm"),
            P("star", None, "tm"),
            P("star", "tm"),
        ),
        out_specs=(P(None, ("star", "tm")), P("tm"), P()),
        check_vma=False,
    )
```

```python
import functools

import jax
import jax.numpy as jnp
from jax import lax
from jax.experimental import pallas as pl
from jax.experimental.pallas import tpu as pltpu
from jax.sharding import PartitionSpec as P

STARS_DEV = 2048
NINST = 1024
ITERS = 3
ATT_DEV = 256
LANES = 128

epsilon = 1e-06
f32 = jnp.float32
bf16 = jnp.bfloat16
VMEM_LIMIT = 16 * 1024 * 1024


def halves(value):
    top = value.astype(bf16).astype(f32)
    return top, (value - top).astype(bf16).astype(f32)


def dot_lanes(left, right):
    return lax.dot_general(left, right, (((1,), (1,)), ((), ())), preferred_element_type=f32)


def dot_plain(left, right):
    return lax.dot_general(left, right, (((1,), (0,)), ((), ())), preferred_element_type=f32)


def lane_pick(row, lane_index):
    table = jnp.broadcast_to(row, lane_index.shape)
    return jnp.take_along_axis(table, lane_index, axis=1, mode="promise_in_bounds")


def table_pick(rows, index):
    high, low = index >> 7, index & (LANES - 1)
    total = jnp.zeros(index.shape, f32)
    for place, row in enumerate(rows):
        total = jnp.where(high == place, lane_pick(row, low), total)
    return total


def one_hot_low(index_row):
    shape = (LANES, LANES)
    low = jnp.broadcast_to(index_row & (LANES - 1), shape)
    hit = lax.broadcasted_iota(jnp.int32, shape, 0) == low
    return jnp.where(hit, 1.0, 0.0).astype(bf16)


def spread_high(index_row, value_row, count):
    shape = (count, LANES)
    high = jnp.broadcast_to(index_row >> 7, shape)
    hit = lax.broadcasted_iota(jnp.int32, shape, 0) == high
    return jnp.where(hit, jnp.broadcast_to(value_row, shape), 0.0)


def block_masks(blocks, width):
    shape = (blocks, LANES)
    row = lax.broadcasted_iota(jnp.int32, shape, 0)
    lane = lax.broadcasted_iota(jnp.int32, shape, 1)
    per_tile = LANES // width
    tiles = blocks // per_tile
    return [row == tile * per_tile + lane // width for tile in range(tiles)], row, lane


def inst_back(rows, coef_ref, index_ref, table_ref, spread_ref):
    slots, blocks = len(coef_ref), rows.shape[0]
    count = NINST // LANES
    for slot in range(slots):
        top, rest = halves(coef_ref[slot][...] * rows)
        index = index_ref[slot][...]
        for block in range(blocks):
            here = slice(block, block + 1)
            pieces = [spread_high(index[here], part[here], count) for part in (top, rest)]
            at = (slot * blocks + block) * LANES
            spread_ref[:, at : at + LANES] = jnp.concatenate(pieces, axis=0).astype(bf16)
    both = dot_lanes(spread_ref[...], table_ref[...])
    return both[:count] + both[count:]


def att_back(rows, att2, starts, width):
    blocks = rows.shape[0]
    size = att2.shape[0] // 2
    top, rest = halves(rows)
    both = dot_lanes(jnp.concatenate([top, rest], axis=0).astype(bf16), att2)
    both = both[:blocks] + both[blocks:]
    both = both[:, :size] + both[:, size:]
    masks, row, lane = block_masks(blocks, width)
    own = jnp.zeros((blocks, LANES), f32)
    for tile, mask in enumerate(masks):
        own = own + jnp.where(mask, both[:, tile * LANES : (tile + 1) * LANES], 0.0)
    shift = (row % (LANES // width)) * width
    out = []
    for tile in range((ATT_DEV + width + LANES - 1) // LANES):
        offset = lane + tile * LANES - starts
        inside = (offset >= 0) & (offset < width)
        picked = jnp.take_along_axis(
            own, jnp.where(inside, offset + shift, 0), axis=1, mode="promise_in_bounds"
        )
        out.append(jnp.sum(jnp.where(inside, picked, 0.0), axis=0, keepdims=True))
    return jnp.concatenate(out, axis=0)


def att_forward(att_rows, att2, starts, width):
    blocks = starts.shape[0]
    masks, row, lane = block_masks(blocks, width)
    tiles = [att_rows[tile : tile + 1] for tile in range(att_rows.shape[0])]
    window = table_pick(tiles, starts + lane % width)
    wide = jnp.concatenate([jnp.where(mask, window, 0.0) for mask in masks], axis=1)
    top, rest = halves(wide)
    left = jnp.concatenate([top, rest], axis=0).astype(bf16)
    both = dot_plain(jnp.concatenate([left, left], axis=1), att2)
    return both[:blocks] + both[blocks:]


def pack_places(slots, blocks, width):
    at = slots * 8
    return slice(0, at), slice(at, 2 * at), slice(2 * at, 2 * at + 8), slice(
        2 * at + 8, 2 * at + 8 + blocks * width
    )


def prepare_index(index_rows, starts, table_ref, ints_ref):
    count = index_rows.shape[0] // 8
    ints_ref[0 : count * 8] = index_rows
    ints_ref[count * 8 :] = starts
    for place in range(count * 8):
        table_ref[:, place * LANES : (place + 1) * LANES] = one_hot_low(
            index_rows[place : place + 1]
        )


def prepare_att(att, att2_ref):
    top = att.astype(bf16)
    att2_ref[...] = jnp.concatenate([top, (att - top.astype(f32)).astype(bf16)], axis=0)


def first_kernel(width, b_hbm, astro_hbm, star_hbm, att_hbm, starts_hbm, coef_hbm, index_hbm,
                 send_ref, pack_ref, table_ref, att2_ref, ints_ref,
                 b_ref, astro_ref, star_ref, starts_ref, coef_ref, index_ref,
                 spread_ref, sems):
    slots, blocks, _ = index_ref.shape
    comps = astro_ref.shape[0]
    places = pack_places(slots, blocks, width)
    pairs = [(index_hbm, index_ref), (starts_hbm, starts_ref), (att_hbm, pack_ref.at[places[3]]),
             (coef_hbm, coef_ref), (b_hbm, b_ref), (astro_hbm, astro_ref), (star_hbm, star_ref)]
    copies = [
        pltpu.make_async_copy(source, target, sems.at[place])
        for place, (source, target) in enumerate(pairs)
    ]
    for copy in copies:
        copy.start()
    for copy in copies[:2]:
        copy.wait()
    index = jnp.concatenate([index_ref[slot] for slot in range(slots)], axis=0)
    starts_row = jnp.broadcast_to(starts_ref[...].astype(f32), (blocks, blocks))
    diagonal = lax.broadcasted_iota(jnp.int32, (blocks, blocks), 0) == lax.broadcasted_iota(
        jnp.int32, (blocks, blocks), 1
    )
    starts = jnp.sum(jnp.where(diagonal, starts_row, 0.0), axis=1, keepdims=True)
    starts = jnp.broadcast_to(starts, (blocks, LANES))
    pack_ref[places[1]] = index.astype(f32)
    pack_ref[places[2]] = starts
    starts = starts.astype(jnp.int32)
    prepare_index(index, starts, table_ref, ints_ref)
    for copy in copies[2:]:
        copy.wait()
    prepare_att(pack_ref[places[3]], att2_ref)
    rows = b_ref[...]
    coefs = [coef_ref.at[slot] for slot in range(slots)]
    indices = [index_ref.at[slot] for slot in range(slots)]
    for slot in range(slots):
        pack_ref[slot * 8 : slot * 8 + 8] = coef_ref[slot]
    send_ref[0:8] = rows
    send_ref[8:16] = inst_back(rows, coefs, indices, table_ref, spread_ref)
    send_ref[16:19] = att_back(rows, att2_ref[...], starts, width)
    send_ref[19:20] = jnp.sum(rows * rows, axis=0, keepdims=True)
    send_ref[20:24] = jnp.zeros((4, LANES), f32)
    for comp in range(comps):
        send_ref[24 + comp * 8 : 32 + comp * 8] = astro_ref[comp]
    send_ref[24 + comps * 8 : 32 + comps * 8] = star_ref[...].astype(f32)


def prepare_kernel(slots, blocks, width, pack_ref, table_ref, att2_ref, ints_ref):
    places = pack_places(slots, blocks, width)
    index = pack_ref[places[1]].astype(jnp.int32)
    starts = pack_ref[places[2]].astype(jnp.int32)
    prepare_index(index, starts, table_ref, ints_ref)
    prepare_att(pack_ref[places[3]], att2_ref)


def places_of(here, core, count):
    out = [here, here ^ 1]
    for pair in range(2, count, 2):
        out += [here ^ (pair + 1 - core), here ^ (pair + core)]
    return out


def tree_sum(values):
    while len(values) > 1:
        values = [values[i] + values[i + 1] for i in range(0, len(values), 2)]
    return values[0]


def first_chip_kernel(count, *refs):
    ins, out_ref = refs[:count], refs[count]
    chip = lax.axis_index("tm") // 2
    extra = ins[0].shape[0] - 24
    base = 8 * count + 16
    for gap in range(count):
        where = chip ^ gap
        out_ref[pl.ds(pl.multiple_of(where * 8, 8), 8)] = ins[gap][0:8]
        out_ref[pl.ds(pl.multiple_of(base + where * 8, 8), 8)] = ins[gap][16:24]
        at = pl.multiple_of(base + 8 * count + where * extra, 8)
        out_ref[pl.ds(at, extra)] = ins[gap][24:]
    out_ref[8 * count : 8 * count + 8] = tree_sum([ref[8:16] for ref in ins])
    out_ref[8 * count + 8 : base] = tree_sum([ref[16:24] for ref in ins])


def group_rows(chip, count, mine, prev_row, after_row):
    half = lax.broadcasted_iota(jnp.int32, (1, LANES), 1) < 64
    first = mine[0:1] + jnp.where(half & (chip > 0), prev_row, 0.0)
    last = jnp.where(half & (chip < count - 1), mine[4:5] + after_row, 0.0)
    return [first, mine[1:4], last]


def chip_parts(core, own, other):
    low = jnp.where(core == 0, own, other)
    top = jnp.where(core == 0, other, own)
    return jnp.concatenate([low[0:2], low[2:3] + top[0:1], top[1:3]], axis=0)


def first_group_kernel(count, own_ref, other_ref, out_ref):
    me = lax.axis_index("tm")
    chip, core = me // 2, me % 2
    low = 8 * count
    base = low + 16

    def part(ref, where):
        where = jnp.clip(where, 0, count - 1)
        return ref[pl.ds(pl.multiple_of(base + where * 8, 8), 8)]

    def of_core(which, where):
        return jnp.where(core == which, part(own_ref, where), part(other_ref, where))

    mine = chip_parts(core, part(own_ref, chip)[0:3], part(other_ref, chip)[0:3])
    prev, after = of_core(1, chip - 1), of_core(0, chip + 1)
    scalars = own_ref[low + 8 : low + 16] + other_ref[low + 8 : low + 16]
    out_ref[0:8] = own_ref[low : low + 8] + other_ref[low : low + 8]
    att = group_rows(chip, count, mine, prev[2:3], after[0:1])
    out_ref[8:16] = jnp.concatenate(att + [scalars[3:6]], axis=0)


def group_kernel(count, *refs):
    *ins, rows_ref, out_ref = refs
    me = lax.axis_index("tm")
    chip = me // 2
    places = places_of(chip, me % 2, count)
    zero = jnp.zeros((8, LANES), f32)
    mine, prev, after = zero, zero, zero
    for ref, where in zip(ins, places):
        for half in range(2):
            at = pl.multiple_of((half * count + where) * 8, 8)
            rows_ref[pl.ds(at, 8)] = ref[half * 8 : half * 8 + 8]
        low = ref[24:32]
        mine = jnp.where(where == chip, low, mine)
        prev = jnp.where(where == chip - 1, low, prev)
        after = jnp.where(where == chip + 1, low, after)
    scalars = tree_sum([ref[24:32] for ref in ins])
    out_ref[0:8] = tree_sum([ref[16:24] for ref in ins])
    att = group_rows(chip, count, mine, prev[4:5], after[0:1])
    out_ref[8:16] = jnp.concatenate(att + [scalars[5:8]], axis=0)


def astro_kernel(first, count, *refs):
    high = STARS_DEV // LANES
    if first:
        keep, (out_ref, table_ref, spread_ref) = refs[:2], refs[2:]
    else:
        keep, (table_ref, rows_ref, out_ref, spread_ref) = refs[:2], refs[2:]
    base = 16 * count + 16
    extra = (keep[0].shape[0] - base) // count
    comps = extra // 8 - 1
    long = 8 * LANES
    core = lax.axis_index("tm") % 2

    def one(place, totals):
        new = []
        for half in range(2):
            if first:
                rows = keep[half][pl.ds(pl.multiple_of(place * 8, 8), 8)]
            else:
                at = ((half ^ core) * count + place) * 8
                rows = rows_ref[pl.ds(pl.multiple_of(at, 8), 8)]
            packed = keep[half][pl.ds(pl.multiple_of(base + place * extra, 8), extra)]
            index = packed[comps * 8 :].astype(jnp.int32)
            at0 = pl.multiple_of((half * count + place) * long, long)
            split = [halves(packed[comp * 8 : comp * 8 + 8] * rows) for comp in range(comps)]
            for block in range(8):
                here = slice(block, block + 1)
                if first:
                    table_ref[:, pl.ds(at0 + block * LANES, LANES)] = one_hot_low(index[here])
                pieces = []
                for part in range(2):
                    for comp in range(comps):
                        pieces.append(spread_high(index[here], split[comp][part][here], high))
                spread_ref[half, :, block * LANES : (block + 1) * LANES] = jnp.concatenate(
                    pieces, axis=0
                ).astype(bf16)
            new.append(
                totals[half] + dot_lanes(spread_ref[half], table_ref[:, pl.ds(at0, long)])
            )
        return tuple(new)

    zero = jnp.zeros((2 * comps * high, LANES), f32)
    own, other = lax.fori_loop(0, count, one, (zero, zero))
    total = own + other
    out_ref[...] = total[: comps * high] + total[comps * high :]


def sum_kernel(*refs):
    refs[-1][...] = tree_sum([ref[...] for ref in refs[:-1]])


def lane_sum(row):
    return jnp.broadcast_to(jnp.sum(row, axis=1, keepdims=True), row.shape)


def next_bidiagonal(total, state):
    squares, mixed, size = (lane_sum(total[row : row + 1]) for row in (13, 14, 15))
    alpha2 = size + epsilon
    alpha = jnp.sqrt(alpha2)
    rest = jnp.maximum(squares / alpha2 - 2.0 * mixed + alpha2 * state[0:1], 0.0)
    beta2 = rest + epsilon
    return alpha, jnp.sqrt(beta2), rest / beta2


def step_kernel(step, width, slots, chips, star_count, *refs):
    keep, packs, tables, att2s, ints, sum_ref = refs[:2], refs[2:4], refs[4:6], refs[6:8], refs[8:10], refs[10]
    refs = refs[11:]
    if step > 0:
        state_ref, old_z_ref, old_g_ref, old_u_ref, old_s_ref = refs[:5]
        refs = refs[5:]
    gathered, refs = refs[:-7], refs[-7:]
    send_ref, state_out, z_ref, g_ref, u_ref, s_ref, spread_ref = refs
    me = lax.axis_index("tm")
    chip, core = me // 2, me % 2
    high = STARS_DEV // LANES
    comps = sum_ref.shape[0] // high
    blocks = 8
    total = tree_sum([ref[...] for ref in gathered])
    back = jnp.concatenate([sum_ref[...], total], axis=0)
    if step == 0:
        squares = lane_sum(total[13:14])
        beta2 = squares + epsilon
        beta = jnp.sqrt(beta2)
        at = pl.ds(pl.multiple_of(chip * 8, 8), 8)
        u = jnp.concatenate([ref[at] for ref in keep], axis=0) / beta
        g = back / beta
        z = g
        state_out[...] = jnp.concatenate(
            [squares / beta2, beta, jnp.zeros((14, LANES), f32)], axis=0
        )
    else:
        state = state_ref[...]
        alpha, beta, left2 = next_bidiagonal(total, state)
        u = (old_s_ref[...] / alpha - alpha * old_u_ref[...]) / beta
        g = (back / alpha - alpha * old_g_ref[...]) / beta
        z = g - (beta / alpha) * old_z_ref[...]
        pieces = [left2, state[1 : 1 + step], beta, jnp.zeros((7 - step, LANES), f32)]
        pieces += [state[9 : 8 + step]] if step > 1 else []
        pieces += [alpha, jnp.zeros((7 - step, LANES), f32)]
        state_out[...] = jnp.concatenate(pieces, axis=0)
    z_ref[...] = z
    g_ref[...] = g
    u_ref[...] = u
    base = comps * high
    inst_rows = z[base : base + 8]
    att_rows = z[base + 8 : base + 13]
    extra = 8 * comps + 8
    here = 16 * chips + 16 + chip * extra
    pieces = [inst_rows[place : place + 1] for place in range(8)]
    rows, insts, atts = [], [], []
    for half in range(2):
        starts = ints[half][slots * 8 :]
        own = jnp.where(core == half, att_rows[0:3], att_rows[2:5])
        part = att_forward(own, att2s[half][...], starts, width)
        packed = keep[half][pl.ds(pl.multiple_of(here, 8), extra)]
        star = packed[comps * 8 :].astype(jnp.int32)
        star_high, star_low = star >> 7, star & (LANES - 1)
        for comp in range(comps):
            picked = jnp.zeros((blocks, LANES), f32)
            for place in range(high):
                at = comp * high + place
                picked = jnp.where(star_high == place, lane_pick(z[at : at + 1], star_low), picked)
            part = part + packed[comp * 8 : comp * 8 + 8] * picked
        coefs = [packs[half].at[slot * 8 : slot * 8 + 8] for slot in range(slots)]
        indices = [ints[half].at[slot * 8 : slot * 8 + 8] for slot in range(slots)]
        for slot in range(slots):
            part = part + coefs[slot][...] * table_pick(pieces, indices[slot][...])
        rows.append(part)
        if step < ITERS - 1:
            insts.append(inst_back(part, coefs, indices, tables[half], spread_ref.at[half]))
            atts.append(att_back(part, att2s[half][...], starts, width))
    both = jnp.concatenate(rows, axis=0)
    s_ref[...] = both

    def squared(value):
        return jnp.sum(value * value, axis=0, keepdims=True)

    size = squared(z[:base]) * (1.0 / chips) + squared(att_rows[:4]) * (1.0 / star_count)
    size = size + squared(inst_rows) * (1.0 / (star_count * chips))
    mixed = [jnp.sum(rows[half] * u[half * 8 : half * 8 + 8], axis=0, keepdims=True) for half in range(2)]
    scalars = [squared(rows[0]) + squared(rows[1]), mixed[0] + mixed[1], size]
    if step == ITERS - 1:
        send_ref[...] = (jnp.concatenate([jnp.zeros((5, LANES), f32)] + scalars, axis=0))
        return
    send_ref[0:16] = jnp.where(core == 0, both, jnp.concatenate(rows[::-1], axis=0))
    send_ref[16:24] = insts[0] + insts[1]
    send_ref[24:32] = jnp.concatenate([chip_parts(core, *atts)] + scalars, axis=0)


def last_kernel(comps, share, star_count, state_ref, *refs):
    gathered, refs = refs[: -ITERS - 3], refs[-ITERS - 3 :]
    z_refs = refs[:ITERS]
    astro_ref, att_ref, inst_ref = refs[ITERS:]
    high = STARS_DEV // LANES
    me = lax.axis_index("tm")
    total = tree_sum([ref[...] for ref in gathered])
    total = jnp.concatenate([jnp.zeros((8, LANES), f32), total], axis=0)
    state = state_ref[...]
    alpha, beta, _ = next_bidiagonal(total, state)
    betas = [state[1 + k : 2 + k] for k in range(ITERS)] + [beta]
    alphas = [state[9 + k : 10 + k] for k in range(ITERS - 1)] + [alpha]
    rho_bar, phi_bar = alphas[0], betas[0]
    weights = [jnp.zeros((1, LANES), f32)] * ITERS
    search = [jnp.zeros((1, LANES), f32)] * ITERS
    search[0] = 1.0 / alphas[0]
    for k in range(ITERS):
        rho = jnp.sqrt(rho_bar * rho_bar + betas[k + 1] * betas[k + 1])
        cosine, sine = rho_bar / rho, betas[k + 1] / rho
        phi = cosine * phi_bar
        phi_bar = sine * phi_bar
        weights = [x + phi / rho * w for x, w in zip(weights, search)]
        if k + 1 < ITERS:
            theta = sine * alphas[k + 1]
            rho_bar = -cosine * alphas[k + 1]
            search = [-(theta / rho) * w for w in search]
            search[k + 1] = 1.0 / alphas[k + 1]
    base = comps * high
    tiles = share // LANES

    def mix(read):
        total = weights[0] * read(z_refs[0])
        for k in range(1, ITERS):
            total = total + weights[k] * read(z_refs[k])
        return total

    for comp in range(comps):
        for tile in range(tiles):
            at = comp * high + me * tiles + tile
            astro_ref[comp : comp + 1, tile * LANES : (tile + 1) * LANES] = mix(
                lambda ref: ref[pl.ds(at, 1)]
            )
    inst_ref[...] = mix(lambda ref: ref[base : base + 8])
    rows = ATT_DEV // LANES
    att_ref[...] = mix(lambda ref: ref[pl.ds(base + 8 + (me % 2) * rows, rows)])


def call(kernel, name, out, args, scratch=(), space=pltpu.VMEM):
    vmem = pl.BlockSpec(memory_space=pltpu.VMEM)
    return pl.pallas_call(
        kernel,
        name=name,
        out_shape=[jax.ShapeDtypeStruct(shape, dtype) for shape, dtype in out],
        in_specs=[pl.BlockSpec(memory_space=space)] * len(args),
        out_specs=[vmem] * len(out),
        scratch_shapes=list(scratch),
        compiler_params=pltpu.CompilerParams(vmem_limit_bytes=VMEM_LIMIT),
    )(*args)


def direct(value, axis, gaps):
    count = lax.axis_size(axis)
    return [value] + [
        lax.ppermute(value, axis, [(i, i ^ gap) for i in range(count)]) for gap in gaps
    ]


def exchange(value, axis):
    tm_count, star_count = lax.axis_size("tm"), lax.axis_size("star")
    count = star_count if axis == "star" else tm_count // 2
    both = ("star", "tm")
    got = []
    for pair in range(2, count, 2):
        steps = []
        for star in range(star_count):
            for tm in range(tm_count):
                gap = pair + 1 - tm % 2
                far = (star ^ gap, tm) if axis == "star" else (star, tm ^ (2 * gap))
                steps.append((star * tm_count + tm, far[0] * tm_count + far[1]))
        got.append(lax.ppermute(value, both, steps))
    near = direct(value, axis, [1 if axis == "star" else 2])
    for value in got:
        near += direct(value, "tm", [1])
    return near


def rows_type(rows):
    return ((rows, LANES), f32)


def per_device(astro_coef, star_index, att_coef, att_start, inst_coef, inst_index, observed):
    tm_count, star_count = lax.axis_size("tm"), lax.axis_size("star")
    comps = astro_coef.shape[1]
    slots = inst_coef.shape[1]
    blocks, width, height = att_coef.shape[1:]
    share = STARS_DEV // tm_count
    high = STARS_DEV // LANES
    chips = tm_count // 2
    far = [2 * gap for gap in range(1, chips)]
    args = [
        observed.reshape(blocks, height),
        astro_coef.reshape(comps, blocks, height),
        star_index.reshape(blocks, height),
        att_coef.reshape(blocks * width, height),
        att_start,
        inst_coef.reshape(slots, blocks, height),
        inst_index.reshape(slots, blocks, height),
    ]
    long = slots * blocks * height
    extra = 8 * comps + 8
    spread = pltpu.VMEM((16, long), bf16)
    prepared = [((LANES, long), bf16), ((2 * blocks * width, height), bf16),
                ((8 * slots + 8, LANES), jnp.int32)]
    here = [pltpu.with_memory_space_constraint(arg, pltpu.HBM) for arg in args]
    send, pack, *mine = call(
        functools.partial(first_kernel, width),
        "first",
        [((24 + extra, LANES), f32), ((16 * slots + 8 + blocks * width, LANES), f32)] + prepared,
        here,
        [pltpu.VMEM(arg.shape, arg.dtype) for arg in args if arg is not args[3]]
        + [spread, pltpu.SemaphoreType.DMA((len(args),))],
        pl.ANY,
    )
    keep = star_table = state = z = g = u = rows = None
    kept = []
    group_type = rows_type(16)
    for step in range(ITERS):
        wide = [pltpu.VMEM((2, 2 * comps * high, blocks * height), bf16)]
        sums_type = ((comps * high, LANES), f32)
        got = exchange(send, "tm") if step else direct(send, "tm", far)
        if step == 0:
            (gathered,) = call(
                functools.partial(first_chip_kernel, chips),
                "chip",
                [((16 * chips + 16 + chips * extra, LANES), f32)],
                got,
            )
            keep = direct(gathered, "tm", [1])
            (group,) = call(
                functools.partial(first_group_kernel, chips), "group", [group_type], keep
            )
            group, late_pack = lax.optimization_barrier((group, pack))
            _, other_pack = direct(late_pack, "tm", [1])
            theirs = call(
                functools.partial(prepare_kernel, slots, blocks, width),
                "prepare",
                prepared,
                [other_pack],
            )
            basics = [pack, other_pack] + [value for both in zip(mine, theirs) for value in both]
        else:
            all_rows, group = call(
                functools.partial(group_kernel, chips),
                "group",
                [rows_type(16 * chips), group_type],
                got,
            )
        across = exchange(group, "star")
        if step == 0:
            sums, star_table = call(
                functools.partial(astro_kernel, True, chips),
                "astro",
                [sums_type, ((LANES, tm_count * blocks * height), bf16)],
                keep,
                wide,
            )
        else:
            (sums,) = call(
                functools.partial(astro_kernel, False, chips),
                "astro",
                [sums_type],
                keep + [star_table, all_rows],
                wide,
            )
        tall = ((comps * high + 16, LANES), f32)
        pair = ((2 * blocks, height), f32)
        older = [] if step == 0 else [state, z, g, u, rows]
        send, state, z, g, u, rows = call(
            functools.partial(step_kernel, step, width, slots, chips, star_count),
            "step",
            [rows_type(32 if step < ITERS - 1 else 8), group_type, tall, tall, pair, pair],
            keep + basics + [sums] + older + across,
            [pltpu.VMEM((2, 16, long), bf16)],
        )
        kept.append(z)
    (send,) = call(sum_kernel, "sum", [rows_type(8)], exchange(send, "tm"))
    across = exchange(send, "star")
    out_astro, out_att, out_inst = call(
        functools.partial(last_kernel, comps, share, star_count),
        "last",
        [((comps, share), f32), ((ATT_DEV // LANES, LANES), f32), ((NINST // LANES, LANES), f32)],
        [state] + across + kept,
    )
    return out_astro, out_att.reshape(-1), out_inst.reshape(-1)


def solution(mesh):
    return jax.shard_map(
        per_device,
        mesh=mesh,
        in_specs=(
            P("star", None, "tm"),
            P("star", "tm"),
            P("star", "tm", None, None),
            P("star", "tm"),
            P("star", None, "tm"),
            P("star", None, "tm"),
            P("star", "tm"),
        ),
        out_specs=(P(None, ("star", "tm")), P("tm"), P()),
        check_vma=False,
    )
```

```python
import functools

import jax
import jax.numpy as jnp
from jax import lax
from jax.experimental import pallas as pl
from jax.experimental.pallas import tpu as pltpu
from jax.sharding import PartitionSpec as P

STARS_DEV = 2048
NINST = 1024
ITERS = 3
ATT_DEV = 256
LANES = 128

epsilon = 1e-06
f32 = jnp.float32
bf16 = jnp.bfloat16
VMEM_LIMIT = 16 * 1024 * 1024


def halves(value):
    top = value.astype(bf16).astype(f32)
    return top, (value - top).astype(bf16).astype(f32)


def dot_lanes(left, right):
    return lax.dot_general(left, right, (((1,), (1,)), ((), ())), preferred_element_type=f32)


def dot_plain(left, right):
    return lax.dot_general(left, right, (((1,), (0,)), ((), ())), preferred_element_type=f32)


def lane_pick(row, lane_index):
    table = jnp.broadcast_to(row, lane_index.shape)
    return jnp.take_along_axis(table, lane_index, axis=1, mode="promise_in_bounds")


def table_pick(rows, index):
    high, low = index >> 7, index & (LANES - 1)
    total = jnp.zeros(index.shape, f32)
    for place, row in enumerate(rows):
        total = jnp.where(high == place, lane_pick(row, low), total)
    return total


def one_hot_low(index_row):
    shape = (LANES, LANES)
    low = jnp.broadcast_to(index_row & (LANES - 1), shape)
    hit = lax.broadcasted_iota(jnp.int32, shape, 0) == low
    return jnp.where(hit, 1.0, 0.0).astype(bf16)


def spread_high(index_row, value_row, count):
    shape = (count, LANES)
    high = jnp.broadcast_to(index_row >> 7, shape)
    hit = lax.broadcasted_iota(jnp.int32, shape, 0) == high
    return jnp.where(hit, jnp.broadcast_to(value_row, shape), 0.0)


def block_masks(blocks, width):
    shape = (blocks, LANES)
    row = lax.broadcasted_iota(jnp.int32, shape, 0)
    lane = lax.broadcasted_iota(jnp.int32, shape, 1)
    per_tile = LANES // width
    tiles = blocks // per_tile
    return [row == tile * per_tile + lane // width for tile in range(tiles)], row, lane


def inst_back(rows, coef_ref, index_ref, table_ref, spread_ref):
    slots, blocks = len(coef_ref), rows.shape[0]
    count = NINST // LANES
    for slot in range(slots):
        top, rest = halves(coef_ref[slot][...] * rows)
        index = index_ref[slot][...]
        for block in range(blocks):
            here = slice(block, block + 1)
            pieces = [spread_high(index[here], part[here], count) for part in (top, rest)]
            at = (slot * blocks + block) * LANES
            spread_ref[:, at : at + LANES] = jnp.concatenate(pieces, axis=0).astype(bf16)
    both = dot_lanes(spread_ref[...], table_ref[...])
    return both[:count] + both[count:]


def att_back(rows, att2, starts, width):
    blocks = rows.shape[0]
    size = att2.shape[0] // 2
    top, rest = halves(rows)
    both = dot_lanes(jnp.concatenate([top, rest], axis=0).astype(bf16), att2)
    both = both[:blocks] + both[blocks:]
    both = both[:, :size] + both[:, size:]
    masks, row, lane = block_masks(blocks, width)
    own = jnp.zeros((blocks, LANES), f32)
    for tile, mask in enumerate(masks):
        own = own + jnp.where(mask, both[:, tile * LANES : (tile + 1) * LANES], 0.0)
    shift = (row % (LANES // width)) * width
    out = []
    for tile in range((ATT_DEV + width + LANES - 1) // LANES):
        offset = lane + tile * LANES - starts
        inside = (offset >= 0) & (offset < width)
        picked = jnp.take_along_axis(
            own, jnp.where(inside, offset + shift, 0), axis=1, mode="promise_in_bounds"
        )
        out.append(jnp.sum(jnp.where(inside, picked, 0.0), axis=0, keepdims=True))
    return jnp.concatenate(out, axis=0)


def att_forward(att_rows, att2, starts, width):
    blocks = starts.shape[0]
    masks, row, lane = block_masks(blocks, width)
    tiles = [att_rows[tile : tile + 1] for tile in range(att_rows.shape[0])]
    window = table_pick(tiles, starts + lane % width)
    wide = jnp.concatenate([jnp.where(mask, window, 0.0) for mask in masks], axis=1)
    top, rest = halves(wide)
    left = jnp.concatenate([top, rest], axis=0).astype(bf16)
    both = dot_plain(jnp.concatenate([left, left], axis=1), att2)
    return both[:blocks] + both[blocks:]


def pack_places(slots, blocks, width):
    at = slots * 8
    return slice(0, at), slice(at, 2 * at), slice(2 * at, 2 * at + 8), slice(
        2 * at + 8, 2 * at + 8 + blocks * width
    )


def prepare_index(index_rows, starts, table_ref, ints_ref):
    count = index_rows.shape[0] // 8
    ints_ref[0 : count * 8] = index_rows
    ints_ref[count * 8 :] = starts
    for place in range(count * 8):
        table_ref[:, place * LANES : (place + 1) * LANES] = one_hot_low(
            index_rows[place : place + 1]
        )


def prepare_att(att, att2_ref):
    top = att.astype(bf16)
    att2_ref[...] = jnp.concatenate([top, (att - top.astype(f32)).astype(bf16)], axis=0)


def first_kernel(width, b_hbm, astro_hbm, star_hbm, att_hbm, starts_hbm, coef_hbm, index_hbm,
                 send_ref, pack_ref, table_ref, att2_ref, ints_ref,
                 b_ref, astro_ref, star_ref, starts_ref, coef_ref, index_ref,
                 spread_ref, sems):
    slots, blocks, _ = index_ref.shape
    comps = astro_ref.shape[0]
    places = pack_places(slots, blocks, width)
    pairs = [(index_hbm, index_ref), (starts_hbm, starts_ref), (att_hbm, pack_ref.at[places[3]]),
             (coef_hbm, coef_ref), (b_hbm, b_ref), (astro_hbm, astro_ref), (star_hbm, star_ref)]
    copies = [
        pltpu.make_async_copy(source, target, sems.at[place])
        for place, (source, target) in enumerate(pairs)
    ]
    for copy in copies:
        copy.start()
    for copy in copies[:2]:
        copy.wait()
    index = jnp.concatenate([index_ref[slot] for slot in range(slots)], axis=0)
    starts_row = jnp.broadcast_to(starts_ref[...].astype(f32), (blocks, blocks))
    diagonal = lax.broadcasted_iota(jnp.int32, (blocks, blocks), 0) == lax.broadcasted_iota(
        jnp.int32, (blocks, blocks), 1
    )
    starts = jnp.sum(jnp.where(diagonal, starts_row, 0.0), axis=1, keepdims=True)
    starts = jnp.broadcast_to(starts, (blocks, LANES))
    pack_ref[places[1]] = index.astype(f32)
    pack_ref[places[2]] = starts
    starts = starts.astype(jnp.int32)
    prepare_index(index, starts, table_ref, ints_ref)
    for copy in copies[2:]:
        copy.wait()
    prepare_att(pack_ref[places[3]], att2_ref)
    rows = b_ref[...]
    coefs = [coef_ref.at[slot] for slot in range(slots)]
    indices = [index_ref.at[slot] for slot in range(slots)]
    for slot in range(slots):
        pack_ref[slot * 8 : slot * 8 + 8] = coef_ref[slot]
    send_ref[0:8] = rows
    send_ref[8:16] = inst_back(rows, coefs, indices, table_ref, spread_ref)
    send_ref[16:19] = att_back(rows, att2_ref[...], starts, width)
    send_ref[19:20] = jnp.sum(rows * rows, axis=0, keepdims=True)
    send_ref[20:24] = jnp.zeros((4, LANES), f32)
    for comp in range(comps):
        send_ref[24 + comp * 8 : 32 + comp * 8] = astro_ref[comp]
    send_ref[24 + comps * 8 : 32 + comps * 8] = star_ref[...].astype(f32)


def prepare_kernel(slots, blocks, width, pack_ref, table_ref, att2_ref, ints_ref):
    places = pack_places(slots, blocks, width)
    index = pack_ref[places[1]].astype(jnp.int32)
    starts = pack_ref[places[2]].astype(jnp.int32)
    prepare_index(index, starts, table_ref, ints_ref)
    prepare_att(pack_ref[places[3]], att2_ref)


def tree_sum(values):
    while len(values) > 1:
        values = [values[i] + values[i + 1] for i in range(0, len(values), 2)]
    return values[0]


def merge_kernel(own_ref, other_ref, out_ref):
    core = lax.axis_index("tm") % 2
    extra = own_ref.shape[0] - 24
    low, top = own_ref[...], other_ref[...]
    low, top = jnp.where(core == 0, low, top), jnp.where(core == 0, top, low)
    out_ref[0:8] = low[0:8]
    out_ref[8:16] = top[0:8]
    out_ref[16:24] = low[8:16] + top[8:16]
    att = chip_parts(low[16:19], top[16:19])
    out_ref[24:32] = jnp.concatenate([att, low[19:22] + top[19:22]], axis=0)
    out_ref[32 : 32 + extra] = low[24:]
    out_ref[32 + extra :] = top[24:]


def group_rows(chip, count, mine, prev_row, after_row):
    half = lax.broadcasted_iota(jnp.int32, (1, LANES), 1) < 64
    first = mine[0:1] + jnp.where(half & (chip > 0), prev_row, 0.0)
    last = jnp.where(half & (chip < count - 1), mine[4:5] + after_row, 0.0)
    return [first, mine[1:4], last]


def chip_parts(low, top):
    return jnp.concatenate([low[0:2], low[2:3] + top[0:1], top[1:3]], axis=0)


def group_kernel(count, *refs):
    ins, (rows_ref, out_ref, *keep) = refs[:count], refs[count:]
    chip = lax.axis_index("tm") // 2
    extra = (ins[0].shape[0] - 32) // 2
    zero = jnp.zeros((8, LANES), f32)
    prev, after = zero, zero
    for gap, ref in enumerate(ins):
        where = chip ^ gap
        for half in range(2):
            at = pl.multiple_of((half * count + where) * 8, 8)
            rows_ref[pl.ds(at, 8)] = ref[half * 8 : half * 8 + 8]
            if keep:
                at = pl.multiple_of((half * count + where) * extra, 8)
                keep[0][pl.ds(at, extra)] = ref[32 + half * extra : 32 + (half + 1) * extra]
        low = ref[24:32]
        prev = jnp.where(where == chip - 1, low, prev)
        after = jnp.where(where == chip + 1, low, after)
    mine = ins[0][24:32]
    scalars = tree_sum([ref[24:32] for ref in ins])
    out_ref[0:8] = tree_sum([ref[16:24] for ref in ins])
    att = group_rows(chip, count, mine, prev[4:5], after[0:1])
    out_ref[8:16] = jnp.concatenate(att + [scalars[5:8]], axis=0)


def astro_kernel(first, count, keep_ref, rows_ref, *refs):
    high = STARS_DEV // LANES
    if first:
        out_ref, table_ref, spread_ref = refs
    else:
        table_ref, out_ref, spread_ref = refs
    extra = keep_ref.shape[0] // (2 * count)
    comps = extra // 8 - 1
    long = 8 * LANES

    def one(place, totals):
        new = []
        for half in range(2):
            slot = half * count + place
            rows = rows_ref[pl.ds(pl.multiple_of(slot * 8, 8), 8)]
            packed = keep_ref[pl.ds(pl.multiple_of(slot * extra, 8), extra)]
            index = packed[comps * 8 :].astype(jnp.int32)
            at0 = pl.multiple_of((half * count + place) * long, long)
            split = [halves(packed[comp * 8 : comp * 8 + 8] * rows) for comp in range(comps)]
            for block in range(8):
                here = slice(block, block + 1)
                if first:
                    table_ref[:, pl.ds(at0 + block * LANES, LANES)] = one_hot_low(index[here])
                pieces = []
                for part in range(2):
                    for comp in range(comps):
                        pieces.append(spread_high(index[here], split[comp][part][here], high))
                spread_ref[half, :, block * LANES : (block + 1) * LANES] = jnp.concatenate(
                    pieces, axis=0
                ).astype(bf16)
            new.append(
                totals[half] + dot_lanes(spread_ref[half], table_ref[:, pl.ds(at0, long)])
            )
        return tuple(new)

    zero = jnp.zeros((2 * comps * high, LANES), f32)
    low, top = lax.fori_loop(0, count, one, (zero, zero))
    total = low + top
    out_ref[...] = total[: comps * high] + total[comps * high :]


def sum_kernel(*refs):
    refs[-1][...] = tree_sum([ref[...] for ref in refs[:-1]])


def lane_sum(row):
    return jnp.broadcast_to(jnp.sum(row, axis=1, keepdims=True), row.shape)


def next_bidiagonal(total, state):
    squares, mixed, size = (lane_sum(total[row : row + 1]) for row in (13, 14, 15))
    alpha2 = size + epsilon
    alpha = jnp.sqrt(alpha2)
    rest = jnp.maximum(squares / alpha2 - 2.0 * mixed + alpha2 * state[0:1], 0.0)
    beta2 = rest + epsilon
    return alpha, jnp.sqrt(beta2), rest / beta2


def step_kernel(step, width, slots, chips, star_count, *refs):
    keep_ref, packs, tables, att2s, ints = refs[0], refs[1:3], refs[3:5], refs[5:7], refs[7:9]
    sum_ref, refs = refs[9], refs[10:]
    if step > 0:
        state_ref, old_z_ref, old_g_ref, old_u_ref, old_s_ref = refs[:5]
        refs = refs[5:]
    else:
        first_rows_ref, refs = refs[0], refs[1:]
    gathered, refs = refs[:-7], refs[-7:]
    send_ref, state_out, z_ref, g_ref, u_ref, s_ref, spread_ref = refs
    me = lax.axis_index("tm")
    chip, core = me // 2, me % 2
    high = STARS_DEV // LANES
    comps = sum_ref.shape[0] // high
    blocks = 8
    total = tree_sum([ref[...] for ref in gathered])
    back = jnp.concatenate([sum_ref[...], total], axis=0)
    if step == 0:
        squares = lane_sum(total[13:14])
        beta2 = squares + epsilon
        beta = jnp.sqrt(beta2)
        places = [pl.multiple_of(((half ^ core) * chips + chip) * 8, 8) for half in range(2)]
        u = jnp.concatenate([first_rows_ref[pl.ds(at, 8)] for at in places], axis=0) / beta
        g = back / beta
        z = g
        state_out[...] = jnp.concatenate(
            [squares / beta2, beta, jnp.zeros((14, LANES), f32)], axis=0
        )
    else:
        state = state_ref[...]
        alpha, beta, left2 = next_bidiagonal(total, state)
        u = (old_s_ref[...] / alpha - alpha * old_u_ref[...]) / beta
        g = (back / alpha - alpha * old_g_ref[...]) / beta
        z = g - (beta / alpha) * old_z_ref[...]
        pieces = [left2, state[1 : 1 + step], beta, jnp.zeros((7 - step, LANES), f32)]
        pieces += [state[9 : 8 + step]] if step > 1 else []
        pieces += [alpha, jnp.zeros((7 - step, LANES), f32)]
        state_out[...] = jnp.concatenate(pieces, axis=0)
    z_ref[...] = z
    g_ref[...] = g
    u_ref[...] = u
    base = comps * high
    inst_rows = z[base : base + 8]
    att_rows = z[base + 8 : base + 13]
    extra = 8 * comps + 8
    pieces = [inst_rows[place : place + 1] for place in range(8)]
    rows, insts, atts = [], [], []
    for half in range(2):
        starts = ints[half][slots * 8 :]
        own = jnp.where(core == half, att_rows[0:3], att_rows[2:5])
        part = att_forward(own, att2s[half][...], starts, width)
        at = pl.multiple_of(((half ^ core) * chips + chip) * extra, 8)
        packed = keep_ref[pl.ds(at, extra)]
        star = packed[comps * 8 :].astype(jnp.int32)
        star_high, star_low = star >> 7, star & (LANES - 1)
        for comp in range(comps):
            picked = jnp.zeros((blocks, LANES), f32)
            for place in range(high):
                at = comp * high + place
                picked = jnp.where(star_high == place, lane_pick(z[at : at + 1], star_low), picked)
            part = part + packed[comp * 8 : comp * 8 + 8] * picked
        coefs = [packs[half].at[slot * 8 : slot * 8 + 8] for slot in range(slots)]
        indices = [ints[half].at[slot * 8 : slot * 8 + 8] for slot in range(slots)]
        for slot in range(slots):
            part = part + coefs[slot][...] * table_pick(pieces, indices[slot][...])
        rows.append(part)
        if step < ITERS - 1:
            insts.append(inst_back(part, coefs, indices, tables[half], spread_ref.at[half]))
            atts.append(att_back(part, att2s[half][...], starts, width))
    both = jnp.concatenate(rows, axis=0)
    s_ref[...] = both

    def squared(value):
        return jnp.sum(value * value, axis=0, keepdims=True)

    size = squared(z[:base]) * (1.0 / chips) + squared(att_rows[:4]) * (1.0 / star_count)
    size = size + squared(inst_rows) * (1.0 / (star_count * chips))
    mixed = [jnp.sum(rows[half] * u[half * 8 : half * 8 + 8], axis=0, keepdims=True) for half in range(2)]
    scalars = [squared(rows[0]) + squared(rows[1]), mixed[0] + mixed[1], size]
    if step == ITERS - 1:
        send_ref[...] = (jnp.concatenate([jnp.zeros((5, LANES), f32)] + scalars, axis=0))
        return
    send_ref[0:16] = jnp.where(core == 0, both, jnp.concatenate(rows[::-1], axis=0))
    send_ref[16:24] = insts[0] + insts[1]
    low, top = (jnp.where(core == half, atts[0], atts[1]) for half in range(2))
    send_ref[24:32] = jnp.concatenate([chip_parts(low, top)] + scalars, axis=0)


def last_kernel(comps, share, state_ref, *refs):
    gathered, z_refs, out_ref = refs[: -ITERS - 1], refs[-ITERS - 1 : -1], refs[-1]
    high = STARS_DEV // LANES
    me = lax.axis_index("tm")
    total = tree_sum([ref[...] for ref in gathered])
    total = jnp.concatenate([jnp.zeros((8, LANES), f32), total], axis=0)
    state = state_ref[...]
    alpha, beta, _ = next_bidiagonal(total, state)
    betas = [state[1 + k : 2 + k] for k in range(ITERS)] + [beta]
    alphas = [state[9 + k : 10 + k] for k in range(ITERS - 1)] + [alpha]
    rho_bar, phi_bar = alphas[0], betas[0]
    weights = [jnp.zeros((1, LANES), f32)] * ITERS
    search = [jnp.zeros((1, LANES), f32)] * ITERS
    search[0] = 1.0 / alphas[0]
    for k in range(ITERS):
        rho = jnp.sqrt(rho_bar * rho_bar + betas[k + 1] * betas[k + 1])
        cosine, sine = rho_bar / rho, betas[k + 1] / rho
        phi = cosine * phi_bar
        phi_bar = sine * phi_bar
        weights = [x + phi / rho * w for x, w in zip(weights, search)]
        if k + 1 < ITERS:
            theta = sine * alphas[k + 1]
            rho_bar = -cosine * alphas[k + 1]
            search = [-(theta / rho) * w for w in search]
            search[k + 1] = 1.0 / alphas[k + 1]
    base = comps * high
    tiles = share // LANES

    def mix(read):
        total = weights[0] * read(z_refs[0])
        for k in range(1, ITERS):
            total = total + weights[k] * read(z_refs[k])
        return total

    rows = ATT_DEV // LANES
    pieces = [mix(lambda ref: ref[base : base + 8])]
    for core in range(2):
        at = base + 8 + core * rows
        pieces.append(mix(lambda ref: ref[at : at + rows]))
        for comp in range(comps):
            place = comp * high + (me // 2 * 2 + core) * tiles
            pieces.append(mix(lambda ref: ref[pl.ds(place, tiles)]))
    unused = out_ref.shape[0] - sum(piece.shape[0] for piece in pieces)
    if unused:
        pieces.append(jnp.zeros((unused, LANES), f32))
    out_ref[...] = jnp.concatenate(pieces, axis=0)


def place_kernel(comps, share, own_ref, other_ref, astro_ref, att_ref, inst_ref):
    core = lax.axis_index("tm") % 2
    tiles, rows = share // LANES, ATT_DEV // LANES
    value = jnp.where(core == 1, own_ref[...], other_ref[...])
    at = 8 + rows + comps * tiles
    mine = jnp.where(core == 0, value[8:at], value[at : 2 * at - 8])
    inst_ref[...] = value[0:8]
    att_ref[...] = mine[:rows]
    for comp in range(comps):
        for tile in range(tiles):
            row = rows + comp * tiles + tile
            astro_ref[comp : comp + 1, tile * LANES : (tile + 1) * LANES] = mine[row : row + 1]


def call(kernel, name, out, args, scratch=(), space=pltpu.VMEM):
    vmem = pl.BlockSpec(memory_space=pltpu.VMEM)
    return pl.pallas_call(
        kernel,
        name=name,
        out_shape=[jax.ShapeDtypeStruct(shape, dtype) for shape, dtype in out],
        in_specs=[pl.BlockSpec(memory_space=space)] * len(args),
        out_specs=[vmem] * len(out),
        scratch_shapes=list(scratch),
        compiler_params=pltpu.CompilerParams(vmem_limit_bytes=VMEM_LIMIT),
    )(*args)


def direct(value, axis, gaps):
    count = lax.axis_size(axis)
    return [value] + [
        lax.ppermute(value, axis, [(i, i ^ gap) for i in range(count)]) for gap in gaps
    ]


def exchange(value, axis):
    tm_count, star_count = lax.axis_size("tm"), lax.axis_size("star")
    got = [value]
    for gap in range(1, star_count if axis == "star" else tm_count // 2):
        steps = []
        for star in range(star_count):
            for tm in range(1, tm_count, 2):
                far = (star ^ gap, tm) if axis == "star" else (star, tm ^ (2 * gap))
                steps.append((star * tm_count + tm, far[0] * tm_count + far[1]))
        got.append(lax.ppermute(value, ("star", "tm"), steps))
    return got


def rows_type(rows):
    return ((rows, LANES), f32)


def per_device(astro_coef, star_index, att_coef, att_start, inst_coef, inst_index, observed):
    tm_count, star_count = lax.axis_size("tm"), lax.axis_size("star")
    comps = astro_coef.shape[1]
    slots = inst_coef.shape[1]
    blocks, width, height = att_coef.shape[1:]
    share = STARS_DEV // tm_count
    high = STARS_DEV // LANES
    chips = tm_count // 2
    args = [
        observed.reshape(blocks, height),
        astro_coef.reshape(comps, blocks, height),
        star_index.reshape(blocks, height),
        att_coef.reshape(blocks * width, height),
        att_start,
        inst_coef.reshape(slots, blocks, height),
        inst_index.reshape(slots, blocks, height),
    ]
    long = slots * blocks * height
    extra = 8 * comps + 8
    spread = pltpu.VMEM((16, long), bf16)
    prepared = [((LANES, long), bf16), ((2 * blocks * width, height), bf16),
                ((8 * slots + 8, LANES), jnp.int32)]
    here = [pltpu.with_memory_space_constraint(arg, pltpu.HBM) for arg in args]
    send, pack, *mine = call(
        functools.partial(first_kernel, width),
        "first",
        [((24 + extra, LANES), f32), ((16 * slots + 8 + blocks * width, LANES), f32)] + prepared,
        here,
        [pltpu.VMEM(arg.shape, arg.dtype) for arg in args if arg is not args[3]]
        + [spread, pltpu.SemaphoreType.DMA((len(args),))],
        pl.ANY,
    )
    (send,) = call(
        merge_kernel, "merge", [rows_type(32 + 2 * extra)], direct(send, "tm", [1])
    )
    send, late_pack = lax.optimization_barrier((send, pack))
    _, other_pack = direct(late_pack, "tm", [1])
    theirs = call(
        functools.partial(prepare_kernel, slots, blocks, width), "prepare", prepared, [other_pack]
    )
    got = exchange(send, "tm")
    theirs, got = lax.optimization_barrier((theirs, got))
    basics = [pack, other_pack] + [value for both in zip(mine, theirs) for value in both]
    keep = star_table = state = z = g = u = rows = None
    kept = []
    group_type = rows_type(16)
    for step in range(ITERS):
        wide = [pltpu.VMEM((2, 2 * comps * high, blocks * height), bf16)]
        sums_type = rows_type(comps * high)
        all_rows, group, *new = call(
            functools.partial(group_kernel, chips),
            "group",
            [rows_type(16 * chips), group_type]
            + ([rows_type(2 * chips * extra)] if step == 0 else []),
            exchange(send, "tm") if step else got,
        )
        across = exchange(group, "star")
        if step == 0:
            (keep,) = new
            sums, star_table = call(
                functools.partial(astro_kernel, True, chips),
                "astro",
                [sums_type, ((LANES, tm_count * blocks * height), bf16)],
                [keep, all_rows],
                wide,
            )
        else:
            (sums,) = call(
                functools.partial(astro_kernel, False, chips),
                "astro",
                [sums_type],
                [keep, all_rows, star_table],
                wide,
            )
        tall = ((comps * high + 16, LANES), f32)
        pair = ((2 * blocks, height), f32)
        older = [all_rows] if step == 0 else [state, z, g, u, rows]
        send, state, z, g, u, rows = call(
            functools.partial(step_kernel, step, width, slots, chips, star_count),
            "step",
            [rows_type(32 if step < ITERS - 1 else 8), group_type, tall, tall, pair, pair],
            [keep] + basics + [sums] + older + across,
            [pltpu.VMEM((2, 16, long), bf16)],
        )
        kept.append(z)
    (send,) = call(sum_kernel, "sum", [rows_type(8)], exchange(send, "tm"))
    across = exchange(send, "star")
    both_parts = 2 * (ATT_DEV // LANES + comps * share // LANES)
    (parts,) = call(
        functools.partial(last_kernel, comps, share),
        "last",
        [rows_type(8 + (both_parts + 7) // 8 * 8)],
        [state] + across + kept,
    )
    received = lax.ppermute(parts, "tm", [(i, i - 1) for i in range(1, tm_count, 2)])
    out_astro, out_att, out_inst = call(
        functools.partial(place_kernel, comps, share),
        "place",
        [((comps, share), f32), ((ATT_DEV // LANES, LANES), f32), ((NINST // LANES, LANES), f32)],
        [parts, received],
    )
    return out_astro, out_att.reshape(-1), out_inst.reshape(-1)


def solution(mesh):
    return jax.shard_map(
        per_device,
        mesh=mesh,
        in_specs=(
            P("star", None, "tm"),
            P("star", "tm"),
            P("star", "tm", None, None),
            P("star", "tm"),
            P("star", None, "tm"),
            P("star", None, "tm"),
            P("star", "tm"),
        ),
        out_specs=(P(None, ("star", "tm")), P("tm"), P()),
        check_vma=False,
    )
```

```python
import functools

import jax
import jax.numpy as jnp
from jax import lax
from jax.experimental import pallas as pl
from jax.experimental.pallas import tpu as pltpu
from jax.sharding import PartitionSpec as P

STARS_DEV = 2048
NINST = 1024
ITERS = 3
ATT_DEV = 256
LANES = 128

epsilon = 1e-06
f32 = jnp.float32
bf16 = jnp.bfloat16
VMEM_LIMIT = 16 * 1024 * 1024


def halves(value):
    top = value.astype(bf16).astype(f32)
    return top, (value - top).astype(bf16).astype(f32)


def dot_lanes(left, right):
    return lax.dot_general(left, right, (((1,), (1,)), ((), ())), preferred_element_type=f32)


def dot_plain(left, right):
    return lax.dot_general(left, right, (((1,), (0,)), ((), ())), preferred_element_type=f32)


def lane_pick(row, lane_index):
    table = jnp.broadcast_to(row, lane_index.shape)
    return jnp.take_along_axis(table, lane_index, axis=1, mode="promise_in_bounds")


def table_pick(rows, index):
    high, low = index >> 7, index & (LANES - 1)
    total = jnp.zeros(index.shape, f32)
    for place, row in enumerate(rows):
        total = jnp.where(high == place, lane_pick(row, low), total)
    return total


def one_hot_low(index_row):
    shape = (LANES, LANES)
    low = jnp.broadcast_to(index_row & (LANES - 1), shape)
    hit = lax.broadcasted_iota(jnp.int32, shape, 0) == low
    return jnp.where(hit, 1.0, 0.0).astype(bf16)


def spread_high(index_row, value_row, count):
    shape = (count, LANES)
    high = jnp.broadcast_to(index_row >> 7, shape)
    hit = lax.broadcasted_iota(jnp.int32, shape, 0) == high
    return jnp.where(hit, jnp.broadcast_to(value_row, shape), 0.0)


def block_masks(blocks, width):
    shape = (blocks, LANES)
    row = lax.broadcasted_iota(jnp.int32, shape, 0)
    lane = lax.broadcasted_iota(jnp.int32, shape, 1)
    per_tile = LANES // width
    tiles = blocks // per_tile
    return [row == tile * per_tile + lane // width for tile in range(tiles)], row, lane


def inst_back(rows, coef_ref, index_ref, table_ref, spread_ref):
    slots, blocks = len(coef_ref), rows.shape[0]
    count = NINST // LANES
    for slot in range(slots):
        top, rest = halves(coef_ref[slot][...] * rows)
        index = index_ref[slot][...]
        for block in range(blocks):
            here = slice(block, block + 1)
            pieces = [spread_high(index[here], part[here], count) for part in (top, rest)]
            at = (slot * blocks + block) * LANES
            spread_ref[:, at : at + LANES] = jnp.concatenate(pieces, axis=0).astype(bf16)
    both = dot_lanes(spread_ref[...], table_ref[...])
    return both[:count] + both[count:]


def att_back(rows, att2, starts, width):
    blocks = rows.shape[0]
    size = att2.shape[0] // 2
    top, rest = halves(rows)
    both = dot_lanes(jnp.concatenate([top, rest], axis=0).astype(bf16), att2)
    both = both[:blocks] + both[blocks:]
    both = both[:, :size] + both[:, size:]
    masks, row, lane = block_masks(blocks, width)
    own = jnp.zeros((blocks, LANES), f32)
    for tile, mask in enumerate(masks):
        own = own + jnp.where(mask, both[:, tile * LANES : (tile + 1) * LANES], 0.0)
    shift = (row % (LANES // width)) * width
    out = []
    for tile in range((ATT_DEV + width + LANES - 1) // LANES):
        offset = lane + tile * LANES - starts
        inside = (offset >= 0) & (offset < width)
        picked = jnp.take_along_axis(
            own, jnp.where(inside, offset + shift, 0), axis=1, mode="promise_in_bounds"
        )
        out.append(jnp.sum(jnp.where(inside, picked, 0.0), axis=0, keepdims=True))
    return jnp.concatenate(out, axis=0)


def att_forward(att_rows, att2, starts, width):
    blocks = starts.shape[0]
    masks, row, lane = block_masks(blocks, width)
    tiles = [att_rows[tile : tile + 1] for tile in range(att_rows.shape[0])]
    window = table_pick(tiles, starts + lane % width)
    wide = jnp.concatenate([jnp.where(mask, window, 0.0) for mask in masks], axis=1)
    top, rest = halves(wide)
    left = jnp.concatenate([top, rest], axis=0).astype(bf16)
    both = dot_plain(jnp.concatenate([left, left], axis=1), att2)
    return both[:blocks] + both[blocks:]


def pack_places(slots, blocks, width):
    at = slots * 8
    return slice(0, at), slice(at, 2 * at), slice(2 * at, 2 * at + 8), slice(
        2 * at + 8, 2 * at + 8 + blocks * width
    )


def prepare_index(index_rows, starts, table_ref, ints_ref):
    count = index_rows.shape[0] // 8
    ints_ref[0 : count * 8] = index_rows
    ints_ref[count * 8 :] = starts
    for place in range(count * 8):
        table_ref[:, place * LANES : (place + 1) * LANES] = one_hot_low(
            index_rows[place : place + 1]
        )


def prepare_att(att, att2_ref):
    top = att.astype(bf16)
    att2_ref[...] = jnp.concatenate([top, (att - top.astype(f32)).astype(bf16)], axis=0)


def first_kernel(width, b_hbm, astro_hbm, star_hbm, att_hbm, starts_hbm, coef_hbm, index_hbm,
                 send_ref, pack_ref, table_ref, att2_ref, ints_ref,
                 b_ref, astro_ref, star_ref, starts_ref, coef_ref, index_ref,
                 spread_ref, sems):
    slots, blocks, _ = index_ref.shape
    comps = astro_ref.shape[0]
    places = pack_places(slots, blocks, width)
    pairs = [(index_hbm, index_ref), (starts_hbm, starts_ref), (att_hbm, pack_ref.at[places[3]]),
             (coef_hbm, coef_ref), (b_hbm, b_ref), (astro_hbm, astro_ref), (star_hbm, star_ref)]
    copies = [
        pltpu.make_async_copy(source, target, sems.at[place])
        for place, (source, target) in enumerate(pairs)
    ]
    for copy in copies:
        copy.start()
    for copy in copies[:2]:
        copy.wait()
    index = jnp.concatenate([index_ref[slot] for slot in range(slots)], axis=0)
    starts_row = jnp.broadcast_to(starts_ref[...].astype(f32), (blocks, blocks))
    diagonal = lax.broadcasted_iota(jnp.int32, (blocks, blocks), 0) == lax.broadcasted_iota(
        jnp.int32, (blocks, blocks), 1
    )
    starts = jnp.sum(jnp.where(diagonal, starts_row, 0.0), axis=1, keepdims=True)
    starts = jnp.broadcast_to(starts, (blocks, LANES))
    pack_ref[places[1]] = index.astype(f32)
    pack_ref[places[2]] = starts
    starts = starts.astype(jnp.int32)
    prepare_index(index, starts, table_ref, ints_ref)
    for copy in copies[2:]:
        copy.wait()
    prepare_att(pack_ref[places[3]], att2_ref)
    rows = b_ref[...]
    coefs = [coef_ref.at[slot] for slot in range(slots)]
    indices = [index_ref.at[slot] for slot in range(slots)]
    for slot in range(slots):
        pack_ref[slot * 8 : slot * 8 + 8] = coef_ref[slot]
    send_ref[0:8] = rows
    send_ref[8:16] = inst_back(rows, coefs, indices, table_ref, spread_ref)
    send_ref[16:19] = att_back(rows, att2_ref[...], starts, width)
    send_ref[19:20] = jnp.sum(rows * rows, axis=0, keepdims=True)
    send_ref[20:24] = jnp.zeros((4, LANES), f32)
    for comp in range(comps):
        send_ref[24 + comp * 8 : 32 + comp * 8] = astro_ref[comp]
    send_ref[24 + comps * 8 : 32 + comps * 8] = star_ref[...].astype(f32)


def prepare_kernel(slots, blocks, width, pack_ref, table_ref, att2_ref, ints_ref):
    places = pack_places(slots, blocks, width)
    index = pack_ref[places[1]].astype(jnp.int32)
    starts = pack_ref[places[2]].astype(jnp.int32)
    prepare_index(index, starts, table_ref, ints_ref)
    prepare_att(pack_ref[places[3]], att2_ref)


def tree_sum(values):
    while len(values) > 1:
        values = [values[i] + values[i + 1] for i in range(0, len(values), 2)]
    return values[0]


def merge_kernel(own_ref, other_ref, out_ref):
    core = lax.axis_index("tm") % 2
    extra = own_ref.shape[0] - 24
    low, top = own_ref[...], other_ref[...]
    low, top = jnp.where(core == 0, low, top), jnp.where(core == 0, top, low)
    out_ref[0:8] = low[0:8]
    out_ref[8:16] = top[0:8]
    out_ref[16:24] = low[8:16] + top[8:16]
    att = chip_parts(low[16:19], top[16:19])
    out_ref[24:32] = jnp.concatenate([att, low[19:22] + top[19:22]], axis=0)
    out_ref[32 : 32 + extra] = low[24:]
    out_ref[32 + extra :] = top[24:]


def group_rows(chip, count, mine, prev_row, after_row):
    half = lax.broadcasted_iota(jnp.int32, (1, LANES), 1) < 64
    first = mine[0:1] + jnp.where(half & (chip > 0), prev_row, 0.0)
    last = jnp.where(half & (chip < count - 1), mine[4:5] + after_row, 0.0)
    return [first, mine[1:4], last]


def chip_parts(low, top):
    return jnp.concatenate([low[0:2], low[2:3] + top[0:1], top[1:3]], axis=0)


def group_kernel(count, *refs):
    ins, (rows_ref, out_ref, *keep) = refs[:count], refs[count:]
    chip = lax.axis_index("tm") // 2
    extra = (ins[0].shape[0] - 32) // 2
    zero = jnp.zeros((8, LANES), f32)
    prev, after = zero, zero
    for gap, ref in enumerate(ins):
        where = chip ^ gap
        for half in range(2):
            at = pl.multiple_of((half * count + where) * 8, 8)
            rows_ref[pl.ds(at, 8)] = ref[half * 8 : half * 8 + 8]
            if keep:
                at = pl.multiple_of((half * count + where) * extra, 8)
                keep[0][pl.ds(at, extra)] = ref[32 + half * extra : 32 + (half + 1) * extra]
        low = ref[24:32]
        prev = jnp.where(where == chip - 1, low, prev)
        after = jnp.where(where == chip + 1, low, after)
    mine = ins[0][24:32]
    scalars = tree_sum([ref[24:32] for ref in ins])
    out_ref[0:8] = tree_sum([ref[16:24] for ref in ins])
    att = group_rows(chip, count, mine, prev[4:5], after[0:1])
    out_ref[8:16] = jnp.concatenate(att + [scalars[5:8]], axis=0)


def astro_kernel(first, count, keep_ref, rows_ref, *refs):
    high = STARS_DEV // LANES
    if first:
        out_ref, table_ref, spread_ref = refs
    else:
        table_ref, out_ref, spread_ref = refs
    extra = keep_ref.shape[0] // (2 * count)
    comps = extra // 8 - 1
    long = 8 * LANES

    def one(place, totals):
        new = []
        for half in range(2):
            slot = half * count + place
            rows = rows_ref[pl.ds(pl.multiple_of(slot * 8, 8), 8)]
            packed = keep_ref[pl.ds(pl.multiple_of(slot * extra, 8), extra)]
            index = packed[comps * 8 :].astype(jnp.int32)
            at0 = pl.multiple_of((half * count + place) * long, long)
            split = [halves(packed[comp * 8 : comp * 8 + 8] * rows) for comp in range(comps)]
            for block in range(8):
                here = slice(block, block + 1)
                if first:
                    table_ref[:, pl.ds(at0 + block * LANES, LANES)] = one_hot_low(index[here])
                pieces = []
                for part in range(2):
                    for comp in range(comps):
                        pieces.append(spread_high(index[here], split[comp][part][here], high))
                spread_ref[half, :, block * LANES : (block + 1) * LANES] = jnp.concatenate(
                    pieces, axis=0
                ).astype(bf16)
            new.append(
                totals[half] + dot_lanes(spread_ref[half], table_ref[:, pl.ds(at0, long)])
            )
        return tuple(new)

    zero = jnp.zeros((2 * comps * high, LANES), f32)
    low, top = lax.fori_loop(0, count, one, (zero, zero))
    total = low + top
    out_ref[...] = total[: comps * high] + total[comps * high :]


def sum_kernel(*refs):
    refs[-1][...] = tree_sum([ref[...] for ref in refs[:-1]])


def lane_sum(row):
    return jnp.broadcast_to(jnp.sum(row, axis=1, keepdims=True), row.shape)


def next_bidiagonal(total, state):
    squares, mixed, size = (lane_sum(total[row : row + 1]) for row in (13, 14, 15))
    alpha2 = size + epsilon
    alpha = jnp.sqrt(alpha2)
    rest = jnp.maximum(squares / alpha2 - 2.0 * mixed + alpha2 * state[0:1], 0.0)
    beta2 = rest + epsilon
    return alpha, jnp.sqrt(beta2), rest / beta2


def step_kernel(step, width, slots, chips, star_count, *refs):
    keep_ref, packs, tables, att2s, ints = refs[0], refs[1:3], refs[3:5], refs[5:7], refs[7:9]
    sum_ref, refs = refs[9], refs[10:]
    if step > 0:
        state_ref, old_z_ref, old_g_ref, old_u_ref, old_s_ref = refs[:5]
        refs = refs[5:]
    else:
        first_rows_ref, refs = refs[0], refs[1:]
    gathered, refs = refs[:-7], refs[-7:]
    send_ref, state_out, z_ref, g_ref, u_ref, s_ref, spread_ref = refs
    me = lax.axis_index("tm")
    chip, core = me // 2, me % 2
    high = STARS_DEV // LANES
    comps = sum_ref.shape[0] // high
    blocks = 8
    total = tree_sum([ref[...] for ref in gathered])
    back = jnp.concatenate([sum_ref[...], total], axis=0)
    if step == 0:
        squares = lane_sum(total[13:14])
        beta2 = squares + epsilon
        beta = jnp.sqrt(beta2)
        places = [pl.multiple_of(((half ^ core) * chips + chip) * 8, 8) for half in range(2)]
        u = jnp.concatenate([first_rows_ref[pl.ds(at, 8)] for at in places], axis=0) / beta
        g = back / beta
        z = g
        state_out[...] = jnp.concatenate(
            [squares / beta2, beta, jnp.zeros((14, LANES), f32)], axis=0
        )
    else:
        state = state_ref[...]
        alpha, beta, left2 = next_bidiagonal(total, state)
        u = (old_s_ref[...] / alpha - alpha * old_u_ref[...]) / beta
        g = (back / alpha - alpha * old_g_ref[...]) / beta
        z = g - (beta / alpha) * old_z_ref[...]
        pieces = [left2, state[1 : 1 + step], beta, jnp.zeros((7 - step, LANES), f32)]
        pieces += [state[9 : 8 + step]] if step > 1 else []
        pieces += [alpha, jnp.zeros((7 - step, LANES), f32)]
        state_out[...] = jnp.concatenate(pieces, axis=0)
    z_ref[...] = z
    g_ref[...] = g
    u_ref[...] = u
    base = comps * high
    inst_rows = z[base : base + 8]
    att_rows = z[base + 8 : base + 13]
    extra = 8 * comps + 8
    pieces = [inst_rows[place : place + 1] for place in range(8)]
    rows, insts, atts = [], [], []
    for half in range(2):
        starts = ints[half][slots * 8 :]
        own = jnp.where(core == half, att_rows[0:3], att_rows[2:5])
        part = att_forward(own, att2s[half][...], starts, width)
        at = pl.multiple_of(((half ^ core) * chips + chip) * extra, 8)
        packed = keep_ref[pl.ds(at, extra)]
        star = packed[comps * 8 :].astype(jnp.int32)
        star_high, star_low = star >> 7, star & (LANES - 1)
        for comp in range(comps):
            picked = jnp.zeros((blocks, LANES), f32)
            for place in range(high):
                at = comp * high + place
                picked = jnp.where(star_high == place, lane_pick(z[at : at + 1], star_low), picked)
            part = part + packed[comp * 8 : comp * 8 + 8] * picked
        coefs = [packs[half].at[slot * 8 : slot * 8 + 8] for slot in range(slots)]
        indices = [ints[half].at[slot * 8 : slot * 8 + 8] for slot in range(slots)]
        for slot in range(slots):
            part = part + coefs[slot][...] * table_pick(pieces, indices[slot][...])
        rows.append(part)
        if step < ITERS - 1:
            insts.append(inst_back(part, coefs, indices, tables[half], spread_ref.at[half]))
            atts.append(att_back(part, att2s[half][...], starts, width))
    both = jnp.concatenate(rows, axis=0)
    s_ref[...] = both

    def squared(value):
        return jnp.sum(value * value, axis=0, keepdims=True)

    size = squared(z[:base]) * (1.0 / chips) + squared(att_rows[:4]) * (1.0 / star_count)
    size = size + squared(inst_rows) * (1.0 / (star_count * chips))
    mixed = [jnp.sum(rows[half] * u[half * 8 : half * 8 + 8], axis=0, keepdims=True) for half in range(2)]
    scalars = [squared(rows[0]) + squared(rows[1]), mixed[0] + mixed[1], size]
    if step == ITERS - 1:
        send_ref[...] = (jnp.concatenate([jnp.zeros((5, LANES), f32)] + scalars, axis=0))
        return
    send_ref[0:16] = jnp.where(core == 0, both, jnp.concatenate(rows[::-1], axis=0))
    send_ref[16:24] = insts[0] + insts[1]
    low, top = (jnp.where(core == half, atts[0], atts[1]) for half in range(2))
    send_ref[24:32] = jnp.concatenate([chip_parts(low, top)] + scalars, axis=0)


def last_kernel(comps, share, state_ref, *refs):
    gathered, z_refs, out_ref = refs[: -ITERS - 1], refs[-ITERS - 1 : -1], refs[-1]
    high = STARS_DEV // LANES
    me = lax.axis_index("tm")
    total = tree_sum([ref[...] for ref in gathered])
    total = jnp.concatenate([jnp.zeros((8, LANES), f32), total], axis=0)
    state = state_ref[...]
    alpha, beta, _ = next_bidiagonal(total, state)
    betas = [state[1 + k : 2 + k] for k in range(ITERS)] + [beta]
    alphas = [state[9 + k : 10 + k] for k in range(ITERS - 1)] + [alpha]
    rho_bar, phi_bar = alphas[0], betas[0]
    weights = [jnp.zeros((1, LANES), f32)] * ITERS
    search = [jnp.zeros((1, LANES), f32)] * ITERS
    search[0] = 1.0 / alphas[0]
    for k in range(ITERS):
        rho = jnp.sqrt(rho_bar * rho_bar + betas[k + 1] * betas[k + 1])
        cosine, sine = rho_bar / rho, betas[k + 1] / rho
        phi = cosine * phi_bar
        phi_bar = sine * phi_bar
        weights = [x + phi / rho * w for x, w in zip(weights, search)]
        if k + 1 < ITERS:
            theta = sine * alphas[k + 1]
            rho_bar = -cosine * alphas[k + 1]
            search = [-(theta / rho) * w for w in search]
            search[k + 1] = 1.0 / alphas[k + 1]
    base = comps * high
    tiles = share // LANES

    def mix(read):
        total = weights[0] * read(z_refs[0])
        for k in range(1, ITERS):
            total = total + weights[k] * read(z_refs[k])
        return total

    rows = ATT_DEV // LANES
    pieces = [mix(lambda ref: ref[base : base + 8])]
    for core in range(2):
        at = base + 8 + core * rows
        pieces.append(mix(lambda ref: ref[at : at + rows]))
        for comp in range(comps):
            place = comp * high + (me // 2 * 2 + core) * tiles
            pieces.append(mix(lambda ref: ref[pl.ds(place, tiles)]))
    unused = out_ref.shape[0] - sum(piece.shape[0] for piece in pieces)
    if unused:
        pieces.append(jnp.zeros((unused, LANES), f32))
    out_ref[...] = jnp.concatenate(pieces, axis=0)


def place_kernel(comps, share, own_ref, other_ref, astro_ref, att_ref, inst_ref):
    core = lax.axis_index("tm") % 2
    tiles, rows = share // LANES, ATT_DEV // LANES
    value = jnp.where(core == 1, own_ref[...], other_ref[...])
    at = 8 + rows + comps * tiles
    mine = jnp.where(core == 0, value[8:at], value[at : 2 * at - 8])
    inst_ref[...] = value[0:8]
    att_ref[...] = mine[:rows]
    for comp in range(comps):
        for tile in range(tiles):
            row = rows + comp * tiles + tile
            astro_ref[comp : comp + 1, tile * LANES : (tile + 1) * LANES] = mine[row : row + 1]


def call(kernel, name, out, args, scratch=(), space=pltpu.VMEM):
    vmem = pl.BlockSpec(memory_space=pltpu.VMEM)
    return pl.pallas_call(
        kernel,
        name=name,
        out_shape=[jax.ShapeDtypeStruct(shape, dtype) for shape, dtype in out],
        in_specs=[pl.BlockSpec(memory_space=space)] * len(args),
        out_specs=[vmem] * len(out),
        scratch_shapes=list(scratch),
        compiler_params=pltpu.CompilerParams(vmem_limit_bytes=VMEM_LIMIT),
    )(*args)


def direct(value, axis, gaps):
    count = lax.axis_size(axis)
    return [value] + [
        lax.ppermute(value, axis, [(i, i ^ gap) for i in range(count)]) for gap in gaps
    ]


def exchange(value, axis):
    tm_count, star_count = lax.axis_size("tm"), lax.axis_size("star")
    got = [value]
    for gap in range(1, star_count if axis == "star" else tm_count // 2):
        steps = []
        for star in range(star_count):
            for tm in range(tm_count):
                far = (star ^ gap, tm) if axis == "star" else (star, tm ^ (2 * gap))
                far = far if tm % 2 else (star, tm)
                steps.append((star * tm_count + tm, far[0] * tm_count + far[1]))
        got.append(lax.ppermute(value, ("star", "tm"), steps))
    return got


def rows_type(rows):
    return ((rows, LANES), f32)


def per_device(astro_coef, star_index, att_coef, att_start, inst_coef, inst_index, observed):
    tm_count, star_count = lax.axis_size("tm"), lax.axis_size("star")
    comps = astro_coef.shape[1]
    slots = inst_coef.shape[1]
    blocks, width, height = att_coef.shape[1:]
    share = STARS_DEV // tm_count
    high = STARS_DEV // LANES
    chips = tm_count // 2
    args = [
        observed.reshape(blocks, height),
        astro_coef.reshape(comps, blocks, height),
        star_index.reshape(blocks, height),
        att_coef.reshape(blocks * width, height),
        att_start,
        inst_coef.reshape(slots, blocks, height),
        inst_index.reshape(slots, blocks, height),
    ]
    long = slots * blocks * height
    extra = 8 * comps + 8
    spread = pltpu.VMEM((16, long), bf16)
    prepared = [((LANES, long), bf16), ((2 * blocks * width, height), bf16),
                ((8 * slots + 8, LANES), jnp.int32)]
    here = [pltpu.with_memory_space_constraint(arg, pltpu.HBM) for arg in args]
    send, pack, *mine = call(
        functools.partial(first_kernel, width),
        "first",
        [((24 + extra, LANES), f32), ((16 * slots + 8 + blocks * width, LANES), f32)] + prepared,
        here,
        [pltpu.VMEM(arg.shape, arg.dtype) for arg in args if arg is not args[3]]
        + [spread, pltpu.SemaphoreType.DMA((len(args),))],
        pl.ANY,
    )
    (send,) = call(
        merge_kernel, "merge", [rows_type(32 + 2 * extra)], direct(send, "tm", [1])
    )
    send, late_pack = lax.optimization_barrier((send, pack))
    _, other_pack = direct(late_pack, "tm", [1])
    theirs = call(
        functools.partial(prepare_kernel, slots, blocks, width), "prepare", prepared, [other_pack]
    )
    got = exchange(send, "tm")
    theirs, got = lax.optimization_barrier((theirs, got))
    basics = [pack, other_pack] + [value for both in zip(mine, theirs) for value in both]
    keep = star_table = state = z = g = u = rows = None
    kept = []
    group_type = rows_type(16)
    for step in range(ITERS):
        wide = [pltpu.VMEM((2, 2 * comps * high, blocks * height), bf16)]
        sums_type = rows_type(comps * high)
        all_rows, group, *new = call(
            functools.partial(group_kernel, chips),
            "group",
            [rows_type(16 * chips), group_type]
            + ([rows_type(2 * chips * extra)] if step == 0 else []),
            exchange(send, "tm") if step else got,
        )
        across = exchange(group, "star")
        if step == 0:
            (keep,) = new
            sums, star_table = call(
                functools.partial(astro_kernel, True, chips),
                "astro",
                [sums_type, ((LANES, tm_count * blocks * height), bf16)],
                [keep, all_rows],
                wide,
            )
        else:
            (sums,) = call(
                functools.partial(astro_kernel, False, chips),
                "astro",
                [sums_type],
                [keep, all_rows, star_table],
                wide,
            )
        tall = ((comps * high + 16, LANES), f32)
        pair = ((2 * blocks, height), f32)
        older = [all_rows] if step == 0 else [state, z, g, u, rows]
        send, state, z, g, u, rows = call(
            functools.partial(step_kernel, step, width, slots, chips, star_count),
            "step",
            [rows_type(32 if step < ITERS - 1 else 8), group_type, tall, tall, pair, pair],
            [keep] + basics + [sums] + older + across,
            [pltpu.VMEM((2, 16, long), bf16)],
        )
        kept.append(z)
    (send,) = call(sum_kernel, "sum", [rows_type(8)], exchange(send, "tm"))
    across = exchange(send, "star")
    both_parts = 2 * (ATT_DEV // LANES + comps * share // LANES)
    (parts,) = call(
        functools.partial(last_kernel, comps, share),
        "last",
        [rows_type(8 + (both_parts + 7) // 8 * 8)],
        [state] + across + kept,
    )
    _, received = direct(parts, "tm", [1])
    out_astro, out_att, out_inst = call(
        functools.partial(place_kernel, comps, share),
        "place",
        [((comps, share), f32), ((ATT_DEV // LANES, LANES), f32), ((NINST // LANES, LANES), f32)],
        [parts, received],
    )
    return out_astro, out_att.reshape(-1), out_inst.reshape(-1)


def solution(mesh):
    return jax.shard_map(
        per_device,
        mesh=mesh,
        in_specs=(
            P("star", None, "tm"),
            P("star", "tm"),
            P("star", "tm", None, None),
            P("star", "tm"),
            P("star", None, "tm"),
            P("star", None, "tm"),
            P("star", "tm"),
        ),
        out_specs=(P(None, ("star", "tm")), P("tm"), P()),
        check_vma=False,
    )
```

```python
import functools

import jax
import jax.numpy as jnp
from jax import lax
from jax.experimental import pallas as pl
from jax.experimental.pallas import tpu as pltpu
from jax.sharding import PartitionSpec as P

STARS_DEV = 2048
NINST = 1024
ITERS = 3
ATT_DEV = 256
LANES = 128

epsilon = 1e-06
f32 = jnp.float32
bf16 = jnp.bfloat16
VMEM_LIMIT = 16 * 1024 * 1024


def halves(value):
    top = value.astype(bf16).astype(f32)
    return top, (value - top).astype(bf16).astype(f32)


def dot_lanes(left, right):
    return lax.dot_general(left, right, (((1,), (1,)), ((), ())), preferred_element_type=f32)


def dot_plain(left, right):
    return lax.dot_general(left, right, (((1,), (0,)), ((), ())), preferred_element_type=f32)


def lane_pick(row, lane_index):
    table = jnp.broadcast_to(row, lane_index.shape)
    return jnp.take_along_axis(table, lane_index, axis=1, mode="promise_in_bounds")


def table_pick(rows, index):
    high, low = index >> 7, index & (LANES - 1)
    total = jnp.zeros(index.shape, f32)
    for place, row in enumerate(rows):
        total = jnp.where(high == place, lane_pick(row, low), total)
    return total


def one_hot_low(index_row):
    shape = (LANES, LANES)
    low = jnp.broadcast_to(index_row & (LANES - 1), shape)
    hit = lax.broadcasted_iota(jnp.int32, shape, 0) == low
    return jnp.where(hit, 1.0, 0.0).astype(bf16)


def spread_high(index_row, value_row, count):
    shape = (count, LANES)
    high = jnp.broadcast_to(index_row >> 7, shape)
    hit = lax.broadcasted_iota(jnp.int32, shape, 0) == high
    return jnp.where(hit, jnp.broadcast_to(value_row, shape), 0.0)


def block_masks(blocks, width):
    shape = (blocks, LANES)
    row = lax.broadcasted_iota(jnp.int32, shape, 0)
    lane = lax.broadcasted_iota(jnp.int32, shape, 1)
    per_tile = LANES // width
    tiles = blocks // per_tile
    return [row == tile * per_tile + lane // width for tile in range(tiles)], row, lane


def inst_back(rows, coef_ref, index_ref, table_ref, spread_ref):
    slots, blocks = len(coef_ref), rows.shape[0]
    count = NINST // LANES
    for slot in range(slots):
        top, rest = halves(coef_ref[slot][...] * rows)
        index = index_ref[slot][...]
        for block in range(blocks):
            here = slice(block, block + 1)
            pieces = [spread_high(index[here], part[here], count) for part in (top, rest)]
            at = (slot * blocks + block) * LANES
            spread_ref[:, at : at + LANES] = jnp.concatenate(pieces, axis=0).astype(bf16)
    both = dot_lanes(spread_ref[...], table_ref[...])
    return both[:count] + both[count:]


def att_back(rows, att2, starts, width):
    blocks = rows.shape[0]
    size = att2.shape[0] // 2
    top, rest = halves(rows)
    both = dot_lanes(jnp.concatenate([top, rest], axis=0).astype(bf16), att2)
    both = both[:blocks] + both[blocks:]
    both = both[:, :size] + both[:, size:]
    masks, row, lane = block_masks(blocks, width)
    own = jnp.zeros((blocks, LANES), f32)
    for tile, mask in enumerate(masks):
        own = own + jnp.where(mask, both[:, tile * LANES : (tile + 1) * LANES], 0.0)
    shift = (row % (LANES // width)) * width
    out = []
    for tile in range((ATT_DEV + width + LANES - 1) // LANES):
        offset = lane + tile * LANES - starts
        inside = (offset >= 0) & (offset < width)
        picked = jnp.take_along_axis(
            own, jnp.where(inside, offset + shift, 0), axis=1, mode="promise_in_bounds"
        )
        out.append(jnp.sum(jnp.where(inside, picked, 0.0), axis=0, keepdims=True))
    return jnp.concatenate(out, axis=0)


def att_forward(att_rows, att2, starts, width):
    blocks = starts.shape[0]
    masks, row, lane = block_masks(blocks, width)
    tiles = [att_rows[tile : tile + 1] for tile in range(att_rows.shape[0])]
    window = table_pick(tiles, starts + lane % width)
    wide = jnp.concatenate([jnp.where(mask, window, 0.0) for mask in masks], axis=1)
    top, rest = halves(wide)
    left = jnp.concatenate([top, rest], axis=0).astype(bf16)
    both = dot_plain(jnp.concatenate([left, left], axis=1), att2)
    return both[:blocks] + both[blocks:]


def pack_places(slots, blocks, width):
    at = slots * 8
    return slice(0, at), slice(at, 2 * at), slice(2 * at, 2 * at + 8), slice(
        2 * at + 8, 2 * at + 8 + blocks * width
    )


def prepare_index(index_rows, starts, table_ref, ints_ref):
    count = index_rows.shape[0] // 8
    ints_ref[0 : count * 8] = index_rows
    ints_ref[count * 8 :] = starts
    for place in range(count * 8):
        table_ref[:, place * LANES : (place + 1) * LANES] = one_hot_low(
            index_rows[place : place + 1]
        )


def prepare_att(att, att2_ref):
    top = att.astype(bf16)
    att2_ref[...] = jnp.concatenate([top, (att - top.astype(f32)).astype(bf16)], axis=0)


def first_kernel(width, b_hbm, astro_hbm, star_hbm, att_hbm, starts_hbm, coef_hbm, index_hbm,
                 send_ref, pack_ref, table_ref, att2_ref, ints_ref,
                 b_ref, astro_ref, star_ref, starts_ref, coef_ref, index_ref,
                 spread_ref, sems):
    slots, blocks, _ = index_ref.shape
    comps = astro_ref.shape[0]
    places = pack_places(slots, blocks, width)
    pairs = [(index_hbm, index_ref), (starts_hbm, starts_ref), (att_hbm, pack_ref.at[places[3]]),
             (coef_hbm, coef_ref), (b_hbm, b_ref), (astro_hbm, astro_ref), (star_hbm, star_ref)]
    copies = [
        pltpu.make_async_copy(source, target, sems.at[place])
        for place, (source, target) in enumerate(pairs)
    ]
    for copy in copies:
        copy.start()
    for copy in copies[:2]:
        copy.wait()
    index = jnp.concatenate([index_ref[slot] for slot in range(slots)], axis=0)
    starts_row = jnp.broadcast_to(starts_ref[...].astype(f32), (blocks, blocks))
    diagonal = lax.broadcasted_iota(jnp.int32, (blocks, blocks), 0) == lax.broadcasted_iota(
        jnp.int32, (blocks, blocks), 1
    )
    starts = jnp.sum(jnp.where(diagonal, starts_row, 0.0), axis=1, keepdims=True)
    starts = jnp.broadcast_to(starts, (blocks, LANES))
    pack_ref[places[1]] = index.astype(f32)
    pack_ref[places[2]] = starts
    starts = starts.astype(jnp.int32)
    prepare_index(index, starts, table_ref, ints_ref)
    for copy in copies[2:]:
        copy.wait()
    prepare_att(pack_ref[places[3]], att2_ref)
    rows = b_ref[...]
    coefs = [coef_ref.at[slot] for slot in range(slots)]
    indices = [index_ref.at[slot] for slot in range(slots)]
    for slot in range(slots):
        pack_ref[slot * 8 : slot * 8 + 8] = coef_ref[slot]
    send_ref[0:8] = rows
    send_ref[8:16] = inst_back(rows, coefs, indices, table_ref, spread_ref)
    send_ref[16:19] = att_back(rows, att2_ref[...], starts, width)
    send_ref[19:20] = jnp.sum(rows * rows, axis=0, keepdims=True)
    send_ref[20:24] = jnp.zeros((4, LANES), f32)
    for comp in range(comps):
        send_ref[24 + comp * 8 : 32 + comp * 8] = astro_ref[comp]
    send_ref[24 + comps * 8 : 32 + comps * 8] = star_ref[...].astype(f32)


def prepare_kernel(slots, blocks, width, pack_ref, table_ref, att2_ref, ints_ref):
    places = pack_places(slots, blocks, width)
    index = pack_ref[places[1]].astype(jnp.int32)
    starts = pack_ref[places[2]].astype(jnp.int32)
    prepare_index(index, starts, table_ref, ints_ref)
    prepare_att(pack_ref[places[3]], att2_ref)


def tree_sum(values):
    while len(values) > 1:
        values = [values[i] + values[i + 1] for i in range(0, len(values), 2)]
    return values[0]


def first_chip_kernel(count, *refs):
    ins, out_ref = refs[:count], refs[count]
    chip = lax.axis_index("tm") // 2
    extra = ins[0].shape[0] - 24
    base = 8 * count + 16
    for gap in range(count):
        where = chip ^ gap
        out_ref[pl.ds(pl.multiple_of(where * 8, 8), 8)] = ins[gap][0:8]
        out_ref[pl.ds(pl.multiple_of(base + where * 8, 8), 8)] = ins[gap][16:24]
        at = pl.multiple_of(base + 8 * count + where * extra, 8)
        out_ref[pl.ds(at, extra)] = ins[gap][24:]
    out_ref[8 * count : 8 * count + 8] = tree_sum([ref[8:16] for ref in ins])
    out_ref[8 * count + 8 : base] = tree_sum([ref[16:24] for ref in ins])


def group_rows(chip, count, mine, prev_row, after_row):
    half = lax.broadcasted_iota(jnp.int32, (1, LANES), 1) < 64
    first = mine[0:1] + jnp.where(half & (chip > 0), prev_row, 0.0)
    last = jnp.where(half & (chip < count - 1), mine[4:5] + after_row, 0.0)
    return [first, mine[1:4], last]


def chip_parts(core, own, other):
    low = jnp.where(core == 0, own, other)
    top = jnp.where(core == 0, other, own)
    return jnp.concatenate([low[0:2], low[2:3] + top[0:1], top[1:3]], axis=0)


def first_group_kernel(count, own_ref, other_ref, out_ref):
    me = lax.axis_index("tm")
    chip, core = me // 2, me % 2
    low = 8 * count
    base = low + 16

    def part(ref, where):
        where = jnp.clip(where, 0, count - 1)
        return ref[pl.ds(pl.multiple_of(base + where * 8, 8), 8)]

    def of_core(which, where):
        return jnp.where(core == which, part(own_ref, where), part(other_ref, where))

    mine = chip_parts(core, part(own_ref, chip)[0:3], part(other_ref, chip)[0:3])
    prev, after = of_core(1, chip - 1), of_core(0, chip + 1)
    scalars = own_ref[low + 8 : low + 16] + other_ref[low + 8 : low + 16]
    out_ref[0:8] = own_ref[low : low + 8] + other_ref[low : low + 8]
    att = group_rows(chip, count, mine, prev[2:3], after[0:1])
    out_ref[8:16] = jnp.concatenate(att + [scalars[3:6]], axis=0)


def group_kernel(count, *refs):
    *ins, rows_ref, out_ref = refs
    me = lax.axis_index("tm")
    chip = me // 2
    places = [chip ^ gap for gap in range(count)]
    zero = jnp.zeros((8, LANES), f32)
    mine, prev, after = zero, zero, zero
    for ref, where in zip(ins, places):
        for half in range(2):
            at = pl.multiple_of((half * count + where) * 8, 8)
            rows_ref[pl.ds(at, 8)] = ref[half * 8 : half * 8 + 8]
        low = ref[24:32]
        mine = jnp.where(where == chip, low, mine)
        prev = jnp.where(where == chip - 1, low, prev)
        after = jnp.where(where == chip + 1, low, after)
    scalars = tree_sum([ref[24:32] for ref in ins])
    out_ref[0:8] = tree_sum([ref[16:24] for ref in ins])
    att = group_rows(chip, count, mine, prev[4:5], after[0:1])
    out_ref[8:16] = jnp.concatenate(att + [scalars[5:8]], axis=0)


def astro_kernel(first, count, *refs):
    high = STARS_DEV // LANES
    if first:
        keep, (out_ref, table_ref, spread_ref) = refs[:2], refs[2:]
    else:
        keep, (table_ref, rows_ref, out_ref, spread_ref) = refs[:2], refs[2:]
    base = 16 * count + 16
    extra = (keep[0].shape[0] - base) // count
    comps = extra // 8 - 1
    long = 8 * LANES
    core = lax.axis_index("tm") % 2

    def one(place, totals):
        new = []
        for half in range(2):
            if first:
                rows = keep[half][pl.ds(pl.multiple_of(place * 8, 8), 8)]
            else:
                at = ((half ^ core) * count + place) * 8
                rows = rows_ref[pl.ds(pl.multiple_of(at, 8), 8)]
            packed = keep[half][pl.ds(pl.multiple_of(base + place * extra, 8), extra)]
            index = packed[comps * 8 :].astype(jnp.int32)
            at0 = pl.multiple_of((half * count + place) * long, long)
            split = [halves(packed[comp * 8 : comp * 8 + 8] * rows) for comp in range(comps)]
            for block in range(8):
                here = slice(block, block + 1)
                if first:
                    table_ref[:, pl.ds(at0 + block * LANES, LANES)] = one_hot_low(index[here])
                pieces = []
                for part in range(2):
                    for comp in range(comps):
                        pieces.append(spread_high(index[here], split[comp][part][here], high))
                spread_ref[half, :, block * LANES : (block + 1) * LANES] = jnp.concatenate(
                    pieces, axis=0
                ).astype(bf16)
            new.append(
                totals[half] + dot_lanes(spread_ref[half], table_ref[:, pl.ds(at0, long)])
            )
        return tuple(new)

    zero = jnp.zeros((2 * comps * high, LANES), f32)
    own, other = lax.fori_loop(0, count, one, (zero, zero))
    total = own + other
    out_ref[...] = total[: comps * high] + total[comps * high :]


def sum_kernel(*refs):
    refs[-1][...] = tree_sum([ref[...] for ref in refs[:-1]])


def lane_sum(row):
    return jnp.broadcast_to(jnp.sum(row, axis=1, keepdims=True), row.shape)


def next_bidiagonal(total, state):
    squares, mixed, size = (lane_sum(total[row : row + 1]) for row in (13, 14, 15))
    alpha2 = size + epsilon
    alpha = jnp.sqrt(alpha2)
    rest = jnp.maximum(squares / alpha2 - 2.0 * mixed + alpha2 * state[0:1], 0.0)
    beta2 = rest + epsilon
    return alpha, jnp.sqrt(beta2), rest / beta2


def step_kernel(step, width, slots, chips, star_count, *refs):
    keep, packs, tables, att2s, ints, sum_ref = refs[:2], refs[2:4], refs[4:6], refs[6:8], refs[8:10], refs[10]
    refs = refs[11:]
    if step > 0:
        state_ref, old_z_ref, old_g_ref, old_u_ref, old_s_ref = refs[:5]
        refs = refs[5:]
    gathered, refs = refs[:-7], refs[-7:]
    send_ref, state_out, z_ref, g_ref, u_ref, s_ref, spread_ref = refs
    me = lax.axis_index("tm")
    chip, core = me // 2, me % 2
    high = STARS_DEV // LANES
    comps = sum_ref.shape[0] // high
    blocks = 8
    total = tree_sum([ref[...] for ref in gathered])
    back = jnp.concatenate([sum_ref[...], total], axis=0)
    if step == 0:
        squares = lane_sum(total[13:14])
        beta2 = squares + epsilon
        beta = jnp.sqrt(beta2)
        at = pl.ds(pl.multiple_of(chip * 8, 8), 8)
        u = jnp.concatenate([ref[at] for ref in keep], axis=0) / beta
        g = back / beta
        z = g
        state_out[...] = jnp.concatenate(
            [squares / beta2, beta, jnp.zeros((14, LANES), f32)], axis=0
        )
    else:
        state = state_ref[...]
        alpha, beta, left2 = next_bidiagonal(total, state)
        u = (old_s_ref[...] / alpha - alpha * old_u_ref[...]) / beta
        g = (back / alpha - alpha * old_g_ref[...]) / beta
        z = g - (beta / alpha) * old_z_ref[...]
        pieces = [left2, state[1 : 1 + step], beta, jnp.zeros((7 - step, LANES), f32)]
        pieces += [state[9 : 8 + step]] if step > 1 else []
        pieces += [alpha, jnp.zeros((7 - step, LANES), f32)]
        state_out[...] = jnp.concatenate(pieces, axis=0)
    z_ref[...] = z
    g_ref[...] = g
    u_ref[...] = u
    base = comps * high
    inst_rows = z[base : base + 8]
    att_rows = z[base + 8 : base + 13]
    extra = 8 * comps + 8
    here = 16 * chips + 16 + chip * extra
    pieces = [inst_rows[place : place + 1] for place in range(8)]
    rows, insts, atts = [], [], []
    for half in range(2):
        starts = ints[half][slots * 8 :]
        own = jnp.where(core == half, att_rows[0:3], att_rows[2:5])
        part = att_forward(own, att2s[half][...], starts, width)
        packed = keep[half][pl.ds(pl.multiple_of(here, 8), extra)]
        star = packed[comps * 8 :].astype(jnp.int32)
        star_high, star_low = star >> 7, star & (LANES - 1)
        for comp in range(comps):
            picked = jnp.zeros((blocks, LANES), f32)
            for place in range(high):
                at = comp * high + place
                picked = jnp.where(star_high == place, lane_pick(z[at : at + 1], star_low), picked)
            part = part + packed[comp * 8 : comp * 8 + 8] * picked
        coefs = [packs[half].at[slot * 8 : slot * 8 + 8] for slot in range(slots)]
        indices = [ints[half].at[slot * 8 : slot * 8 + 8] for slot in range(slots)]
        for slot in range(slots):
            part = part + coefs[slot][...] * table_pick(pieces, indices[slot][...])
        rows.append(part)
        if step < ITERS - 1:
            insts.append(inst_back(part, coefs, indices, tables[half], spread_ref.at[half]))
            atts.append(att_back(part, att2s[half][...], starts, width))
    both = jnp.concatenate(rows, axis=0)
    s_ref[...] = both

    def squared(value):
        return jnp.sum(value * value, axis=0, keepdims=True)

    size = squared(z[:base]) * (1.0 / chips) + squared(att_rows[:4]) * (1.0 / star_count)
    size = size + squared(inst_rows) * (1.0 / (star_count * chips))
    mixed = [jnp.sum(rows[half] * u[half * 8 : half * 8 + 8], axis=0, keepdims=True) for half in range(2)]
    scalars = [squared(rows[0]) + squared(rows[1]), mixed[0] + mixed[1], size]
    if step == ITERS - 1:
        send_ref[...] = (jnp.concatenate([jnp.zeros((5, LANES), f32)] + scalars, axis=0))
        return
    send_ref[0:16] = jnp.where(core == 0, both, jnp.concatenate(rows[::-1], axis=0))
    send_ref[16:24] = insts[0] + insts[1]
    send_ref[24:32] = jnp.concatenate([chip_parts(core, *atts)] + scalars, axis=0)


def last_kernel(comps, share, star_count, state_ref, *refs):
    gathered, refs = refs[: -ITERS - 3], refs[-ITERS - 3 :]
    z_refs = refs[:ITERS]
    astro_ref, att_ref, inst_ref = refs[ITERS:]
    high = STARS_DEV // LANES
    me = lax.axis_index("tm")
    total = tree_sum([ref[...] for ref in gathered])
    total = jnp.concatenate([jnp.zeros((8, LANES), f32), total], axis=0)
    state = state_ref[...]
    alpha, beta, _ = next_bidiagonal(total, state)
    betas = [state[1 + k : 2 + k] for k in range(ITERS)] + [beta]
    alphas = [state[9 + k : 10 + k] for k in range(ITERS - 1)] + [alpha]
    rho_bar, phi_bar = alphas[0], betas[0]
    weights = [jnp.zeros((1, LANES), f32)] * ITERS
    search = [jnp.zeros((1, LANES), f32)] * ITERS
    search[0] = 1.0 / alphas[0]
    for k in range(ITERS):
        rho = jnp.sqrt(rho_bar * rho_bar + betas[k + 1] * betas[k + 1])
        cosine, sine = rho_bar / rho, betas[k + 1] / rho
        phi = cosine * phi_bar
        phi_bar = sine * phi_bar
        weights = [x + phi / rho * w for x, w in zip(weights, search)]
        if k + 1 < ITERS:
            theta = sine * alphas[k + 1]
            rho_bar = -cosine * alphas[k + 1]
            search = [-(theta / rho) * w for w in search]
            search[k + 1] = 1.0 / alphas[k + 1]
    base = comps * high
    tiles = share // LANES

    def mix(read):
        total = weights[0] * read(z_refs[0])
        for k in range(1, ITERS):
            total = total + weights[k] * read(z_refs[k])
        return total

    for comp in range(comps):
        for tile in range(tiles):
            at = comp * high + me * tiles + tile
            astro_ref[comp : comp + 1, tile * LANES : (tile + 1) * LANES] = mix(
                lambda ref: ref[pl.ds(at, 1)]
            )
    inst_ref[...] = mix(lambda ref: ref[base : base + 8])
    rows = ATT_DEV // LANES
    att_ref[...] = mix(lambda ref: ref[pl.ds(base + 8 + (me % 2) * rows, rows)])


def call(kernel, name, out, args, scratch=(), space=pltpu.VMEM):
    vmem = pl.BlockSpec(memory_space=pltpu.VMEM)
    return pl.pallas_call(
        kernel,
        name=name,
        out_shape=[jax.ShapeDtypeStruct(shape, dtype) for shape, dtype in out],
        in_specs=[pl.BlockSpec(memory_space=space)] * len(args),
        out_specs=[vmem] * len(out),
        scratch_shapes=list(scratch),
        compiler_params=pltpu.CompilerParams(vmem_limit_bytes=VMEM_LIMIT),
    )(*args)


def direct(value, axis, gaps):
    count = lax.axis_size(axis)
    return [value] + [
        lax.ppermute(value, axis, [(i, i ^ gap) for i in range(count)]) for gap in gaps
    ]


def exchange(value, axis):
    tm_count, star_count = lax.axis_size("tm"), lax.axis_size("star")
    got = [value]
    for gap in range(1, star_count if axis == "star" else tm_count // 2):
        steps = []
        for star in range(star_count):
            for tm in range(tm_count):
                far = (star ^ gap, tm ^ 1) if axis == "star" else (star, tm ^ (2 * gap + 1))
                steps.append((star * tm_count + tm, far[0] * tm_count + far[1]))
        got.append(lax.ppermute(value, ("star", "tm"), steps))
    return got


def rows_type(rows):
    return ((rows, LANES), f32)


def per_device(astro_coef, star_index, att_coef, att_start, inst_coef, inst_index, observed):
    tm_count, star_count = lax.axis_size("tm"), lax.axis_size("star")
    comps = astro_coef.shape[1]
    slots = inst_coef.shape[1]
    blocks, width, height = att_coef.shape[1:]
    share = STARS_DEV // tm_count
    high = STARS_DEV // LANES
    chips = tm_count // 2
    far = [2 * gap for gap in range(1, chips)]
    args = [
        observed.reshape(blocks, height),
        astro_coef.reshape(comps, blocks, height),
        star_index.reshape(blocks, height),
        att_coef.reshape(blocks * width, height),
        att_start,
        inst_coef.reshape(slots, blocks, height),
        inst_index.reshape(slots, blocks, height),
    ]
    long = slots * blocks * height
    extra = 8 * comps + 8
    spread = pltpu.VMEM((16, long), bf16)
    prepared = [((LANES, long), bf16), ((2 * blocks * width, height), bf16),
                ((8 * slots + 8, LANES), jnp.int32)]
    here = [pltpu.with_memory_space_constraint(arg, pltpu.HBM) for arg in args]
    send, pack, *mine = call(
        functools.partial(first_kernel, width),
        "first",
        [((24 + extra, LANES), f32), ((16 * slots + 8 + blocks * width, LANES), f32)] + prepared,
        here,
        [pltpu.VMEM(arg.shape, arg.dtype) for arg in args if arg is not args[3]]
        + [spread, pltpu.SemaphoreType.DMA((len(args),))],
        pl.ANY,
    )
    keep = star_table = state = z = g = u = rows = None
    kept = []
    group_type = rows_type(16)
    for step in range(ITERS):
        wide = [pltpu.VMEM((2, 2 * comps * high, blocks * height), bf16)]
        sums_type = ((comps * high, LANES), f32)
        got = exchange(send, "tm") if step else direct(send, "tm", far)
        if step == 0:
            (gathered,) = call(
                functools.partial(first_chip_kernel, chips),
                "chip",
                [((16 * chips + 16 + chips * extra, LANES), f32)],
                got,
            )
            keep = direct(gathered, "tm", [1])
            (group,) = call(
                functools.partial(first_group_kernel, chips), "group", [group_type], keep
            )
            group, late_pack = lax.optimization_barrier((group, pack))
            _, other_pack = direct(late_pack, "tm", [1])
            theirs = call(
                functools.partial(prepare_kernel, slots, blocks, width),
                "prepare",
                prepared,
                [other_pack],
            )
            basics = [pack, other_pack] + [value for both in zip(mine, theirs) for value in both]
        else:
            all_rows, group = call(
                functools.partial(group_kernel, chips),
                "group",
                [rows_type(16 * chips), group_type],
                got,
            )
        across = exchange(group, "star")
        if step == 0:
            sums, star_table = call(
                functools.partial(astro_kernel, True, chips),
                "astro",
                [sums_type, ((LANES, tm_count * blocks * height), bf16)],
                keep,
                wide,
            )
        else:
            (sums,) = call(
                functools.partial(astro_kernel, False, chips),
                "astro",
                [sums_type],
                keep + [star_table, all_rows],
                wide,
            )
        tall = ((comps * high + 16, LANES), f32)
        pair = ((2 * blocks, height), f32)
        older = [] if step == 0 else [state, z, g, u, rows]
        send, state, z, g, u, rows = call(
            functools.partial(step_kernel, step, width, slots, chips, star_count),
            "step",
            [rows_type(32 if step < ITERS - 1 else 8), group_type, tall, tall, pair, pair],
            keep + basics + [sums] + older + across,
            [pltpu.VMEM((2, 16, long), bf16)],
        )
        kept.append(z)
    (send,) = call(sum_kernel, "sum", [rows_type(8)], exchange(send, "tm"))
    across = exchange(send, "star")
    out_astro, out_att, out_inst = call(
        functools.partial(last_kernel, comps, share, star_count),
        "last",
        [((comps, share), f32), ((ATT_DEV // LANES, LANES), f32), ((NINST // LANES, LANES), f32)],
        [state] + across + kept,
    )
    return out_astro, out_att.reshape(-1), out_inst.reshape(-1)


def solution(mesh):
    return jax.shard_map(
        per_device,
        mesh=mesh,
        in_specs=(
            P("star", None, "tm"),
            P("star", "tm"),
            P("star", "tm", None, None),
            P("star", "tm"),
            P("star", None, "tm"),
            P("star", None, "tm"),
            P("star", "tm"),
        ),
        out_specs=(P(None, ("star", "tm")), P("tm"), P()),
        check_vma=False,
    )
```

```python
import functools

import jax
import jax.numpy as jnp
from jax import lax
from jax.experimental import pallas as pl
from jax.experimental.pallas import tpu as pltpu
from jax.sharding import PartitionSpec as P

STARS_DEV = 2048
NINST = 1024
ITERS = 3
ATT_DEV = 256
LANES = 128

epsilon = 1e-06
f32 = jnp.float32
bf16 = jnp.bfloat16
VMEM_LIMIT = 16 * 1024 * 1024


def halves(value):
    top = value.astype(bf16).astype(f32)
    return top, (value - top).astype(bf16).astype(f32)


def dot_lanes(left, right):
    return lax.dot_general(left, right, (((1,), (1,)), ((), ())), preferred_element_type=f32)


def dot_plain(left, right):
    return lax.dot_general(left, right, (((1,), (0,)), ((), ())), preferred_element_type=f32)


def lane_pick(row, lane_index):
    table = jnp.broadcast_to(row, lane_index.shape)
    return jnp.take_along_axis(table, lane_index, axis=1, mode="promise_in_bounds")


def table_pick(rows, index):
    high, low = index >> 7, index & (LANES - 1)
    total = jnp.zeros(index.shape, f32)
    for place, row in enumerate(rows):
        total = jnp.where(high == place, lane_pick(row, low), total)
    return total


def one_hot_low(index_row):
    shape = (LANES, LANES)
    low = jnp.broadcast_to(index_row & (LANES - 1), shape)
    hit = lax.broadcasted_iota(jnp.int32, shape, 0) == low
    return jnp.where(hit, 1.0, 0.0).astype(bf16)


def spread_high(index_row, value_row, count):
    shape = (count, LANES)
    high = jnp.broadcast_to(index_row >> 7, shape)
    hit = lax.broadcasted_iota(jnp.int32, shape, 0) == high
    return jnp.where(hit, jnp.broadcast_to(value_row, shape), 0.0)


def block_masks(blocks, width):
    shape = (blocks, LANES)
    row = lax.broadcasted_iota(jnp.int32, shape, 0)
    lane = lax.broadcasted_iota(jnp.int32, shape, 1)
    per_tile = LANES // width
    tiles = blocks // per_tile
    return [row == tile * per_tile + lane // width for tile in range(tiles)], row, lane


def inst_back(rows, coef_ref, index_ref, table_ref, spread_ref):
    slots, blocks = len(coef_ref), rows.shape[0]
    count = NINST // LANES
    for slot in range(slots):
        top, rest = halves(coef_ref[slot][...] * rows)
        index = index_ref[slot][...]
        for block in range(blocks):
            here = slice(block, block + 1)
            pieces = [spread_high(index[here], part[here], count) for part in (top, rest)]
            at = (slot * blocks + block) * LANES
            spread_ref[:, at : at + LANES] = jnp.concatenate(pieces, axis=0).astype(bf16)
    both = dot_lanes(spread_ref[...], table_ref[...])
    return both[:count] + both[count:]


def att_back(rows, att2, starts, width):
    blocks = rows.shape[0]
    size = att2.shape[0] // 2
    top, rest = halves(rows)
    both = dot_lanes(jnp.concatenate([top, rest], axis=0).astype(bf16), att2)
    both = both[:blocks] + both[blocks:]
    both = both[:, :size] + both[:, size:]
    masks, row, lane = block_masks(blocks, width)
    own = jnp.zeros((blocks, LANES), f32)
    for tile, mask in enumerate(masks):
        own = own + jnp.where(mask, both[:, tile * LANES : (tile + 1) * LANES], 0.0)
    shift = (row % (LANES // width)) * width
    out = []
    for tile in range((ATT_DEV + width + LANES - 1) // LANES):
        offset = lane + tile * LANES - starts
        inside = (offset >= 0) & (offset < width)
        picked = jnp.take_along_axis(
            own, jnp.where(inside, offset + shift, 0), axis=1, mode="promise_in_bounds"
        )
        out.append(jnp.sum(jnp.where(inside, picked, 0.0), axis=0, keepdims=True))
    return jnp.concatenate(out, axis=0)


def att_forward(att_rows, att2, starts, width):
    blocks = starts.shape[0]
    masks, row, lane = block_masks(blocks, width)
    tiles = [att_rows[tile : tile + 1] for tile in range(att_rows.shape[0])]
    window = table_pick(tiles, starts + lane % width)
    wide = jnp.concatenate([jnp.where(mask, window, 0.0) for mask in masks], axis=1)
    top, rest = halves(wide)
    left = jnp.concatenate([top, rest], axis=0).astype(bf16)
    both = dot_plain(jnp.concatenate([left, left], axis=1), att2)
    return both[:blocks] + both[blocks:]


def pack_places(slots, blocks, width):
    at = slots * 8
    return slice(0, at), slice(at, 2 * at), slice(2 * at, 2 * at + 8), slice(
        2 * at + 8, 2 * at + 8 + blocks * width
    )


def prepare_index(index_rows, starts, table_ref, ints_ref):
    count = index_rows.shape[0] // 8
    ints_ref[0 : count * 8] = index_rows
    ints_ref[count * 8 :] = starts
    for place in range(count * 8):
        table_ref[:, place * LANES : (place + 1) * LANES] = one_hot_low(
            index_rows[place : place + 1]
        )


def prepare_att(att, att2_ref):
    top = att.astype(bf16)
    att2_ref[...] = jnp.concatenate([top, (att - top.astype(f32)).astype(bf16)], axis=0)


def first_kernel(width, b_hbm, astro_hbm, star_hbm, att_hbm, starts_hbm, coef_hbm, index_hbm,
                 send_ref, pack_ref, table_ref, att2_ref, ints_ref,
                 b_ref, astro_ref, star_ref, starts_ref, coef_ref, index_ref,
                 spread_ref, sems):
    slots, blocks, _ = index_ref.shape
    comps = astro_ref.shape[0]
    places = pack_places(slots, blocks, width)
    pairs = [(index_hbm, index_ref), (starts_hbm, starts_ref), (att_hbm, pack_ref.at[places[3]]),
             (coef_hbm, coef_ref), (b_hbm, b_ref), (astro_hbm, astro_ref), (star_hbm, star_ref)]
    copies = [
        pltpu.make_async_copy(source, target, sems.at[place])
        for place, (source, target) in enumerate(pairs)
    ]
    for copy in copies:
        copy.start()
    for copy in copies[:2]:
        copy.wait()
    index = jnp.concatenate([index_ref[slot] for slot in range(slots)], axis=0)
    starts_row = jnp.broadcast_to(starts_ref[...].astype(f32), (blocks, blocks))
    diagonal = lax.broadcasted_iota(jnp.int32, (blocks, blocks), 0) == lax.broadcasted_iota(
        jnp.int32, (blocks, blocks), 1
    )
    starts = jnp.sum(jnp.where(diagonal, starts_row, 0.0), axis=1, keepdims=True)
    starts = jnp.broadcast_to(starts, (blocks, LANES))
    pack_ref[places[1]] = index.astype(f32)
    pack_ref[places[2]] = starts
    starts = starts.astype(jnp.int32)
    prepare_index(index, starts, table_ref, ints_ref)
    for copy in copies[2:]:
        copy.wait()
    prepare_att(pack_ref[places[3]], att2_ref)
    rows = b_ref[...]
    coefs = [coef_ref.at[slot] for slot in range(slots)]
    indices = [index_ref.at[slot] for slot in range(slots)]
    for slot in range(slots):
        pack_ref[slot * 8 : slot * 8 + 8] = coef_ref[slot]
    send_ref[0:8] = rows
    send_ref[8:16] = inst_back(rows, coefs, indices, table_ref, spread_ref)
    send_ref[16:19] = att_back(rows, att2_ref[...], starts, width)
    send_ref[19:20] = jnp.sum(rows * rows, axis=0, keepdims=True)
    send_ref[20:24] = jnp.zeros((4, LANES), f32)
    for comp in range(comps):
        send_ref[24 + comp * 8 : 32 + comp * 8] = astro_ref[comp]
    send_ref[24 + comps * 8 : 32 + comps * 8] = star_ref[...].astype(f32)


def prepare_kernel(slots, blocks, width, pack_ref, table_ref, att2_ref, ints_ref):
    places = pack_places(slots, blocks, width)
    index = pack_ref[places[1]].astype(jnp.int32)
    starts = pack_ref[places[2]].astype(jnp.int32)
    prepare_index(index, starts, table_ref, ints_ref)
    prepare_att(pack_ref[places[3]], att2_ref)


def tree_sum(values):
    while len(values) > 1:
        values = [values[i] + values[i + 1] for i in range(0, len(values), 2)]
    return values[0]


def first_chip_kernel(count, *refs):
    ins, out_ref = refs[:count], refs[count]
    chip = lax.axis_index("tm") // 2
    extra = ins[0].shape[0] - 24
    base = 8 * count + 16
    for gap in range(count):
        where = chip ^ gap
        out_ref[pl.ds(pl.multiple_of(where * 8, 8), 8)] = ins[gap][0:8]
        out_ref[pl.ds(pl.multiple_of(base + where * 8, 8), 8)] = ins[gap][16:24]
        at = pl.multiple_of(base + 8 * count + where * extra, 8)
        out_ref[pl.ds(at, extra)] = ins[gap][24:]
    out_ref[8 * count : 8 * count + 8] = tree_sum([ref[8:16] for ref in ins])
    out_ref[8 * count + 8 : base] = tree_sum([ref[16:24] for ref in ins])


def group_rows(chip, count, mine, prev_row, after_row):
    half = lax.broadcasted_iota(jnp.int32, (1, LANES), 1) < 64
    first = mine[0:1] + jnp.where(half & (chip > 0), prev_row, 0.0)
    last = jnp.where(half & (chip < count - 1), mine[4:5] + after_row, 0.0)
    return [first, mine[1:4], last]


def chip_parts(core, own, other):
    low = jnp.where(core == 0, own, other)
    top = jnp.where(core == 0, other, own)
    return jnp.concatenate([low[0:2], low[2:3] + top[0:1], top[1:3]], axis=0)


def first_group_kernel(count, own_ref, other_ref, out_ref):
    me = lax.axis_index("tm")
    chip, core = me // 2, me % 2
    low = 8 * count
    base = low + 16

    def part(ref, where):
        where = jnp.clip(where, 0, count - 1)
        return ref[pl.ds(pl.multiple_of(base + where * 8, 8), 8)]

    def of_core(which, where):
        return jnp.where(core == which, part(own_ref, where), part(other_ref, where))

    mine = chip_parts(core, part(own_ref, chip)[0:3], part(other_ref, chip)[0:3])
    prev, after = of_core(1, chip - 1), of_core(0, chip + 1)
    scalars = own_ref[low + 8 : low + 16] + other_ref[low + 8 : low + 16]
    out_ref[0:8] = own_ref[low : low + 8] + other_ref[low : low + 8]
    att = group_rows(chip, count, mine, prev[2:3], after[0:1])
    out_ref[8:16] = jnp.concatenate(att + [scalars[3:6]], axis=0)


def group_kernel(count, *refs):
    *ins, rows_ref, out_ref = refs
    me = lax.axis_index("tm")
    chip = me // 2
    places = [chip ^ gap for gap in range(count)]
    zero = jnp.zeros((8, LANES), f32)
    mine, prev, after = zero, zero, zero
    for ref, where in zip(ins, places):
        for half in range(2):
            at = pl.multiple_of((half * count + where) * 8, 8)
            rows_ref[pl.ds(at, 8)] = ref[half * 8 : half * 8 + 8]
        low = ref[24:32]
        mine = jnp.where(where == chip, low, mine)
        prev = jnp.where(where == chip - 1, low, prev)
        after = jnp.where(where == chip + 1, low, after)
    scalars = tree_sum([ref[24:32] for ref in ins])
    out_ref[0:8] = tree_sum([ref[16:24] for ref in ins])
    att = group_rows(chip, count, mine, prev[4:5], after[0:1])
    out_ref[8:16] = jnp.concatenate(att + [scalars[5:8]], axis=0)


def kept(count, keep_ref):
    base = 16 * count + 16
    extra = (keep_ref.shape[0] - base) // count
    return base, extra, extra // 8 - 1


def star_sums(count, place, keep_ref, rows, table_ref, spread_ref, build):
    high = STARS_DEV // LANES
    base, extra, comps = kept(count, keep_ref)
    long = 8 * LANES
    packed = keep_ref[pl.ds(pl.multiple_of(base + place * extra, 8), extra)]
    index = packed[comps * 8 :].astype(jnp.int32)
    at0 = pl.multiple_of(place * long, long)
    split = [halves(packed[comp * 8 : comp * 8 + 8] * rows) for comp in range(comps)]
    for block in range(8):
        here = slice(block, block + 1)
        if build:
            table_ref[:, pl.ds(at0 + block * LANES, LANES)] = one_hot_low(index[here])
        pieces = []
        for part in range(2):
            for comp in range(comps):
                pieces.append(spread_high(index[here], split[comp][part][here], high))
        spread_ref[:, block * LANES : (block + 1) * LANES] = jnp.concatenate(
            pieces, axis=0
        ).astype(bf16)
    return dot_lanes(spread_ref[...], table_ref[:, pl.ds(at0, long)])


def star_rows(count, keep_ref, sums):
    high = STARS_DEV // LANES
    base, extra, comps = kept(count, keep_ref)
    chip = lax.axis_index("tm") // 2
    packed = keep_ref[pl.ds(pl.multiple_of(base + chip * extra, 8), extra)]
    star = packed[comps * 8 :].astype(jnp.int32)
    star_high, star_low = star >> 7, star & (LANES - 1)
    total = jnp.zeros((8, LANES), f32)
    for comp in range(comps):
        picked = jnp.zeros((8, LANES), f32)
        for place in range(high):
            at = comp * high + place
            picked = jnp.where(star_high == place, lane_pick(sums[at : at + 1], star_low), picked)
        total = total + packed[comp * 8 : comp * 8 + 8] * picked
    return total


def first_sums(count, keep_ref, table_ref, spread_ref):
    size = spread_ref.shape[0]

    def one(place, total):
        rows = keep_ref[pl.ds(pl.multiple_of(place * 8, 8), 8)]
        return total + star_sums(count, place, keep_ref, rows, table_ref, spread_ref, True)

    total = lax.fori_loop(0, count, one, jnp.zeros((size, LANES), f32))
    return total[: size // 2] + total[size // 2 :]


def astro_own_kernel(count, keep_ref, out_ref, table_ref, spread_ref):
    out_ref[...] = first_sums(count, keep_ref, table_ref, spread_ref)


def astro_other_kernel(count, own_ref, keep_ref, part_ref, out_ref, ya_ref, table_ref, spread_ref):
    total = part_ref[...] + first_sums(count, keep_ref, table_ref, spread_ref)
    out_ref[...] = total
    ya_ref[0:8] = star_rows(count, own_ref, total)
    ya_ref[8:16] = star_rows(count, keep_ref, total)


def astro_kernel(count, own_ref, other_ref, own_table, other_table, rows_ref, out_ref, ya_ref,
                 spread_ref):
    core = lax.axis_index("tm") % 2
    size = spread_ref.shape[1]
    sources = ((own_ref, own_table), (other_ref, other_table))

    def one(place, totals):
        new = []
        for half, (keep_ref, table_ref) in enumerate(sources):
            at = ((half ^ core) * count + place) * 8
            rows = rows_ref[pl.ds(pl.multiple_of(at, 8), 8)]
            part = star_sums(count, place, keep_ref, rows, table_ref, spread_ref.at[half], False)
            new.append(totals[half] + part)
        return tuple(new)

    zero = jnp.zeros((size, LANES), f32)
    own, other = lax.fori_loop(0, count, one, (zero, zero))
    total = own + other
    total = total[: size // 2] + total[size // 2 :]
    out_ref[...] = total
    ya_ref[0:8] = star_rows(count, own_ref, total)
    ya_ref[8:16] = star_rows(count, other_ref, total)


def sum_kernel(*refs):
    refs[-1][...] = tree_sum([ref[...] for ref in refs[:-1]])


def lane_sum(row):
    return jnp.broadcast_to(jnp.sum(row, axis=1, keepdims=True), row.shape)


def next_bidiagonal(total, state):
    squares, mixed, size = (lane_sum(total[row : row + 1]) for row in (13, 14, 15))
    alpha2 = size + epsilon
    alpha = jnp.sqrt(alpha2)
    rest = jnp.maximum(squares / alpha2 - 2.0 * mixed + alpha2 * state[0:1], 0.0)
    beta2 = rest + epsilon
    return alpha, jnp.sqrt(beta2), rest / beta2


def step_kernel(step, width, slots, chips, star_count, *refs):
    packs, tables, att2s, ints = refs[0:2], refs[2:4], refs[4:6], refs[6:8]
    sum_ref, ya_ref, refs = refs[8], refs[9], refs[10:]
    if step > 0:
        state_ref, old_z_ref, old_g_ref, old_u_ref, old_s_ref, old_gs_ref = refs[:6]
        refs = refs[6:]
    else:
        keep, refs = refs[:2], refs[2:]
    gathered, refs = refs[:-8], refs[-8:]
    send_ref, state_out, z_ref, g_ref, u_ref, s_ref, gs_ref, spread_ref = refs
    me = lax.axis_index("tm")
    chip, core = me // 2, me % 2
    high = STARS_DEV // LANES
    comps = sum_ref.shape[0] // high
    blocks = 8
    total = tree_sum([ref[...] for ref in gathered])
    back = jnp.concatenate([sum_ref[...], total], axis=0)
    base = comps * high
    pieces = [total[place : place + 1] for place in range(8)]
    att_back_rows = total[8:13]
    forward, starts, coefs, indices = [], [], [], []
    for half in range(2):
        starts.append(ints[half][slots * 8 :])
        own = jnp.where(core == half, att_back_rows[0:3], att_back_rows[2:5])
        part = att_forward(own, att2s[half][...], starts[half], width)
        part = part + ya_ref[half * 8 : half * 8 + 8]
        coefs.append([packs[half].at[slot * 8 : slot * 8 + 8] for slot in range(slots)])
        indices.append([ints[half].at[slot * 8 : slot * 8 + 8] for slot in range(slots)])
        for slot in range(slots):
            part = part + coefs[half][slot][...] * table_pick(pieces, indices[half][slot][...])
        forward.append(part)
    forward = jnp.concatenate(forward, axis=0)
    if step == 0:
        squares = lane_sum(total[13:14])
        beta2 = squares + epsilon
        beta = jnp.sqrt(beta2)
        at = pl.ds(pl.multiple_of(chip * 8, 8), 8)
        u = jnp.concatenate([ref[at] for ref in keep], axis=0) / beta
        g = back / beta
        z = g
        gs = forward / beta
        both = gs
        state_out[...] = jnp.concatenate(
            [squares / beta2, beta, jnp.zeros((14, LANES), f32)], axis=0
        )
    else:
        state = state_ref[...]
        alpha, beta, left2 = next_bidiagonal(total, state)
        u = (old_s_ref[...] / alpha - alpha * old_u_ref[...]) / beta
        g = (back / alpha - alpha * old_g_ref[...]) / beta
        z = g - (beta / alpha) * old_z_ref[...]
        gs = (forward / alpha - alpha * old_gs_ref[...]) / beta
        both = gs - (beta / alpha) * old_s_ref[...]
        pieces = [left2, state[1 : 1 + step], beta, jnp.zeros((7 - step, LANES), f32)]
        pieces += [state[9 : 8 + step]] if step > 1 else []
        pieces += [alpha, jnp.zeros((7 - step, LANES), f32)]
        state_out[...] = jnp.concatenate(pieces, axis=0)
    z_ref[...] = z
    g_ref[...] = g
    u_ref[...] = u
    gs_ref[...] = gs
    s_ref[...] = both
    inst_rows = z[base : base + 8]
    att_rows = z[base + 8 : base + 13]
    rows = [both[0:8], both[8:16]]
    insts, atts = [], []
    for half in range(2):
        if step < ITERS - 1:
            insts.append(
                inst_back(rows[half], coefs[half], indices[half], tables[half], spread_ref.at[half])
            )
            atts.append(att_back(rows[half], att2s[half][...], starts[half], width))

    def squared(value):
        return jnp.sum(value * value, axis=0, keepdims=True)

    size = squared(z[:base]) * (1.0 / chips) + squared(att_rows[:4]) * (1.0 / star_count)
    size = size + squared(inst_rows) * (1.0 / (star_count * chips))
    mixed = [jnp.sum(rows[half] * u[half * 8 : half * 8 + 8], axis=0, keepdims=True) for half in range(2)]
    scalars = [squared(rows[0]) + squared(rows[1]), mixed[0] + mixed[1], size]
    if step == ITERS - 1:
        send_ref[...] = jnp.concatenate([jnp.zeros((5, LANES), f32)] + scalars, axis=0)
        return
    send_ref[0:16] = jnp.where(core == 0, both, jnp.concatenate(rows[::-1], axis=0))
    send_ref[16:24] = insts[0] + insts[1]
    send_ref[24:32] = jnp.concatenate([chip_parts(core, *atts)] + scalars, axis=0)


def last_kernel(comps, share, star_count, state_ref, *refs):
    gathered, refs = refs[: -ITERS - 3], refs[-ITERS - 3 :]
    z_refs = refs[:ITERS]
    astro_ref, att_ref, inst_ref = refs[ITERS:]
    high = STARS_DEV // LANES
    me = lax.axis_index("tm")
    total = tree_sum([ref[...] for ref in gathered])
    total = jnp.concatenate([jnp.zeros((8, LANES), f32), total], axis=0)
    state = state_ref[...]
    alpha, beta, _ = next_bidiagonal(total, state)
    betas = [state[1 + k : 2 + k] for k in range(ITERS)] + [beta]
    alphas = [state[9 + k : 10 + k] for k in range(ITERS - 1)] + [alpha]
    rho_bar, phi_bar = alphas[0], betas[0]
    weights = [jnp.zeros((1, LANES), f32)] * ITERS
    search = [jnp.zeros((1, LANES), f32)] * ITERS
    search[0] = 1.0 / alphas[0]
    for k in range(ITERS):
        rho = jnp.sqrt(rho_bar * rho_bar + betas[k + 1] * betas[k + 1])
        cosine, sine = rho_bar / rho, betas[k + 1] / rho
        phi = cosine * phi_bar
        phi_bar = sine * phi_bar
        weights = [x + phi / rho * w for x, w in zip(weights, search)]
        if k + 1 < ITERS:
            theta = sine * alphas[k + 1]
            rho_bar = -cosine * alphas[k + 1]
            search = [-(theta / rho) * w for w in search]
            search[k + 1] = 1.0 / alphas[k + 1]
    base = comps * high
    tiles = share // LANES

    def mix(read):
        total = weights[0] * read(z_refs[0])
        for k in range(1, ITERS):
            total = total + weights[k] * read(z_refs[k])
        return total

    for comp in range(comps):
        for tile in range(tiles):
            at = comp * high + me * tiles + tile
            astro_ref[comp : comp + 1, tile * LANES : (tile + 1) * LANES] = mix(
                lambda ref: ref[pl.ds(at, 1)]
            )
    inst_ref[...] = mix(lambda ref: ref[base : base + 8])
    rows = ATT_DEV // LANES
    att_ref[...] = mix(lambda ref: ref[pl.ds(base + 8 + (me % 2) * rows, rows)])


def call(kernel, name, out, args, scratch=(), space=pltpu.VMEM):
    vmem = pl.BlockSpec(memory_space=pltpu.VMEM)
    return pl.pallas_call(
        kernel,
        name=name,
        out_shape=[jax.ShapeDtypeStruct(shape, dtype) for shape, dtype in out],
        in_specs=[pl.BlockSpec(memory_space=space)] * len(args),
        out_specs=[vmem] * len(out),
        scratch_shapes=list(scratch),
        compiler_params=pltpu.CompilerParams(vmem_limit_bytes=VMEM_LIMIT),
    )(*args)


def direct(value, axis, gaps):
    count = lax.axis_size(axis)
    return [value] + [
        lax.ppermute(value, axis, [(i, i ^ gap) for i in range(count)]) for gap in gaps
    ]


def exchange(value, axis):
    tm_count, star_count = lax.axis_size("tm"), lax.axis_size("star")
    got = [value]
    for gap in range(1, star_count if axis == "star" else tm_count // 2):
        steps = []
        for star in range(star_count):
            for tm in range(tm_count):
                far = (star ^ gap, tm ^ 1) if axis == "star" else (star, tm ^ (2 * gap + 1))
                steps.append((star * tm_count + tm, far[0] * tm_count + far[1]))
        got.append(lax.ppermute(value, ("star", "tm"), steps))
    return got


def rows_type(rows):
    return ((rows, LANES), f32)


def per_device(astro_coef, star_index, att_coef, att_start, inst_coef, inst_index, observed):
    tm_count, star_count = lax.axis_size("tm"), lax.axis_size("star")
    comps = astro_coef.shape[1]
    slots = inst_coef.shape[1]
    blocks, width, height = att_coef.shape[1:]
    share = STARS_DEV // tm_count
    high = STARS_DEV // LANES
    chips = tm_count // 2
    far = [2 * gap for gap in range(1, chips)]
    args = [
        observed.reshape(blocks, height),
        astro_coef.reshape(comps, blocks, height),
        star_index.reshape(blocks, height),
        att_coef.reshape(blocks * width, height),
        att_start,
        inst_coef.reshape(slots, blocks, height),
        inst_index.reshape(slots, blocks, height),
    ]
    long = slots * blocks * height
    extra = 8 * comps + 8
    spread = pltpu.VMEM((16, long), bf16)
    prepared = [((LANES, long), bf16), ((2 * blocks * width, height), bf16),
                ((8 * slots + 8, LANES), jnp.int32)]
    here = [pltpu.with_memory_space_constraint(arg, pltpu.HBM) for arg in args]
    send, pack, *mine = call(
        functools.partial(first_kernel, width),
        "first",
        [((24 + extra, LANES), f32), ((16 * slots + 8 + blocks * width, LANES), f32)] + prepared,
        here,
        [pltpu.VMEM(arg.shape, arg.dtype) for arg in args if arg is not args[3]]
        + [spread, pltpu.SemaphoreType.DMA((len(args),))],
        pl.ANY,
    )
    state = z = g = u = rows = gs = None
    solutions = []
    group_type = rows_type(16)
    for step in range(ITERS):
        wide = (2 * comps * high, blocks * height)
        sums_type = rows_type(comps * high)
        pair = rows_type(2 * blocks)
        got = exchange(send, "tm") if step else direct(send, "tm", far)
        if step == 0:
            (gathered,) = call(
                functools.partial(first_chip_kernel, chips),
                "chip",
                [((16 * chips + 16 + chips * extra, LANES), f32)],
                got,
            )
            keep = direct(gathered, "tm", [1])
            table_type = ((LANES, chips * blocks * height), bf16)
            own_sums, own_table = call(
                functools.partial(astro_own_kernel, chips),
                "astro_own",
                [sums_type, table_type],
                [gathered],
                [pltpu.VMEM(wide, bf16)],
            )
            keep[1], own_sums = lax.optimization_barrier((keep[1], own_sums))
            (group,) = call(
                functools.partial(first_group_kernel, chips), "group", [group_type], keep
            )
            group, late_pack = lax.optimization_barrier((group, pack))
            _, other_pack = direct(late_pack, "tm", [1])
            theirs = call(
                functools.partial(prepare_kernel, slots, blocks, width),
                "prepare",
                prepared,
                [other_pack],
            )
            basics = [pack, other_pack] + [value for both in zip(mine, theirs) for value in both]
        else:
            all_rows, group = call(
                functools.partial(group_kernel, chips),
                "group",
                [rows_type(16 * chips), group_type],
                got,
            )
        across = exchange(group, "star")
        if step == 0:
            sums, ya, other_table = call(
                functools.partial(astro_other_kernel, chips),
                "astro",
                [sums_type, pair, table_type],
                keep + [own_sums],
                [pltpu.VMEM(wide, bf16)],
            )
        else:
            sums, ya = call(
                functools.partial(astro_kernel, chips),
                "astro",
                [sums_type, pair],
                keep + [own_table, other_table, all_rows],
                [pltpu.VMEM((2,) + wide, bf16)],
            )
        tall = ((comps * high + 16, LANES), f32)
        older = keep if step == 0 else [state, z, g, u, rows, gs]
        send, state, z, g, u, rows, gs = call(
            functools.partial(step_kernel, step, width, slots, chips, star_count),
            "step",
            [rows_type(32 if step < ITERS - 1 else 8), group_type, tall, tall, pair, pair,
             pair],
            basics + [sums, ya] + older + across,
            [pltpu.VMEM((2, 16, long), bf16)],
        )
        solutions.append(z)
    (send,) = call(sum_kernel, "sum", [rows_type(8)], exchange(send, "tm"))
    across = exchange(send, "star")
    out_astro, out_att, out_inst = call(
        functools.partial(last_kernel, comps, share, star_count),
        "last",
        [((comps, share), f32), ((ATT_DEV // LANES, LANES), f32), ((NINST // LANES, LANES), f32)],
        [state] + across + solutions,
    )
    return out_astro, out_att.reshape(-1), out_inst.reshape(-1)


def solution(mesh):
    return jax.shard_map(
        per_device,
        mesh=mesh,
        in_specs=(
            P("star", None, "tm"),
            P("star", "tm"),
            P("star", "tm", None, None),
            P("star", "tm"),
            P("star", None, "tm"),
            P("star", None, "tm"),
            P("star", "tm"),
        ),
        out_specs=(P(None, ("star", "tm")), P("tm"), P()),
        check_vma=False,
    )
```

```python
import functools

import jax
import jax.numpy as jnp
from jax import lax
from jax.experimental import pallas as pl
from jax.experimental.pallas import tpu as pltpu
from jax.sharding import PartitionSpec as P

STARS_DEV = 2048
NINST = 1024
ITERS = 3
ATT_DEV = 256
LANES = 128

epsilon = 1e-06
f32 = jnp.float32
bf16 = jnp.bfloat16
VMEM_LIMIT = 16 * 1024 * 1024


def halves(value):
    top = value.astype(bf16).astype(f32)
    return top, (value - top).astype(bf16).astype(f32)


def dot_lanes(left, right):
    return lax.dot_general(left, right, (((1,), (1,)), ((), ())), preferred_element_type=f32)


def dot_plain(left, right):
    return lax.dot_general(left, right, (((1,), (0,)), ((), ())), preferred_element_type=f32)


def lane_pick(row, lane_index):
    table = jnp.broadcast_to(row, lane_index.shape)
    return jnp.take_along_axis(table, lane_index, axis=1, mode="promise_in_bounds")


def table_pick(rows, index):
    high, low = index >> 7, index & (LANES - 1)
    total = jnp.zeros(index.shape, f32)
    for place, row in enumerate(rows):
        total = jnp.where(high == place, lane_pick(row, low), total)
    return total


def one_hot_low(index_row):
    shape = (LANES, LANES)
    low = jnp.broadcast_to(index_row & (LANES - 1), shape)
    hit = lax.broadcasted_iota(jnp.int32, shape, 0) == low
    return jnp.where(hit, 1.0, 0.0).astype(bf16)


def spread_high(index_row, value_row, count):
    shape = (count, LANES)
    high = jnp.broadcast_to(index_row >> 7, shape)
    hit = lax.broadcasted_iota(jnp.int32, shape, 0) == high
    return jnp.where(hit, jnp.broadcast_to(value_row, shape), 0.0)


def block_masks(blocks, width):
    shape = (blocks, LANES)
    row = lax.broadcasted_iota(jnp.int32, shape, 0)
    lane = lax.broadcasted_iota(jnp.int32, shape, 1)
    per_tile = LANES // width
    tiles = blocks // per_tile
    return [row == tile * per_tile + lane // width for tile in range(tiles)], row, lane


def inst_back(rows, coef_ref, index_ref, table_ref, spread_ref):
    slots, blocks = len(coef_ref), rows.shape[0]
    count = NINST // LANES
    for slot in range(slots):
        top, rest = halves(coef_ref[slot][...] * rows)
        index = index_ref[slot][...]
        for block in range(blocks):
            here = slice(block, block + 1)
            pieces = [spread_high(index[here], part[here], count) for part in (top, rest)]
            at = (slot * blocks + block) * LANES
            spread_ref[:, at : at + LANES] = jnp.concatenate(pieces, axis=0).astype(bf16)
    both = dot_lanes(spread_ref[...], table_ref[...])
    return both[:count] + both[count:]


def att_back(rows, att2, starts, width):
    blocks = rows.shape[0]
    size = att2.shape[0] // 2
    top, rest = halves(rows)
    both = dot_lanes(jnp.concatenate([top, rest], axis=0).astype(bf16), att2)
    both = both[:blocks] + both[blocks:]
    both = both[:, :size] + both[:, size:]
    masks, row, lane = block_masks(blocks, width)
    own = jnp.zeros((blocks, LANES), f32)
    for tile, mask in enumerate(masks):
        own = own + jnp.where(mask, both[:, tile * LANES : (tile + 1) * LANES], 0.0)
    shift = (row % (LANES // width)) * width
    out = []
    for tile in range((ATT_DEV + width + LANES - 1) // LANES):
        offset = lane + tile * LANES - starts
        inside = (offset >= 0) & (offset < width)
        picked = jnp.take_along_axis(
            own, jnp.where(inside, offset + shift, 0), axis=1, mode="promise_in_bounds"
        )
        out.append(jnp.sum(jnp.where(inside, picked, 0.0), axis=0, keepdims=True))
    return jnp.concatenate(out, axis=0)


def att_forward(att_rows, att2, starts, width):
    blocks = starts.shape[0]
    masks, row, lane = block_masks(blocks, width)
    tiles = [att_rows[tile : tile + 1] for tile in range(att_rows.shape[0])]
    window = table_pick(tiles, starts + lane % width)
    wide = jnp.concatenate([jnp.where(mask, window, 0.0) for mask in masks], axis=1)
    top, rest = halves(wide)
    left = jnp.concatenate([top, rest], axis=0).astype(bf16)
    both = dot_plain(jnp.concatenate([left, left], axis=1), att2)
    return both[:blocks] + both[blocks:]


def pack_places(slots, blocks, width):
    at = slots * 8
    return slice(0, at), slice(at, 2 * at), slice(2 * at, 2 * at + 8), slice(
        2 * at + 8, 2 * at + 8 + blocks * width
    )


def prepare_index(index_rows, starts, table_ref, ints_ref):
    count = index_rows.shape[0] // 8
    ints_ref[0 : count * 8] = index_rows
    ints_ref[count * 8 :] = starts
    for place in range(count * 8):
        table_ref[:, place * LANES : (place + 1) * LANES] = one_hot_low(
            index_rows[place : place + 1]
        )


def prepare_att(att, att2_ref):
    top = att.astype(bf16)
    att2_ref[...] = jnp.concatenate([top, (att - top.astype(f32)).astype(bf16)], axis=0)


def first_kernel(width, b_hbm, astro_hbm, star_hbm, att_hbm, starts_hbm, coef_hbm, index_hbm,
                 send_ref, pack_ref, table_ref, att2_ref, ints_ref,
                 b_ref, astro_ref, star_ref, starts_ref, coef_ref, index_ref,
                 spread_ref, sems):
    slots, blocks, _ = index_ref.shape
    comps = astro_ref.shape[0]
    places = pack_places(slots, blocks, width)
    pairs = [(index_hbm, index_ref), (starts_hbm, starts_ref), (att_hbm, pack_ref.at[places[3]]),
             (coef_hbm, coef_ref), (b_hbm, b_ref), (astro_hbm, astro_ref), (star_hbm, star_ref)]
    copies = [
        pltpu.make_async_copy(source, target, sems.at[place])
        for place, (source, target) in enumerate(pairs)
    ]
    for copy in copies:
        copy.start()
    for copy in copies[:2]:
        copy.wait()
    index = jnp.concatenate([index_ref[slot] for slot in range(slots)], axis=0)
    starts_row = jnp.broadcast_to(starts_ref[...].astype(f32), (blocks, blocks))
    diagonal = lax.broadcasted_iota(jnp.int32, (blocks, blocks), 0) == lax.broadcasted_iota(
        jnp.int32, (blocks, blocks), 1
    )
    starts = jnp.sum(jnp.where(diagonal, starts_row, 0.0), axis=1, keepdims=True)
    starts = jnp.broadcast_to(starts, (blocks, LANES))
    pack_ref[places[1]] = index.astype(f32)
    pack_ref[places[2]] = starts
    starts = starts.astype(jnp.int32)
    prepare_index(index, starts, table_ref, ints_ref)
    for copy in copies[2:]:
        copy.wait()
    prepare_att(pack_ref[places[3]], att2_ref)
    rows = b_ref[...]
    coefs = [coef_ref.at[slot] for slot in range(slots)]
    indices = [index_ref.at[slot] for slot in range(slots)]
    for slot in range(slots):
        pack_ref[slot * 8 : slot * 8 + 8] = coef_ref[slot]
    send_ref[0:8] = rows
    send_ref[8:16] = inst_back(rows, coefs, indices, table_ref, spread_ref)
    send_ref[16:19] = att_back(rows, att2_ref[...], starts, width)
    send_ref[19:20] = jnp.sum(rows * rows, axis=0, keepdims=True)
    send_ref[20:24] = jnp.zeros((4, LANES), f32)
    for comp in range(comps):
        send_ref[24 + comp * 8 : 32 + comp * 8] = astro_ref[comp]
    send_ref[24 + comps * 8 : 32 + comps * 8] = star_ref[...].astype(f32)


def prepare_kernel(slots, blocks, width, pack_ref, table_ref, att2_ref, ints_ref):
    places = pack_places(slots, blocks, width)
    index = pack_ref[places[1]].astype(jnp.int32)
    starts = pack_ref[places[2]].astype(jnp.int32)
    prepare_index(index, starts, table_ref, ints_ref)
    prepare_att(pack_ref[places[3]], att2_ref)


def tree_sum(values):
    while len(values) > 1:
        values = [values[i] + values[i + 1] for i in range(0, len(values), 2)]
    return values[0]


def first_chip_kernel(count, *refs):
    ins, out_ref = refs[:count], refs[count]
    chip = lax.axis_index("tm") // 2
    size = ins[0].shape[0]
    for gap in range(count):
        at = pl.multiple_of((chip ^ gap) * size, 8)
        out_ref[pl.ds(at, size)] = ins[gap][...]


def group_rows(chip, count, mine, prev_row, after_row):
    half = lax.broadcasted_iota(jnp.int32, (1, LANES), 1) < 64
    first = mine[0:1] + jnp.where(half & (chip > 0), prev_row, 0.0)
    last = jnp.where(half & (chip < count - 1), mine[4:5] + after_row, 0.0)
    return [first, mine[1:4], last]


def chip_parts(core, own, other):
    low = jnp.where(core == 0, own, other)
    top = jnp.where(core == 0, other, own)
    return jnp.concatenate([low[0:2], low[2:3] + top[0:1], top[1:3]], axis=0)


def first_group_kernel(count, own_ref, other_ref, out_ref):
    me = lax.axis_index("tm")
    chip, core = me // 2, me % 2
    size = own_ref.shape[0] // count

    def part(ref, where, start):
        where = jnp.clip(where, 0, count - 1)
        return ref[pl.ds(pl.multiple_of(where * size + start, 8), 8)]

    def of_core(which, where):
        mine = (core == which) == (where == chip)
        return jnp.where(mine, part(own_ref, where, 16), part(other_ref, where, 16))

    def total(start):
        return tree_sum(
            [part(own_ref, chip ^ gap, start) + part(other_ref, chip ^ gap, start) for gap in range(count)]
        )

    mine = chip_parts(core, part(own_ref, chip, 16)[0:3], part(other_ref, chip, 16)[0:3])
    prev, after = of_core(1, chip - 1), of_core(0, chip + 1)
    out_ref[0:8] = total(8)
    att = group_rows(chip, count, mine, prev[2:3], after[0:1])
    out_ref[8:16] = jnp.concatenate(att + [total(16)[3:6]], axis=0)


def group_kernel(count, *refs):
    *ins, rows_ref, out_ref = refs
    me = lax.axis_index("tm")
    chip = me // 2
    places = [chip ^ gap for gap in range(count)]
    zero = jnp.zeros((8, LANES), f32)
    mine, prev, after = zero, zero, zero
    for ref, where in zip(ins, places):
        for half in range(2):
            at = pl.multiple_of((half * count + where) * 8, 8)
            rows_ref[pl.ds(at, 8)] = ref[half * 8 : half * 8 + 8]
        low = ref[24:32]
        mine = jnp.where(where == chip, low, mine)
        prev = jnp.where(where == chip - 1, low, prev)
        after = jnp.where(where == chip + 1, low, after)
    scalars = tree_sum([ref[24:32] for ref in ins])
    out_ref[0:8] = tree_sum([ref[16:24] for ref in ins])
    att = group_rows(chip, count, mine, prev[4:5], after[0:1])
    out_ref[8:16] = jnp.concatenate(att + [scalars[5:8]], axis=0)


def kept(count, keep_ref):
    size = keep_ref.shape[0] // count
    return size, size - 24, (size - 24) // 8 - 1


def star_sums(count, place, keep_ref, rows, table_ref, spread_ref, build):
    high = STARS_DEV // LANES
    size, extra, comps = kept(count, keep_ref)
    long = 8 * LANES
    packed = keep_ref[pl.ds(pl.multiple_of(place * size + 24, 8), extra)]
    index = packed[comps * 8 :].astype(jnp.int32)
    at0 = pl.multiple_of(place * long, long)
    split = [halves(packed[comp * 8 : comp * 8 + 8] * rows) for comp in range(comps)]
    for block in range(8):
        here = slice(block, block + 1)
        if build:
            table_ref[:, pl.ds(at0 + block * LANES, LANES)] = one_hot_low(index[here])
        pieces = []
        for part in range(2):
            for comp in range(comps):
                pieces.append(spread_high(index[here], split[comp][part][here], high))
        spread_ref[:, block * LANES : (block + 1) * LANES] = jnp.concatenate(
            pieces, axis=0
        ).astype(bf16)
    return dot_lanes(spread_ref[...], table_ref[:, pl.ds(at0, long)])


def star_rows(count, keep_ref, sums):
    high = STARS_DEV // LANES
    size, extra, comps = kept(count, keep_ref)
    chip = lax.axis_index("tm") // 2
    packed = keep_ref[pl.ds(pl.multiple_of(chip * size + 24, 8), extra)]
    star = packed[comps * 8 :].astype(jnp.int32)
    star_high, star_low = star >> 7, star & (LANES - 1)
    total = jnp.zeros((8, LANES), f32)
    for comp in range(comps):
        picked = jnp.zeros((8, LANES), f32)
        for place in range(high):
            at = comp * high + place
            picked = jnp.where(star_high == place, lane_pick(sums[at : at + 1], star_low), picked)
        total = total + packed[comp * 8 : comp * 8 + 8] * picked
    return total


def first_sums(count, keep_ref, table_ref, spread_ref):
    size = spread_ref.shape[0]

    def one(place, total):
        rows = keep_ref[pl.ds(pl.multiple_of(place * kept(count, keep_ref)[0], 8), 8)]
        return total + star_sums(count, place, keep_ref, rows, table_ref, spread_ref, True)

    total = lax.fori_loop(0, count, one, jnp.zeros((size, LANES), f32))
    return total[: size // 2] + total[size // 2 :]


def astro_own_kernel(count, keep_ref, out_ref, table_ref, spread_ref):
    out_ref[...] = first_sums(count, keep_ref, table_ref, spread_ref)


def astro_other_kernel(count, own_ref, keep_ref, part_ref, out_ref, ya_ref, table_ref, spread_ref):
    total = part_ref[...] + first_sums(count, keep_ref, table_ref, spread_ref)
    out_ref[...] = total
    ya_ref[0:8] = star_rows(count, own_ref, total)
    ya_ref[8:16] = star_rows(count, keep_ref, total)


def astro_kernel(count, own_ref, other_ref, own_table, other_table, rows_ref, out_ref, ya_ref,
                 spread_ref):
    me = lax.axis_index("tm")
    size = spread_ref.shape[1]
    sources = ((own_ref, own_table), (other_ref, other_table))

    def one(place, totals):
        new = []
        for half, (keep_ref, table_ref) in enumerate(sources):
            core = half ^ (me % 2) ^ jnp.where(place == me // 2, 0, 1)
            at = (core * count + place) * 8
            rows = rows_ref[pl.ds(pl.multiple_of(at, 8), 8)]
            part = star_sums(count, place, keep_ref, rows, table_ref, spread_ref.at[half], False)
            new.append(totals[half] + part)
        return tuple(new)

    zero = jnp.zeros((size, LANES), f32)
    own, other = lax.fori_loop(0, count, one, (zero, zero))
    total = own + other
    total = total[: size // 2] + total[size // 2 :]
    out_ref[...] = total
    ya_ref[0:8] = star_rows(count, own_ref, total)
    ya_ref[8:16] = star_rows(count, other_ref, total)


def sum_kernel(*refs):
    refs[-1][...] = tree_sum([ref[...] for ref in refs[:-1]])


def lane_sum(row):
    return jnp.broadcast_to(jnp.sum(row, axis=1, keepdims=True), row.shape)


def next_bidiagonal(total, state):
    squares, mixed, size = (lane_sum(total[row : row + 1]) for row in (13, 14, 15))
    alpha2 = size + epsilon
    alpha = jnp.sqrt(alpha2)
    rest = jnp.maximum(squares / alpha2 - 2.0 * mixed + alpha2 * state[0:1], 0.0)
    beta2 = rest + epsilon
    return alpha, jnp.sqrt(beta2), rest / beta2


def step_kernel(step, width, slots, chips, star_count, *refs):
    packs, tables, att2s, ints = refs[0:2], refs[2:4], refs[4:6], refs[6:8]
    sum_ref, ya_ref, refs = refs[8], refs[9], refs[10:]
    if step > 0:
        state_ref, old_z_ref, old_g_ref, old_u_ref, old_s_ref, old_gs_ref = refs[:6]
        refs = refs[6:]
    else:
        keep, refs = refs[:2], refs[2:]
    gathered, refs = refs[:-8], refs[-8:]
    send_ref, state_out, z_ref, g_ref, u_ref, s_ref, gs_ref, spread_ref = refs
    me = lax.axis_index("tm")
    chip, core = me // 2, me % 2
    high = STARS_DEV // LANES
    comps = sum_ref.shape[0] // high
    blocks = 8
    total = tree_sum([ref[...] for ref in gathered])
    back = jnp.concatenate([sum_ref[...], total], axis=0)
    base = comps * high
    pieces = [total[place : place + 1] for place in range(8)]
    att_back_rows = total[8:13]
    forward, starts, coefs, indices = [], [], [], []
    for half in range(2):
        starts.append(ints[half][slots * 8 :])
        own = jnp.where(core == half, att_back_rows[0:3], att_back_rows[2:5])
        part = att_forward(own, att2s[half][...], starts[half], width)
        part = part + ya_ref[half * 8 : half * 8 + 8]
        coefs.append([packs[half].at[slot * 8 : slot * 8 + 8] for slot in range(slots)])
        indices.append([ints[half].at[slot * 8 : slot * 8 + 8] for slot in range(slots)])
        for slot in range(slots):
            part = part + coefs[half][slot][...] * table_pick(pieces, indices[half][slot][...])
        forward.append(part)
    forward = jnp.concatenate(forward, axis=0)
    if step == 0:
        squares = lane_sum(total[13:14])
        beta2 = squares + epsilon
        beta = jnp.sqrt(beta2)
        at = pl.ds(pl.multiple_of(chip * kept(chips, keep[0])[0], 8), 8)
        u = jnp.concatenate([ref[at] for ref in keep], axis=0) / beta
        g = back / beta
        z = g
        gs = forward / beta
        both = gs
        state_out[...] = jnp.concatenate(
            [squares / beta2, beta, jnp.zeros((14, LANES), f32)], axis=0
        )
    else:
        state = state_ref[...]
        alpha, beta, left2 = next_bidiagonal(total, state)
        u = (old_s_ref[...] / alpha - alpha * old_u_ref[...]) / beta
        g = (back / alpha - alpha * old_g_ref[...]) / beta
        z = g - (beta / alpha) * old_z_ref[...]
        gs = (forward / alpha - alpha * old_gs_ref[...]) / beta
        both = gs - (beta / alpha) * old_s_ref[...]
        pieces = [left2, state[1 : 1 + step], beta, jnp.zeros((7 - step, LANES), f32)]
        pieces += [state[9 : 8 + step]] if step > 1 else []
        pieces += [alpha, jnp.zeros((7 - step, LANES), f32)]
        state_out[...] = jnp.concatenate(pieces, axis=0)
    z_ref[...] = z
    g_ref[...] = g
    u_ref[...] = u
    gs_ref[...] = gs
    s_ref[...] = both
    inst_rows = z[base : base + 8]
    att_rows = z[base + 8 : base + 13]
    rows = [both[0:8], both[8:16]]
    insts, atts = [], []
    for half in range(2):
        if step < ITERS - 1:
            insts.append(
                inst_back(rows[half], coefs[half], indices[half], tables[half], spread_ref.at[half])
            )
            atts.append(att_back(rows[half], att2s[half][...], starts[half], width))

    def squared(value):
        return jnp.sum(value * value, axis=0, keepdims=True)

    size = squared(z[:base]) * (1.0 / chips) + squared(att_rows[:4]) * (1.0 / star_count)
    size = size + squared(inst_rows) * (1.0 / (star_count * chips))
    mixed = [jnp.sum(rows[half] * u[half * 8 : half * 8 + 8], axis=0, keepdims=True) for half in range(2)]
    scalars = [squared(rows[0]) + squared(rows[1]), mixed[0] + mixed[1], size]
    if step == ITERS - 1:
        send_ref[...] = jnp.concatenate([jnp.zeros((5, LANES), f32)] + scalars, axis=0)
        return
    send_ref[0:16] = jnp.where(core == 0, both, jnp.concatenate(rows[::-1], axis=0))
    send_ref[16:24] = insts[0] + insts[1]
    send_ref[24:32] = jnp.concatenate([chip_parts(core, *atts)] + scalars, axis=0)


def last_kernel(comps, share, star_count, state_ref, *refs):
    gathered, refs = refs[: -ITERS - 3], refs[-ITERS - 3 :]
    z_refs = refs[:ITERS]
    astro_ref, att_ref, inst_ref = refs[ITERS:]
    high = STARS_DEV // LANES
    me = lax.axis_index("tm")
    total = tree_sum([ref[...] for ref in gathered])
    total = jnp.concatenate([jnp.zeros((8, LANES), f32), total], axis=0)
    state = state_ref[...]
    alpha, beta, _ = next_bidiagonal(total, state)
    betas = [state[1 + k : 2 + k] for k in range(ITERS)] + [beta]
    alphas = [state[9 + k : 10 + k] for k in range(ITERS - 1)] + [alpha]
    rho_bar, phi_bar = alphas[0], betas[0]
    weights = [jnp.zeros((1, LANES), f32)] * ITERS
    search = [jnp.zeros((1, LANES), f32)] * ITERS
    search[0] = 1.0 / alphas[0]
    for k in range(ITERS):
        rho = jnp.sqrt(rho_bar * rho_bar + betas[k + 1] * betas[k + 1])
        cosine, sine = rho_bar / rho, betas[k + 1] / rho
        phi = cosine * phi_bar
        phi_bar = sine * phi_bar
        weights = [x + phi / rho * w for x, w in zip(weights, search)]
        if k + 1 < ITERS:
            theta = sine * alphas[k + 1]
            rho_bar = -cosine * alphas[k + 1]
            search = [-(theta / rho) * w for w in search]
            search[k + 1] = 1.0 / alphas[k + 1]
    base = comps * high
    tiles = share // LANES

    def mix(read):
        total = weights[0] * read(z_refs[0])
        for k in range(1, ITERS):
            total = total + weights[k] * read(z_refs[k])
        return total

    for comp in range(comps):
        for tile in range(tiles):
            at = comp * high + me * tiles + tile
            astro_ref[comp : comp + 1, tile * LANES : (tile + 1) * LANES] = mix(
                lambda ref: ref[pl.ds(at, 1)]
            )
    inst_ref[...] = mix(lambda ref: ref[base : base + 8])
    rows = ATT_DEV // LANES
    att_ref[...] = mix(lambda ref: ref[pl.ds(base + 8 + (me % 2) * rows, rows)])


def call(kernel, name, out, args, scratch=(), space=pltpu.VMEM):
    vmem = pl.BlockSpec(memory_space=pltpu.VMEM)
    return pl.pallas_call(
        kernel,
        name=name,
        out_shape=[jax.ShapeDtypeStruct(shape, dtype) for shape, dtype in out],
        in_specs=[pl.BlockSpec(memory_space=space)] * len(args),
        out_specs=[vmem] * len(out),
        scratch_shapes=list(scratch),
        compiler_params=pltpu.CompilerParams(vmem_limit_bytes=VMEM_LIMIT),
    )(*args)


def direct(value, axis, gaps):
    count = lax.axis_size(axis)
    return [value] + [
        lax.ppermute(value, axis, [(i, i ^ gap) for i in range(count)]) for gap in gaps
    ]


def exchange(value, axis):
    tm_count, star_count = lax.axis_size("tm"), lax.axis_size("star")
    got = [value]
    for gap in range(1, star_count if axis == "star" else tm_count // 2):
        steps = []
        for star in range(star_count):
            for tm in range(tm_count):
                far = (star ^ gap, tm ^ 1) if axis == "star" else (star, tm ^ (2 * gap + 1))
                steps.append((star * tm_count + tm, far[0] * tm_count + far[1]))
        got.append(lax.ppermute(value, ("star", "tm"), steps))
    return got


def rows_type(rows):
    return ((rows, LANES), f32)


def per_device(astro_coef, star_index, att_coef, att_start, inst_coef, inst_index, observed):
    tm_count, star_count = lax.axis_size("tm"), lax.axis_size("star")
    comps = astro_coef.shape[1]
    slots = inst_coef.shape[1]
    blocks, width, height = att_coef.shape[1:]
    share = STARS_DEV // tm_count
    high = STARS_DEV // LANES
    chips = tm_count // 2
    args = [
        observed.reshape(blocks, height),
        astro_coef.reshape(comps, blocks, height),
        star_index.reshape(blocks, height),
        att_coef.reshape(blocks * width, height),
        att_start,
        inst_coef.reshape(slots, blocks, height),
        inst_index.reshape(slots, blocks, height),
    ]
    long = slots * blocks * height
    extra = 8 * comps + 8
    spread = pltpu.VMEM((16, long), bf16)
    prepared = [((LANES, long), bf16), ((2 * blocks * width, height), bf16),
                ((8 * slots + 8, LANES), jnp.int32)]
    here = [pltpu.with_memory_space_constraint(arg, pltpu.HBM) for arg in args]
    send, pack, *mine = call(
        functools.partial(first_kernel, width),
        "first",
        [((24 + extra, LANES), f32), ((16 * slots + 8 + blocks * width, LANES), f32)] + prepared,
        here,
        [pltpu.VMEM(arg.shape, arg.dtype) for arg in args if arg is not args[3]]
        + [spread, pltpu.SemaphoreType.DMA((len(args),))],
        pl.ANY,
    )
    state = z = g = u = rows = gs = None
    solutions = []
    group_type = rows_type(16)
    for step in range(ITERS):
        wide = (2 * comps * high, blocks * height)
        sums_type = rows_type(comps * high)
        pair = rows_type(2 * blocks)
        got = exchange(send, "tm")
        if step == 0:
            (gathered,) = call(
                functools.partial(first_chip_kernel, chips),
                "chip",
                [rows_type(chips * (24 + extra))],
                got,
            )
            keep = direct(gathered, "tm", [1])
            table_type = ((LANES, chips * blocks * height), bf16)
            own_sums, own_table = call(
                functools.partial(astro_own_kernel, chips),
                "astro_own",
                [sums_type, table_type],
                [gathered],
                [pltpu.VMEM(wide, bf16)],
            )
            keep[1], own_sums = lax.optimization_barrier((keep[1], own_sums))
            (group,) = call(
                functools.partial(first_group_kernel, chips), "group", [group_type], keep
            )
            group, late_pack = lax.optimization_barrier((group, pack))
            _, other_pack = direct(late_pack, "tm", [1])
            theirs = call(
                functools.partial(prepare_kernel, slots, blocks, width),
                "prepare",
                prepared,
                [other_pack],
            )
            basics = [pack, other_pack] + [value for both in zip(mine, theirs) for value in both]
        else:
            all_rows, group = call(
                functools.partial(group_kernel, chips),
                "group",
                [rows_type(16 * chips), group_type],
                got,
            )
        across = exchange(group, "star")
        if step == 0:
            sums, ya, other_table = call(
                functools.partial(astro_other_kernel, chips),
                "astro",
                [sums_type, pair, table_type],
                keep + [own_sums],
                [pltpu.VMEM(wide, bf16)],
            )
        else:
            sums, ya = call(
                functools.partial(astro_kernel, chips),
                "astro",
                [sums_type, pair],
                keep + [own_table, other_table, all_rows],
                [pltpu.VMEM((2,) + wide, bf16)],
            )
        tall = ((comps * high + 16, LANES), f32)
        older = keep if step == 0 else [state, z, g, u, rows, gs]
        send, state, z, g, u, rows, gs = call(
            functools.partial(step_kernel, step, width, slots, chips, star_count),
            "step",
            [rows_type(32 if step < ITERS - 1 else 8), group_type, tall, tall, pair, pair,
             pair],
            basics + [sums, ya] + older + across,
            [pltpu.VMEM((2, 16, long), bf16)],
        )
        solutions.append(z)
    (send,) = call(sum_kernel, "sum", [rows_type(8)], exchange(send, "tm"))
    across = exchange(send, "star")
    out_astro, out_att, out_inst = call(
        functools.partial(last_kernel, comps, share, star_count),
        "last",
        [((comps, share), f32), ((ATT_DEV // LANES, LANES), f32), ((NINST // LANES, LANES), f32)],
        [state] + across + solutions,
    )
    return out_astro, out_att.reshape(-1), out_inst.reshape(-1)


def solution(mesh):
    return jax.shard_map(
        per_device,
        mesh=mesh,
        in_specs=(
            P("star", None, "tm"),
            P("star", "tm"),
            P("star", "tm", None, None),
            P("star", "tm"),
            P("star", None, "tm"),
            P("star", None, "tm"),
            P("star", "tm"),
        ),
        out_specs=(P(None, ("star", "tm")), P("tm"), P()),
        check_vma=False,
    )
```

```python
import functools

import jax
import jax.numpy as jnp
from jax import lax
from jax.experimental import pallas as pl
from jax.experimental.pallas import tpu as pltpu
from jax.sharding import PartitionSpec as P

STARS_DEV = 2048
NINST = 1024
ITERS = 3
ATT_DEV = 256
LANES = 128

epsilon = 1e-06
f32 = jnp.float32
bf16 = jnp.bfloat16
VMEM_LIMIT = 16 * 1024 * 1024


def halves(value):
    top = value.astype(bf16).astype(f32)
    return top, (value - top).astype(bf16).astype(f32)


def dot_lanes(left, right):
    return lax.dot_general(left, right, (((1,), (1,)), ((), ())), preferred_element_type=f32)


def dot_plain(left, right):
    return lax.dot_general(left, right, (((1,), (0,)), ((), ())), preferred_element_type=f32)


def lane_pick(row, lane_index):
    table = jnp.broadcast_to(row, lane_index.shape)
    return jnp.take_along_axis(table, lane_index, axis=1, mode="promise_in_bounds")


def table_pick(rows, index):
    high, low = index >> 7, index & (LANES - 1)
    total = jnp.zeros(index.shape, f32)
    for place, row in enumerate(rows):
        total = jnp.where(high == place, lane_pick(row, low), total)
    return total


def one_hot_low(index_row):
    shape = (LANES, LANES)
    low = jnp.broadcast_to(index_row & (LANES - 1), shape)
    hit = lax.broadcasted_iota(jnp.int32, shape, 0) == low
    return jnp.where(hit, 1.0, 0.0).astype(bf16)


def spread_high(index_row, value_row, count):
    shape = (count, LANES)
    high = jnp.broadcast_to(index_row >> 7, shape)
    hit = lax.broadcasted_iota(jnp.int32, shape, 0) == high
    return jnp.where(hit, jnp.broadcast_to(value_row, shape), 0.0)


def block_masks(blocks, width):
    shape = (blocks, LANES)
    row = lax.broadcasted_iota(jnp.int32, shape, 0)
    lane = lax.broadcasted_iota(jnp.int32, shape, 1)
    per_tile = LANES // width
    tiles = blocks // per_tile
    return [row == tile * per_tile + lane // width for tile in range(tiles)], row, lane


def inst_back(rows, coef_ref, index_ref, table_ref, spread_ref):
    slots, blocks = len(coef_ref), rows.shape[0]
    count = NINST // LANES
    for slot in range(slots):
        top, rest = halves(coef_ref[slot][...] * rows)
        index = index_ref[slot][...]
        for block in range(blocks):
            here = slice(block, block + 1)
            pieces = [spread_high(index[here], part[here], count) for part in (top, rest)]
            at = (slot * blocks + block) * LANES
            spread_ref[:, at : at + LANES] = jnp.concatenate(pieces, axis=0).astype(bf16)
    both = dot_lanes(spread_ref[...], table_ref[...])
    return both[:count] + both[count:]


def att_back(rows, att2, starts, width):
    blocks = rows.shape[0]
    size = att2.shape[0] // 2
    top, rest = halves(rows)
    both = dot_lanes(jnp.concatenate([top, rest], axis=0).astype(bf16), att2)
    both = both[:blocks] + both[blocks:]
    both = both[:, :size] + both[:, size:]
    masks, row, lane = block_masks(blocks, width)
    own = jnp.zeros((blocks, LANES), f32)
    for tile, mask in enumerate(masks):
        own = own + jnp.where(mask, both[:, tile * LANES : (tile + 1) * LANES], 0.0)
    shift = (row % (LANES // width)) * width
    out = []
    for tile in range((ATT_DEV + width + LANES - 1) // LANES):
        offset = lane + tile * LANES - starts
        inside = (offset >= 0) & (offset < width)
        picked = jnp.take_along_axis(
            own, jnp.where(inside, offset + shift, 0), axis=1, mode="promise_in_bounds"
        )
        out.append(jnp.sum(jnp.where(inside, picked, 0.0), axis=0, keepdims=True))
    return jnp.concatenate(out, axis=0)


def att_forward(att_rows, att2, starts, width):
    blocks = starts.shape[0]
    masks, row, lane = block_masks(blocks, width)
    tiles = [att_rows[tile : tile + 1] for tile in range(att_rows.shape[0])]
    window = table_pick(tiles, starts + lane % width)
    wide = jnp.concatenate([jnp.where(mask, window, 0.0) for mask in masks], axis=1)
    top, rest = halves(wide)
    left = jnp.concatenate([top, rest], axis=0).astype(bf16)
    both = dot_plain(jnp.concatenate([left, left], axis=1), att2)
    return both[:blocks] + both[blocks:]


def pack_places(slots, blocks, width):
    at = slots * 8
    return slice(0, at), slice(at, 2 * at), slice(2 * at, 2 * at + 8), slice(
        2 * at + 8, 2 * at + 8 + blocks * width
    )


def prepare_index(index_rows, starts, table_ref, ints_ref):
    count = index_rows.shape[0] // 8
    ints_ref[0 : count * 8] = index_rows
    ints_ref[count * 8 :] = starts
    for place in range(count * 8):
        table_ref[:, place * LANES : (place + 1) * LANES] = one_hot_low(
            index_rows[place : place + 1]
        )


def prepare_att(att, att2_ref):
    top = att.astype(bf16)
    att2_ref[...] = jnp.concatenate([top, (att - top.astype(f32)).astype(bf16)], axis=0)


def first_kernel(width, b_hbm, astro_hbm, star_hbm, att_hbm, starts_hbm, coef_hbm, index_hbm,
                 send_ref, pack_ref, table_ref, att2_ref, ints_ref,
                 b_ref, astro_ref, star_ref, starts_ref, coef_ref, index_ref,
                 spread_ref, sems):
    slots, blocks, _ = index_ref.shape
    comps = astro_ref.shape[0]
    places = pack_places(slots, blocks, width)
    pairs = [(index_hbm, index_ref), (starts_hbm, starts_ref), (att_hbm, pack_ref.at[places[3]]),
             (coef_hbm, coef_ref), (b_hbm, b_ref), (astro_hbm, astro_ref), (star_hbm, star_ref)]
    copies = [
        pltpu.make_async_copy(source, target, sems.at[place])
        for place, (source, target) in enumerate(pairs)
    ]
    for copy in copies:
        copy.start()
    for copy in copies[:2]:
        copy.wait()
    index = jnp.concatenate([index_ref[slot] for slot in range(slots)], axis=0)
    starts_row = jnp.broadcast_to(starts_ref[...].astype(f32), (blocks, blocks))
    diagonal = lax.broadcasted_iota(jnp.int32, (blocks, blocks), 0) == lax.broadcasted_iota(
        jnp.int32, (blocks, blocks), 1
    )
    starts = jnp.sum(jnp.where(diagonal, starts_row, 0.0), axis=1, keepdims=True)
    starts = jnp.broadcast_to(starts, (blocks, LANES))
    pack_ref[places[1]] = index.astype(f32)
    pack_ref[places[2]] = starts
    starts = starts.astype(jnp.int32)
    prepare_index(index, starts, table_ref, ints_ref)
    for copy in copies[2:]:
        copy.wait()
    prepare_att(pack_ref[places[3]], att2_ref)
    rows = b_ref[...]
    coefs = [coef_ref.at[slot] for slot in range(slots)]
    indices = [index_ref.at[slot] for slot in range(slots)]
    for slot in range(slots):
        pack_ref[slot * 8 : slot * 8 + 8] = coef_ref[slot]
    send_ref[0:8] = rows
    send_ref[8:16] = inst_back(rows, coefs, indices, table_ref, spread_ref)
    send_ref[16:19] = att_back(rows, att2_ref[...], starts, width)
    send_ref[19:20] = jnp.sum(rows * rows, axis=0, keepdims=True)
    send_ref[20:24] = jnp.zeros((4, LANES), f32)
    for comp in range(comps):
        send_ref[24 + comp * 8 : 32 + comp * 8] = astro_ref[comp]
    send_ref[24 + comps * 8 : 32 + comps * 8] = star_ref[...].astype(f32)


def prepare_kernel(slots, blocks, width, pack_ref, table_ref, att2_ref, ints_ref):
    places = pack_places(slots, blocks, width)
    index = pack_ref[places[1]].astype(jnp.int32)
    starts = pack_ref[places[2]].astype(jnp.int32)
    prepare_index(index, starts, table_ref, ints_ref)
    prepare_att(pack_ref[places[3]], att2_ref)


def tree_sum(values):
    while len(values) > 1:
        values = [values[i] + values[i + 1] for i in range(0, len(values), 2)]
    return values[0]


def first_chip_kernel(count, *refs):
    ins, out_ref = refs[:count], refs[count]
    chip = lax.axis_index("tm") // 2
    size = ins[0].shape[0]
    for gap in range(count):
        at = pl.multiple_of((chip ^ gap) * size, 8)
        out_ref[pl.ds(at, size)] = ins[gap][...]


def group_rows(chip, count, mine, prev_row, after_row):
    half = lax.broadcasted_iota(jnp.int32, (1, LANES), 1) < 64
    first = mine[0:1] + jnp.where(half & (chip > 0), prev_row, 0.0)
    last = jnp.where(half & (chip < count - 1), mine[4:5] + after_row, 0.0)
    return [first, mine[1:4], last]


def chip_parts(core, own, other):
    low = jnp.where(core == 0, own, other)
    top = jnp.where(core == 0, other, own)
    return jnp.concatenate([low[0:2], low[2:3] + top[0:1], top[1:3]], axis=0)


def first_group_kernel(count, own_ref, other_ref, out_ref):
    me = lax.axis_index("tm")
    chip, core = me // 2, me % 2
    size = own_ref.shape[0] // count

    def part(ref, where, start):
        where = jnp.clip(where, 0, count - 1)
        return ref[pl.ds(pl.multiple_of(where * size + start, 8), 8)]

    def of_core(which, where):
        mine = (core == which) == (where == chip)
        return jnp.where(mine, part(own_ref, where, 16), part(other_ref, where, 16))

    def total(start):
        return tree_sum(
            [part(own_ref, chip ^ gap, start) + part(other_ref, chip ^ gap, start) for gap in range(count)]
        )

    mine = chip_parts(core, part(own_ref, chip, 16)[0:3], part(other_ref, chip, 16)[0:3])
    prev, after = of_core(1, chip - 1), of_core(0, chip + 1)
    out_ref[0:8] = total(8)
    att = group_rows(chip, count, mine, prev[2:3], after[0:1])
    out_ref[8:16] = jnp.concatenate(att + [total(16)[3:6]], axis=0)


def group_kernel(count, *refs):
    *ins, rows_ref, out_ref = refs
    me = lax.axis_index("tm")
    chip = me // 2
    places = [chip ^ gap for gap in range(count)]
    zero = jnp.zeros((8, LANES), f32)
    mine, prev, after = zero, zero, zero
    for ref, where in zip(ins, places):
        for half in range(2):
            at = pl.multiple_of((half * count + where) * 8, 8)
            rows_ref[pl.ds(at, 8)] = ref[half * 8 : half * 8 + 8]
        low = ref[24:32]
        mine = jnp.where(where == chip, low, mine)
        prev = jnp.where(where == chip - 1, low, prev)
        after = jnp.where(where == chip + 1, low, after)
    scalars = tree_sum([ref[24:32] for ref in ins])
    out_ref[0:8] = tree_sum([ref[16:24] for ref in ins])
    att = group_rows(chip, count, mine, prev[4:5], after[0:1])
    out_ref[8:16] = jnp.concatenate(att + [scalars[5:8]], axis=0)


def kept(count, keep_ref):
    size = keep_ref.shape[0] // count
    return size, size - 24, (size - 24) // 8 - 1


def star_sums(count, place, keep_ref, rows, table_ref, spread_ref, build):
    high = STARS_DEV // LANES
    size, extra, comps = kept(count, keep_ref)
    long = 8 * LANES
    packed = keep_ref[pl.ds(pl.multiple_of(place * size + 24, 8), extra)]
    index = packed[comps * 8 :].astype(jnp.int32)
    at0 = pl.multiple_of(place * long, long)
    split = [halves(packed[comp * 8 : comp * 8 + 8] * rows) for comp in range(comps)]
    for block in range(8):
        here = slice(block, block + 1)
        if build:
            table_ref[:, pl.ds(at0 + block * LANES, LANES)] = one_hot_low(index[here])
        pieces = []
        for part in range(2):
            for comp in range(comps):
                pieces.append(spread_high(index[here], split[comp][part][here], high))
        spread_ref[:, block * LANES : (block + 1) * LANES] = jnp.concatenate(
            pieces, axis=0
        ).astype(bf16)
    return dot_lanes(spread_ref[...], table_ref[:, pl.ds(at0, long)])


def star_rows(count, keep_ref, sums):
    high = STARS_DEV // LANES
    size, extra, comps = kept(count, keep_ref)
    chip = lax.axis_index("tm") // 2
    packed = keep_ref[pl.ds(pl.multiple_of(chip * size + 24, 8), extra)]
    star = packed[comps * 8 :].astype(jnp.int32)
    star_high, star_low = star >> 7, star & (LANES - 1)
    total = jnp.zeros((8, LANES), f32)
    for comp in range(comps):
        picked = jnp.zeros((8, LANES), f32)
        for place in range(high):
            at = comp * high + place
            picked = jnp.where(star_high == place, lane_pick(sums[at : at + 1], star_low), picked)
        total = total + packed[comp * 8 : comp * 8 + 8] * picked
    return total


def first_sums(count, keep_ref, table_ref, spread_ref):
    size = spread_ref.shape[0]

    def one(place, total):
        rows = keep_ref[pl.ds(pl.multiple_of(place * kept(count, keep_ref)[0], 8), 8)]
        return total + star_sums(count, place, keep_ref, rows, table_ref, spread_ref, True)

    total = lax.fori_loop(0, count, one, jnp.zeros((size, LANES), f32))
    return total[: size // 2] + total[size // 2 :]


def astro_own_kernel(count, keep_ref, out_ref, table_ref, spread_ref):
    out_ref[...] = first_sums(count, keep_ref, table_ref, spread_ref)


def astro_other_kernel(count, own_ref, keep_ref, part_ref, out_ref, ya_ref, table_ref, spread_ref):
    total = part_ref[...] + first_sums(count, keep_ref, table_ref, spread_ref)
    out_ref[...] = total
    ya_ref[0:8] = star_rows(count, own_ref, total)
    ya_ref[8:16] = star_rows(count, keep_ref, total)


def astro_kernel(count, own_ref, other_ref, own_table, other_table, rows_ref, out_ref, ya_ref,
                 spread_ref):
    me = lax.axis_index("tm")
    size = spread_ref.shape[1]
    sources = ((own_ref, own_table), (other_ref, other_table))

    def one(place, totals):
        new = []
        for half, (keep_ref, table_ref) in enumerate(sources):
            core = half ^ (me % 2) ^ jnp.where(place == me // 2, 0, 1)
            at = (core * count + place) * 8
            rows = rows_ref[pl.ds(pl.multiple_of(at, 8), 8)]
            part = star_sums(count, place, keep_ref, rows, table_ref, spread_ref.at[half], False)
            new.append(totals[half] + part)
        return tuple(new)

    zero = jnp.zeros((size, LANES), f32)
    own, other = lax.fori_loop(0, count, one, (zero, zero))
    total = own + other
    total = total[: size // 2] + total[size // 2 :]
    out_ref[...] = total
    ya_ref[0:8] = star_rows(count, own_ref, total)
    ya_ref[8:16] = star_rows(count, other_ref, total)


def sum_kernel(*refs):
    refs[-1][...] = tree_sum([ref[...] for ref in refs[:-1]])


def lane_sum(row):
    return jnp.broadcast_to(jnp.sum(row, axis=1, keepdims=True), row.shape)


def next_bidiagonal(total, state):
    squares, mixed, size = (lane_sum(total[row : row + 1]) for row in (13, 14, 15))
    alpha2 = size + epsilon
    alpha = jnp.sqrt(alpha2)
    rest = jnp.maximum(squares / alpha2 - 2.0 * mixed + alpha2 * state[0:1], 0.0)
    beta2 = rest + epsilon
    return alpha, jnp.sqrt(beta2), rest / beta2


def step_kernel(step, width, slots, chips, star_count, *refs):
    packs, tables, att2s, ints = refs[0:2], refs[2:4], refs[4:6], refs[6:8]
    sum_ref, ya_ref, refs = refs[8], refs[9], refs[10:]
    if step > 0:
        state_ref, old_z_ref, old_g_ref, old_u_ref, old_s_ref, old_gs_ref = refs[:6]
        refs = refs[6:]
    else:
        keep, refs = refs[:2], refs[2:]
    gathered, refs = refs[:-8], refs[-8:]
    send_ref, state_out, z_ref, g_ref, u_ref, s_ref, gs_ref, spread_ref = refs
    me = lax.axis_index("tm")
    chip, core = me // 2, me % 2
    high = STARS_DEV // LANES
    comps = sum_ref.shape[0] // high
    blocks = 8
    total = tree_sum([ref[...] for ref in gathered])
    back = jnp.concatenate([sum_ref[...], total], axis=0)
    base = comps * high
    pieces = [total[place : place + 1] for place in range(8)]
    att_back_rows = total[8:13]
    forward, starts, coefs, indices = [], [], [], []
    for half in range(2):
        starts.append(ints[half][slots * 8 :])
        own = jnp.where(core == half, att_back_rows[0:3], att_back_rows[2:5])
        part = att_forward(own, att2s[half][...], starts[half], width)
        part = part + ya_ref[half * 8 : half * 8 + 8]
        coefs.append([packs[half].at[slot * 8 : slot * 8 + 8] for slot in range(slots)])
        indices.append([ints[half].at[slot * 8 : slot * 8 + 8] for slot in range(slots)])
        for slot in range(slots):
            part = part + coefs[half][slot][...] * table_pick(pieces, indices[half][slot][...])
        forward.append(part)
    forward = jnp.concatenate(forward, axis=0)
    if step == 0:
        squares = lane_sum(total[13:14])
        beta2 = squares + epsilon
        beta = jnp.sqrt(beta2)
        at = pl.ds(pl.multiple_of(chip * kept(chips, keep[0])[0], 8), 8)
        u = jnp.concatenate([ref[at] for ref in keep], axis=0) / beta
        g = back / beta
        z = g
        gs = forward / beta
        both = gs
        state_out[...] = jnp.concatenate(
            [squares / beta2, beta, jnp.zeros((14, LANES), f32)], axis=0
        )
    else:
        state = state_ref[...]
        alpha, beta, left2 = next_bidiagonal(total, state)
        u = (old_s_ref[...] / alpha - alpha * old_u_ref[...]) / beta
        g = (back / alpha - alpha * old_g_ref[...]) / beta
        z = g - (beta / alpha) * old_z_ref[...]
        gs = (forward / alpha - alpha * old_gs_ref[...]) / beta
        both = gs - (beta / alpha) * old_s_ref[...]
        pieces = [left2, state[1 : 1 + step], beta, jnp.zeros((7 - step, LANES), f32)]
        pieces += [state[9 : 8 + step]] if step > 1 else []
        pieces += [alpha, jnp.zeros((7 - step, LANES), f32)]
        state_out[...] = jnp.concatenate(pieces, axis=0)
    z_ref[...] = z
    g_ref[...] = g
    u_ref[...] = u
    gs_ref[...] = gs
    s_ref[...] = both
    inst_rows = z[base : base + 8]
    att_rows = z[base + 8 : base + 13]
    rows = [both[0:8], both[8:16]]
    insts, atts = [], []
    for half in range(2):
        if step < ITERS - 1:
            insts.append(
                inst_back(rows[half], coefs[half], indices[half], tables[half], spread_ref.at[half])
            )
            atts.append(att_back(rows[half], att2s[half][...], starts[half], width))

    def squared(value):
        return jnp.sum(value * value, axis=0, keepdims=True)

    size = squared(z[:base]) * (1.0 / chips) + squared(att_rows[:4]) * (1.0 / star_count)
    size = size + squared(inst_rows) * (1.0 / (star_count * chips))
    mixed = [jnp.sum(rows[half] * u[half * 8 : half * 8 + 8], axis=0, keepdims=True) for half in range(2)]
    scalars = [squared(rows[0]) + squared(rows[1]), mixed[0] + mixed[1], size]
    if step == ITERS - 1:
        send_ref[...] = jnp.concatenate([jnp.zeros((5, LANES), f32)] + scalars, axis=0)
        return
    send_ref[0:16] = jnp.where(core == 0, both, jnp.concatenate(rows[::-1], axis=0))
    send_ref[16:24] = insts[0] + insts[1]
    send_ref[24:32] = jnp.concatenate([chip_parts(core, *atts)] + scalars, axis=0)


def last_kernel(comps, share, star_count, state_ref, *refs):
    gathered, refs = refs[: -ITERS - 3], refs[-ITERS - 3 :]
    z_refs = refs[:ITERS]
    astro_ref, att_ref, inst_ref = refs[ITERS:]
    high = STARS_DEV // LANES
    me = lax.axis_index("tm")
    total = tree_sum([ref[...] for ref in gathered])
    total = jnp.concatenate([jnp.zeros((8, LANES), f32), total], axis=0)
    state = state_ref[...]
    alpha, beta, _ = next_bidiagonal(total, state)
    betas = [state[1 + k : 2 + k] for k in range(ITERS)] + [beta]
    alphas = [state[9 + k : 10 + k] for k in range(ITERS - 1)] + [alpha]
    rho_bar, phi_bar = alphas[0], betas[0]
    weights = [jnp.zeros((1, LANES), f32)] * ITERS
    search = [jnp.zeros((1, LANES), f32)] * ITERS
    search[0] = 1.0 / alphas[0]
    for k in range(ITERS):
        rho = jnp.sqrt(rho_bar * rho_bar + betas[k + 1] * betas[k + 1])
        cosine, sine = rho_bar / rho, betas[k + 1] / rho
        phi = cosine * phi_bar
        phi_bar = sine * phi_bar
        weights = [x + phi / rho * w for x, w in zip(weights, search)]
        if k + 1 < ITERS:
            theta = sine * alphas[k + 1]
            rho_bar = -cosine * alphas[k + 1]
            search = [-(theta / rho) * w for w in search]
            search[k + 1] = 1.0 / alphas[k + 1]
    base = comps * high
    tiles = share // LANES

    def mix(read):
        total = weights[0] * read(z_refs[0])
        for k in range(1, ITERS):
            total = total + weights[k] * read(z_refs[k])
        return total

    for comp in range(comps):
        for tile in range(tiles):
            at = comp * high + me * tiles + tile
            astro_ref[comp : comp + 1, tile * LANES : (tile + 1) * LANES] = mix(
                lambda ref: ref[pl.ds(at, 1)]
            )
    inst_ref[...] = mix(lambda ref: ref[base : base + 8])
    rows = ATT_DEV // LANES
    att_ref[...] = mix(lambda ref: ref[pl.ds(base + 8 + (me % 2) * rows, rows)])


def call(kernel, name, out, args, scratch=(), space=pltpu.VMEM):
    vmem = pl.BlockSpec(memory_space=pltpu.VMEM)
    return pl.pallas_call(
        kernel,
        name=name,
        out_shape=[jax.ShapeDtypeStruct(shape, dtype) for shape, dtype in out],
        in_specs=[pl.BlockSpec(memory_space=space)] * len(args),
        out_specs=[vmem] * len(out),
        scratch_shapes=list(scratch),
        compiler_params=pltpu.CompilerParams(vmem_limit_bytes=VMEM_LIMIT),
    )(*args)


def direct(value, axis, gaps):
    count = lax.axis_size(axis)
    return [value] + [
        lax.ppermute(value, axis, [(i, i ^ gap) for i in range(count)]) for gap in gaps
    ]


def exchange(value, axis):
    tm_count, star_count = lax.axis_size("tm"), lax.axis_size("star")
    count = star_count if axis == "star" else tm_count // 2
    got = {0: value}
    for gap in range(count - 1, 0, -1) if axis == "tm" else range(1, count):
        steps = []
        for star in range(star_count):
            for tm in range(tm_count):
                far = (star ^ gap, tm ^ 1) if axis == "star" else (star, tm ^ (2 * gap + 1))
                steps.append((star * tm_count + tm, far[0] * tm_count + far[1]))
        got[gap] = lax.ppermute(value, ("star", "tm"), steps)
    return [got[gap] for gap in range(count)]


def rows_type(rows):
    return ((rows, LANES), f32)


def per_device(astro_coef, star_index, att_coef, att_start, inst_coef, inst_index, observed):
    tm_count, star_count = lax.axis_size("tm"), lax.axis_size("star")
    comps = astro_coef.shape[1]
    slots = inst_coef.shape[1]
    blocks, width, height = att_coef.shape[1:]
    share = STARS_DEV // tm_count
    high = STARS_DEV // LANES
    chips = tm_count // 2
    args = [
        observed.reshape(blocks, height),
        astro_coef.reshape(comps, blocks, height),
        star_index.reshape(blocks, height),
        att_coef.reshape(blocks * width, height),
        att_start,
        inst_coef.reshape(slots, blocks, height),
        inst_index.reshape(slots, blocks, height),
    ]
    long = slots * blocks * height
    extra = 8 * comps + 8
    spread = pltpu.VMEM((16, long), bf16)
    prepared = [((LANES, long), bf16), ((2 * blocks * width, height), bf16),
                ((8 * slots + 8, LANES), jnp.int32)]
    here = [pltpu.with_memory_space_constraint(arg, pltpu.HBM) for arg in args]
    send, pack, *mine = call(
        functools.partial(first_kernel, width),
        "first",
        [((24 + extra, LANES), f32), ((16 * slots + 8 + blocks * width, LANES), f32)] + prepared,
        here,
        [pltpu.VMEM(arg.shape, arg.dtype) for arg in args if arg is not args[3]]
        + [spread, pltpu.SemaphoreType.DMA((len(args),))],
        pl.ANY,
    )
    state = z = g = u = rows = gs = None
    solutions = []
    group_type = rows_type(16)
    for step in range(ITERS):
        wide = (2 * comps * high, blocks * height)
        sums_type = rows_type(comps * high)
        pair = rows_type(2 * blocks)
        got = exchange(send, "tm")
        if step == 0:
            (gathered,) = call(
                functools.partial(first_chip_kernel, chips),
                "chip",
                [rows_type(chips * (24 + extra))],
                got,
            )
            keep = direct(gathered, "tm", [1])
            table_type = ((LANES, chips * blocks * height), bf16)
            own_sums, own_table = call(
                functools.partial(astro_own_kernel, chips),
                "astro_own",
                [sums_type, table_type],
                [gathered],
                [pltpu.VMEM(wide, bf16)],
            )
            keep[1], own_sums = lax.optimization_barrier((keep[1], own_sums))
            (group,) = call(
                functools.partial(first_group_kernel, chips), "group", [group_type], keep
            )
            group, late_pack = lax.optimization_barrier((group, pack))
            _, other_pack = direct(late_pack, "tm", [1])
            theirs = call(
                functools.partial(prepare_kernel, slots, blocks, width),
                "prepare",
                prepared,
                [other_pack],
            )
            basics = [pack, other_pack] + [value for both in zip(mine, theirs) for value in both]
        else:
            all_rows, group = call(
                functools.partial(group_kernel, chips),
                "group",
                [rows_type(16 * chips), group_type],
                got,
            )
        across = exchange(group, "star")
        if step == 0:
            sums, ya, other_table = call(
                functools.partial(astro_other_kernel, chips),
                "astro",
                [sums_type, pair, table_type],
                keep + [own_sums],
                [pltpu.VMEM(wide, bf16)],
            )
        else:
            sums, ya = call(
                functools.partial(astro_kernel, chips),
                "astro",
                [sums_type, pair],
                keep + [own_table, other_table, all_rows],
                [pltpu.VMEM((2,) + wide, bf16)],
            )
        tall = ((comps * high + 16, LANES), f32)
        older = keep if step == 0 else [state, z, g, u, rows, gs]
        send, state, z, g, u, rows, gs = call(
            functools.partial(step_kernel, step, width, slots, chips, star_count),
            "step",
            [rows_type(32 if step < ITERS - 1 else 8), group_type, tall, tall, pair, pair,
             pair],
            basics + [sums, ya] + older + across,
            [pltpu.VMEM((2, 16, long), bf16)],
        )
        solutions.append(z)
    (send,) = call(sum_kernel, "sum", [rows_type(8)], exchange(send, "tm"))
    across = exchange(send, "star")
    out_astro, out_att, out_inst = call(
        functools.partial(last_kernel, comps, share, star_count),
        "last",
        [((comps, share), f32), ((ATT_DEV // LANES, LANES), f32), ((NINST // LANES, LANES), f32)],
        [state] + across + solutions,
    )
    return out_astro, out_att.reshape(-1), out_inst.reshape(-1)


def solution(mesh):
    return jax.shard_map(
        per_device,
        mesh=mesh,
        in_specs=(
            P("star", None, "tm"),
            P("star", "tm"),
            P("star", "tm", None, None),
            P("star", "tm"),
            P("star", None, "tm"),
            P("star", None, "tm"),
            P("star", "tm"),
        ),
        out_specs=(P(None, ("star", "tm")), P("tm"), P()),
        check_vma=False,
    )
```

```python
import functools

import jax
import jax.numpy as jnp
from jax import lax
from jax.experimental import pallas as pl
from jax.experimental.pallas import tpu as pltpu
from jax.sharding import PartitionSpec as P

STARS_DEV = 2048
NINST = 1024
ITERS = 3
ATT_DEV = 256
LANES = 128

epsilon = 1e-06
f32 = jnp.float32
bf16 = jnp.bfloat16
VMEM_LIMIT = 16 * 1024 * 1024


def halves(value):
    top = value.astype(bf16).astype(f32)
    return top, (value - top).astype(bf16).astype(f32)


def dot_lanes(left, right):
    return lax.dot_general(left, right, (((1,), (1,)), ((), ())), preferred_element_type=f32)


def dot_plain(left, right):
    return lax.dot_general(left, right, (((1,), (0,)), ((), ())), preferred_element_type=f32)


def lane_pick(row, lane_index):
    table = jnp.broadcast_to(row, lane_index.shape)
    return jnp.take_along_axis(table, lane_index, axis=1, mode="promise_in_bounds")


def table_pick(rows, index):
    high, low = index >> 7, index & (LANES - 1)
    total = jnp.zeros(index.shape, f32)
    for place, row in enumerate(rows):
        total = jnp.where(high == place, lane_pick(row, low), total)
    return total


def one_hot_low(index_row):
    shape = (LANES, LANES)
    low = jnp.broadcast_to(index_row & (LANES - 1), shape)
    hit = lax.broadcasted_iota(jnp.int32, shape, 0) == low
    return jnp.where(hit, 1.0, 0.0).astype(bf16)


def spread_high(index_row, value_row, count):
    shape = (count, LANES)
    high = jnp.broadcast_to(index_row >> 7, shape)
    hit = lax.broadcasted_iota(jnp.int32, shape, 0) == high
    return jnp.where(hit, jnp.broadcast_to(value_row, shape), 0.0)


def block_masks(blocks, width):
    shape = (blocks, LANES)
    row = lax.broadcasted_iota(jnp.int32, shape, 0)
    lane = lax.broadcasted_iota(jnp.int32, shape, 1)
    per_tile = LANES // width
    tiles = blocks // per_tile
    return [row == tile * per_tile + lane // width for tile in range(tiles)], row, lane


def inst_back(rows, coef_ref, index_ref, table_ref):
    slots, blocks = len(coef_ref), rows.shape[0]
    count = NINST // LANES
    long = blocks * LANES
    both = jnp.zeros((2 * count, LANES), f32)
    for slot in range(slots):
        top, rest = halves(coef_ref[slot][...] * rows)
        index = index_ref[slot][...]
        wide = []
        for block in range(blocks):
            here = slice(block, block + 1)
            pieces = [spread_high(index[here], part[here], count) for part in (top, rest)]
            wide.append(jnp.concatenate(pieces, axis=0).astype(bf16))
        table = table_ref[:, slot * long : (slot + 1) * long]
        both = both + dot_lanes(jnp.concatenate(wide, axis=1), table)
    return both[:count] + both[count:]


def att_back(rows, att2, starts, width):
    blocks = rows.shape[0]
    size = att2.shape[0] // 2
    top, rest = halves(rows)
    both = dot_lanes(jnp.concatenate([top, rest], axis=0).astype(bf16), att2)
    both = both[:blocks] + both[blocks:]
    both = both[:, :size] + both[:, size:]
    masks, row, lane = block_masks(blocks, width)
    own = jnp.zeros((blocks, LANES), f32)
    for tile, mask in enumerate(masks):
        own = own + jnp.where(mask, both[:, tile * LANES : (tile + 1) * LANES], 0.0)
    shift = (row % (LANES // width)) * width
    out = []
    for tile in range((ATT_DEV + width + LANES - 1) // LANES):
        offset = lane + tile * LANES - starts
        inside = (offset >= 0) & (offset < width)
        picked = jnp.take_along_axis(
            own, jnp.where(inside, offset + shift, 0), axis=1, mode="promise_in_bounds"
        )
        out.append(jnp.sum(jnp.where(inside, picked, 0.0), axis=0, keepdims=True))
    return jnp.concatenate(out, axis=0)


def att_forward(att_rows, att2, starts, width):
    blocks = starts.shape[0]
    masks, row, lane = block_masks(blocks, width)
    tiles = [att_rows[tile : tile + 1] for tile in range(att_rows.shape[0])]
    window = table_pick(tiles, starts + lane % width)
    wide = jnp.concatenate([jnp.where(mask, window, 0.0) for mask in masks], axis=1)
    top, rest = halves(wide)
    left = jnp.concatenate([top, rest], axis=0).astype(bf16)
    both = dot_plain(jnp.concatenate([left, left], axis=1), att2)
    return both[:blocks] + both[blocks:]


def pack_places(slots, blocks, width):
    at = slots * 8
    return slice(0, at), slice(at, 2 * at), slice(2 * at, 2 * at + 8), slice(
        2 * at + 8, 2 * at + 8 + blocks * width
    )


def prepare_index(index_rows, starts, table_ref, ints_ref):
    count = index_rows.shape[0] // 8
    ints_ref[0 : count * 8] = index_rows
    ints_ref[count * 8 :] = starts
    for place in range(count * 8):
        table_ref[:, place * LANES : (place + 1) * LANES] = one_hot_low(
            index_rows[place : place + 1]
        )


def prepare_att(att, att2_ref):
    top = att.astype(bf16)
    att2_ref[...] = jnp.concatenate([top, (att - top.astype(f32)).astype(bf16)], axis=0)


def first_kernel(width, b_hbm, astro_hbm, star_hbm, att_hbm, starts_hbm, coef_hbm, index_hbm,
                 send_ref, pack_ref, table_ref, att2_ref, ints_ref,
                 b_ref, astro_ref, star_ref, starts_ref, coef_ref, index_ref,
                 sems):
    slots, blocks, _ = index_ref.shape
    comps = astro_ref.shape[0]
    places = pack_places(slots, blocks, width)
    pairs = [(index_hbm, index_ref), (starts_hbm, starts_ref), (att_hbm, pack_ref.at[places[3]]),
             (coef_hbm, coef_ref), (b_hbm, b_ref), (astro_hbm, astro_ref), (star_hbm, star_ref)]
    copies = [
        pltpu.make_async_copy(source, target, sems.at[place])
        for place, (source, target) in enumerate(pairs)
    ]
    for copy in copies:
        copy.start()
    for copy in copies[:2]:
        copy.wait()
    index = jnp.concatenate([index_ref[slot] for slot in range(slots)], axis=0)
    starts_row = jnp.broadcast_to(starts_ref[...].astype(f32), (blocks, blocks))
    diagonal = lax.broadcasted_iota(jnp.int32, (blocks, blocks), 0) == lax.broadcasted_iota(
        jnp.int32, (blocks, blocks), 1
    )
    starts = jnp.sum(jnp.where(diagonal, starts_row, 0.0), axis=1, keepdims=True)
    starts = jnp.broadcast_to(starts, (blocks, LANES))
    pack_ref[places[1]] = index.astype(f32)
    pack_ref[places[2]] = starts
    starts = starts.astype(jnp.int32)
    prepare_index(index, starts, table_ref, ints_ref)
    for copy in copies[2:]:
        copy.wait()
    prepare_att(pack_ref[places[3]], att2_ref)
    rows = b_ref[...]
    coefs = [coef_ref.at[slot] for slot in range(slots)]
    indices = [index_ref.at[slot] for slot in range(slots)]
    for slot in range(slots):
        pack_ref[slot * 8 : slot * 8 + 8] = coef_ref[slot]
    send_ref[0:8] = rows
    send_ref[8:16] = inst_back(rows, coefs, indices, table_ref)
    send_ref[16:19] = att_back(rows, att2_ref[...], starts, width)
    send_ref[19:20] = jnp.sum(rows * rows, axis=0, keepdims=True)
    send_ref[20:24] = jnp.zeros((4, LANES), f32)
    for comp in range(comps):
        send_ref[24 + comp * 8 : 32 + comp * 8] = astro_ref[comp]
    send_ref[24 + comps * 8 : 32 + comps * 8] = star_ref[...].astype(f32)


def prepare_kernel(slots, blocks, width, pack_ref, table_ref, att2_ref, ints_ref):
    places = pack_places(slots, blocks, width)
    index = pack_ref[places[1]].astype(jnp.int32)
    starts = pack_ref[places[2]].astype(jnp.int32)
    prepare_index(index, starts, table_ref, ints_ref)
    prepare_att(pack_ref[places[3]], att2_ref)


def tree_sum(values):
    while len(values) > 1:
        values = [values[i] + values[i + 1] for i in range(0, len(values), 2)]
    return values[0]


def first_chip_kernel(count, *refs):
    ins, out_ref = refs[:count], refs[count]
    chip = lax.axis_index("tm") // 2
    size = ins[0].shape[0]
    for gap in range(count):
        at = pl.multiple_of((chip ^ gap) * size, 8)
        out_ref[pl.ds(at, size)] = ins[gap][...]


def group_rows(chip, count, mine, prev_row, after_row):
    half = lax.broadcasted_iota(jnp.int32, (1, LANES), 1) < 64
    first = mine[0:1] + jnp.where(half & (chip > 0), prev_row, 0.0)
    last = jnp.where(half & (chip < count - 1), mine[4:5] + after_row, 0.0)
    return [first, mine[1:4], last]


def chip_parts(core, own, other):
    low = jnp.where(core == 0, own, other)
    top = jnp.where(core == 0, other, own)
    return jnp.concatenate([low[0:2], low[2:3] + top[0:1], top[1:3]], axis=0)


def first_group_kernel(count, own_ref, other_ref, out_ref):
    me = lax.axis_index("tm")
    chip, core = me // 2, me % 2
    size = own_ref.shape[0] // count

    def part(ref, where, start):
        where = jnp.clip(where, 0, count - 1)
        return ref[pl.ds(pl.multiple_of(where * size + start, 8), 8)]

    def of_core(which, where):
        mine = (core == which) == (where == chip)
        return jnp.where(mine, part(own_ref, where, 16), part(other_ref, where, 16))

    def total(start):
        return tree_sum(
            [part(own_ref, chip ^ gap, start) + part(other_ref, chip ^ gap, start) for gap in range(count)]
        )

    mine = chip_parts(core, part(own_ref, chip, 16)[0:3], part(other_ref, chip, 16)[0:3])
    prev, after = of_core(1, chip - 1), of_core(0, chip + 1)
    out_ref[0:8] = total(8)
    att = group_rows(chip, count, mine, prev[2:3], after[0:1])
    out_ref[8:16] = jnp.concatenate(att + [total(16)[3:6]], axis=0)


def group_kernel(count, *refs):
    *ins, rows_ref, out_ref = refs
    me = lax.axis_index("tm")
    chip = me // 2
    places = [chip ^ gap for gap in range(count)]
    zero = jnp.zeros((8, LANES), f32)
    mine, prev, after = zero, zero, zero
    for ref, where in zip(ins, places):
        for half in range(2):
            at = pl.multiple_of((half * count + where) * 8, 8)
            rows_ref[pl.ds(at, 8)] = ref[half * 8 : half * 8 + 8]
        low = ref[24:32]
        mine = jnp.where(where == chip, low, mine)
        prev = jnp.where(where == chip - 1, low, prev)
        after = jnp.where(where == chip + 1, low, after)
    scalars = tree_sum([ref[24:32] for ref in ins])
    out_ref[0:8] = tree_sum([ref[16:24] for ref in ins])
    att = group_rows(chip, count, mine, prev[4:5], after[0:1])
    out_ref[8:16] = jnp.concatenate(att + [scalars[5:8]], axis=0)


def kept(count, keep_ref):
    size = keep_ref.shape[0] // count
    return size, size - 24, (size - 24) // 8 - 1


def star_sums(count, place, keep_ref, rows, table_ref, spread_ref, build):
    high = STARS_DEV // LANES
    size, extra, comps = kept(count, keep_ref)
    long = 8 * LANES
    packed = keep_ref[pl.ds(pl.multiple_of(place * size + 24, 8), extra)]
    index = packed[comps * 8 :].astype(jnp.int32)
    at0 = pl.multiple_of(place * long, long)
    split = [halves(packed[comp * 8 : comp * 8 + 8] * rows) for comp in range(comps)]
    for block in range(8):
        here = slice(block, block + 1)
        if build:
            table_ref[:, pl.ds(at0 + block * LANES, LANES)] = one_hot_low(index[here])
        pieces = []
        for part in range(2):
            for comp in range(comps):
                pieces.append(spread_high(index[here], split[comp][part][here], high))
        spread_ref[:, block * LANES : (block + 1) * LANES] = jnp.concatenate(
            pieces, axis=0
        ).astype(bf16)
    return dot_lanes(spread_ref[...], table_ref[:, pl.ds(at0, long)])


def star_rows(count, keep_ref, sums):
    high = STARS_DEV // LANES
    size, extra, comps = kept(count, keep_ref)
    chip = lax.axis_index("tm") // 2
    packed = keep_ref[pl.ds(pl.multiple_of(chip * size + 24, 8), extra)]
    star = packed[comps * 8 :].astype(jnp.int32)
    star_high, star_low = star >> 7, star & (LANES - 1)
    total = jnp.zeros((8, LANES), f32)
    for comp in range(comps):
        picked = jnp.zeros((8, LANES), f32)
        for place in range(high):
            at = comp * high + place
            picked = jnp.where(star_high == place, lane_pick(sums[at : at + 1], star_low), picked)
        total = total + packed[comp * 8 : comp * 8 + 8] * picked
    return total


def first_sums(count, keep_ref, table_ref, spread_ref):
    size = spread_ref.shape[0]

    def one(place, total):
        rows = keep_ref[pl.ds(pl.multiple_of(place * kept(count, keep_ref)[0], 8), 8)]
        return total + star_sums(count, place, keep_ref, rows, table_ref, spread_ref, True)

    total = lax.fori_loop(0, count, one, jnp.zeros((size, LANES), f32))
    return total[: size // 2] + total[size // 2 :]


def astro_own_kernel(count, keep_ref, out_ref, table_ref, spread_ref):
    out_ref[...] = first_sums(count, keep_ref, table_ref, spread_ref)


def astro_other_kernel(count, own_ref, keep_ref, part_ref, out_ref, ya_ref, table_ref, spread_ref):
    total = part_ref[...] + first_sums(count, keep_ref, table_ref, spread_ref)
    out_ref[...] = total
    ya_ref[0:8] = star_rows(count, own_ref, total)
    ya_ref[8:16] = star_rows(count, keep_ref, total)


def astro_kernel(count, own_ref, other_ref, own_table, other_table, rows_ref, out_ref, ya_ref,
                 spread_ref):
    me = lax.axis_index("tm")
    size = spread_ref.shape[1]
    sources = ((own_ref, own_table), (other_ref, other_table))

    def one(place, totals):
        new = []
        for half, (keep_ref, table_ref) in enumerate(sources):
            core = half ^ (me % 2) ^ jnp.where(place == me // 2, 0, 1)
            at = (core * count + place) * 8
            rows = rows_ref[pl.ds(pl.multiple_of(at, 8), 8)]
            part = star_sums(count, place, keep_ref, rows, table_ref, spread_ref.at[half], False)
            new.append(totals[half] + part)
        return tuple(new)

    zero = jnp.zeros((size, LANES), f32)
    own, other = lax.fori_loop(0, count, one, (zero, zero))
    total = own + other
    total = total[: size // 2] + total[size // 2 :]
    out_ref[...] = total
    ya_ref[0:8] = star_rows(count, own_ref, total)
    ya_ref[8:16] = star_rows(count, other_ref, total)


def sum_kernel(*refs):
    refs[-1][...] = tree_sum([ref[...] for ref in refs[:-1]])


def lane_sum(row):
    return jnp.broadcast_to(jnp.sum(row, axis=1, keepdims=True), row.shape)


def next_bidiagonal(total, state):
    squares, mixed, size = (lane_sum(total[row : row + 1]) for row in (13, 14, 15))
    alpha2 = size + epsilon
    alpha = jnp.sqrt(alpha2)
    rest = jnp.maximum(squares / alpha2 - 2.0 * mixed + alpha2 * state[0:1], 0.0)
    beta2 = rest + epsilon
    return alpha, jnp.sqrt(beta2), rest / beta2


def step_kernel(step, width, slots, chips, star_count, *refs):
    packs, tables, att2s, ints = refs[0:2], refs[2:4], refs[4:6], refs[6:8]
    sum_ref, ya_ref, refs = refs[8], refs[9], refs[10:]
    if step > 0:
        state_ref, old_z_ref, old_g_ref, old_u_ref, old_s_ref, old_gs_ref = refs[:6]
        refs = refs[6:]
    else:
        keep, refs = refs[:2], refs[2:]
    gathered, refs = refs[:-7], refs[-7:]
    send_ref, state_out, z_ref, g_ref, u_ref, s_ref, gs_ref = refs
    me = lax.axis_index("tm")
    chip, core = me // 2, me % 2
    high = STARS_DEV // LANES
    comps = sum_ref.shape[0] // high
    blocks = 8
    total = tree_sum([ref[...] for ref in gathered])
    back = jnp.concatenate([sum_ref[...], total], axis=0)
    base = comps * high
    pieces = [total[place : place + 1] for place in range(8)]
    att_back_rows = total[8:13]
    forward, starts, coefs, indices = [], [], [], []
    for half in range(2):
        starts.append(ints[half][slots * 8 :])
        own = jnp.where(core == half, att_back_rows[0:3], att_back_rows[2:5])
        part = att_forward(own, att2s[half][...], starts[half], width)
        part = part + ya_ref[half * 8 : half * 8 + 8]
        coefs.append([packs[half].at[slot * 8 : slot * 8 + 8] for slot in range(slots)])
        indices.append([ints[half].at[slot * 8 : slot * 8 + 8] for slot in range(slots)])
        for slot in range(slots):
            part = part + coefs[half][slot][...] * table_pick(pieces, indices[half][slot][...])
        forward.append(part)
    forward = jnp.concatenate(forward, axis=0)
    if step == 0:
        squares = lane_sum(total[13:14])
        beta2 = squares + epsilon
        beta = jnp.sqrt(beta2)
        at = pl.ds(pl.multiple_of(chip * kept(chips, keep[0])[0], 8), 8)
        u = jnp.concatenate([ref[at] for ref in keep], axis=0) / beta
        g = back / beta
        z = g
        gs = forward / beta
        both = gs
        state_out[...] = jnp.concatenate(
            [squares / beta2, beta, jnp.zeros((14, LANES), f32)], axis=0
        )
    else:
        state = state_ref[...]
        alpha, beta, left2 = next_bidiagonal(total, state)
        u = (old_s_ref[...] / alpha - alpha * old_u_ref[...]) / beta
        g = (back / alpha - alpha * old_g_ref[...]) / beta
        z = g - (beta / alpha) * old_z_ref[...]
        gs = (forward / alpha - alpha * old_gs_ref[...]) / beta
        both = gs - (beta / alpha) * old_s_ref[...]
        pieces = [left2, state[1 : 1 + step], beta, jnp.zeros((7 - step, LANES), f32)]
        pieces += [state[9 : 8 + step]] if step > 1 else []
        pieces += [alpha, jnp.zeros((7 - step, LANES), f32)]
        state_out[...] = jnp.concatenate(pieces, axis=0)
    z_ref[...] = z
    g_ref[...] = g
    u_ref[...] = u
    gs_ref[...] = gs
    s_ref[...] = both
    inst_rows = z[base : base + 8]
    att_rows = z[base + 8 : base + 13]
    rows = [both[0:8], both[8:16]]
    insts, atts = [], []
    for half in range(2):
        if step < ITERS - 1:
            insts.append(inst_back(rows[half], coefs[half], indices[half], tables[half]))
            atts.append(att_back(rows[half], att2s[half][...], starts[half], width))

    def squared(value):
        return jnp.sum(value * value, axis=0, keepdims=True)

    size = squared(z[:base]) * (1.0 / chips) + squared(att_rows[:4]) * (1.0 / star_count)
    size = size + squared(inst_rows) * (1.0 / (star_count * chips))
    mixed = [jnp.sum(rows[half] * u[half * 8 : half * 8 + 8], axis=0, keepdims=True) for half in range(2)]
    scalars = [squared(rows[0]) + squared(rows[1]), mixed[0] + mixed[1], size]
    if step == ITERS - 1:
        send_ref[...] = jnp.concatenate([jnp.zeros((5, LANES), f32)] + scalars, axis=0)
        return
    send_ref[0:16] = jnp.where(core == 0, both, jnp.concatenate(rows[::-1], axis=0))
    send_ref[16:24] = insts[0] + insts[1]
    send_ref[24:32] = jnp.concatenate([chip_parts(core, *atts)] + scalars, axis=0)


def last_kernel(comps, share, star_count, state_ref, *refs):
    gathered, refs = refs[: -ITERS - 3], refs[-ITERS - 3 :]
    z_refs = refs[:ITERS]
    astro_ref, att_ref, inst_ref = refs[ITERS:]
    high = STARS_DEV // LANES
    me = lax.axis_index("tm")
    total = tree_sum([ref[...] for ref in gathered])
    total = jnp.concatenate([jnp.zeros((8, LANES), f32), total], axis=0)
    state = state_ref[...]
    alpha, beta, _ = next_bidiagonal(total, state)
    betas = [state[1 + k : 2 + k] for k in range(ITERS)] + [beta]
    alphas = [state[9 + k : 10 + k] for k in range(ITERS - 1)] + [alpha]
    rho_bar, phi_bar = alphas[0], betas[0]
    weights = [jnp.zeros((1, LANES), f32)] * ITERS
    search = [jnp.zeros((1, LANES), f32)] * ITERS
    search[0] = 1.0 / alphas[0]
    for k in range(ITERS):
        rho = jnp.sqrt(rho_bar * rho_bar + betas[k + 1] * betas[k + 1])
        cosine, sine = rho_bar / rho, betas[k + 1] / rho
        phi = cosine * phi_bar
        phi_bar = sine * phi_bar
        weights = [x + phi / rho * w for x, w in zip(weights, search)]
        if k + 1 < ITERS:
            theta = sine * alphas[k + 1]
            rho_bar = -cosine * alphas[k + 1]
            search = [-(theta / rho) * w for w in search]
            search[k + 1] = 1.0 / alphas[k + 1]
    base = comps * high
    tiles = share // LANES

    def mix(read):
        total = weights[0] * read(z_refs[0])
        for k in range(1, ITERS):
            total = total + weights[k] * read(z_refs[k])
        return total

    for comp in range(comps):
        for tile in range(tiles):
            at = comp * high + me * tiles + tile
            astro_ref[comp : comp + 1, tile * LANES : (tile + 1) * LANES] = mix(
                lambda ref: ref[pl.ds(at, 1)]
            )
    inst_ref[...] = mix(lambda ref: ref[base : base + 8])
    rows = ATT_DEV // LANES
    att_ref[...] = mix(lambda ref: ref[pl.ds(base + 8 + (me % 2) * rows, rows)])


def call(kernel, name, out, args, scratch=(), space=pltpu.VMEM):
    vmem = pl.BlockSpec(memory_space=pltpu.VMEM)
    return pl.pallas_call(
        kernel,
        name=name,
        out_shape=[jax.ShapeDtypeStruct(shape, dtype) for shape, dtype in out],
        in_specs=[pl.BlockSpec(memory_space=space)] * len(args),
        out_specs=[vmem] * len(out),
        scratch_shapes=list(scratch),
        compiler_params=pltpu.CompilerParams(vmem_limit_bytes=VMEM_LIMIT),
    )(*args)


def direct(value, axis, gaps):
    count = lax.axis_size(axis)
    return [value] + [
        lax.ppermute(value, axis, [(i, i ^ gap) for i in range(count)]) for gap in gaps
    ]


def exchange(value, axis):
    tm_count, star_count = lax.axis_size("tm"), lax.axis_size("star")
    got = [value]
    for gap in range(1, star_count if axis == "star" else tm_count // 2):
        steps = []
        for star in range(star_count):
            for tm in range(tm_count):
                far = (star ^ gap, tm ^ 1) if axis == "star" else (star, tm ^ (2 * gap + 1))
                steps.append((star * tm_count + tm, far[0] * tm_count + far[1]))
        got.append(lax.ppermute(value, ("star", "tm"), steps))
    return got


def rows_type(rows):
    return ((rows, LANES), f32)


def per_device(astro_coef, star_index, att_coef, att_start, inst_coef, inst_index, observed):
    tm_count, star_count = lax.axis_size("tm"), lax.axis_size("star")
    comps = astro_coef.shape[1]
    slots = inst_coef.shape[1]
    blocks, width, height = att_coef.shape[1:]
    share = STARS_DEV // tm_count
    high = STARS_DEV // LANES
    chips = tm_count // 2
    args = [
        observed.reshape(blocks, height),
        astro_coef.reshape(comps, blocks, height),
        star_index.reshape(blocks, height),
        att_coef.reshape(blocks * width, height),
        att_start,
        inst_coef.reshape(slots, blocks, height),
        inst_index.reshape(slots, blocks, height),
    ]
    long = slots * blocks * height
    extra = 8 * comps + 8
    prepared = [((LANES, long), bf16), ((2 * blocks * width, height), bf16),
                ((8 * slots + 8, LANES), jnp.int32)]
    here = [pltpu.with_memory_space_constraint(arg, pltpu.HBM) for arg in args]
    send, pack, *mine = call(
        functools.partial(first_kernel, width),
        "first",
        [((24 + extra, LANES), f32), ((16 * slots + 8 + blocks * width, LANES), f32)] + prepared,
        here,
        [pltpu.VMEM(arg.shape, arg.dtype) for arg in args if arg is not args[3]]
        + [pltpu.SemaphoreType.DMA((len(args),))],
        pl.ANY,
    )
    state = z = g = u = rows = gs = None
    solutions = []
    group_type = rows_type(16)
    for step in range(ITERS):
        wide = (2 * comps * high, blocks * height)
        sums_type = rows_type(comps * high)
        pair = rows_type(2 * blocks)
        got = exchange(send, "tm")
        if step == 0:
            (gathered,) = call(
                functools.partial(first_chip_kernel, chips),
                "chip",
                [rows_type(chips * (24 + extra))],
                got,
            )
            keep = direct(gathered, "tm", [1])
            table_type = ((LANES, chips * blocks * height), bf16)
            own_sums, own_table = call(
                functools.partial(astro_own_kernel, chips),
                "astro_own",
                [sums_type, table_type],
                [gathered],
                [pltpu.VMEM(wide, bf16)],
            )
            keep[1], own_sums = lax.optimization_barrier((keep[1], own_sums))
            (group,) = call(
                functools.partial(first_group_kernel, chips), "group", [group_type], keep
            )
            group, late_pack = lax.optimization_barrier((group, pack))
            _, other_pack = direct(late_pack, "tm", [1])
            theirs = call(
                functools.partial(prepare_kernel, slots, blocks, width),
                "prepare",
                prepared,
                [other_pack],
            )
            basics = [pack, other_pack] + [value for both in zip(mine, theirs) for value in both]
        else:
            all_rows, group = call(
                functools.partial(group_kernel, chips),
                "group",
                [rows_type(16 * chips), group_type],
                got,
            )
        across = exchange(group, "star")
        if step == 0:
            sums, ya, other_table = call(
                functools.partial(astro_other_kernel, chips),
                "astro",
                [sums_type, pair, table_type],
                keep + [own_sums],
                [pltpu.VMEM(wide, bf16)],
            )
        else:
            sums, ya = call(
                functools.partial(astro_kernel, chips),
                "astro",
                [sums_type, pair],
                keep + [own_table, other_table, all_rows],
                [pltpu.VMEM((2,) + wide, bf16)],
            )
        tall = ((comps * high + 16, LANES), f32)
        older = keep if step == 0 else [state, z, g, u, rows, gs]
        send, state, z, g, u, rows, gs = call(
            functools.partial(step_kernel, step, width, slots, chips, star_count),
            "step",
            [rows_type(32 if step < ITERS - 1 else 8), group_type, tall, tall, pair, pair,
             pair],
            basics + [sums, ya] + older + across,
        )
        solutions.append(z)
    (send,) = call(sum_kernel, "sum", [rows_type(8)], exchange(send, "tm"))
    across = exchange(send, "star")
    out_astro, out_att, out_inst = call(
        functools.partial(last_kernel, comps, share, star_count),
        "last",
        [((comps, share), f32), ((ATT_DEV // LANES, LANES), f32), ((NINST // LANES, LANES), f32)],
        [state] + across + solutions,
    )
    return out_astro, out_att.reshape(-1), out_inst.reshape(-1)


def solution(mesh):
    return jax.shard_map(
        per_device,
        mesh=mesh,
        in_specs=(
            P("star", None, "tm"),
            P("star", "tm"),
            P("star", "tm", None, None),
            P("star", "tm"),
            P("star", None, "tm"),
            P("star", None, "tm"),
            P("star", "tm"),
        ),
        out_specs=(P(None, ("star", "tm")), P("tm"), P()),
        check_vma=False,
    )
```

```python
import functools

import jax
import jax.numpy as jnp
from jax import lax
from jax.experimental import pallas as pl
from jax.experimental.pallas import tpu as pltpu
from jax.sharding import PartitionSpec as P

STARS_DEV = 2048
NINST = 1024
ITERS = 3
ATT_DEV = 256
LANES = 128

epsilon = 1e-06
f32 = jnp.float32
bf16 = jnp.bfloat16
VMEM_LIMIT = 16 * 1024 * 1024


def halves(value):
    top = value.astype(bf16).astype(f32)
    return top, (value - top).astype(bf16).astype(f32)


def dot_lanes(left, right):
    return lax.dot_general(left, right, (((1,), (1,)), ((), ())), preferred_element_type=f32)


def dot_plain(left, right):
    return lax.dot_general(left, right, (((1,), (0,)), ((), ())), preferred_element_type=f32)


def lane_pick(row, lane_index):
    table = jnp.broadcast_to(row, lane_index.shape)
    return jnp.take_along_axis(table, lane_index, axis=1, mode="promise_in_bounds")


def table_pick(rows, index):
    high, low = index >> 7, index & (LANES - 1)
    total = jnp.zeros(index.shape, f32)
    for place, row in enumerate(rows):
        total = jnp.where(high == place, lane_pick(row, low), total)
    return total


def one_hot_low(index_row):
    shape = (LANES, LANES)
    low = jnp.broadcast_to(index_row & (LANES - 1), shape)
    hit = lax.broadcasted_iota(jnp.int32, shape, 0) == low
    return jnp.where(hit, 1.0, 0.0).astype(bf16)


def spread_high(index_row, value_row, count):
    shape = (count, LANES)
    high = jnp.broadcast_to(index_row >> 7, shape)
    hit = lax.broadcasted_iota(jnp.int32, shape, 0) == high
    return jnp.where(hit, jnp.broadcast_to(value_row, shape), 0.0)


def block_masks(blocks, width):
    shape = (blocks, LANES)
    row = lax.broadcasted_iota(jnp.int32, shape, 0)
    lane = lax.broadcasted_iota(jnp.int32, shape, 1)
    per_tile = LANES // width
    tiles = blocks // per_tile
    return [row == tile * per_tile + lane // width for tile in range(tiles)], row, lane


def inst_back(rows, coef_ref, index_ref, table_ref, spread_ref):
    slots, blocks = len(coef_ref), rows.shape[0]
    count = NINST // LANES
    for slot in range(slots):
        top, rest = halves(coef_ref[slot][...] * rows)
        index = index_ref[slot][...]
        for block in range(blocks):
            here = slice(block, block + 1)
            pieces = [spread_high(index[here], part[here], count) for part in (top, rest)]
            at = (slot * blocks + block) * LANES
            spread_ref[:, at : at + LANES] = jnp.concatenate(pieces, axis=0).astype(bf16)
    both = dot_lanes(spread_ref[...], table_ref[...])
    return both[:count] + both[count:]


def att_back(rows, att2, starts, width):
    blocks = rows.shape[0]
    size = att2.shape[0] // 2
    top, rest = halves(rows)
    both = dot_lanes(jnp.concatenate([top, rest], axis=0).astype(bf16), att2)
    both = both[:blocks] + both[blocks:]
    both = both[:, :size] + both[:, size:]
    masks, row, lane = block_masks(blocks, width)
    own = jnp.zeros((blocks, LANES), f32)
    for tile, mask in enumerate(masks):
        own = own + jnp.where(mask, both[:, tile * LANES : (tile + 1) * LANES], 0.0)
    shift = (row % (LANES // width)) * width
    out = []
    for tile in range((ATT_DEV + width + LANES - 1) // LANES):
        offset = lane + tile * LANES - starts
        inside = (offset >= 0) & (offset < width)
        picked = jnp.take_along_axis(
            own, jnp.where(inside, offset + shift, 0), axis=1, mode="promise_in_bounds"
        )
        out.append(jnp.sum(jnp.where(inside, picked, 0.0), axis=0, keepdims=True))
    return jnp.concatenate(out, axis=0)


def att_forward(att_rows, att2, starts, width):
    blocks = starts.shape[0]
    masks, row, lane = block_masks(blocks, width)
    tiles = [att_rows[tile : tile + 1] for tile in range(att_rows.shape[0])]
    window = table_pick(tiles, starts + lane % width)
    wide = jnp.concatenate([jnp.where(mask, window, 0.0) for mask in masks], axis=1)
    top, rest = halves(wide)
    left = jnp.concatenate([top, rest], axis=0).astype(bf16)
    both = dot_plain(jnp.concatenate([left, left], axis=1), att2)
    return both[:blocks] + both[blocks:]


def pack_places(slots, blocks, width):
    at = slots * 8
    return slice(0, at), slice(at, 2 * at), slice(2 * at, 2 * at + 8), slice(
        2 * at + 8, 2 * at + 8 + blocks * width
    )


def prepare_index(index_rows, starts, table_ref, ints_ref):
    count = index_rows.shape[0] // 8
    ints_ref[0 : count * 8] = index_rows
    ints_ref[count * 8 :] = starts
    for place in range(count * 8):
        table_ref[:, place * LANES : (place + 1) * LANES] = one_hot_low(
            index_rows[place : place + 1]
        )


def prepare_att(att, att2_ref):
    top = att.astype(bf16)
    att2_ref[...] = jnp.concatenate([top, (att - top.astype(f32)).astype(bf16)], axis=0)


def first_kernel(width, b_hbm, astro_hbm, star_hbm, att_hbm, starts_hbm, coef_hbm, index_hbm,
                 send_ref, pack_ref, table_ref, att2_ref, ints_ref,
                 b_ref, astro_ref, star_ref, starts_ref, coef_ref, index_ref,
                 spread_ref, sems):
    slots, blocks, _ = index_ref.shape
    comps = astro_ref.shape[0]
    places = pack_places(slots, blocks, width)
    pairs = [(index_hbm, index_ref), (starts_hbm, starts_ref), (att_hbm, pack_ref.at[places[3]]),
             (coef_hbm, coef_ref), (b_hbm, b_ref), (astro_hbm, astro_ref), (star_hbm, star_ref)]
    copies = [
        pltpu.make_async_copy(source, target, sems.at[place])
        for place, (source, target) in enumerate(pairs)
    ]
    for copy in copies:
        copy.start()
    for copy in copies[:2]:
        copy.wait()
    index = jnp.concatenate([index_ref[slot] for slot in range(slots)], axis=0)
    starts_row = jnp.broadcast_to(starts_ref[...].astype(f32), (blocks, blocks))
    diagonal = lax.broadcasted_iota(jnp.int32, (blocks, blocks), 0) == lax.broadcasted_iota(
        jnp.int32, (blocks, blocks), 1
    )
    starts = jnp.sum(jnp.where(diagonal, starts_row, 0.0), axis=1, keepdims=True)
    starts = jnp.broadcast_to(starts, (blocks, LANES))
    pack_ref[places[1]] = index.astype(f32)
    pack_ref[places[2]] = starts
    starts = starts.astype(jnp.int32)
    prepare_index(index, starts, table_ref, ints_ref)
    for copy in copies[2:]:
        copy.wait()
    prepare_att(pack_ref[places[3]], att2_ref)
    rows = b_ref[...]
    coefs = [coef_ref.at[slot] for slot in range(slots)]
    indices = [index_ref.at[slot] for slot in range(slots)]
    for slot in range(slots):
        pack_ref[slot * 8 : slot * 8 + 8] = coef_ref[slot]
    send_ref[0:8] = rows
    send_ref[8:16] = inst_back(rows, coefs, indices, table_ref, spread_ref)
    send_ref[16:19] = att_back(rows, att2_ref[...], starts, width)
    send_ref[19:20] = jnp.sum(rows * rows, axis=0, keepdims=True)
    send_ref[20:24] = jnp.zeros((4, LANES), f32)
    for comp in range(comps):
        send_ref[24 + comp * 8 : 32 + comp * 8] = astro_ref[comp]
    send_ref[24 + comps * 8 : 32 + comps * 8] = star_ref[...].astype(f32)


def prepare_kernel(slots, blocks, width, pack_ref, table_ref, att2_ref, ints_ref):
    places = pack_places(slots, blocks, width)
    index = pack_ref[places[1]].astype(jnp.int32)
    starts = pack_ref[places[2]].astype(jnp.int32)
    prepare_index(index, starts, table_ref, ints_ref)
    prepare_att(pack_ref[places[3]], att2_ref)


def tree_sum(values):
    while len(values) > 1:
        values = [values[i] + values[i + 1] for i in range(0, len(values), 2)]
    return values[0]


def first_chip_kernel(count, *refs):
    ins, out_ref = refs[:count], refs[count]
    chip = lax.axis_index("tm") // 2
    size = ins[0].shape[0]
    for gap in range(count):
        at = pl.multiple_of((chip ^ gap) * size, 8)
        out_ref[pl.ds(at, size)] = ins[gap][...]


def group_rows(chip, count, mine, prev_row, after_row):
    half = lax.broadcasted_iota(jnp.int32, (1, LANES), 1) < 64
    first = mine[0:1] + jnp.where(half & (chip > 0), prev_row, 0.0)
    last = jnp.where(half & (chip < count - 1), mine[4:5] + after_row, 0.0)
    return [first, mine[1:4], last]


def chip_parts(core, own, other):
    low = jnp.where(core == 0, own, other)
    top = jnp.where(core == 0, other, own)
    return jnp.concatenate([low[0:2], low[2:3] + top[0:1], top[1:3]], axis=0)


def first_group_kernel(count, own_ref, other_ref, out_ref):
    me = lax.axis_index("tm")
    chip, core = me // 2, me % 2
    size = own_ref.shape[0] // count

    def part(ref, where, start):
        where = jnp.clip(where, 0, count - 1)
        return ref[pl.ds(pl.multiple_of(where * size + start, 8), 8)]

    def of_core(which, where):
        mine = (core == which) == (where == chip)
        return jnp.where(mine, part(own_ref, where, 16), part(other_ref, where, 16))

    def total(start):
        return tree_sum(
            [part(own_ref, chip ^ gap, start) + part(other_ref, chip ^ gap, start) for gap in range(count)]
        )

    mine = chip_parts(core, part(own_ref, chip, 16)[0:3], part(other_ref, chip, 16)[0:3])
    prev, after = of_core(1, chip - 1), of_core(0, chip + 1)
    out_ref[0:8] = total(8)
    att = group_rows(chip, count, mine, prev[2:3], after[0:1])
    out_ref[8:16] = jnp.concatenate(att + [total(16)[3:6]], axis=0)


def group_kernel(count, *refs):
    *ins, rows_ref, out_ref = refs
    me = lax.axis_index("tm")
    chip = me // 2
    places = [chip ^ gap for gap in range(count)]
    zero = jnp.zeros((8, LANES), f32)
    mine, prev, after = zero, zero, zero
    for ref, where in zip(ins, places):
        for half in range(2):
            at = pl.multiple_of((half * count + where) * 8, 8)
            rows_ref[pl.ds(at, 8)] = ref[half * 8 : half * 8 + 8]
        low = ref[24:32]
        mine = jnp.where(where == chip, low, mine)
        prev = jnp.where(where == chip - 1, low, prev)
        after = jnp.where(where == chip + 1, low, after)
    scalars = tree_sum([ref[24:32] for ref in ins])
    out_ref[0:8] = tree_sum([ref[16:24] for ref in ins])
    att = group_rows(chip, count, mine, prev[4:5], after[0:1])
    out_ref[8:16] = jnp.concatenate(att + [scalars[5:8]], axis=0)


def kept(count, keep_ref):
    size = keep_ref.shape[0] // count
    return size, size - 24, (size - 24) // 8 - 1


def star_sums(count, place, keep_ref, rows, table_ref, spread_ref, build):
    high = STARS_DEV // LANES
    size, extra, comps = kept(count, keep_ref)
    long = 8 * LANES
    packed = keep_ref[pl.ds(pl.multiple_of(place * size + 24, 8), extra)]
    index = packed[comps * 8 :].astype(jnp.int32)
    at0 = pl.multiple_of(place * long, long)
    split = [halves(packed[comp * 8 : comp * 8 + 8] * rows) for comp in range(comps)]
    for block in range(8):
        here = slice(block, block + 1)
        if build:
            table_ref[:, pl.ds(at0 + block * LANES, LANES)] = one_hot_low(index[here])
        pieces = []
        for part in range(2):
            for comp in range(comps):
                pieces.append(spread_high(index[here], split[comp][part][here], high))
        spread_ref[:, block * LANES : (block + 1) * LANES] = jnp.concatenate(
            pieces, axis=0
        ).astype(bf16)
    return dot_lanes(spread_ref[...], table_ref[:, pl.ds(at0, long)])


def star_rows(count, keep_ref, sums):
    high = STARS_DEV // LANES
    size, extra, comps = kept(count, keep_ref)
    chip = lax.axis_index("tm") // 2
    packed = keep_ref[pl.ds(pl.multiple_of(chip * size + 24, 8), extra)]
    star = packed[comps * 8 :].astype(jnp.int32)
    star_high, star_low = star >> 7, star & (LANES - 1)
    total = jnp.zeros((8, LANES), f32)
    for comp in range(comps):
        picked = jnp.zeros((8, LANES), f32)
        for place in range(high):
            at = comp * high + place
            picked = jnp.where(star_high == place, lane_pick(sums[at : at + 1], star_low), picked)
        total = total + packed[comp * 8 : comp * 8 + 8] * picked
    return total


def first_sums(count, keep_ref, table_ref, spread_ref):
    size = spread_ref.shape[0]

    def one(place, total):
        rows = keep_ref[pl.ds(pl.multiple_of(place * kept(count, keep_ref)[0], 8), 8)]
        return total + star_sums(count, place, keep_ref, rows, table_ref, spread_ref, True)

    total = lax.fori_loop(0, count, one, jnp.zeros((size, LANES), f32))
    return total[: size // 2] + total[size // 2 :]


def astro_own_kernel(count, keep_ref, out_ref, table_ref, spread_ref):
    out_ref[...] = first_sums(count, keep_ref, table_ref, spread_ref)


def astro_other_kernel(count, own_ref, keep_ref, part_ref, out_ref, ya_ref, table_ref, spread_ref):
    total = part_ref[...] + first_sums(count, keep_ref, table_ref, spread_ref)
    out_ref[...] = total
    ya_ref[0:8] = star_rows(count, own_ref, total)
    ya_ref[8:16] = star_rows(count, keep_ref, total)


def astro_kernel(count, own_ref, other_ref, own_table, other_table, rows_ref, out_ref, ya_ref,
                 spread_ref):
    me = lax.axis_index("tm")
    size = spread_ref.shape[1]
    sources = ((own_ref, own_table), (other_ref, other_table))

    def one(place, totals):
        new = []
        for half, (keep_ref, table_ref) in enumerate(sources):
            core = half ^ (me % 2) ^ jnp.where(place == me // 2, 0, 1)
            at = (core * count + place) * 8
            rows = rows_ref[pl.ds(pl.multiple_of(at, 8), 8)]
            part = star_sums(count, place, keep_ref, rows, table_ref, spread_ref.at[half], False)
            new.append(totals[half] + part)
        return tuple(new)

    zero = jnp.zeros((size, LANES), f32)
    own, other = lax.fori_loop(0, count, one, (zero, zero))
    total = own + other
    total = total[: size // 2] + total[size // 2 :]
    out_ref[...] = total
    ya_ref[0:8] = star_rows(count, own_ref, total)
    ya_ref[8:16] = star_rows(count, other_ref, total)


def sum_kernel(*refs):
    refs[-1][...] = tree_sum([ref[...] for ref in refs[:-1]])


def lane_sum(row):
    return jnp.broadcast_to(jnp.sum(row, axis=1, keepdims=True), row.shape)


def next_bidiagonal(total, state):
    squares, mixed, size = (lane_sum(total[row : row + 1]) for row in (13, 14, 15))
    alpha2 = size + epsilon
    alpha = jnp.sqrt(alpha2)
    rest = jnp.maximum(squares / alpha2 - 2.0 * mixed + alpha2 * state[0:1], 0.0)
    beta2 = rest + epsilon
    return alpha, jnp.sqrt(beta2), rest / beta2


def step_kernel(step, width, slots, chips, star_count, *refs):
    packs, tables, att2s, ints = refs[0:2], refs[2:4], refs[4:6], refs[6:8]
    sum_ref, ya_ref, refs = refs[8], refs[9], refs[10:]
    if step > 0:
        state_ref, old_z_ref, old_g_ref, old_u_ref, old_s_ref, old_gs_ref = refs[:6]
        refs = refs[6:]
    else:
        keep, refs = refs[:2], refs[2:]
    gathered, refs = refs[:-8], refs[-8:]
    send_ref, state_out, z_ref, g_ref, u_ref, s_ref, gs_ref, spread_ref = refs
    me = lax.axis_index("tm")
    chip, core = me // 2, me % 2
    high = STARS_DEV // LANES
    comps = sum_ref.shape[0] // high
    blocks = 8
    total = tree_sum([ref[...] for ref in gathered])
    back = jnp.concatenate([sum_ref[...], total], axis=0)
    base = comps * high
    pieces = [total[place : place + 1] for place in range(8)]
    att_back_rows = total[8:13]
    forward, starts, coefs, indices = [], [], [], []
    for half in range(2):
        starts.append(ints[half][slots * 8 :])
        own = jnp.where(core == half, att_back_rows[0:3], att_back_rows[2:5])
        part = att_forward(own, att2s[half][...], starts[half], width)
        part = part + ya_ref[half * 8 : half * 8 + 8]
        coefs.append([packs[half].at[slot * 8 : slot * 8 + 8] for slot in range(slots)])
        indices.append([ints[half].at[slot * 8 : slot * 8 + 8] for slot in range(slots)])
        for slot in range(slots):
            part = part + coefs[half][slot][...] * table_pick(pieces, indices[half][slot][...])
        forward.append(part)
    forward = jnp.concatenate(forward, axis=0)
    if step == 0:
        squares = lane_sum(total[13:14])
        beta2 = squares + epsilon
        beta = jnp.sqrt(beta2)
        at = pl.ds(pl.multiple_of(chip * kept(chips, keep[0])[0], 8), 8)
        u = jnp.concatenate([ref[at] for ref in keep], axis=0) / beta
        g = back / beta
        z = g
        gs = forward / beta
        both = gs
        state_out[...] = jnp.concatenate(
            [squares / beta2, beta, jnp.zeros((14, LANES), f32)], axis=0
        )
    else:
        state = state_ref[...]
        alpha, beta, left2 = next_bidiagonal(total, state)
        u = (old_s_ref[...] / alpha - alpha * old_u_ref[...]) / beta
        g = (back / alpha - alpha * old_g_ref[...]) / beta
        z = g - (beta / alpha) * old_z_ref[...]
        gs = (forward / alpha - alpha * old_gs_ref[...]) / beta
        both = gs - (beta / alpha) * old_s_ref[...]
        pieces = [left2, state[1 : 1 + step], beta, jnp.zeros((7 - step, LANES), f32)]
        pieces += [state[9 : 8 + step]] if step > 1 else []
        pieces += [alpha, jnp.zeros((7 - step, LANES), f32)]
        state_out[...] = jnp.concatenate(pieces, axis=0)
    z_ref[...] = z
    g_ref[...] = g
    u_ref[...] = u
    gs_ref[...] = gs
    s_ref[...] = both
    inst_rows = z[base : base + 8]
    att_rows = z[base + 8 : base + 13]
    rows = [both[0:8], both[8:16]]
    insts, atts = [], []
    for half in range(2):
        if step < ITERS - 1:
            insts.append(
                inst_back(rows[half], coefs[half], indices[half], tables[half], spread_ref.at[half])
            )
            atts.append(att_back(rows[half], att2s[half][...], starts[half], width))

    def squared(value):
        return jnp.sum(value * value, axis=0, keepdims=True)

    size = squared(z[:base]) * (1.0 / chips) + squared(att_rows[:4]) * (1.0 / star_count)
    size = size + squared(inst_rows) * (1.0 / (star_count * chips))
    mixed = [jnp.sum(rows[half] * u[half * 8 : half * 8 + 8], axis=0, keepdims=True) for half in range(2)]
    scalars = [squared(rows[0]) + squared(rows[1]), mixed[0] + mixed[1], size]
    if step == ITERS - 1:
        send_ref[...] = jnp.concatenate([jnp.zeros((5, LANES), f32)] + scalars, axis=0)
        return
    send_ref[0:16] = jnp.where(core == 0, both, jnp.concatenate(rows[::-1], axis=0))
    send_ref[16:24] = insts[0] + insts[1]
    send_ref[24:32] = jnp.concatenate([chip_parts(core, *atts)] + scalars, axis=0)


def last_kernel(comps, share, star_count, state_ref, *refs):
    gathered, refs = refs[: -ITERS - 3], refs[-ITERS - 3 :]
    z_refs = refs[:ITERS]
    astro_ref, att_ref, inst_ref = refs[ITERS:]
    high = STARS_DEV // LANES
    me = lax.axis_index("tm")
    total = tree_sum([ref[...] for ref in gathered])
    total = jnp.concatenate([jnp.zeros((8, LANES), f32), total], axis=0)
    state = state_ref[...]
    alpha, beta, _ = next_bidiagonal(total, state)
    betas = [state[1 + k : 2 + k] for k in range(ITERS)] + [beta]
    alphas = [state[9 + k : 10 + k] for k in range(ITERS - 1)] + [alpha]
    rho_bar, phi_bar = alphas[0], betas[0]
    weights = [jnp.zeros((1, LANES), f32)] * ITERS
    search = [jnp.zeros((1, LANES), f32)] * ITERS
    search[0] = 1.0 / alphas[0]
    for k in range(ITERS):
        rho = jnp.sqrt(rho_bar * rho_bar + betas[k + 1] * betas[k + 1])
        cosine, sine = rho_bar / rho, betas[k + 1] / rho
        phi = cosine * phi_bar
        phi_bar = sine * phi_bar
        weights = [x + phi / rho * w for x, w in zip(weights, search)]
        if k + 1 < ITERS:
            theta = sine * alphas[k + 1]
            rho_bar = -cosine * alphas[k + 1]
            search = [-(theta / rho) * w for w in search]
            search[k + 1] = 1.0 / alphas[k + 1]
    base = comps * high
    tiles = share // LANES

    def mix(read):
        total = weights[0] * read(z_refs[0])
        for k in range(1, ITERS):
            total = total + weights[k] * read(z_refs[k])
        return total

    for comp in range(comps):
        for tile in range(tiles):
            at = comp * high + me * tiles + tile
            astro_ref[comp : comp + 1, tile * LANES : (tile + 1) * LANES] = mix(
                lambda ref: ref[pl.ds(at, 1)]
            )
    inst_ref[...] = mix(lambda ref: ref[base : base + 8])
    rows = ATT_DEV // LANES
    att_ref[...] = mix(lambda ref: ref[pl.ds(base + 8 + (me % 2) * rows, rows)])


def call(kernel, name, out, args, scratch=(), space=pltpu.VMEM):
    vmem = pl.BlockSpec(memory_space=pltpu.VMEM)
    return pl.pallas_call(
        kernel,
        name=name,
        out_shape=[jax.ShapeDtypeStruct(shape, dtype) for shape, dtype in out],
        in_specs=[pl.BlockSpec(memory_space=space)] * len(args),
        out_specs=[vmem] * len(out),
        scratch_shapes=list(scratch),
        compiler_params=pltpu.CompilerParams(vmem_limit_bytes=VMEM_LIMIT),
    )(*args)


def direct(value, axis, gaps):
    count = lax.axis_size(axis)
    return [value] + [
        lax.ppermute(value, axis, [(i, i ^ gap) for i in range(count)]) for gap in gaps
    ]


def exchange(value, axis):
    tm_count, star_count = lax.axis_size("tm"), lax.axis_size("star")
    got = [value]
    for gap in range(1, star_count if axis == "star" else tm_count // 2):
        steps = []
        for star in range(star_count):
            for tm in range(tm_count):
                far = (star ^ gap, tm ^ 1) if axis == "star" else (star, tm ^ (2 * gap + 1))
                steps.append((star * tm_count + tm, far[0] * tm_count + far[1]))
        got.append(lax.ppermute(value, ("star", "tm"), steps))
    return got


def rows_type(rows):
    return ((rows, LANES), f32)


def per_device(astro_coef, star_index, att_coef, att_start, inst_coef, inst_index, observed):
    tm_count, star_count = lax.axis_size("tm"), lax.axis_size("star")
    comps = astro_coef.shape[1]
    slots = inst_coef.shape[1]
    blocks, width, height = att_coef.shape[1:]
    share = STARS_DEV // tm_count
    high = STARS_DEV // LANES
    chips = tm_count // 2
    args = [
        observed.reshape(blocks, height),
        astro_coef.reshape(comps, blocks, height),
        star_index.reshape(blocks, height),
        att_coef.reshape(blocks * width, height),
        att_start,
        inst_coef.reshape(slots, blocks, height),
        inst_index.reshape(slots, blocks, height),
    ]
    long = slots * blocks * height
    extra = 8 * comps + 8
    spread = pltpu.VMEM((16, long), bf16)
    prepared = [((LANES, long), bf16), ((2 * blocks * width, height), bf16),
                ((8 * slots + 8, LANES), jnp.int32)]
    here = [pltpu.with_memory_space_constraint(arg, pltpu.HBM) for arg in args]
    send, pack, *mine = call(
        functools.partial(first_kernel, width),
        "first",
        [((24 + extra, LANES), f32), ((16 * slots + 8 + blocks * width, LANES), f32)] + prepared,
        here,
        [pltpu.VMEM(arg.shape, arg.dtype) for arg in args if arg is not args[3]]
        + [spread, pltpu.SemaphoreType.DMA((len(args),))],
        pl.ANY,
    )
    state = z = g = u = rows = gs = None
    solutions = []
    group_type = rows_type(16)
    for step in range(ITERS):
        wide = (2 * comps * high, blocks * height)
        sums_type = rows_type(comps * high)
        pair = rows_type(2 * blocks)
        got = exchange(send, "tm")
        if step == 0:
            (gathered,) = call(
                functools.partial(first_chip_kernel, chips),
                "chip",
                [rows_type(chips * (24 + extra))],
                got,
            )
            keep = direct(gathered, "tm", [1])
            table_type = ((LANES, chips * blocks * height), bf16)
            own_sums, own_table = call(
                functools.partial(astro_own_kernel, chips),
                "astro_own",
                [sums_type, table_type],
                [gathered],
                [pltpu.VMEM(wide, bf16)],
            )
            own_sums, late_pack = lax.optimization_barrier((own_sums, pack))
            keep[1], own_sums = lax.optimization_barrier((keep[1], own_sums))
            (group,) = call(
                functools.partial(first_group_kernel, chips), "group", [group_type], keep
            )
            _, other_pack = direct(late_pack, "tm", [1])
            theirs = call(
                functools.partial(prepare_kernel, slots, blocks, width),
                "prepare",
                prepared,
                [other_pack],
            )
            basics = [pack, other_pack] + [value for both in zip(mine, theirs) for value in both]
        else:
            all_rows, group = call(
                functools.partial(group_kernel, chips),
                "group",
                [rows_type(16 * chips), group_type],
                got,
            )
        across = exchange(group, "star")
        if step == 0:
            sums, ya, other_table = call(
                functools.partial(astro_other_kernel, chips),
                "astro",
                [sums_type, pair, table_type],
                keep + [own_sums],
                [pltpu.VMEM(wide, bf16)],
            )
        else:
            sums, ya = call(
                functools.partial(astro_kernel, chips),
                "astro",
                [sums_type, pair],
                keep + [own_table, other_table, all_rows],
                [pltpu.VMEM((2,) + wide, bf16)],
            )
        tall = ((comps * high + 16, LANES), f32)
        older = keep if step == 0 else [state, z, g, u, rows, gs]
        send, state, z, g, u, rows, gs = call(
            functools.partial(step_kernel, step, width, slots, chips, star_count),
            "step",
            [rows_type(32 if step < ITERS - 1 else 8), group_type, tall, tall, pair, pair,
             pair],
            basics + [sums, ya] + older + across,
            [pltpu.VMEM((2, 16, long), bf16)],
        )
        solutions.append(z)
    (send,) = call(sum_kernel, "sum", [rows_type(8)], exchange(send, "tm"))
    across = exchange(send, "star")
    out_astro, out_att, out_inst = call(
        functools.partial(last_kernel, comps, share, star_count),
        "last",
        [((comps, share), f32), ((ATT_DEV // LANES, LANES), f32), ((NINST // LANES, LANES), f32)],
        [state] + across + solutions,
    )
    return out_astro, out_att.reshape(-1), out_inst.reshape(-1)


def solution(mesh):
    return jax.shard_map(
        per_device,
        mesh=mesh,
        in_specs=(
            P("star", None, "tm"),
            P("star", "tm"),
            P("star", "tm", None, None),
            P("star", "tm"),
            P("star", None, "tm"),
            P("star", None, "tm"),
            P("star", "tm"),
        ),
        out_specs=(P(None, ("star", "tm")), P("tm"), P()),
        check_vma=False,
    )
```

```python
import functools

import jax
import jax.numpy as jnp
from jax import lax
from jax.experimental import pallas as pl
from jax.experimental.pallas import tpu as pltpu
from jax.sharding import PartitionSpec as P

STARS_DEV = 2048
NINST = 1024
ITERS = 3
ATT_DEV = 256
LANES = 128

epsilon = 1e-06
f32 = jnp.float32
bf16 = jnp.bfloat16
VMEM_LIMIT = 16 * 1024 * 1024


def halves(value):
    top = value.astype(bf16).astype(f32)
    return top, (value - top).astype(bf16).astype(f32)


def dot_lanes(left, right):
    return lax.dot_general(left, right, (((1,), (1,)), ((), ())), preferred_element_type=f32)


def dot_plain(left, right):
    return lax.dot_general(left, right, (((1,), (0,)), ((), ())), preferred_element_type=f32)


def lane_pick(row, lane_index):
    table = jnp.broadcast_to(row, lane_index.shape)
    return jnp.take_along_axis(table, lane_index, axis=1, mode="promise_in_bounds")


def table_pick(rows, index):
    high, low = index >> 7, index & (LANES - 1)
    total = jnp.zeros(index.shape, f32)
    for place, row in enumerate(rows):
        total = jnp.where(high == place, lane_pick(row, low), total)
    return total


def one_hot_low(index_row):
    shape = (LANES, LANES)
    low = jnp.broadcast_to(index_row & (LANES - 1), shape)
    hit = lax.broadcasted_iota(jnp.int32, shape, 0) == low
    return jnp.where(hit, 1.0, 0.0).astype(bf16)


def spread_high(index_row, value_row, count):
    shape = (count, LANES)
    high = jnp.broadcast_to(index_row >> 7, shape)
    hit = lax.broadcasted_iota(jnp.int32, shape, 0) == high
    return jnp.where(hit, jnp.broadcast_to(value_row, shape), 0.0)


def block_masks(blocks, width):
    shape = (blocks, LANES)
    row = lax.broadcasted_iota(jnp.int32, shape, 0)
    lane = lax.broadcasted_iota(jnp.int32, shape, 1)
    per_tile = LANES // width
    tiles = blocks // per_tile
    return [row == tile * per_tile + lane // width for tile in range(tiles)], row, lane


def inst_back(rows, coef_ref, index_ref, table_ref, spread_ref):
    slots, blocks = len(coef_ref), rows.shape[0]
    count = NINST // LANES
    for slot in range(slots):
        top, rest = halves(coef_ref[slot][...] * rows)
        index = index_ref[slot][...]
        for block in range(blocks):
            here = slice(block, block + 1)
            pieces = [spread_high(index[here], part[here], count) for part in (top, rest)]
            at = (slot * blocks + block) * LANES
            spread_ref[:, at : at + LANES] = jnp.concatenate(pieces, axis=0).astype(bf16)
    both = dot_lanes(spread_ref[...], table_ref[...])
    return both[:count] + both[count:]


def att_back(rows, att2, starts, width):
    blocks = rows.shape[0]
    size = att2.shape[0] // 2
    top, rest = halves(rows)
    both = dot_lanes(jnp.concatenate([top, rest], axis=0).astype(bf16), att2)
    both = both[:blocks] + both[blocks:]
    both = both[:, :size] + both[:, size:]
    masks, row, lane = block_masks(blocks, width)
    own = jnp.zeros((blocks, LANES), f32)
    for tile, mask in enumerate(masks):
        own = own + jnp.where(mask, both[:, tile * LANES : (tile + 1) * LANES], 0.0)
    shift = (row % (LANES // width)) * width
    out = []
    for tile in range((ATT_DEV + width + LANES - 1) // LANES):
        offset = lane + tile * LANES - starts
        inside = (offset >= 0) & (offset < width)
        picked = jnp.take_along_axis(
            own, jnp.where(inside, offset + shift, 0), axis=1, mode="promise_in_bounds"
        )
        out.append(jnp.sum(jnp.where(inside, picked, 0.0), axis=0, keepdims=True))
    return jnp.concatenate(out, axis=0)


def att_forward(att_rows, att2, starts, width):
    blocks = starts.shape[0]
    masks, row, lane = block_masks(blocks, width)
    tiles = [att_rows[tile : tile + 1] for tile in range(att_rows.shape[0])]
    window = table_pick(tiles, starts + lane % width)
    wide = jnp.concatenate([jnp.where(mask, window, 0.0) for mask in masks], axis=1)
    top, rest = halves(wide)
    left = jnp.concatenate([top, rest], axis=0).astype(bf16)
    both = dot_plain(jnp.concatenate([left, left], axis=1), att2)
    return both[:blocks] + both[blocks:]


def pack_places(slots, blocks, width):
    at = slots * 8
    return slice(0, at), slice(at, 2 * at), slice(2 * at, 2 * at + 8), slice(
        2 * at + 8, 2 * at + 8 + blocks * width
    )


def prepare_index(index_rows, starts, table_ref, ints_ref):
    count = index_rows.shape[0] // 8
    ints_ref[0 : count * 8] = index_rows
    ints_ref[count * 8 :] = starts
    for place in range(count * 8):
        table_ref[:, place * LANES : (place + 1) * LANES] = one_hot_low(
            index_rows[place : place + 1]
        )


def prepare_att(att, att2_ref):
    top = att.astype(bf16)
    att2_ref[...] = jnp.concatenate([top, (att - top.astype(f32)).astype(bf16)], axis=0)


def first_kernel(width, b_hbm, astro_hbm, star_hbm, att_hbm, starts_hbm, coef_hbm, index_hbm,
                 send_ref, pack_ref, table_ref, att2_ref, ints_ref,
                 b_ref, astro_ref, star_ref, starts_ref, coef_ref, index_ref,
                 spread_ref, sems):
    slots, blocks, _ = index_ref.shape
    comps = astro_ref.shape[0]
    places = pack_places(slots, blocks, width)
    pairs = [(index_hbm, index_ref), (starts_hbm, starts_ref), (att_hbm, pack_ref.at[places[3]]),
             (coef_hbm, coef_ref), (b_hbm, b_ref), (astro_hbm, astro_ref), (star_hbm, star_ref)]
    copies = [
        pltpu.make_async_copy(source, target, sems.at[place])
        for place, (source, target) in enumerate(pairs)
    ]
    for copy in copies:
        copy.start()
    for copy in copies[:2]:
        copy.wait()
    index = jnp.concatenate([index_ref[slot] for slot in range(slots)], axis=0)
    starts_row = jnp.broadcast_to(starts_ref[...].astype(f32), (blocks, blocks))
    diagonal = lax.broadcasted_iota(jnp.int32, (blocks, blocks), 0) == lax.broadcasted_iota(
        jnp.int32, (blocks, blocks), 1
    )
    starts = jnp.sum(jnp.where(diagonal, starts_row, 0.0), axis=1, keepdims=True)
    starts = jnp.broadcast_to(starts, (blocks, LANES))
    pack_ref[places[1]] = index.astype(f32)
    pack_ref[places[2]] = starts
    starts = starts.astype(jnp.int32)
    prepare_index(index, starts, table_ref, ints_ref)
    for copy in copies[2:]:
        copy.wait()
    prepare_att(pack_ref[places[3]], att2_ref)
    rows = b_ref[...]
    coefs = [coef_ref.at[slot] for slot in range(slots)]
    indices = [index_ref.at[slot] for slot in range(slots)]
    for slot in range(slots):
        pack_ref[slot * 8 : slot * 8 + 8] = coef_ref[slot]
    send_ref[0:8] = rows
    send_ref[8:16] = inst_back(rows, coefs, indices, table_ref, spread_ref)
    send_ref[16:19] = att_back(rows, att2_ref[...], starts, width)
    send_ref[19:20] = jnp.sum(rows * rows, axis=0, keepdims=True)
    send_ref[20:24] = jnp.zeros((4, LANES), f32)
    for comp in range(comps):
        send_ref[24 + comp * 8 : 32 + comp * 8] = astro_ref[comp]
    send_ref[24 + comps * 8 : 32 + comps * 8] = star_ref[...].astype(f32)


def prepare_kernel(slots, blocks, width, pack_ref, table_ref, att2_ref, ints_ref):
    places = pack_places(slots, blocks, width)
    index = pack_ref[places[1]].astype(jnp.int32)
    starts = pack_ref[places[2]].astype(jnp.int32)
    prepare_index(index, starts, table_ref, ints_ref)
    prepare_att(pack_ref[places[3]], att2_ref)


def tree_sum(values):
    while len(values) > 1:
        values = [values[i] + values[i + 1] for i in range(0, len(values), 2)]
    return values[0]


def first_chip_kernel(count, *refs):
    ins, out_ref = refs[:count], refs[count]
    chip = lax.axis_index("tm") // 2
    size = ins[0].shape[0]
    for gap in range(count):
        at = pl.multiple_of((chip ^ gap) * size, 8)
        out_ref[pl.ds(at, size)] = ins[gap][...]


def group_rows(chip, count, mine, prev_row, after_row):
    half = lax.broadcasted_iota(jnp.int32, (1, LANES), 1) < 64
    first = mine[0:1] + jnp.where(half & (chip > 0), prev_row, 0.0)
    last = jnp.where(half & (chip < count - 1), mine[4:5] + after_row, 0.0)
    return [first, mine[1:4], last]


def chip_parts(core, own, other):
    low = jnp.where(core == 0, own, other)
    top = jnp.where(core == 0, other, own)
    return jnp.concatenate([low[0:2], low[2:3] + top[0:1], top[1:3]], axis=0)


def first_group_kernel(count, own_ref, other_ref, out_ref):
    me = lax.axis_index("tm")
    chip, core = me // 2, me % 2
    size = own_ref.shape[0] // count

    def part(ref, where, start):
        where = jnp.clip(where, 0, count - 1)
        return ref[pl.ds(pl.multiple_of(where * size + start, 8), 8)]

    def of_core(which, where):
        mine = (core == which) == (where == chip)
        return jnp.where(mine, part(own_ref, where, 16), part(other_ref, where, 16))

    def total(start):
        return tree_sum(
            [part(own_ref, chip ^ gap, start) + part(other_ref, chip ^ gap, start) for gap in range(count)]
        )

    mine = chip_parts(core, part(own_ref, chip, 16)[0:3], part(other_ref, chip, 16)[0:3])
    prev, after = of_core(1, chip - 1), of_core(0, chip + 1)
    out_ref[0:8] = total(8)
    att = group_rows(chip, count, mine, prev[2:3], after[0:1])
    out_ref[8:16] = jnp.concatenate(att + [total(16)[3:6]], axis=0)


def group_kernel(count, *refs):
    *ins, rows_ref, out_ref = refs
    me = lax.axis_index("tm")
    chip = me // 2
    places = [chip ^ gap for gap in range(count)]
    zero = jnp.zeros((8, LANES), f32)
    mine, prev, after = zero, zero, zero
    for ref, where in zip(ins, places):
        for half in range(2):
            at = pl.multiple_of((half * count + where) * 8, 8)
            rows_ref[pl.ds(at, 8)] = ref[half * 8 : half * 8 + 8]
        low = ref[24:32]
        mine = jnp.where(where == chip, low, mine)
        prev = jnp.where(where == chip - 1, low, prev)
        after = jnp.where(where == chip + 1, low, after)
    scalars = tree_sum([ref[24:32] for ref in ins])
    out_ref[0:8] = tree_sum([ref[16:24] for ref in ins])
    att = group_rows(chip, count, mine, prev[4:5], after[0:1])
    out_ref[8:16] = jnp.concatenate(att + [scalars[5:8]], axis=0)


def kept(count, keep_ref):
    size = keep_ref.shape[0] // count
    return size, size - 24, (size - 24) // 8 - 1


def star_sums(count, place, keep_ref, rows, table_ref, spread_ref, build):
    high = STARS_DEV // LANES
    size, extra, comps = kept(count, keep_ref)
    long = 8 * LANES
    packed = keep_ref[pl.ds(pl.multiple_of(place * size + 24, 8), extra)]
    index = packed[comps * 8 :].astype(jnp.int32)
    at0 = pl.multiple_of(place * long, long)
    split = [halves(packed[comp * 8 : comp * 8 + 8] * rows) for comp in range(comps)]
    for block in range(8):
        here = slice(block, block + 1)
        if build:
            table_ref[:, pl.ds(at0 + block * LANES, LANES)] = one_hot_low(index[here])
        pieces = []
        for part in range(2):
            for comp in range(comps):
                pieces.append(spread_high(index[here], split[comp][part][here], high))
        spread_ref[:, block * LANES : (block + 1) * LANES] = jnp.concatenate(
            pieces, axis=0
        ).astype(bf16)
    return dot_lanes(spread_ref[...], table_ref[:, pl.ds(at0, long)])


def star_rows(count, keep_ref, sums):
    high = STARS_DEV // LANES
    size, extra, comps = kept(count, keep_ref)
    chip = lax.axis_index("tm") // 2
    packed = keep_ref[pl.ds(pl.multiple_of(chip * size + 24, 8), extra)]
    star = packed[comps * 8 :].astype(jnp.int32)
    star_high, star_low = star >> 7, star & (LANES - 1)
    total = jnp.zeros((8, LANES), f32)
    for comp in range(comps):
        picked = jnp.zeros((8, LANES), f32)
        for place in range(high):
            at = comp * high + place
            picked = jnp.where(star_high == place, lane_pick(sums[at : at + 1], star_low), picked)
        total = total + packed[comp * 8 : comp * 8 + 8] * picked
    return total


def first_sums(count, keep_ref, table_ref, spread_ref):
    size = spread_ref.shape[0]

    def one(place, total):
        rows = keep_ref[pl.ds(pl.multiple_of(place * kept(count, keep_ref)[0], 8), 8)]
        return total + star_sums(count, place, keep_ref, rows, table_ref, spread_ref, True)

    total = lax.fori_loop(0, count, one, jnp.zeros((size, LANES), f32))
    return total[: size // 2] + total[size // 2 :]


def astro_own_kernel(count, keep_ref, out_ref, table_ref, spread_ref):
    out_ref[...] = first_sums(count, keep_ref, table_ref, spread_ref)


def astro_other_kernel(count, own_ref, keep_ref, part_ref, out_ref, ya_ref, table_ref, spread_ref):
    total = part_ref[...] + first_sums(count, keep_ref, table_ref, spread_ref)
    out_ref[...] = total
    ya_ref[0:8] = star_rows(count, own_ref, total)
    ya_ref[8:16] = star_rows(count, keep_ref, total)


def astro_kernel(count, own_ref, other_ref, own_table, other_table, rows_ref, out_ref, ya_ref,
                 spread_ref):
    me = lax.axis_index("tm")
    size = spread_ref.shape[1]
    sources = ((own_ref, own_table), (other_ref, other_table))

    def one(place, totals):
        new = []
        for half, (keep_ref, table_ref) in enumerate(sources):
            core = half ^ (me % 2) ^ jnp.where(place == me // 2, 0, 1)
            at = (core * count + place) * 8
            rows = rows_ref[pl.ds(pl.multiple_of(at, 8), 8)]
            part = star_sums(count, place, keep_ref, rows, table_ref, spread_ref.at[half], False)
            new.append(totals[half] + part)
        return tuple(new)

    zero = jnp.zeros((size, LANES), f32)
    own, other = lax.fori_loop(0, count, one, (zero, zero))
    total = own + other
    total = total[: size // 2] + total[size // 2 :]
    out_ref[...] = total
    ya_ref[0:8] = star_rows(count, own_ref, total)
    ya_ref[8:16] = star_rows(count, other_ref, total)


def sum_kernel(*refs):
    refs[-1][...] = tree_sum([ref[...] for ref in refs[:-1]])


def lane_sum(row):
    return jnp.broadcast_to(jnp.sum(row, axis=1, keepdims=True), row.shape)


def next_bidiagonal(total, state):
    squares, mixed, size = (lane_sum(total[row : row + 1]) for row in (13, 14, 15))
    alpha2 = size + epsilon
    alpha = jnp.sqrt(alpha2)
    rest = jnp.maximum(squares / alpha2 - 2.0 * mixed + alpha2 * state[0:1], 0.0)
    beta2 = rest + epsilon
    return alpha, jnp.sqrt(beta2), rest / beta2


def step_kernel(step, width, slots, chips, star_count, *refs):
    packs, tables, att2s, ints = refs[0:2], refs[2:4], refs[4:6], refs[6:8]
    sum_ref, ya_ref, refs = refs[8], refs[9], refs[10:]
    if step > 0:
        state_ref, old_z_ref, old_g_ref, old_u_ref, old_s_ref, old_gs_ref = refs[:6]
        refs = refs[6:]
    else:
        keep, refs = refs[:2], refs[2:]
    gathered, refs = refs[:-8], refs[-8:]
    send_ref, state_out, z_ref, g_ref, u_ref, s_ref, gs_ref, spread_ref = refs
    me = lax.axis_index("tm")
    chip, core = me // 2, me % 2
    high = STARS_DEV // LANES
    comps = sum_ref.shape[0] // high
    blocks = 8
    total = tree_sum([ref[...] for ref in gathered])
    back = jnp.concatenate([sum_ref[...], total], axis=0)
    base = comps * high
    pieces = [total[place : place + 1] for place in range(8)]
    att_back_rows = total[8:13]
    forward, starts, coefs, indices = [], [], [], []
    for half in range(2):
        starts.append(ints[half][slots * 8 :])
        own = jnp.where(core == half, att_back_rows[0:3], att_back_rows[2:5])
        part = att_forward(own, att2s[half][...], starts[half], width)
        part = part + ya_ref[half * 8 : half * 8 + 8]
        coefs.append([packs[half].at[slot * 8 : slot * 8 + 8] for slot in range(slots)])
        indices.append([ints[half].at[slot * 8 : slot * 8 + 8] for slot in range(slots)])
        for slot in range(slots):
            part = part + coefs[half][slot][...] * table_pick(pieces, indices[half][slot][...])
        forward.append(part)
    forward = jnp.concatenate(forward, axis=0)
    if step == 0:
        squares = lane_sum(total[13:14])
        beta2 = squares + epsilon
        beta = jnp.sqrt(beta2)
        at = pl.ds(pl.multiple_of(chip * kept(chips, keep[0])[0], 8), 8)
        u = jnp.concatenate([ref[at] for ref in keep], axis=0) / beta
        g = back / beta
        z = g
        gs = forward / beta
        both = gs
        state_out[...] = jnp.concatenate(
            [squares / beta2, beta, jnp.zeros((14, LANES), f32)], axis=0
        )
    else:
        state = state_ref[...]
        alpha, beta, left2 = next_bidiagonal(total, state)
        u = (old_s_ref[...] / alpha - alpha * old_u_ref[...]) / beta
        g = (back / alpha - alpha * old_g_ref[...]) / beta
        z = g - (beta / alpha) * old_z_ref[...]
        gs = (forward / alpha - alpha * old_gs_ref[...]) / beta
        both = gs - (beta / alpha) * old_s_ref[...]
        pieces = [left2, state[1 : 1 + step], beta, jnp.zeros((7 - step, LANES), f32)]
        pieces += [state[9 : 8 + step]] if step > 1 else []
        pieces += [alpha, jnp.zeros((7 - step, LANES), f32)]
        state_out[...] = jnp.concatenate(pieces, axis=0)
    z_ref[...] = z
    g_ref[...] = g
    u_ref[...] = u
    gs_ref[...] = gs
    s_ref[...] = both
    inst_rows = z[base : base + 8]
    att_rows = z[base + 8 : base + 13]
    rows = [both[0:8], both[8:16]]
    insts, atts = [], []
    for half in range(2):
        if step < ITERS - 1:
            insts.append(
                inst_back(rows[half], coefs[half], indices[half], tables[half], spread_ref.at[half])
            )
            atts.append(att_back(rows[half], att2s[half][...], starts[half], width))

    def squared(value):
        return jnp.sum(value * value, axis=0, keepdims=True)

    size = squared(z[:base]) * (1.0 / chips) + squared(att_rows[:4]) * (1.0 / star_count)
    size = size + squared(inst_rows) * (1.0 / (star_count * chips))
    mixed = [jnp.sum(rows[half] * u[half * 8 : half * 8 + 8], axis=0, keepdims=True) for half in range(2)]
    scalars = [squared(rows[0]) + squared(rows[1]), mixed[0] + mixed[1], size]
    if step == ITERS - 1:
        send_ref[...] = jnp.concatenate([jnp.zeros((5, LANES), f32)] + scalars, axis=0)
        return
    send_ref[0:16] = jnp.where(core == 0, both, jnp.concatenate(rows[::-1], axis=0))
    send_ref[16:24] = insts[0] + insts[1]
    send_ref[24:32] = jnp.concatenate([chip_parts(core, *atts)] + scalars, axis=0)


def last_kernel(comps, share, star_count, state_ref, *refs):
    gathered, refs = refs[: -ITERS - 3], refs[-ITERS - 3 :]
    z_refs = refs[:ITERS]
    astro_ref, att_ref, inst_ref = refs[ITERS:]
    high = STARS_DEV // LANES
    me = lax.axis_index("tm")
    total = tree_sum([ref[...] for ref in gathered])
    total = jnp.concatenate([jnp.zeros((8, LANES), f32), total], axis=0)
    state = state_ref[...]
    alpha, beta, _ = next_bidiagonal(total, state)
    betas = [state[1 + k : 2 + k] for k in range(ITERS)] + [beta]
    alphas = [state[9 + k : 10 + k] for k in range(ITERS - 1)] + [alpha]
    rho_bar, phi_bar = alphas[0], betas[0]
    weights = [jnp.zeros((1, LANES), f32)] * ITERS
    search = [jnp.zeros((1, LANES), f32)] * ITERS
    search[0] = 1.0 / alphas[0]
    for k in range(ITERS):
        rho = jnp.sqrt(rho_bar * rho_bar + betas[k + 1] * betas[k + 1])
        cosine, sine = rho_bar / rho, betas[k + 1] / rho
        phi = cosine * phi_bar
        phi_bar = sine * phi_bar
        weights = [x + phi / rho * w for x, w in zip(weights, search)]
        if k + 1 < ITERS:
            theta = sine * alphas[k + 1]
            rho_bar = -cosine * alphas[k + 1]
            search = [-(theta / rho) * w for w in search]
            search[k + 1] = 1.0 / alphas[k + 1]
    base = comps * high
    tiles = share // LANES

    def mix(read):
        total = weights[0] * read(z_refs[0])
        for k in range(1, ITERS):
            total = total + weights[k] * read(z_refs[k])
        return total

    for comp in range(comps):
        for tile in range(tiles):
            at = comp * high + me * tiles + tile
            astro_ref[comp : comp + 1, tile * LANES : (tile + 1) * LANES] = mix(
                lambda ref: ref[pl.ds(at, 1)]
            )
    inst_ref[...] = mix(lambda ref: ref[base : base + 8])
    rows = ATT_DEV // LANES
    att_ref[...] = mix(lambda ref: ref[pl.ds(base + 8 + (me % 2) * rows, rows)])


def call(kernel, name, out, args, scratch=(), space=pltpu.VMEM):
    vmem = pl.BlockSpec(memory_space=pltpu.VMEM)
    return pl.pallas_call(
        kernel,
        name=name,
        out_shape=[jax.ShapeDtypeStruct(shape, dtype) for shape, dtype in out],
        in_specs=[pl.BlockSpec(memory_space=space)] * len(args),
        out_specs=[vmem] * len(out),
        scratch_shapes=list(scratch),
        compiler_params=pltpu.CompilerParams(vmem_limit_bytes=VMEM_LIMIT),
    )(*args)


def direct(value, axis, gaps):
    count = lax.axis_size(axis)
    return [value] + [
        lax.ppermute(value, axis, [(i, i ^ gap) for i in range(count)]) for gap in gaps
    ]


def exchange(value, axis):
    tm_count, star_count = lax.axis_size("tm"), lax.axis_size("star")
    got = [value]
    for gap in range(1, star_count if axis == "star" else tm_count // 2):
        steps = []
        for star in range(star_count):
            for tm in range(tm_count):
                far = (star ^ gap, tm ^ 1) if axis == "star" else (star, tm ^ (2 * gap + 1))
                steps.append((star * tm_count + tm, far[0] * tm_count + far[1]))
        got.append(lax.ppermute(value, ("star", "tm"), steps))
    return got


def rows_type(rows):
    return ((rows, LANES), f32)


def per_device(astro_coef, star_index, att_coef, att_start, inst_coef, inst_index, observed):
    tm_count, star_count = lax.axis_size("tm"), lax.axis_size("star")
    comps = astro_coef.shape[1]
    slots = inst_coef.shape[1]
    blocks, width, height = att_coef.shape[1:]
    share = STARS_DEV // tm_count
    high = STARS_DEV // LANES
    chips = tm_count // 2
    args = [
        observed.reshape(blocks, height),
        astro_coef.reshape(comps, blocks, height),
        star_index.reshape(blocks, height),
        att_coef.reshape(blocks * width, height),
        att_start,
        inst_coef.reshape(slots, blocks, height),
        inst_index.reshape(slots, blocks, height),
    ]
    long = slots * blocks * height
    extra = 8 * comps + 8
    spread = pltpu.VMEM((16, long), bf16)
    prepared = [((LANES, long), bf16), ((2 * blocks * width, height), bf16),
                ((8 * slots + 8, LANES), jnp.int32)]
    here = [pltpu.with_memory_space_constraint(arg, pltpu.HBM) for arg in args]
    send, pack, *mine = call(
        functools.partial(first_kernel, width),
        "first",
        [((24 + extra, LANES), f32), ((16 * slots + 8 + blocks * width, LANES), f32)] + prepared,
        here,
        [pltpu.VMEM(arg.shape, arg.dtype) for arg in args if arg is not args[3]]
        + [spread, pltpu.SemaphoreType.DMA((len(args),))],
        pl.ANY,
    )
    state = z = g = u = rows = gs = None
    solutions = []
    group_type = rows_type(16)
    for step in range(ITERS):
        wide = (2 * comps * high, blocks * height)
        sums_type = rows_type(comps * high)
        pair = rows_type(2 * blocks)
        got = exchange(send, "tm")
        if step == 0:
            (gathered,) = call(
                functools.partial(first_chip_kernel, chips),
                "chip",
                [rows_type(chips * (24 + extra))],
                got,
            )
            keep = direct(gathered, "tm", [1])
            table_type = ((LANES, chips * blocks * height), bf16)
            own_sums, own_table = call(
                functools.partial(astro_own_kernel, chips),
                "astro_own",
                [sums_type, table_type],
                [gathered],
                [pltpu.VMEM(wide, bf16)],
            )
            keep[1], own_sums, late_pack = lax.optimization_barrier((keep[1], own_sums, pack))
            (group,) = call(
                functools.partial(first_group_kernel, chips), "group", [group_type], keep
            )
            _, other_pack = direct(late_pack, "tm", [1])
            theirs = call(
                functools.partial(prepare_kernel, slots, blocks, width),
                "prepare",
                prepared,
                [other_pack],
            )
            basics = [pack, other_pack] + [value for both in zip(mine, theirs) for value in both]
        else:
            all_rows, group = call(
                functools.partial(group_kernel, chips),
                "group",
                [rows_type(16 * chips), group_type],
                got,
            )
        across = exchange(group, "star")
        if step == 0:
            sums, ya, other_table = call(
                functools.partial(astro_other_kernel, chips),
                "astro",
                [sums_type, pair, table_type],
                keep + [own_sums],
                [pltpu.VMEM(wide, bf16)],
            )
        else:
            sums, ya = call(
                functools.partial(astro_kernel, chips),
                "astro",
                [sums_type, pair],
                keep + [own_table, other_table, all_rows],
                [pltpu.VMEM((2,) + wide, bf16)],
            )
        tall = ((comps * high + 16, LANES), f32)
        older = keep if step == 0 else [state, z, g, u, rows, gs]
        send, state, z, g, u, rows, gs = call(
            functools.partial(step_kernel, step, width, slots, chips, star_count),
            "step",
            [rows_type(32 if step < ITERS - 1 else 8), group_type, tall, tall, pair, pair,
             pair],
            basics + [sums, ya] + older + across,
            [pltpu.VMEM((2, 16, long), bf16)],
        )
        solutions.append(z)
    (send,) = call(sum_kernel, "sum", [rows_type(8)], exchange(send, "tm"))
    across = exchange(send, "star")
    out_astro, out_att, out_inst = call(
        functools.partial(last_kernel, comps, share, star_count),
        "last",
        [((comps, share), f32), ((ATT_DEV // LANES, LANES), f32), ((NINST // LANES, LANES), f32)],
        [state] + across + solutions,
    )
    return out_astro, out_att.reshape(-1), out_inst.reshape(-1)


def solution(mesh):
    return jax.shard_map(
        per_device,
        mesh=mesh,
        in_specs=(
            P("star", None, "tm"),
            P("star", "tm"),
            P("star", "tm", None, None),
            P("star", "tm"),
            P("star", None, "tm"),
            P("star", None, "tm"),
            P("star", "tm"),
        ),
        out_specs=(P(None, ("star", "tm")), P("tm"), P()),
        check_vma=False,
    )
```
